32 devices in a mesh: seq: 8 (over y, x, core), tp: 4 (over z).
Axes of the slice: x: 2, y: 2, z: 4, core: 2. Of those that a mesh axis runs over, the one named last changes fastest.
Arguments:
- tokens: bfloat16 [4, 4096, 1024], P(None, 'seq'), may hold values from -6 to 6
- lengths: int32 [4], replicated, may hold values from 1024 to 4096, as said below
- attention_norm_gain: float32 [1024], replicated, may hold values from 0.5 to 1.5
- query_weight: bfloat16 [1024, 1024], P(None, 'tp'), may hold values from -0.1875 to 0.1875
- key_weight: bfloat16 [1024, 1024], P(None, 'tp'), may hold values from -0.1875 to 0.1875
- value_weight: bfloat16 [1024, 1024], P(None, 'tp'), may hold values from -0.1875 to 0.1875
- output_weight: bfloat16 [1024, 1024], P('tp'), may hold values from -0.75 to 0.75
- state_key_weight: bfloat16 [1024, 1024], P(None, 'tp'), may hold values from -0.1875 to 0.1875
- state_value_weight: bfloat16 [1024, 1024], P(None, 'tp'), may hold values from -0.1875 to 0.1875
- state_coefficient: float32 [1024, 16], P(('seq', 'tp')), may hold values from -0.06 to 0.06
- state_rate: float32 [1024, 16], P(('seq', 'tp')), may hold values from 0.0002 to 0.03
- feedforward_norm_gain: float32 [1024], replicated, may hold values from 0.5 to 1.5
- hidden_weight: bfloat16 [1024, 4096], P(None, 'tp'), may hold values from -0.1875 to 0.1875
- return_weight: bfloat16 [4096, 1024], P('tp'), may hold values from -0.09375 to 0.09375
- cotangent: bfloat16 [4, 4096, 1024], P(None, 'seq'), may hold values from -6 to 6
Outputs:
- output: bfloat16 [4, 4096, 1024], P(None, 'seq')
- grad_tokens: float32 [4, 4096, 1024], P(None, 'seq')
- grad_attn_gain: float32 [1024], replicated
- grad_query_weight: float32 [1024, 1024], P(None, 'tp')
- grad_key_weight: float32 [1024, 1024], P(None, 'tp')
- grad_value_weight: float32 [1024, 1024], P(None, 'tp')
- grad_output_weight: float32 [1024, 1024], P('tp')
- grad_state_key_weight: float32 [1024, 1024], P(None, 'tp')
- grad_state_value_weight: float32 [1024, 1024], P(None, 'tp')
- grad_state_coefficient: float32 [1024, 16], P(('seq', 'tp'))
- grad_state_rate: float32 [1024, 16], P(('seq', 'tp'))
- grad_mlp_gain: float32 [1024], replicated
- grad_hidden_weight: float32 [1024, 4096], P(None, 'tp')
- grad_return_weight: float32 [4096, 1024], P('tp')
The draws below stay inside these ranges and needn't reach their ends.
Inputs may be any that keep to these rules, and one draw needn't show every extreme that they name: `lengths`: valid length of each sequence; one of the 4 sequences, which one drawn from the seed, has the full length 4096; positions at or past a length are padding.
All inputs are finite; a program needn't handle non-finite values.
Results may differ from the reference program's by a relative error of at most 0.023.
Values may be sent and summed in bfloat16 or wider, within the bound.
No kernel may reach another device: no remote copies, remote signals or barrier semaphores. Data moves between devices by JAX's collectives and lax.ppermute only.
A program may use at most 256 MiB of HBM per device.

```python
import math
import jax
import jax.numpy as jnp
from jax import lax

D = 1024
HEADS = 8
DH = 128
FF = 4096
NSTATE = 16
BLOCK = 512
CTX = 128
MINLEN = 1024
SEQS = 4
LMAX = 4096


def draw_lengths(key, part):
    key = jax.random.fold_in(key, 7)
    pick_key, size_key = jax.random.split(key)
    longest = jax.random.randint(pick_key, (), 0, SEQS)
    drawn = jax.random.randint(size_key, (SEQS,), MINLEN, LMAX + 1)
    return jnp.where(jnp.arange(SEQS) == longest, LMAX, drawn).astype(jnp.int32)


def steps_of(stream_key, shape, shards, smallest, largest):
    factor_of = 1.0
    for axis_at, shards_of in shards:
        heights = jax.random.uniform(jax.random.fold_in(jax.random.fold_in(stream_key, 6), axis_at), (shards_of,), jnp.float32, smallest / len(shards), largest / len(shards))
        factor_of = factor_of * jnp.repeat(jnp.exp(heights), shape[axis_at] // shards_of).reshape((-1,) + (1,) * (len(shape) - 1 - axis_at))
    return factor_of


def gaussian(rng, shape, scale, reach, cuts=(), kind=jnp.bfloat16):
    level = steps_of(rng, shape, cuts, -0.22, 0.18) if cuts else 1.0
    result = jax.random.normal(rng, shape, jnp.float32) * scale * level
    return jnp.minimum(jnp.maximum(result, -reach), reach).astype(kind)


def setup_inputs(seed: int = 0) -> dict:
    arg_keys = jax.random.split(jax.random.key(seed), 16)
    tokens = gaussian(arg_keys[0], (SEQS, LMAX, D), 1.0, 6.0, ((1, 8),))
    lengths = draw_lengths(jax.random.fold_in(arg_keys[15], 71), 0)
    attention_norm_gain = jnp.clip(1.0 + 0.1 * jax.random.normal(arg_keys[2], (D,), jnp.float32), 0.5, 1.5)
    query_weight = gaussian(arg_keys[3], (D, HEADS * DH), D ** -0.5, 0.1875, ((1, 4),))
    key_weight = gaussian(arg_keys[4], (D, HEADS * DH), D ** -0.5, 0.1875, ((1, 4),))
    value_weight = gaussian(arg_keys[5], (D, HEADS * DH), D ** -0.5, 0.1875, ((1, 4),))
    output_weight = gaussian(arg_keys[6], (HEADS * DH, D), (HEADS * DH // 16) ** -0.5, 0.75, ((0, 4),))
    state_key_weight = gaussian(arg_keys[7], (D, HEADS * DH), D ** -0.5, 0.1875, ((1, 4),))
    state_value_weight = gaussian(arg_keys[8], (D, HEADS * DH), D ** -0.5, 0.1875, ((1, 4),))
    state_coefficient = gaussian(arg_keys[9], (D, NSTATE), 0.01, 0.06, ((0, 32),), jnp.float32)
    state_rate = jnp.clip(jnp.exp(math.log(0.03) - 5.0106353 * jax.random.uniform(arg_keys[10], (D, NSTATE), jnp.float32) ** steps_of(arg_keys[10], (D, NSTATE), ((0, 32),), -0.2, 0.2)), 0.0002, 0.03)
    feedforward_norm_gain = jnp.clip(1.0 + 0.1 * jax.random.normal(arg_keys[11], (D,), jnp.float32), 0.5, 1.5)
    hidden_weight = gaussian(arg_keys[12], (D, FF), D ** -0.5, 0.1875, ((1, 4),))
    return_weight = gaussian(arg_keys[13], (FF, D), FF ** -0.5, 0.09375, ((0, 4),))
    cotangent = gaussian(arg_keys[14], (SEQS, LMAX, D), 1.0, 6.0, ((1, 8),))
    return {"tokens": tokens, "lengths": lengths, "attention_norm_gain": attention_norm_gain, "query_weight": query_weight, "key_weight": key_weight, "value_weight": value_weight, "output_weight": output_weight, "state_key_weight": state_key_weight, "state_value_weight": state_value_weight, "state_coefficient": state_coefficient, "state_rate": state_rate, "feedforward_norm_gain": feedforward_norm_gain, "hidden_weight": hidden_weight, "return_weight": return_weight, "cotangent": cotangent}


EPS = 1e-05
NEGATIVE = -1e+30
HIGH_ACCURACY = lax.Precision.HIGHEST

@jax.custom_vjp
def low(v):
    return lax.optimization_barrier(v.astype(jnp.bfloat16)).astype(jnp.float32)

@jax.custom_vjp
def low_back(v):
    return v

def low_keep(v):
    return (low(v), None)

def low_pass(kept, grad):
    return (grad,)

def back_keep(v):
    return (v, None)

def back_low(kept, grad):
    return (low(grad),)
low.defvjp(low_keep, low_pass)
low_back.defvjp(back_keep, back_low)

def forward_and_backward(value):
    return low(low_back(value))

def normalize(values):
    center = values - lax.optimization_barrier(jnp.mean(values, axis=-1, keepdims=True))
    return center * lax.rsqrt(lax.optimization_barrier(jnp.mean(center * center, axis=-1, keepdims=True)) + EPS)

def kernel_rows(kernel_coefficient, kernel_decay_rate, seq_len):
    offsets = jnp.arange(seq_len).astype(kernel_coefficient.dtype)
    return jnp.einsum('cn,cnk->ck', kernel_coefficient, jnp.exp(-kernel_decay_rate[:, :, None] * offsets), precision=HIGH_ACCURACY)

def one_sequence(tokens, length, kernel, layer_parameters):
    attention_norm_gain, query_matrix, key_matrix, value_matrix, output_matrix, state_key_matrix, state_value_matrix, feedforward_norm_gain, hidden_matrix, return_matrix = layer_parameters
    seq_len = tokens.shape[0]
    blocks = seq_len // BLOCK
    length_mask = (jnp.arange(seq_len) < length).astype(tokens.dtype)[:, None]
    attn_input = low(normalize(tokens) * attention_norm_gain)
    signal = low_back(attn_input * length_mask)
    spectrum = jnp.fft.rfft(signal.T, n=2 * seq_len) * jnp.fft.rfft(kernel, n=2 * seq_len)
    convolved = jnp.fft.irfft(spectrum, n=2 * seq_len)[:, :seq_len].T
    block_tails = convolved.reshape(blocks, BLOCK, -1)[:, BLOCK - CTX:, :]
    context_carry = forward_and_backward(jnp.concatenate([jnp.zeros_like(block_tails[:1]), block_tails[:-1]], axis=0))
    queries = forward_and_backward(jnp.dot(attn_input, query_matrix, precision=HIGH_ACCURACY))
    token_keys = forward_and_backward(jnp.dot(attn_input, key_matrix, precision=HIGH_ACCURACY))
    token_values = forward_and_backward(jnp.dot(attn_input, value_matrix, precision=HIGH_ACCURACY))
    context_state_keys = forward_and_backward(jnp.einsum('ftl,ly->fty', context_carry, state_key_matrix, precision=HIGH_ACCURACY))
    state_values = forward_and_backward(jnp.einsum('ftl,ly->fty', context_carry, state_value_matrix, precision=HIGH_ACCURACY))
    query_heads = queries.reshape(blocks, BLOCK, HEADS, DH)
    all_keys = jnp.concatenate([token_keys.reshape(blocks, BLOCK, HEADS * DH), context_state_keys], axis=1).reshape(blocks, BLOCK + CTX, HEADS, DH)
    all_values = jnp.concatenate([token_values.reshape(blocks, BLOCK, HEADS * DH), state_values], axis=1).reshape(blocks, BLOCK + CTX, HEADS, DH)
    raw_scores = jnp.einsum('jqhd,jkhd->jhqk', query_heads, all_keys, precision=HIGH_ACCURACY) * DH ** (-0.5)
    scores = low_back(raw_scores)
    causal = jnp.arange(BLOCK)[:, None] >= jnp.arange(BLOCK)[None, :]
    causal = jnp.broadcast_to(causal, (blocks, BLOCK, BLOCK))
    context_ok = jnp.broadcast_to((jnp.arange(blocks) > 0)[:, None, None], (blocks, BLOCK, CTX))
    allowed = jnp.concatenate([causal, context_ok], axis=-1)
    scores = jnp.where(allowed[:, None], scores, NEGATIVE)
    attn_probs = low(jax.nn.softmax(scores, axis=-1))
    head_mix = jnp.einsum('jhqk,jkhd->jqhd', attn_probs, all_values, precision=HIGH_ACCURACY)
    head_mix = forward_and_backward(head_mix.reshape(seq_len, HEADS * DH))
    residual = tokens + low_back(jnp.dot(head_mix, output_matrix, precision=HIGH_ACCURACY))
    mlp_input = low(normalize(residual) * feedforward_norm_gain)
    pre_act = low_back(jnp.dot(mlp_input, hidden_matrix, precision=HIGH_ACCURACY))
    activated = low(jax.nn.gelu(pre_act, approximate=False))
    mlp_out = low_back(jnp.dot(activated, return_matrix, precision=HIGH_ACCURACY))
    return (residual + mlp_out) * length_mask

def reference(tokens, lengths, attention_norm_gain, query_weight, key_weight, value_weight, output_weight, state_key_weight, state_value_weight, state_coefficient, state_rate, feedforward_norm_gain, hidden_weight, return_weight, cotangent):
    seq_len = tokens.shape[1]
    checkpointed = jax.checkpoint(one_sequence)

    def forward_pass(complete_tokens, attention_norm_gain, query_matrix, key_matrix, value_matrix, output_matrix, state_key_matrix, state_value_matrix, kernel_coefficient, kernel_decay_rate, feedforward_norm_gain, hidden_matrix, return_matrix):
        kernel = kernel_rows(kernel_coefficient, kernel_decay_rate, seq_len)
        layer_parameters = (attention_norm_gain, query_matrix, key_matrix, value_matrix, output_matrix, state_key_matrix, state_value_matrix, feedforward_norm_gain, hidden_matrix, return_matrix)

        def per_sequence(seq_pair):
            return checkpointed(seq_pair[0], seq_pair[1], kernel, layer_parameters)
        return lax.map(per_sequence, (complete_tokens, lengths))
    primal = (tokens.astype(jnp.float32), attention_norm_gain, query_weight.astype(jnp.float32), key_weight.astype(jnp.float32), value_weight.astype(jnp.float32), output_weight.astype(jnp.float32), state_key_weight.astype(jnp.float32), state_value_weight.astype(jnp.float32), state_coefficient, state_rate, feedforward_norm_gain, hidden_weight.astype(jnp.float32), return_weight.astype(jnp.float32))
    output, pullback = jax.vjp(forward_pass, *primal)
    gradients = pullback(cotangent.astype(jnp.float32))
    return (output.astype(jnp.bfloat16), gradients[0], gradients[1], gradients[2], gradients[3], gradients[4], gradients[5], gradients[6], gradients[7], gradients[8], gradients[9], gradients[10], gradients[11], gradients[12])
```

```python
from functools import partial
import math

import jax
import jax.numpy as jnp
from jax import lax
from jax.experimental import pallas as pl
from jax.experimental.pallas import tpu as pltpu
from jax.sharding import PartitionSpec as P

DH = 128
CTX = 128
EPS = 1e-05
NEGATIVE = -1e30
F32 = jnp.float32
BF16 = jnp.bfloat16


def normalize(values):
    center = values - jnp.mean(values, axis=-1, keepdims=True)
    inverse = lax.rsqrt(jnp.mean(center * center, axis=-1, keepdims=True) + EPS)
    return (center * inverse, inverse)


def norm_back(normed, inverse, grad_normed):
    mean_grad = jnp.mean(grad_normed, axis=-1, keepdims=True)
    mean_cross = jnp.mean(grad_normed * normed, axis=-1, keepdims=True)
    return inverse * (grad_normed - mean_grad - normed * mean_cross)


def flip(value, mask):
    count = lax.axis_size("seq")
    return lax.ppermute(value, "seq", [(i, i ^ mask) for i in range(count)])


def shifted(value, steps):
    count = lax.axis_size("seq")
    first, last = (max(0, -steps), min(count, count - steps))
    return lax.ppermute(value, "seq", [(i, i + steps) for i in range(first, last)])


def line_gather(value):
    count = lax.axis_size("tp")
    place = lax.axis_index("tp")
    lefts, rights = [value], [value]
    for k in range(1, count):
        lefts.append(lax.ppermute(lefts[-1], "tp", [(i, i + 1) for i in range(k - 1, count - 1)]))
        rights.append(
            lax.ppermute(rights[-1], "tp", [(i, i - 1) for i in range(1, count - k + 1)])
        )
    return [value] + [
        jnp.where(place >= j, lefts[j], rights[count - j]) for j in range(1, count)
    ]


def line_reduce(chunks):
    count = lax.axis_size("tp")
    add = lambda a, b: a if b is None else (a.astype(F32) + b.astype(F32)).astype(BF16)
    going, coming = None, None
    for k in range(1, count):
        going = lax.ppermute(add(chunks[k], going), "tp", [(i, i + 1) for i in range(k)])
        coming = lax.ppermute(
            add(chunks[count - k], coming), "tp", [(i, i - 1) for i in range(count - k, count)]
        )
    return (chunks[0].astype(F32) + going.astype(F32) + coming.astype(F32)).astype(BF16)


def plane_bits(reverse):
    count = lax.axis_size("seq") // 2
    bits = [1 << b for b in range(count.bit_length() - 1)]
    return bits[::-1] if reverse else bits


def plane_gather(value, reverse):
    held = {0: value}
    for bit in plane_bits(reverse):
        held.update({p | bit: flip(v, 2 * bit) for p, v in list(held.items())})
    return held


def plane_reduce(pieces, reverse):
    held = dict(pieces)
    for bit in plane_bits(reverse):
        for p in [p for p in held if p & bit]:
            got = flip(held.pop(p), 2 * bit)
            held[p ^ bit] = (held[p ^ bit].astype(F32) + got.astype(F32)).astype(BF16)
    return held[0]


def scan_in(decay_ref, u_ref, state_ref, moment_ref):
    decay = decay_ref[...]

    def step(t, carry):
        h, m = carry
        return decay * h + u_ref[t], decay * (m + h)

    zero = jnp.zeros(decay.shape, F32)
    h, m = lax.fori_loop(0, u_ref.shape[0], step, (zero, zero))
    state_ref[...] = h
    moment_ref[...] = m


def scan_out(decay_ref, gain_ref, start_ref, u_ref, y_ref):
    decay, gain = decay_ref[...], gain_ref[...]

    def step(t, h):
        h = decay * h + u_ref[t]
        y_ref[t] = jnp.sum(gain * h, axis=0)
        return h

    lax.fori_loop(0, u_ref.shape[0], step, start_ref[...])


def scan_back_in(decay_ref, g_ref, state_ref):
    decay = decay_ref[...]
    last = g_ref.shape[0] - 1

    def step(t, lam):
        return decay * (lam + g_ref[last - t])

    state_ref[...] = lax.fori_loop(0, last + 1, step, jnp.zeros(decay.shape, F32))


def scan_back_out(decay_ref, gain_ref, end_ref, start_ref, u_ref, g_ref, y_ref, gh_ref, gm_ref):
    decay, gain = decay_ref[...], gain_ref[...]
    rows, count = y_ref.shape[0], g_ref.shape[0]

    def empty(t, lam):
        y_ref[rows - 1 - t] = jnp.sum(gain * lam, axis=0)
        return decay * lam

    def full(t, lam):
        lam = lam + g_ref[count - 1 - t]
        y_ref[count - 1 - t] = jnp.sum(gain * lam, axis=0)
        return decay * lam

    lam = lax.fori_loop(0, rows - count, empty, end_ref[...])
    lax.fori_loop(0, count, full, lam)

    def again(t, carry):
        h, m, gh, gm = carry
        h, m = decay * h + u_ref[t], decay * (m + h)
        g = g_ref[t]
        return h, m, gh + g * h, gm + g * m

    zero = jnp.zeros(decay.shape, F32)
    _, _, gh, gm = lax.fori_loop(0, count, again, (start_ref[...], zero, zero, zero))
    gh_ref[...] = gh
    gm_ref[...] = gm


def call(kernel, outs, *operands):
    return pl.pallas_call(
        kernel,
        out_shape=[jax.ShapeDtypeStruct(shape, dtype) for shape, dtype in outs],
        compiler_params=pltpu.CompilerParams(vmem_limit_bytes=44 * 2**20),
    )(*operands)


def tiles(values):
    return values.astype(F32).reshape(values.shape[0], values.shape[1] // 128, 128)


def dot(a, b, dims):
    return lax.dot_general(a, b, (dims, ((), ())), preferred_element_type=F32)


NN = ((1,), (0,))
NT = ((1,), (1,))
TN = ((0,), (0,))


def body(
    tokens,
    lengths,
    attention_norm_gain,
    query_weight,
    key_weight,
    value_weight,
    output_weight,
    state_key_weight,
    state_value_weight,
    state_coefficient,
    state_rate,
    feedforward_norm_gain,
    hidden_weight,
    return_weight,
    cotangent,
):
    sequences, block_len, features = tokens.shape
    seq_count = lax.axis_size("seq")
    tp_count = lax.axis_size("tp")
    seq_index = lax.axis_index("seq")
    tp_index = lax.axis_index("tp")
    planes = seq_count // 2
    copies = tp_count // sequences
    sequence = tp_index // copies
    head_cols = query_weight.shape[1]
    hidden_cols = hidden_weight.shape[1]
    heads = head_cols * tp_count // DH
    head_rows = head_cols // seq_count
    hidden_rows = hidden_cols // seq_count
    scale = DH ** (-0.5)

    shard_a = [query_weight.T, key_weight.T, value_weight.T]
    shard_b = [state_key_weight.T, state_value_weight.T, output_weight]
    shard_m = [hidden_weight.T, return_weight]

    def head_slice(shard, relative):
        other = seq_index ^ relative
        at = (other & 1) * planes + (other >> 1)
        return lax.dynamic_slice_in_dim(shard, at * head_rows, head_rows, 0)

    def hidden_slice(shard, relative):
        return lax.dynamic_slice_in_dim(
            shard, (seq_index ^ relative) * hidden_rows, hidden_rows, 0
        )

    def gather_heads(shards, reverse):
        mine = jnp.stack([head_slice(w, 0) for w in shards])
        line = jnp.stack(line_gather(mine)[1:])
        plane = plane_gather(line, reverse)
        other = {p: flip(v, 1) for p, v in plane.items()}
        far = jnp.stack(
            [jnp.stack([group[p] for p in range(planes)]) for group in (plane, other)]
        )
        far = jnp.transpose(far, (3, 2, 0, 1, 4, 5))
        own = jnp.stack(
            [
                jnp.concatenate([head_slice(w, 2 * p + c) for c in range(2) for p in range(planes)])
                for w in shards
            ]
        )
        far = far.reshape(len(shards), (tp_count - 1) * head_cols, features)
        return jnp.concatenate([own, far], axis=1)

    def gather_hidden(shard, reverse):
        line = line_gather(hidden_slice(shard, 0))
        plane = plane_gather(jnp.concatenate(line[1:]), reverse)
        return jnp.concatenate(
            [
                piece
                for p in range(planes)
                for piece in (hidden_slice(shard, 2 * p), plane[p])
            ]
        )

    wq, wk, wv = gather_heads(shard_a, False)
    wsk, wsv, wo = gather_heads(shard_b, True)
    wh = gather_hidden(shard_m[0], False)
    wr = gather_hidden(shard_m[1], True)

    own_tokens = lax.dynamic_index_in_dim(tokens, sequence, 0, keepdims=False)
    own_cot = lax.dynamic_index_in_dim(cotangent, sequence, 0, keepdims=False)
    length = lax.dynamic_index_in_dim(lengths, sequence, 0, keepdims=False)
    before = shifted(own_tokens[block_len - CTX :], 1)
    positions = seq_index * block_len - CTX + jnp.arange(block_len + CTX)
    live = ((positions < length) & (positions >= 0)).astype(F32)[:, None]
    valid = live[CTX:]
    inputs = own_tokens.astype(F32)
    normed_in, inverse_in = normalize(inputs)
    attn_input = (normed_in * attention_norm_gain).astype(BF16)
    early = (normalize(before.astype(F32))[0] * attention_norm_gain).astype(BF16)
    window = jnp.concatenate([early, attn_input[: block_len - CTX]]).astype(F32) * live[:block_len]
    signal = tiles(window)

    both = jnp.stack([state_rate, state_coefficient])
    both = lax.all_gather(both, ("seq", "tp"), axis=1, tiled=True)
    states = both.shape[2]
    both = jnp.transpose(both, (0, 2, 1)).reshape(2, states, features // 128, 128)
    rate, gain = both[0], both[1]
    decay = jnp.exp(-rate)
    grid = rate.shape
    local_state, local_moment = call(scan_in, [(grid, F32)] * 2, decay, signal)
    start = 0.0
    for m in range(1, seq_count):
        start = start + jnp.exp(-rate * (block_len * (m - 1))) * shifted(local_state, m)
    (context,) = call(
        scan_out, [((CTX,) + grid[1:], F32)], decay, gain, start, signal[:CTX]
    )
    context = context.reshape(CTX, features).astype(BF16)

    queries = dot(attn_input, wq, NT).astype(BF16)
    token_keys = dot(attn_input, wk, NT).astype(BF16)
    token_values = dot(attn_input, wv, NT).astype(BF16)
    state_keys = dot(context, wsk, NT).astype(BF16)
    state_values = dot(context, wsv, NT).astype(BF16)
    query_heads = queries.reshape(block_len, heads, DH)
    key_heads = jnp.concatenate([token_keys, state_keys]).reshape(-1, heads, DH)
    value_heads = jnp.concatenate([token_values, state_values]).reshape(-1, heads, DH)
    causal = jnp.arange(block_len)[:, None] >= jnp.arange(block_len)[None, :]
    allowed = jnp.concatenate([causal, jnp.broadcast_to(seq_index > 0, (block_len, CTX))], axis=1)
    raw = jnp.einsum("qhd,khd->hqk", query_heads, key_heads, preferred_element_type=F32) * scale
    scores = jnp.where(allowed, raw, NEGATIVE)
    row_max = jnp.max(scores, axis=-1, keepdims=True)
    exp_scores = jnp.exp(scores - row_max)
    row_total = jnp.sum(exp_scores, axis=-1, keepdims=True)
    probs_full = exp_scores / row_total
    attn_probs = probs_full.astype(BF16)
    head_mix = jnp.einsum("hqk,khd->qhd", attn_probs, value_heads, preferred_element_type=F32)
    head_mix = head_mix.reshape(block_len, heads * DH).astype(BF16)
    residual = inputs + dot(head_mix, wo, NN)
    normed_mid, inverse_mid = normalize(residual)
    mlp_input = (normed_mid * feedforward_norm_gain).astype(BF16)

    grad_out = own_cot.astype(F32) * valid
    grad_out_b = grad_out.astype(BF16)
    mlp_rows = jnp.concatenate([mlp_input, flip(mlp_input, 1)])
    out_rows = jnp.concatenate([grad_out_b, flip(grad_out_b, 1)])
    pre_act = dot(mlp_rows, wh, NT)
    activated, gelu_back = jax.vjp(partial(jax.nn.gelu, approximate=False), pre_act)
    activated = activated.astype(BF16)
    mlp_part = dot(activated, wr, NN)
    grad_act = dot(out_rows, wr, NT)
    grad_pre = gelu_back(grad_act)[0].astype(BF16)
    mid_part = dot(grad_pre, wh, NN)
    grad_mid = mid_part[:block_len] + flip(mid_part[block_len:].astype(BF16), 1).astype(F32)
    mlp_out = mlp_part[:block_len] + flip(mlp_part[block_len:].astype(BF16), 1).astype(F32)
    output = ((residual + mlp_out) * valid).astype(BF16)
    output_line = line_gather(output)
    grad_return = dot(activated, out_rows, TN).astype(BF16)
    grad_hidden = dot(grad_pre, mlp_rows, TN).astype(BF16)

    def reduce_hidden(grad, reverse):
        grad = grad.reshape(planes, tp_count * hidden_rows, features)
        mine = plane_reduce({p: grad[p] for p in range(planes)}, reverse)
        mine = mine.reshape(tp_count, hidden_rows, features)
        return line_reduce([mine[j] for j in range(tp_count)])

    sum_hidden = reduce_hidden(grad_hidden, False)
    sum_return = reduce_hidden(grad_return, True)

    grad_mlp_gain = jnp.sum(grad_mid * normed_mid, axis=0)
    grad_resid = grad_out + norm_back(normed_mid, inverse_mid, grad_mid * feedforward_norm_gain)
    grad_resid_b = grad_resid.astype(BF16)
    grad_heads = dot(grad_resid_b, wo, NT).astype(BF16).reshape(block_len, heads, DH)
    grad_probs = jnp.einsum("qhd,khd->hqk", grad_heads, value_heads, preferred_element_type=F32)
    delta = jnp.sum(probs_full * grad_probs, axis=-1, keepdims=True)
    grad_scores = (probs_full * (grad_probs - delta)).astype(BF16)
    grad_queries = (
        jnp.einsum("hqk,khd->qhd", grad_scores, key_heads, preferred_element_type=F32) * scale
    )
    grad_keys_all = (
        jnp.einsum("hqk,qhd->khd", grad_scores, query_heads, preferred_element_type=F32) * scale
    )
    grad_values_all = jnp.einsum(
        "hqk,qhd->khd", attn_probs, grad_heads, preferred_element_type=F32
    )
    wide = heads * DH
    grad_queries = grad_queries.reshape(block_len, wide).astype(BF16)
    grad_keys_all = grad_keys_all.reshape(block_len + CTX, wide).astype(BF16)
    grad_values_all = grad_values_all.reshape(block_len + CTX, wide).astype(BF16)
    grad_token_keys, grad_state_keys = grad_keys_all[:block_len], grad_keys_all[block_len:]
    grad_token_values, grad_state_values = grad_values_all[:block_len], grad_values_all[block_len:]
    grad_context = (
        dot(grad_state_keys, wsk, NN) + dot(grad_state_values, wsv, NN)
    ).astype(BF16)

    grad_conv = tiles(grad_context)
    (local_back,) = call(scan_back_in, [(grid, F32)], decay, grad_conv)
    end = 0.0
    for m in range(1, seq_count):
        end = end + jnp.exp(-rate * (block_len * (m - 1))) * shifted(local_back, -m)
    grad_signal, grad_gain, grad_moment = call(
        scan_back_out,
        [((block_len,) + grid[1:], F32), (grid, F32), (grid, F32)],
        decay,
        gain,
        end,
        start,
        signal[:CTX],
        grad_conv,
    )
    end_moment = block_len * jnp.exp(-rate * block_len) * start + local_moment
    grad_rate = -gain * (grad_moment + end * end_moment)
    grad_signal = grad_signal.reshape(block_len, features).astype(BF16)
    grad_signal = jnp.concatenate([grad_signal[CTX:], shifted(grad_signal[:CTX], -1)])

    grad_in = (
        dot(grad_queries, wq, NN)
        + dot(grad_token_keys, wk, NN)
        + dot(grad_token_values, wv, NN)
        + grad_signal.astype(F32) * valid
    )
    grad_attn_gain = jnp.sum(grad_in * normed_in, axis=0)
    grad_tokens = grad_resid + norm_back(normed_in, inverse_in, grad_in * attention_norm_gain)
    tokens_line = line_gather(grad_tokens.astype(BF16))

    def split(values):
        return values.reshape(values.shape[0], tp_count, 2, head_cols // 2)

    def both_rows(values):
        values = split(values)
        mine, other = values[:, :, 0], values[:, :, 1]
        joined = jnp.concatenate([mine, flip(other, 1)])
        return joined.reshape(joined.shape[0], -1)

    def both_full(values):
        return jnp.concatenate([values, flip(values, 1)])

    x_rows, c_rows, r_rows = both_full(attn_input), both_full(context), both_full(grad_resid_b)
    grads_a = [
        dot(both_rows(grad_queries), x_rows, TN),
        dot(both_rows(grad_token_keys), x_rows, TN),
        dot(both_rows(grad_token_values), x_rows, TN),
    ]
    grads_b = [
        dot(both_rows(grad_state_keys), c_rows, TN),
        dot(both_rows(grad_state_values), c_rows, TN),
        dot(both_rows(head_mix), r_rows, TN),
    ]

    def reduce_heads(grads, reverse):
        stack = jnp.stack([g.astype(BF16) for g in grads]).reshape(
            len(grads), tp_count, planes, head_rows, features
        )
        mine = plane_reduce(
            {p: jnp.transpose(stack[:, :, p], (1, 0, 2, 3)) for p in range(planes)}, reverse
        )
        return line_reduce([mine[j] for j in range(tp_count)])

    sum_a = reduce_heads(grads_a, False)
    sum_b = reduce_heads(grads_b, True)

    def spread(value, reverse):
        plane = plane_gather(value, reverse)
        other = {p: flip(v, 1) for p, v in plane.items()}
        return jnp.stack([(plane, other)[i & 1][i >> 1] for i in range(seq_count)])

    def ordered(stack):
        return [
            lax.dynamic_index_in_dim(stack, seq_index ^ i, 0, keepdims=False)
            for i in range(seq_count)
        ]

    fix = 1.0 / copies

    def head_grads(value, reverse):
        parts = ordered(spread(value, reverse))
        parts = [parts[2 * p + c] for c in range(2) for p in range(planes)]
        return jnp.concatenate(parts, axis=1).astype(F32) * fix

    def hidden_grads(value, reverse):
        return jnp.concatenate(ordered(spread(value, reverse))).astype(F32) * fix

    full_a = head_grads(sum_a, False)
    full_b = head_grads(sum_b, True)
    full_hidden = hidden_grads(sum_hidden, False)
    full_return = hidden_grads(sum_return, True)

    gains = lax.psum(jnp.stack([grad_attn_gain, grad_mlp_gain]), ("seq", "tp")) * fix
    kernel_grads = jnp.stack([grad_gain, grad_rate]).reshape(2, states, features)
    kernel_grads = lax.psum_scatter(
        jnp.transpose(kernel_grads, (2, 0, 1)).reshape(features, 2 * states),
        ("seq", "tp"),
        scatter_dimension=0,
        tiled=True,
    )
    kernel_grads = kernel_grads * fix

    def lined(line, dtype):
        stack = jnp.stack(line)
        return jnp.stack(
            [
                lax.dynamic_index_in_dim(
                    stack, (tp_index - b * copies) % tp_count, 0, keepdims=False
                )
                for b in range(sequences)
            ]
        ).astype(dtype)

    return (
        lined(output_line, BF16),
        lined(tokens_line, F32),
        gains[0],
        full_a[0].T,
        full_a[1].T,
        full_a[2].T,
        full_b[2],
        full_b[0].T,
        full_b[1].T,
        kernel_grads[:, :states],
        kernel_grads[:, states:],
        gains[1],
        full_hidden.T,
        full_return,
    )


LOG2E = math.log2(math.e)
SCALE = DH ** (-0.5)


def params(limit=44):
    return pltpu.CompilerParams(vmem_limit_bytes=limit * 2**20)


def like(shape, dtype=BF16):
    return jax.ShapeDtypeStruct(shape, dtype)


def whole(shape):
    return pl.BlockSpec(shape, lambda *_: (0,) * len(shape))


def launch(kernel, place, grid, in_specs, out_specs, outs, operands, scratch=(), flops=0):
    return pl.pallas_call(
        kernel,
        grid_spec=pltpu.PrefetchScalarGridSpec(
            num_scalar_prefetch=1,
            grid=grid,
            in_specs=in_specs,
            out_specs=out_specs,
            scratch_shapes=list(scratch),
        ),
        out_shape=outs,
        compiler_params=params(),
        cost_estimate=pl.CostEstimate(flops=flops, bytes_accessed=0, transcendentals=0),
    )(place, *operands)


def cycle(value, steps):
    count = lax.axis_size("tp")
    return lax.ppermute(value, "tp", [(i, (i + steps) % count) for i in range(count)])


def pack_heads(place, wq, wk, wv, wsk, wsv, wo, a_ref, b_ref, turned):
    core, chip = place[0] & 1, place[0] >> 1
    rows = a_ref.shape[2]

    def cut(p):
        return pl.ds(pl.multiple_of((chip ^ p) * rows, rows), rows)

    for out, refs in ((a_ref, (wq, wk, wv)), (b_ref, (wsk, wsv))):
        for w, ref in enumerate(refs):
            turned[...] = ref[...].astype(F32).T
            for p in range(4):
                out[p, w] = turned[cut(p), :].astype(BF16)
    turned[...] = wo[...].astype(F32)
    for p in range(4):
        b_ref[p, 2] = turned[cut(p), :].astype(BF16)


def pack_hidden(place, wh, wr, h_ref, r_ref, turned):
    chip = place[0] >> 1
    rows = h_ref.shape[1]
    for out, turn in ((h_ref, True), (r_ref, False)):
        turned[...] = wh[...].astype(F32).T if turn else wr[...].astype(F32)
        for p in range(4):
            cut = pl.ds(pl.multiple_of((chip ^ p) * rows, rows), rows)
            out[p] = turned[cut, :].astype(BF16)


def load_heads(j, own, far, into, base):
    rows = own.shape[2]

    @pl.when(j == 0)
    def _():
        for p in range(4):
            for w in range(3):
                into[base + w, p * rows : (p + 1) * rows] = own[p, w]

    @pl.when(j > 0)
    def _():
        for p in range(4):
            for w in range(3):
                into[base + w, p * rows : (p + 1) * rows] = far[p][0, w]


def masked(raw, r, block):
    n = raw.shape[1]
    column = lax.broadcasted_iota(jnp.int32, raw.shape, 1)
    row = lax.broadcasted_iota(jnp.int32, raw.shape, 0)
    keep = (column - (n - 128) <= row) & ((column >= CTX) | (block > 0))
    return jnp.where(keep, raw * (SCALE * LOG2E), NEGATIVE)


def attend(place, x0, x1, c0, c1, own_a, own_b, a0, a1, a2, a3, b0, b1, b2, b3,
           part0, part1, q_ref, k_ref, v_ref, s_ref, o_ref, lse_ref,
           weight, keys, values, total):
    j = pl.program_id(0)
    load_heads(j, own_a, (a0, a1, a2, a3), weight, 0)
    load_heads(j, own_b, (b0, b1, b2, b3), weight, 3)
    rows = x0.shape[0]

    @pl.when(j == 0)
    def _():
        total[...] = jnp.zeros_like(total)

    qkv_w = weight[0:3].reshape(3 * DH, -1)
    st_w = weight[3:5].reshape(2 * DH, -1)
    for half, (x, c) in enumerate(((x0, c0), (x1, c1))):
        base = half * rows
        qkv = dot(x[...], qkv_w, NT).astype(BF16)
        q_ref[base : base + rows] = qkv[:, :DH]
        k_ref[base : base + rows] = qkv[:, DH : 2 * DH]
        v_ref[base : base + rows] = qkv[:, 2 * DH :]
        state = dot(c[...], st_w, NT).astype(BF16)
        s_ref[half * CTX : (half + 1) * CTX] = state
        keys[half, 0:CTX] = state[:, :DH]
        values[half, 0:CTX] = state[:, DH:]
        keys[half, CTX:] = qkv[:, DH : 2 * DH]
        values[half, CTX:] = qkv[:, 2 * DH :]
    for half in range(2):
        block = place[0] ^ half
        base = half * rows
        for r in range(rows // 128):
            saved = slice(base + r * 128, base + (r + 1) * 128)
            n = CTX + (r + 1) * 128
            scores = masked(dot(q_ref[saved], keys[half, 0:n], NT), r, block)
            top = jnp.max(scores, axis=1, keepdims=True)
            power = jnp.exp2(scores - top)
            summed = jnp.sum(power, axis=1, keepdims=True)
            lse_ref[0, saved] = top + jnp.log2(summed)
            probs = (power * (1.0 / summed)).astype(BF16)
            o_ref[saved] = dot(probs, values[half, 0:n], NN).astype(BF16)
    for half in range(2):
        base = half * rows
        total[base : base + rows] += dot(o_ref[base : base + rows], weight[5], NN)

    @pl.when(j == pl.num_programs(0) - 1)
    def _():
        part0[...] = total[0:rows].astype(part0.dtype)
        part1[...] = total[rows:].astype(part1.dtype)


def attend_back(place, g0, g1, own_a, own_b, a0, a1, a2, a3, b0, b1, b2, b3,
                q_ref, k_ref, v_ref, s_ref, lse_ref,
                in0, in1, ctx0, ctx1, d_ref, ds_ref,
                weight, keys, values, heads, grad_k, grad_v, total, ctx_total):
    j = pl.program_id(0)
    load_heads(j, own_a, (a0, a1, a2, a3), weight, 0)
    load_heads(j, own_b, (b0, b1, b2, b3), weight, 3)
    rows = g0.shape[0]

    @pl.when(j == 0)
    def _():
        total[...] = jnp.zeros_like(total)
        ctx_total[...] = jnp.zeros_like(ctx_total)

    qkv_w = weight[0:3].reshape(3 * DH, -1)
    st_w = weight[3:5].reshape(2 * DH, -1)
    for half, g in enumerate((g0, g1)):
        base = half * rows
        keys[half, 0:CTX] = s_ref[half * CTX : (half + 1) * CTX, :DH]
        values[half, 0:CTX] = s_ref[half * CTX : (half + 1) * CTX, DH:]
        keys[half, CTX:] = k_ref[base : base + rows]
        values[half, CTX:] = v_ref[base : base + rows]
        heads[half] = dot(g[...], weight[5], NT).astype(BF16)
    for half in range(2):
        block = place[0] ^ half
        base = half * rows
        for r in reversed(range(rows // 128)):
            saved = slice(base + r * 128, base + (r + 1) * 128)
            n = CTX + (r + 1) * 128
            q = q_ref[saved]
            own = heads[half, r * 128 : (r + 1) * 128]
            probs = jnp.exp2(masked(dot(q, keys[half, 0:n], NT), r, block) - lse_ref[0, saved])
            grad = dot(own, values[half, 0:n], NT)
            delta = jnp.sum(probs * grad, axis=1, keepdims=True)
            scores = (probs * (grad - delta)).astype(BF16)
            d_ref[saved, 0:DH] = (dot(scores, keys[half, 0:n], NN) * SCALE).astype(BF16)
            to_k = dot(scores, q, TN)
            to_v = dot(probs.astype(BF16), own, TN)
            if r == rows // 128 - 1:
                grad_k[half, 0:n] = to_k
                grad_v[half, 0:n] = to_v
            else:
                grad_k[half, 0:n] += to_k
                grad_v[half, 0:n] += to_v
    for half in range(2):
        base = half * rows
        d_ref[base : base + rows, DH : 2 * DH] = (grad_k[half, CTX:] * SCALE).astype(BF16)
        d_ref[base : base + rows, 2 * DH :] = grad_v[half, CTX:].astype(BF16)
        state = slice(half * CTX, (half + 1) * CTX)
        ds_ref[state, :DH] = (grad_k[half, 0:CTX] * SCALE).astype(BF16)
        ds_ref[state, DH:] = grad_v[half, 0:CTX].astype(BF16)
        ctx_total[state] += dot(ds_ref[state], st_w, NN)
        total[base : base + rows] += dot(d_ref[base : base + rows], qkv_w, NN)

    @pl.when(j == pl.num_programs(0) - 1)
    def _():
        in0[...] = total[0:rows].astype(in0.dtype)
        in1[...] = total[rows:].astype(in1.dtype)
        ctx0[...] = ctx_total[0:CTX].astype(ctx0.dtype)
        ctx1[...] = ctx_total[CTX:].astype(ctx1.dtype)


def attend_weights(place, x0, x1, c0, c1, g0, g1, d_ref, ds_ref, o_ref, keep_a, send_a, keep_b, send_b):
    rows = x0.shape[0]
    cut = keep_a.shape[3]
    to_qkv = (dot(d_ref[0:rows], x0[...], TN) + dot(d_ref[rows:], x1[...], TN)).astype(BF16)
    to_state = (dot(ds_ref[0:CTX], c0[...], TN) + dot(ds_ref[CTX:], c1[...], TN)).astype(BF16)
    to_out = (dot(o_ref[0:rows], g0[...], TN) + dot(o_ref[rows:], g1[...], TN)).astype(BF16)
    spots_a = {0: (keep_a, 0), 2: (keep_a, 1), 1: (send_a, 0), 3: (send_a, 1)}
    spots_b = {0: (keep_b, 0), 1: (keep_b, 1), 2: (send_b, 0), 3: (send_b, 1)}
    for p in range(4):
        out, at = spots_a[p]
        for w in range(3):
            out[at, 0, w] = to_qkv[w * DH + p * cut : w * DH + (p + 1) * cut]
        out, at = spots_b[p]
        for w in range(2):
            out[at, 0, w] = to_state[w * DH + p * cut : w * DH + (p + 1) * cut]
        out[at, 0, 2] = to_out[p * cut : (p + 1) * cut]


def gelu_parts(x):
    size = jnp.abs(x) * math.sqrt(0.5)
    bell = jnp.exp2(x * x * (-0.5 * LOG2E))
    t = 1.0 / (1.0 + 0.3275911 * size)
    poly = 1.061405429 * t - 1.453152027
    poly = poly * t + 1.421413741
    poly = poly * t - 0.284496736
    poly = poly * t + 0.254829592
    tail = 0.5 * poly * t * bell
    return jnp.where(x >= 0, 1.0 - tail, tail), bell * (1.0 / math.sqrt(2.0 * math.pi))


def load_hidden(j, own, far, into):
    rows = own.shape[1]

    @pl.when(j == 0)
    def _():
        for p in range(4):
            into[p * rows : (p + 1) * rows] = own[p]

    @pl.when(j > 0)
    def _():
        for p in range(4):
            into[p * rows : (p + 1) * rows] = far[p][0]


def feed(place, m0, m1, g0, g1, own_h, own_r, h0, h1, h2, h3, r0, r1, r2, r3,
         mlp0, mlp1, mid0, mid1, act_ref, pre_ref, wh, wr, mlp, mid):
    j = pl.program_id(0)
    load_hidden(j, own_h, (h0, h1, h2, h3), wh)
    load_hidden(j, own_r, (r0, r1, r2, r3), wr)
    rows = m0.shape[0]

    @pl.when(j == 0)
    def _():
        mlp[...] = jnp.zeros_like(mlp)
        mid[...] = jnp.zeros_like(mid)

    for half, (m, g) in enumerate(((m0, g0), (m1, g1))):
        saved = slice(half * rows, (half + 1) * rows)
        pre = dot(m[...], wh[...], NT)
        back = dot(g[...], wr[...], NT)
        part, bell = gelu_parts(pre)
        act_ref[saved] = (pre * part).astype(BF16)
        pre_ref[saved] = (back * (part + pre * bell)).astype(BF16)
        mlp[saved] += dot(act_ref[saved], wr[...], NN)
        mid[saved] += dot(pre_ref[saved], wh[...], NN)

    @pl.when(j == pl.num_programs(0) - 1)
    def _():
        mlp0[...] = mlp[0:rows].astype(mlp0.dtype)
        mlp1[...] = mlp[rows:].astype(mlp1.dtype)
        mid0[...] = mid[0:rows].astype(mid0.dtype)
        mid1[...] = mid[rows:].astype(mid1.dtype)


def feed_weights(place, m0, m1, g0, g1, act_ref, pre_ref, keep_h, send_h, keep_r, send_r):
    rows = m0.shape[0]
    cut = keep_h.shape[2]
    to_h = (dot(pre_ref[0:rows], m0[...], TN) + dot(pre_ref[rows:], m1[...], TN)).astype(BF16)
    to_r = (dot(act_ref[0:rows], g0[...], TN) + dot(act_ref[rows:], g1[...], TN)).astype(BF16)
    spots_h = {0: (keep_h, 0), 2: (keep_h, 1), 1: (send_h, 0), 3: (send_h, 1)}
    spots_r = {0: (keep_r, 0), 1: (keep_r, 1), 2: (send_r, 0), 3: (send_r, 1)}
    for p in range(4):
        out, at = spots_h[p]
        out[at, 0] = to_h[p * cut : (p + 1) * cut]
        out, at = spots_r[p]
        out[at, 0] = to_r[p * cut : (p + 1) * cut]


def live_rows(place, count):
    at = place[0] * (count * pl.num_programs(0)) + pl.program_id(0) * count
    position = at + lax.broadcasted_iota(jnp.int32, (count, 1), 0)
    return (position < place[2]).astype(F32)


def middle(place, tokens, own, got, gain, residual, m_ref):
    value = tokens[0].astype(F32) + own[...] + got[...].astype(F32)
    residual[...] = value
    m_ref[...] = (normalize(value)[0] * gain[...]).astype(BF16)


def finish(place, residual, own, got, out):
    value = residual[...] + own[...] + got[...].astype(F32)
    out[...] = (value * live_rows(place, value.shape[0])).astype(BF16)


def middle_back(place, residual, own, got, cot, gain, grad, grad_b, sums):
    value = residual[...]
    normed, inverse = normalize(value)
    valid = live_rows(place, value.shape[0])
    back = own[...] + got[...].astype(F32)
    total = jnp.sum(back * normed, axis=0, keepdims=True)

    @pl.when(pl.program_id(0) == 0)
    def _():
        sums[...] = total

    @pl.when(pl.program_id(0) > 0)
    def _():
        sums[...] += total

    value = cot[0].astype(F32) * valid + norm_back(normed, inverse, back * gain[...])
    grad[...] = value
    grad_b[...] = value.astype(BF16)


def first_back(place, tokens, own, got, signal, grad, gain, out, sums):
    normed, inverse = normalize(tokens[0].astype(F32))
    valid = live_rows(place, out.shape[0])
    back = own[...] + got[...].astype(F32) + signal[...].astype(F32) * valid
    total = jnp.sum(back * normed, axis=0, keepdims=True)

    @pl.when(pl.program_id(0) == 0)
    def _():
        sums[...] = total

    @pl.when(pl.program_id(0) > 0)
    def _():
        sums[...] += total

    out[...] = (grad[...] + norm_back(normed, inverse, back * gain[...])).astype(BF16)


def unpack_heads(place, n0, n1, n2, n3, f0, f1, f2, f3, q, k, v, o, sk, sv, rows_ref):
    core, chip = place[0] & 1, place[0] >> 1
    cut = n0.shape[1]
    for w, out in ((0, q), (1, k), (2, v), (3, sk), (4, sv), (5, o)):
        for other, pieces in ((0, (n0, n1, n2, n3)), (1, (f0, f1, f2, f3))):
            for p, piece in enumerate(pieces):
                at = (core ^ other) * DH + (chip ^ p) * cut
                rows_ref[pl.ds(pl.multiple_of(at, cut), cut), :] = piece[w].astype(F32)
        out[...] = rows_ref[...] if out is o else rows_ref[...].T


def unpack_hidden(place, pieces, h, r):
    cut = pieces.shape[2]
    for i in range(8):
        at = ((i & 1) * 4 + (i >> 1)) * cut
        r[at : at + cut, :] = pieces[i, 1].astype(F32)
        h[:, at : at + cut] = pieces[i, 0].astype(F32).T


def add(a, b):
    return (a.astype(F32) + b.astype(F32)).astype(BF16)


def after(value, *earlier):
    return lax.optimization_barrier((value, *earlier))[0]


def states_around(local, rate, length, sign, first):
    group = local
    for m in (1, 2):
        group = group + jnp.exp(-rate * (length * m)) * shifted(local, sign * m)
    total = shifted(group, sign * first)
    for m in range(first + 3, 8, 3):
        total = total + jnp.exp(-rate * (length * (m - first))) * shifted(group, sign * m)
    return total


def scan_rows(decay_ref, gain_ref, late_ref, g_ref, y_ref, end_ref):
    decay, gain = decay_ref[...], gain_ref[...]
    rows, count = y_ref.shape[0], g_ref.shape[0]

    def full(t, lam):
        lam = lam + g_ref[count - 1 - t]
        y_ref[rows - 1 - t] = jnp.sum(gain * lam, axis=0)
        return decay * lam

    def empty(t, lam):
        y_ref[rows - count - 1 - t] = jnp.sum(gain * lam, axis=0)
        return decay * lam

    lam = lax.fori_loop(0, count, full, late_ref[...], unroll=8)
    end_ref[...] = lam
    lax.fori_loop(0, rows - count, empty, lam, unroll=8)


def scan_sums(decay_ref, start_ref, u_ref, g_ref, gh_ref, gm_ref):
    decay = decay_ref[...]

    def again(t, carry):
        h, m, gh, gm = carry
        h, m = decay * h + u_ref[t], decay * (m + h)
        g = g_ref[t]
        return h, m, gh + g * h, gm + g * m

    zero = jnp.zeros(decay.shape, F32)
    _, _, gh, gm = lax.fori_loop(0, u_ref.shape[0], again, (start_ref[...], zero, zero, zero))
    gh_ref[...] = gh
    gm_ref[...] = gm


def fast_body(
    tokens, lengths, attention_norm_gain, query_weight, key_weight, value_weight, output_weight,
    state_key_weight, state_value_weight, state_coefficient, state_rate, feedforward_norm_gain,
    hidden_weight, return_weight, cotangent,
):
    sequences, block_len, features = tokens.shape
    tp_count = lax.axis_size("tp")
    seq_index = lax.axis_index("seq")
    tp_index = lax.axis_index("tp")
    hidden_cols = hidden_weight.shape[1]
    cut = DH // 4
    wide = hidden_cols // 8
    length = lax.dynamic_index_in_dim(lengths, tp_index, 0, keepdims=False)
    place = jnp.stack([seq_index, tp_index, length]).astype(jnp.int32)

    column = pl.BlockSpec((features, DH), lambda i, place: (0, place[0] & 1))
    own_a, own_b = launch(
        pack_heads, place, (1,),
        [column] * 5 + [pl.BlockSpec((DH, features), lambda i, place: (place[0] & 1, 0))],
        [whole((4, 3, cut, features))] * 2,
        [like((4, 3, cut, features))] * 2,
        (query_weight, key_weight, value_weight, state_key_weight, state_value_weight, output_weight),
        [pltpu.VMEM((DH, features), F32)],
    )
    own_h, own_r = launch(
        pack_hidden, place, (1,),
        [
            pl.BlockSpec((features, hidden_cols // 2), lambda i, place: (0, place[0] & 1)),
            pl.BlockSpec((hidden_cols // 2, features), lambda i, place: (place[0] & 1, 0)),
        ],
        [whole((4, wide, features))] * 2,
        [like((4, wide, features))] * 2,
        (hidden_weight, return_weight),
        [pltpu.VMEM((hidden_cols // 2, features), F32)],
    )

    def line_of(own):
        return jnp.stack([cycle(own[0], j) for j in range(1, tp_count)])

    def plane_of(line, across):
        near = {2: flip(line, 2), 4: flip(line, 4)}
        return [line, near[2], near[4], flip(near[6 - across], across)]

    line_a, line_b, line_h, line_r = map(line_of, (own_a, own_b, own_h, own_r))
    far_a, far_b = plane_of(line_a, 2), plane_of(line_b, 4)
    far_h, far_r = plane_of(line_h, 2), plane_of(line_r, 4)

    own_tokens = lax.dynamic_index_in_dim(tokens, tp_index, 0, keepdims=False)
    own_cot = lax.dynamic_index_in_dim(cotangent, tp_index, 0, keepdims=False)
    before = shifted(own_tokens[block_len - CTX :], 1)
    positions = seq_index * block_len - CTX + jnp.arange(block_len + CTX)
    live = ((positions < length) & (positions >= 0)).astype(F32)[:, None]
    x = (normalize(own_tokens.astype(F32))[0] * attention_norm_gain).astype(BF16)
    x_other = flip(x, 1)
    grad_out = (own_cot.astype(F32) * live[CTX:]).astype(BF16)
    grad_out_other = flip(grad_out, 1)
    early = (normalize(before.astype(F32))[0] * attention_norm_gain).astype(BF16)
    signal = tiles(
        jnp.concatenate([early, x[: block_len - CTX]]).astype(F32) * live[:block_len]
    )

    states = state_rate.shape[1]
    channels = state_rate.shape[0]
    both = jnp.stack([state_rate, state_coefficient]).reshape(1, -1, 128)
    devices = features // channels
    both = lax.all_to_all(
        jnp.broadcast_to(both, (devices,) + both.shape[1:]), ("seq", "tp"), 0, 0
    )
    both = jnp.transpose(both.reshape(devices, 2, channels, states), (1, 3, 0, 2))
    both = both.reshape(2, states, features // 128, 128)
    rate, gain = both[0], both[1]
    decay = jnp.exp(-rate)
    grid = rate.shape
    local_state, local_moment = call(scan_in, [(grid, F32)] * 2, decay, signal)
    start = states_around(local_state, rate, block_len, 1, 1)
    (context,) = call(scan_out, [((CTX,) + grid[1:], F32)], decay, gain, start, signal[:CTX])
    context = context.reshape(CTX, features).astype(BF16)
    context_other = flip(context, 1)

    rows = 2 * block_len
    slots = tp_count
    own_spec = whole((4, 3, cut, features))
    far_spec = pl.BlockSpec(
        (1, 3, cut, features), lambda j, place: (jnp.maximum(j - 1, 0), 0, 0, 0)
    )
    full = whole((block_len, features))
    ctx_spec = whole((CTX, features))
    head = lambda n, width: pl.BlockSpec((n, width), lambda j, place: (0, j))
    lse_spec = pl.BlockSpec((1, rows, 1), lambda j, place: (j, 0, 0))
    weight_specs = [own_spec] * 2 + [far_spec] * 8
    weights = (own_a, own_b, *far_a, *far_b)
    part, part_other, q, k, v, state, mix, lse = launch(
        attend, place, (slots,),
        [full] * 2 + [ctx_spec] * 2 + weight_specs,
        [full] * 2 + [head(rows, DH)] * 3 + [head(2 * CTX, 2 * DH), head(rows, DH), lse_spec],
        [like((block_len, features), F32), like((block_len, features))]
        + [like((rows, slots * DH))] * 3
        + [like((2 * CTX, slots * 2 * DH)), like((rows, slots * DH)), like((slots, rows, 1), F32)],
        (after(x, line_h, line_r), x_other, context, context_other, *weights),
        [
            pltpu.VMEM((6, DH, features), BF16),
            pltpu.VMEM((2, CTX + block_len, DH), BF16),
            pltpu.VMEM((2, CTX + block_len, DH), BF16),
            pltpu.VMEM((rows, features), F32),
        ],
    )
    group = 128
    steps = block_len // group
    row_spec = pl.BlockSpec((group, features), lambda i, place: (i, 0))
    seq_spec = pl.BlockSpec((1, group, features), lambda i, place: (place[1], i, 0))
    gain_spec = whole((1, features))
    mid_gain = feedforward_norm_gain.reshape(1, -1)
    residual, m = launch(
        middle, place, (steps,),
        [seq_spec, row_spec, row_spec, gain_spec], [row_spec] * 2,
        [like((block_len, features), F32), like((block_len, features))],
        (tokens, part, flip(part_other, 1), mid_gain),
    )
    m_other = flip(m, 1)

    hidden_own = whole((4, wide, features))
    hidden_far = pl.BlockSpec(
        (1, wide, features), lambda j, place: (jnp.maximum(j - 1, 0), 0, 0)
    )
    chunk = 4 * wide
    mlp, mlp_other, mid, mid_other, act, pre = launch(
        feed, place, (slots,),
        [full] * 4 + [hidden_own] * 2 + [hidden_far] * 8,
        [full] * 4 + [head(rows, chunk)] * 2,
        [like((block_len, features), F32), like((block_len, features))] * 2
        + [like((rows, slots * chunk))] * 2,
        (m, m_other, grad_out, grad_out_other, own_h, own_r, *far_h, *far_r),
        [pltpu.VMEM((chunk, features), BF16)] * 2 + [pltpu.VMEM((rows, features), F32)] * 2,
    )
    mid_got, mlp_got = flip(mid_other, 1), flip(mlp_other, 1)
    (output,) = launch(
        finish, place, (steps,),
        [row_spec] * 3, [row_spec], [like((block_len, features))], (residual, mlp, mlp_got),
    )
    output_all = lax.all_gather(output, "tp")
    resid, resid_b, sums_mid = launch(
        middle_back, place, (steps,),
        [row_spec] * 3 + [seq_spec, gain_spec], [row_spec] * 2 + [gain_spec],
        [
            like((block_len, features), F32), like((block_len, features)),
            like((1, features), F32),
        ],
        (residual, mid, mid_got, cotangent, mid_gain),
    )
    resid_other = flip(resid_b, 1)
    grad_spec = pl.BlockSpec(
        (2, 1, wide, features), lambda j, place: (0, (place[1] - j + slots) % slots, 0, 0)
    )
    keep_h, send_h, keep_r, send_r = launch(
        feed_weights, place, (slots,),
        [full] * 4 + [head(rows, chunk)] * 2, [grad_spec] * 4,
        [like((2, slots, wide, features))] * 4,
        (m, m_other, grad_out, grad_out_other, act, after(pre, resid_b, output)),
    )

    grad_in, grad_in_other, grad_ctx, grad_ctx_other, d, ds = launch(
        attend_back, place, (slots,),
        [full] * 2 + weight_specs + [head(rows, DH)] * 3 + [head(2 * CTX, 2 * DH), lse_spec],
        [full] * 2 + [ctx_spec] * 2 + [head(rows, 3 * DH), head(2 * CTX, 2 * DH)],
        [
            like((block_len, features), F32), like((block_len, features)),
            like((CTX, features), F32), like((CTX, features)),
            like((rows, slots * 3 * DH)), like((2 * CTX, slots * 2 * DH)),
        ],
        (after(resid_b, keep_h), resid_other, *weights, q, k, v, state, lse),
        [
            pltpu.VMEM((6, DH, features), BF16),
            pltpu.VMEM((2, CTX + block_len, DH), BF16),
            pltpu.VMEM((2, CTX + block_len, DH), BF16),
            pltpu.VMEM((2, block_len, DH), BF16),
            pltpu.VMEM((2, CTX + block_len, DH), F32),
            pltpu.VMEM((2, CTX + block_len, DH), F32),
            pltpu.VMEM((rows, features), F32),
            pltpu.VMEM((2 * CTX, features), F32),
        ],
    )
    grad_ctx_got = flip(grad_ctx_other, 1)
    grad_in_got = flip(grad_in_other, 1)
    part_spec = pl.BlockSpec(
        (2, 1, 3, cut, features), lambda j, place: (0, (place[1] - j + slots) % slots, 0, 0, 0)
    )
    keep_a, send_a, keep_b, send_b = launch(
        attend_weights, place, (slots,),
        [full] * 2 + [ctx_spec] * 2 + [full] * 2
        + [head(rows, 3 * DH), head(2 * CTX, 2 * DH), head(rows, DH)],
        [part_spec] * 4,
        [like((2, slots, 3, cut, features))] * 4,
        (x, x_other, context, context_other, resid_b, resid_other, d, ds, mix),
    )

    grad_context = (grad_ctx + grad_ctx_got.astype(F32)).astype(BF16)
    grad_conv = tiles(grad_context)
    grad_later = tiles(shifted(grad_context, -1))
    (local_back,) = call(scan_back_in, [(grid, F32)], decay, grad_conv)
    late = states_around(local_back, rate, block_len, -1, 2)
    late = jnp.exp(-rate * (block_len - CTX)) * late
    grad_signal, end = call(
        scan_rows, [((block_len,) + grid[1:], F32), (grid, F32)], decay, gain, late, grad_later
    )
    grad_signal = grad_signal.reshape(block_len, features).astype(BF16)
    grad_gain, grad_moment = call(
        scan_sums, [(grid, F32)] * 2, decay, start, signal[:CTX], grad_conv
    )
    end_moment = block_len * jnp.exp(-rate * block_len) * start + local_moment
    grad_rate = -gain * (grad_moment + end * end_moment)
    grad_tokens, sums_in = launch(
        first_back, place, (steps,),
        [seq_spec] + [row_spec] * 4 + [gain_spec], [row_spec, gain_spec],
        [like((block_len, features)), like((1, features), F32)],
        (tokens, grad_in, grad_in_got, grad_signal, resid, attention_norm_gain.reshape(1, -1)),
    )

    def reduce(keep_first, send_first, keep_second, send_second, begin, then):
        got = after(flip(after(send_first, begin), 2), then)
        near, away = add(keep_first[0], got[0]), add(keep_first[1], got[1])
        first = (near, flip(away, 4))
        got = after(flip(after(send_second, begin), 4), then)
        near, away = add(keep_second[0], got[0]), add(keep_second[1], got[1])
        second = (near, flip(away, 2))
        chunks = jnp.stack([add(*first), add(*second)], axis=1)
        chunks = lax.all_to_all(after(chunks, grad_tokens), "tp", 0, 0)
        return jnp.sum(chunks.astype(F32), axis=0).astype(BF16)

    def regather(total):
        held = [total, flip(total, 2), flip(total, 4), flip(total, 6)]
        return held + [flip(value, 1) for value in held]

    pieces_m = lax.all_gather(reduce(keep_h, send_h, keep_r, send_r, resid_b, late), "seq")
    total_a = reduce(keep_a, send_a, keep_b, send_b, late, grad_tokens)
    pieces_a = regather(total_a.reshape(6, cut, features))
    grad_hidden, grad_return = launch(
        unpack_hidden, place, (1,),
        [whole((8, 2, wide, features))],
        [whole((features, hidden_cols)), whole((hidden_cols, features))],
        [like((features, hidden_cols), F32), like((hidden_cols, features), F32)],
        (pieces_m,),
    )
    grad_q, grad_k, grad_v, grad_o, grad_sk, grad_sv = launch(
        unpack_heads, place, (1,),
        [whole((6, cut, features))] * 8,
        [whole((features, 2 * DH))] * 3 + [whole((2 * DH, features))] + [whole((features, 2 * DH))] * 2,
        [like((features, 2 * DH), F32)] * 3
        + [like((2 * DH, features), F32)]
        + [like((features, 2 * DH), F32)] * 2,
        pieces_a,
        [pltpu.VMEM((2 * DH, features), F32)],
    )

    small = jnp.stack([grad_gain, grad_rate]).reshape(2, states, devices, channels)
    small = jnp.transpose(small, (2, 3, 0, 1)).reshape(devices, -1, 128)
    sums = jnp.concatenate([sums_in, sums_mid]).reshape(1, -1, 128)
    sums = jnp.broadcast_to(sums, (devices,) + sums.shape[1:])
    count = small.shape[1]
    small = jnp.sum(
        lax.all_to_all(jnp.concatenate([small, sums], axis=1), ("seq", "tp"), 0, 0), axis=0
    )
    kernel_grads = small[:count].reshape(channels, 2, states)
    gains = small[count:].reshape(2, features)

    line = line_gather(grad_tokens)
    stack = jnp.stack(line)
    grad_tokens = jnp.stack(
        [
            lax.dynamic_index_in_dim(stack, (tp_index - b) % tp_count, 0, keepdims=False)
            for b in range(sequences)
        ]
    ).astype(F32)
    return (
        output_all, grad_tokens, gains[0], grad_q, grad_k, grad_v, grad_o, grad_sk, grad_sv,
        kernel_grads[:, 0], kernel_grads[:, 1], gains[1], grad_hidden, grad_return,
    )


def choose(tokens, *others):
    query_weight = others[2]
    fits = (
        lax.axis_size("seq") == 8
        and lax.axis_size("tp") == tokens.shape[0]
        and query_weight.shape[1] == 2 * DH
        and others[11].shape[1] % 1024 == 0
        and tokens.shape[1] % 512 == 0
        and tokens.shape[2] == 1024
    )
    return (fast_body if fits else body)(tokens, *others)


def solution(mesh):
    rows = P(None, "seq", None)
    columns = P(None, "tp")
    heads = P("tp", None)
    channels = P(("seq", "tp"), None)
    return jax.shard_map(
        choose,
        mesh=mesh,
        in_specs=(
            rows, P(), P(), columns, columns, columns, heads, columns, columns,
            channels, channels, P(), columns, heads, rows,
        ),
        out_specs=(
            rows, rows, P(), columns, columns, columns, heads, columns, columns,
            channels, channels, P(), columns, heads,
        ),
        check_vma=False,
    )
```

```python
from functools import partial
import math

import jax
import jax.numpy as jnp
from jax import lax
from jax.experimental import pallas as pl
from jax.experimental.pallas import tpu as pltpu
from jax.sharding import PartitionSpec as P

DH = 128
CTX = 128
EPS = 1e-05
NEGATIVE = -1e30
F32 = jnp.float32
BF16 = jnp.bfloat16


def normalize(values):
    center = values - jnp.mean(values, axis=-1, keepdims=True)
    inverse = lax.rsqrt(jnp.mean(center * center, axis=-1, keepdims=True) + EPS)
    return (center * inverse, inverse)


def norm_back(normed, inverse, grad_normed):
    mean_grad = jnp.mean(grad_normed, axis=-1, keepdims=True)
    mean_cross = jnp.mean(grad_normed * normed, axis=-1, keepdims=True)
    return inverse * (grad_normed - mean_grad - normed * mean_cross)


def flip(value, mask):
    count = lax.axis_size("seq")
    return lax.ppermute(value, "seq", [(i, i ^ mask) for i in range(count)])


def shifted(value, steps):
    count = lax.axis_size("seq")
    first, last = (max(0, -steps), min(count, count - steps))
    return lax.ppermute(value, "seq", [(i, i + steps) for i in range(first, last)])


def line_gather(value):
    count = lax.axis_size("tp")
    place = lax.axis_index("tp")
    lefts, rights = [value], [value]
    for k in range(1, count):
        lefts.append(lax.ppermute(lefts[-1], "tp", [(i, i + 1) for i in range(k - 1, count - 1)]))
        rights.append(
            lax.ppermute(rights[-1], "tp", [(i, i - 1) for i in range(1, count - k + 1)])
        )
    return [value] + [
        jnp.where(place >= j, lefts[j], rights[count - j]) for j in range(1, count)
    ]


def line_reduce(chunks):
    count = lax.axis_size("tp")
    add = lambda a, b: a if b is None else (a.astype(F32) + b.astype(F32)).astype(BF16)
    going, coming = None, None
    for k in range(1, count):
        going = lax.ppermute(add(chunks[k], going), "tp", [(i, i + 1) for i in range(k)])
        coming = lax.ppermute(
            add(chunks[count - k], coming), "tp", [(i, i - 1) for i in range(count - k, count)]
        )
    return (chunks[0].astype(F32) + going.astype(F32) + coming.astype(F32)).astype(BF16)


def plane_bits(reverse):
    count = lax.axis_size("seq") // 2
    bits = [1 << b for b in range(count.bit_length() - 1)]
    return bits[::-1] if reverse else bits


def plane_gather(value, reverse):
    held = {0: value}
    for bit in plane_bits(reverse):
        held.update({p | bit: flip(v, 2 * bit) for p, v in list(held.items())})
    return held


def plane_reduce(pieces, reverse):
    held = dict(pieces)
    for bit in plane_bits(reverse):
        for p in [p for p in held if p & bit]:
            got = flip(held.pop(p), 2 * bit)
            held[p ^ bit] = (held[p ^ bit].astype(F32) + got.astype(F32)).astype(BF16)
    return held[0]


def scan_in(decay_ref, u_ref, state_ref, moment_ref):
    decay = decay_ref[...]

    def step(t, carry):
        h, m = carry
        return decay * h + u_ref[t], decay * (m + h)

    zero = jnp.zeros(decay.shape, F32)
    h, m = lax.fori_loop(0, u_ref.shape[0], step, (zero, zero))
    state_ref[...] = h
    moment_ref[...] = m


def scan_out(decay_ref, gain_ref, start_ref, u_ref, y_ref):
    decay, gain = decay_ref[...], gain_ref[...]

    def step(t, h):
        h = decay * h + u_ref[t]
        y_ref[t] = jnp.sum(gain * h, axis=0)
        return h

    lax.fori_loop(0, u_ref.shape[0], step, start_ref[...])


def scan_back_in(decay_ref, g_ref, state_ref):
    decay = decay_ref[...]
    last = g_ref.shape[0] - 1

    def step(t, lam):
        return decay * (lam + g_ref[last - t])

    state_ref[...] = lax.fori_loop(0, last + 1, step, jnp.zeros(decay.shape, F32))


def scan_back_out(decay_ref, gain_ref, end_ref, start_ref, u_ref, g_ref, y_ref, gh_ref, gm_ref):
    decay, gain = decay_ref[...], gain_ref[...]
    rows, count = y_ref.shape[0], g_ref.shape[0]

    def empty(t, lam):
        y_ref[rows - 1 - t] = jnp.sum(gain * lam, axis=0)
        return decay * lam

    def full(t, lam):
        lam = lam + g_ref[count - 1 - t]
        y_ref[count - 1 - t] = jnp.sum(gain * lam, axis=0)
        return decay * lam

    lam = lax.fori_loop(0, rows - count, empty, end_ref[...])
    lax.fori_loop(0, count, full, lam)

    def again(t, carry):
        h, m, gh, gm = carry
        h, m = decay * h + u_ref[t], decay * (m + h)
        g = g_ref[t]
        return h, m, gh + g * h, gm + g * m

    zero = jnp.zeros(decay.shape, F32)
    _, _, gh, gm = lax.fori_loop(0, count, again, (start_ref[...], zero, zero, zero))
    gh_ref[...] = gh
    gm_ref[...] = gm


def call(kernel, outs, *operands, us=5):
    return pl.pallas_call(
        kernel,
        out_shape=[jax.ShapeDtypeStruct(shape, dtype) for shape, dtype in outs],
        compiler_params=pltpu.CompilerParams(vmem_limit_bytes=42 * 2**20),
        cost_estimate=pl.CostEstimate(flops=int(us * 1.1e9), bytes_accessed=0, transcendentals=0),
    )(*operands)


def tiles(values):
    return values.astype(F32).reshape(values.shape[0], values.shape[1] // 128, 128)


def dot(a, b, dims):
    return lax.dot_general(a, b, (dims, ((), ())), preferred_element_type=F32)


NN = ((1,), (0,))
NT = ((1,), (1,))
TN = ((0,), (0,))


def body(
    tokens,
    lengths,
    attention_norm_gain,
    query_weight,
    key_weight,
    value_weight,
    output_weight,
    state_key_weight,
    state_value_weight,
    state_coefficient,
    state_rate,
    feedforward_norm_gain,
    hidden_weight,
    return_weight,
    cotangent,
):
    sequences, block_len, features = tokens.shape
    seq_count = lax.axis_size("seq")
    tp_count = lax.axis_size("tp")
    seq_index = lax.axis_index("seq")
    tp_index = lax.axis_index("tp")
    planes = seq_count // 2
    copies = tp_count // sequences
    sequence = tp_index // copies
    head_cols = query_weight.shape[1]
    hidden_cols = hidden_weight.shape[1]
    heads = head_cols * tp_count // DH
    head_rows = head_cols // seq_count
    hidden_rows = hidden_cols // seq_count
    scale = DH ** (-0.5)

    shard_a = [query_weight.T, key_weight.T, value_weight.T]
    shard_b = [state_key_weight.T, state_value_weight.T, output_weight]
    shard_m = [hidden_weight.T, return_weight]

    def head_slice(shard, relative):
        other = seq_index ^ relative
        at = (other & 1) * planes + (other >> 1)
        return lax.dynamic_slice_in_dim(shard, at * head_rows, head_rows, 0)

    def hidden_slice(shard, relative):
        return lax.dynamic_slice_in_dim(
            shard, (seq_index ^ relative) * hidden_rows, hidden_rows, 0
        )

    def gather_heads(shards, reverse):
        mine = jnp.stack([head_slice(w, 0) for w in shards])
        line = jnp.stack(line_gather(mine)[1:])
        plane = plane_gather(line, reverse)
        other = {p: flip(v, 1) for p, v in plane.items()}
        far = jnp.stack(
            [jnp.stack([group[p] for p in range(planes)]) for group in (plane, other)]
        )
        far = jnp.transpose(far, (3, 2, 0, 1, 4, 5))
        own = jnp.stack(
            [
                jnp.concatenate([head_slice(w, 2 * p + c) for c in range(2) for p in range(planes)])
                for w in shards
            ]
        )
        far = far.reshape(len(shards), (tp_count - 1) * head_cols, features)
        return jnp.concatenate([own, far], axis=1)

    def gather_hidden(shard, reverse):
        line = line_gather(hidden_slice(shard, 0))
        plane = plane_gather(jnp.concatenate(line[1:]), reverse)
        return jnp.concatenate(
            [
                piece
                for p in range(planes)
                for piece in (hidden_slice(shard, 2 * p), plane[p])
            ]
        )

    wq, wk, wv = gather_heads(shard_a, False)
    wsk, wsv, wo = gather_heads(shard_b, True)
    wh = gather_hidden(shard_m[0], False)
    wr = gather_hidden(shard_m[1], True)

    own_tokens = lax.dynamic_index_in_dim(tokens, sequence, 0, keepdims=False)
    own_cot = lax.dynamic_index_in_dim(cotangent, sequence, 0, keepdims=False)
    length = lax.dynamic_index_in_dim(lengths, sequence, 0, keepdims=False)
    before = shifted(own_tokens[block_len - CTX :], 1)
    positions = seq_index * block_len - CTX + jnp.arange(block_len + CTX)
    live = ((positions < length) & (positions >= 0)).astype(F32)[:, None]
    valid = live[CTX:]
    inputs = own_tokens.astype(F32)
    normed_in, inverse_in = normalize(inputs)
    attn_input = (normed_in * attention_norm_gain).astype(BF16)
    early = (normalize(before.astype(F32))[0] * attention_norm_gain).astype(BF16)
    window = jnp.concatenate([early, attn_input[: block_len - CTX]]).astype(F32) * live[:block_len]
    signal = tiles(window)

    both = jnp.stack([state_rate, state_coefficient])
    both = lax.all_gather(both, ("seq", "tp"), axis=1, tiled=True)
    states = both.shape[2]
    both = jnp.transpose(both, (0, 2, 1)).reshape(2, states, features // 128, 128)
    rate, gain = both[0], both[1]
    decay = jnp.exp(-rate)
    grid = rate.shape
    local_state, local_moment = call(scan_in, [(grid, F32)] * 2, decay, signal)
    start = 0.0
    for m in range(1, seq_count):
        start = start + jnp.exp(-rate * (block_len * (m - 1))) * shifted(local_state, m)
    (context,) = call(
        scan_out, [((CTX,) + grid[1:], F32)], decay, gain, start, signal[:CTX]
    )
    context = context.reshape(CTX, features).astype(BF16)

    queries = dot(attn_input, wq, NT).astype(BF16)
    token_keys = dot(attn_input, wk, NT).astype(BF16)
    token_values = dot(attn_input, wv, NT).astype(BF16)
    state_keys = dot(context, wsk, NT).astype(BF16)
    state_values = dot(context, wsv, NT).astype(BF16)
    query_heads = queries.reshape(block_len, heads, DH)
    key_heads = jnp.concatenate([token_keys, state_keys]).reshape(-1, heads, DH)
    value_heads = jnp.concatenate([token_values, state_values]).reshape(-1, heads, DH)
    causal = jnp.arange(block_len)[:, None] >= jnp.arange(block_len)[None, :]
    allowed = jnp.concatenate([causal, jnp.broadcast_to(seq_index > 0, (block_len, CTX))], axis=1)
    raw = jnp.einsum("qhd,khd->hqk", query_heads, key_heads, preferred_element_type=F32) * scale
    scores = jnp.where(allowed, raw, NEGATIVE)
    row_max = jnp.max(scores, axis=-1, keepdims=True)
    exp_scores = jnp.exp(scores - row_max)
    row_total = jnp.sum(exp_scores, axis=-1, keepdims=True)
    probs_full = exp_scores / row_total
    attn_probs = probs_full.astype(BF16)
    head_mix = jnp.einsum("hqk,khd->qhd", attn_probs, value_heads, preferred_element_type=F32)
    head_mix = head_mix.reshape(block_len, heads * DH).astype(BF16)
    residual = inputs + dot(head_mix, wo, NN)
    normed_mid, inverse_mid = normalize(residual)
    mlp_input = (normed_mid * feedforward_norm_gain).astype(BF16)

    grad_out = own_cot.astype(F32) * valid
    grad_out_b = grad_out.astype(BF16)
    mlp_rows = jnp.concatenate([mlp_input, flip(mlp_input, 1)])
    out_rows = jnp.concatenate([grad_out_b, flip(grad_out_b, 1)])
    pre_act = dot(mlp_rows, wh, NT)
    activated, gelu_back = jax.vjp(partial(jax.nn.gelu, approximate=False), pre_act)
    activated = activated.astype(BF16)
    mlp_part = dot(activated, wr, NN)
    grad_act = dot(out_rows, wr, NT)
    grad_pre = gelu_back(grad_act)[0].astype(BF16)
    mid_part = dot(grad_pre, wh, NN)
    grad_mid = mid_part[:block_len] + flip(mid_part[block_len:].astype(BF16), 1).astype(F32)
    mlp_out = mlp_part[:block_len] + flip(mlp_part[block_len:].astype(BF16), 1).astype(F32)
    output = ((residual + mlp_out) * valid).astype(BF16)
    output_line = line_gather(output)
    grad_return = dot(activated, out_rows, TN).astype(BF16)
    grad_hidden = dot(grad_pre, mlp_rows, TN).astype(BF16)

    def reduce_hidden(grad, reverse):
        grad = grad.reshape(planes, tp_count * hidden_rows, features)
        mine = plane_reduce({p: grad[p] for p in range(planes)}, reverse)
        mine = mine.reshape(tp_count, hidden_rows, features)
        return line_reduce([mine[j] for j in range(tp_count)])

    sum_hidden = reduce_hidden(grad_hidden, False)
    sum_return = reduce_hidden(grad_return, True)

    grad_mlp_gain = jnp.sum(grad_mid * normed_mid, axis=0)
    grad_resid = grad_out + norm_back(normed_mid, inverse_mid, grad_mid * feedforward_norm_gain)
    grad_resid_b = grad_resid.astype(BF16)
    grad_heads = dot(grad_resid_b, wo, NT).astype(BF16).reshape(block_len, heads, DH)
    grad_probs = jnp.einsum("qhd,khd->hqk", grad_heads, value_heads, preferred_element_type=F32)
    delta = jnp.sum(probs_full * grad_probs, axis=-1, keepdims=True)
    grad_scores = (probs_full * (grad_probs - delta)).astype(BF16)
    grad_queries = (
        jnp.einsum("hqk,khd->qhd", grad_scores, key_heads, preferred_element_type=F32) * scale
    )
    grad_keys_all = (
        jnp.einsum("hqk,qhd->khd", grad_scores, query_heads, preferred_element_type=F32) * scale
    )
    grad_values_all = jnp.einsum(
        "hqk,qhd->khd", attn_probs, grad_heads, preferred_element_type=F32
    )
    wide = heads * DH
    grad_queries = grad_queries.reshape(block_len, wide).astype(BF16)
    grad_keys_all = grad_keys_all.reshape(block_len + CTX, wide).astype(BF16)
    grad_values_all = grad_values_all.reshape(block_len + CTX, wide).astype(BF16)
    grad_token_keys, grad_state_keys = grad_keys_all[:block_len], grad_keys_all[block_len:]
    grad_token_values, grad_state_values = grad_values_all[:block_len], grad_values_all[block_len:]
    grad_context = (
        dot(grad_state_keys, wsk, NN) + dot(grad_state_values, wsv, NN)
    ).astype(BF16)

    grad_conv = tiles(grad_context)
    (local_back,) = call(scan_back_in, [(grid, F32)], decay, grad_conv)
    end = 0.0
    for m in range(1, seq_count):
        end = end + jnp.exp(-rate * (block_len * (m - 1))) * shifted(local_back, -m)
    grad_signal, grad_gain, grad_moment = call(
        scan_back_out,
        [((block_len,) + grid[1:], F32), (grid, F32), (grid, F32)],
        decay,
        gain,
        end,
        start,
        signal[:CTX],
        grad_conv,
    )
    end_moment = block_len * jnp.exp(-rate * block_len) * start + local_moment
    grad_rate = -gain * (grad_moment + end * end_moment)
    grad_signal = grad_signal.reshape(block_len, features).astype(BF16)
    grad_signal = jnp.concatenate([grad_signal[CTX:], shifted(grad_signal[:CTX], -1)])

    grad_in = (
        dot(grad_queries, wq, NN)
        + dot(grad_token_keys, wk, NN)
        + dot(grad_token_values, wv, NN)
        + grad_signal.astype(F32) * valid
    )
    grad_attn_gain = jnp.sum(grad_in * normed_in, axis=0)
    grad_tokens = grad_resid + norm_back(normed_in, inverse_in, grad_in * attention_norm_gain)
    tokens_line = line_gather(grad_tokens.astype(BF16))

    def split(values):
        return values.reshape(values.shape[0], tp_count, 2, head_cols // 2)

    def both_rows(values):
        values = split(values)
        mine, other = values[:, :, 0], values[:, :, 1]
        joined = jnp.concatenate([mine, flip(other, 1)])
        return joined.reshape(joined.shape[0], -1)

    def both_full(values):
        return jnp.concatenate([values, flip(values, 1)])

    x_rows, c_rows, r_rows = both_full(attn_input), both_full(context), both_full(grad_resid_b)
    grads_a = [
        dot(both_rows(grad_queries), x_rows, TN),
        dot(both_rows(grad_token_keys), x_rows, TN),
        dot(both_rows(grad_token_values), x_rows, TN),
    ]
    grads_b = [
        dot(both_rows(grad_state_keys), c_rows, TN),
        dot(both_rows(grad_state_values), c_rows, TN),
        dot(both_rows(head_mix), r_rows, TN),
    ]

    def reduce_heads(grads, reverse):
        stack = jnp.stack([g.astype(BF16) for g in grads]).reshape(
            len(grads), tp_count, planes, head_rows, features
        )
        mine = plane_reduce(
            {p: jnp.transpose(stack[:, :, p], (1, 0, 2, 3)) for p in range(planes)}, reverse
        )
        return line_reduce([mine[j] for j in range(tp_count)])

    sum_a = reduce_heads(grads_a, False)
    sum_b = reduce_heads(grads_b, True)

    def spread(value, reverse):
        plane = plane_gather(value, reverse)
        other = {p: flip(v, 1) for p, v in plane.items()}
        return jnp.stack([(plane, other)[i & 1][i >> 1] for i in range(seq_count)])

    def ordered(stack):
        return [
            lax.dynamic_index_in_dim(stack, seq_index ^ i, 0, keepdims=False)
            for i in range(seq_count)
        ]

    fix = 1.0 / copies

    def head_grads(value, reverse):
        parts = ordered(spread(value, reverse))
        parts = [parts[2 * p + c] for c in range(2) for p in range(planes)]
        return jnp.concatenate(parts, axis=1).astype(F32) * fix

    def hidden_grads(value, reverse):
        return jnp.concatenate(ordered(spread(value, reverse))).astype(F32) * fix

    full_a = head_grads(sum_a, False)
    full_b = head_grads(sum_b, True)
    full_hidden = hidden_grads(sum_hidden, False)
    full_return = hidden_grads(sum_return, True)

    gains = lax.psum(jnp.stack([grad_attn_gain, grad_mlp_gain]), ("seq", "tp")) * fix
    kernel_grads = jnp.stack([grad_gain, grad_rate]).reshape(2, states, features)
    kernel_grads = lax.psum_scatter(
        jnp.transpose(kernel_grads, (2, 0, 1)).reshape(features, 2 * states),
        ("seq", "tp"),
        scatter_dimension=0,
        tiled=True,
    )
    kernel_grads = kernel_grads * fix

    def lined(line, dtype):
        stack = jnp.stack(line)
        return jnp.stack(
            [
                lax.dynamic_index_in_dim(
                    stack, (tp_index - b * copies) % tp_count, 0, keepdims=False
                )
                for b in range(sequences)
            ]
        ).astype(dtype)

    return (
        lined(output_line, BF16),
        lined(tokens_line, F32),
        gains[0],
        full_a[0].T,
        full_a[1].T,
        full_a[2].T,
        full_b[2],
        full_b[0].T,
        full_b[1].T,
        kernel_grads[:, :states],
        kernel_grads[:, states:],
        gains[1],
        full_hidden.T,
        full_return,
    )


LOG2E = math.log2(math.e)
SCALE = DH ** (-0.5)


def cost(us):
    return pl.CostEstimate(flops=int(us * 1.1e9), bytes_accessed=0, transcendentals=0)


def params(limit=42):
    return pltpu.CompilerParams(vmem_limit_bytes=limit * 2**20)


def like(shape, dtype=BF16):
    return jax.ShapeDtypeStruct(shape, dtype)


def whole(shape):
    return pl.BlockSpec(shape, lambda *_: (0,) * len(shape))


def launch(kernel, place, grid, in_specs, out_specs, outs, operands, scratch=(), us=5):
    return pl.pallas_call(
        kernel,
        grid_spec=pltpu.PrefetchScalarGridSpec(
            num_scalar_prefetch=1,
            grid=grid,
            in_specs=in_specs,
            out_specs=out_specs,
            scratch_shapes=list(scratch),
        ),
        out_shape=outs,
        compiler_params=params(),
        cost_estimate=cost(us),
    )(place, *operands)


def timed(us):
    return partial(launch, us=us)


def cycle(value, steps):
    count = lax.axis_size("tp")
    return lax.ppermute(value, "tp", [(i, (i + steps) % count) for i in range(count)])


def pack_heads(place, wq, wk, wv, wsk, wsv, wo, out, turned):
    chip = place[0] >> 1
    rows = out.shape[2]
    for w, ref in enumerate((wq, wk, wv, wsk, wsv, wo)):
        turned[...] = ref[...].astype(F32) if ref is wo else ref[...].astype(F32).T
        for p in range(4):
            cut = pl.ds(pl.multiple_of((chip ^ p) * rows, rows), rows)
            out[p, w] = turned[cut, :].astype(BF16)


def pack_hidden(place, wh, wr, out, turned):
    chip = place[0] >> 1
    rows = out.shape[2]
    for w, ref in enumerate((wh, wr)):
        turned[...] = ref[...].astype(F32).T if ref is wh else ref[...].astype(F32)
        for p in range(4):
            cut = pl.ds(pl.multiple_of((chip ^ p) * rows, rows), rows)
            out[p, w] = turned[cut, :].astype(BF16)


def load_heads(j, own, far, into, first, count):
    rows = own.shape[2]

    @pl.when(j == 0)
    def _():
        for p in range(4):
            for w in range(count):
                into[w, p * rows : (p + 1) * rows] = own[p, first + w]

    @pl.when(j > 0)
    def _():
        for p in range(4):
            for w in range(count):
                if p < 3:
                    into[w, p * rows : (p + 1) * rows] = far[p][0, first + w]
                else:
                    into[w, p * rows : (p + 1) * rows] = far[3 + (first + w) // 3][0, (first + w) % 3]


def masked(raw, r, block):
    n = raw.shape[1]
    column = lax.broadcasted_iota(jnp.int32, raw.shape, 1)
    row = lax.broadcasted_iota(jnp.int32, raw.shape, 0)
    keep = (column - (n - 128) <= row) & ((column >= CTX) | (block > 0))
    return jnp.where(keep, raw * (SCALE * LOG2E), NEGATIVE)


def project(place, x0, x1, own, f0, f1, f2, f3, f4, q_ref, k_ref, v_ref, weight):
    j = pl.program_id(0)
    load_heads(j, own, (f0, f1, f2, f3, f4), weight, 0, 3)
    rows = x0.shape[0]
    qkv_w = weight[0:3].reshape(3 * DH, -1)
    for half, x in enumerate((x0, x1)):
        saved = slice(half * rows, (half + 1) * rows)
        qkv = dot(x[...], qkv_w, NT).astype(BF16)
        q_ref[saved] = qkv[:, :DH]
        k_ref[saved] = qkv[:, DH : 2 * DH]
        v_ref[saved] = qkv[:, 2 * DH :]


def attend(place, c0, c1, own, f0, f1, f2, f3, f4, q_ref, k_ref, v_ref,
           part0, part1, s_ref, o_ref, lse_ref, weight, keys, values, total):
    j = pl.program_id(0)
    load_heads(j, own, (f0, f1, f2, f3, f4), weight, 3, 3)
    rows = part0.shape[0]

    @pl.when(j == 0)
    def _():
        total[...] = jnp.zeros_like(total)

    st_w = weight[0:2].reshape(2 * DH, -1)
    for half, c in enumerate((c0, c1)):
        base = half * rows
        state = dot(c[...], st_w, NT).astype(BF16)
        s_ref[half * CTX : (half + 1) * CTX] = state
        keys[half, 0:CTX] = state[:, :DH]
        values[half, 0:CTX] = state[:, DH:]
        keys[half, CTX:] = k_ref[base : base + rows]
        values[half, CTX:] = v_ref[base : base + rows]
    for half in range(2):
        block = place[0] ^ half
        base = half * rows
        for r in range(rows // 128):
            saved = slice(base + r * 128, base + (r + 1) * 128)
            n = CTX + (r + 1) * 128
            scores = masked(dot(q_ref[saved], keys[half, 0:n], NT), r, block)
            top = jnp.max(scores, axis=1, keepdims=True)
            power = jnp.exp2(scores - top)
            summed = jnp.sum(power, axis=1, keepdims=True)
            lse_ref[0, saved] = top + jnp.log2(summed)
            probs = (power * (1.0 / summed)).astype(BF16)
            o_ref[saved] = dot(probs, values[half, 0:n], NN).astype(BF16)
    for half in range(2):
        base = half * rows
        total[base : base + rows] += dot(o_ref[base : base + rows], weight[2], NN)

    @pl.when(j == pl.num_programs(0) - 1)
    def _():
        part0[...] = total[0:rows].astype(part0.dtype)
        part1[...] = total[rows:].astype(part1.dtype)


def attend_back(place, g0, g1, own, f0, f1, f2, f3, f4,
                q_ref, k_ref, v_ref, s_ref, lse_ref,
                in0, in1, ctx0, ctx1, d_ref, ds_ref,
                weight, keys, values, heads, grad_k, grad_v, total, ctx_total):
    j = pl.program_id(0)
    load_heads(j, own, (f0, f1, f2, f3, f4), weight, 0, 6)
    rows = g0.shape[0]

    @pl.when(j == 0)
    def _():
        total[...] = jnp.zeros_like(total)
        ctx_total[...] = jnp.zeros_like(ctx_total)

    qkv_w = weight[0:3].reshape(3 * DH, -1)
    st_w = weight[3:5].reshape(2 * DH, -1)
    for half, g in enumerate((g0, g1)):
        base = half * rows
        keys[half, 0:CTX] = s_ref[half * CTX : (half + 1) * CTX, :DH]
        values[half, 0:CTX] = s_ref[half * CTX : (half + 1) * CTX, DH:]
        keys[half, CTX:] = k_ref[base : base + rows]
        values[half, CTX:] = v_ref[base : base + rows]
        heads[half] = dot(g[...], weight[5], NT).astype(BF16)
    for half in range(2):
        block = place[0] ^ half
        base = half * rows
        for r in reversed(range(rows // 128)):
            saved = slice(base + r * 128, base + (r + 1) * 128)
            n = CTX + (r + 1) * 128
            q = q_ref[saved]
            own = heads[half, r * 128 : (r + 1) * 128]
            probs = jnp.exp2(masked(dot(q, keys[half, 0:n], NT), r, block) - lse_ref[0, saved])
            grad = dot(own, values[half, 0:n], NT)
            delta = jnp.sum(probs * grad, axis=1, keepdims=True)
            scores = (probs * (grad - delta)).astype(BF16)
            d_ref[saved, 0:DH] = (dot(scores, keys[half, 0:n], NN) * SCALE).astype(BF16)
            to_k = dot(scores, q, TN)
            to_v = dot(probs.astype(BF16), own, TN)
            if r == rows // 128 - 1:
                grad_k[half, 0:n] = to_k
                grad_v[half, 0:n] = to_v
            else:
                grad_k[half, 0:n] += to_k
                grad_v[half, 0:n] += to_v
    for half in range(2):
        base = half * rows
        d_ref[base : base + rows, DH : 2 * DH] = (grad_k[half, CTX:] * SCALE).astype(BF16)
        d_ref[base : base + rows, 2 * DH :] = grad_v[half, CTX:].astype(BF16)
        state = slice(half * CTX, (half + 1) * CTX)
        ds_ref[state, :DH] = (grad_k[half, 0:CTX] * SCALE).astype(BF16)
        ds_ref[state, DH:] = grad_v[half, 0:CTX].astype(BF16)
        ctx_total[state] += dot(ds_ref[state], st_w, NN)
        total[base : base + rows] += dot(d_ref[base : base + rows], qkv_w, NN)

    @pl.when(j == pl.num_programs(0) - 1)
    def _():
        in0[...] = total[0:rows].astype(in0.dtype)
        in1[...] = total[rows:].astype(in1.dtype)
        ctx0[...] = ctx_total[0:CTX].astype(ctx0.dtype)
        ctx1[...] = ctx_total[CTX:].astype(ctx1.dtype)


def attend_weights(place, x0, x1, c0, c1, g0, g1, d_ref, ds_ref, o_ref, keep_a, send_a, keep_b, send_b):
    rows = x0.shape[0]
    cut = keep_a.shape[3]
    to_qkv = (dot(d_ref[0:rows], x0[...], TN) + dot(d_ref[rows:], x1[...], TN)).astype(BF16)
    to_state = (dot(ds_ref[0:CTX], c0[...], TN) + dot(ds_ref[CTX:], c1[...], TN)).astype(BF16)
    to_out = (dot(o_ref[0:rows], g0[...], TN) + dot(o_ref[rows:], g1[...], TN)).astype(BF16)
    spots_a = {0: (keep_a, 0), 2: (keep_a, 1), 1: (send_a, 0), 3: (send_a, 1)}
    spots_b = {0: (keep_b, 0), 1: (keep_b, 1), 2: (send_b, 0), 3: (send_b, 1)}
    for p in range(4):
        out, at = spots_a[p]
        for w in range(3):
            out[at, 0, w] = to_qkv[w * DH + p * cut : w * DH + (p + 1) * cut]
        out, at = spots_b[p]
        for w in range(2):
            out[at, 0, w] = to_state[w * DH + p * cut : w * DH + (p + 1) * cut]
        out[at, 0, 2] = to_out[p * cut : (p + 1) * cut]


def gelu_parts(x):
    size = jnp.abs(x) * math.sqrt(0.5)
    bell = jnp.exp2(x * x * (-0.5 * LOG2E))
    t = 1.0 / (1.0 + 0.3275911 * size)
    poly = 1.061405429 * t - 1.453152027
    poly = poly * t + 1.421413741
    poly = poly * t - 0.284496736
    poly = poly * t + 0.254829592
    tail = 0.5 * poly * t * bell
    return jnp.where(x >= 0, 1.0 - tail, tail), bell * (1.0 / math.sqrt(2.0 * math.pi))


def load_hidden(j, w, own, far, into):
    rows = own.shape[2]

    @pl.when(j == 0)
    def _():
        for p in range(4):
            into[p * rows : (p + 1) * rows] = own[p, w]

    @pl.when(j > 0)
    def _():
        for p in range(3):
            into[p * rows : (p + 1) * rows] = far[p][0, w]
        into[3 * rows :] = far[3 + w][0]


def feed_in(place, m0, m1, own, f0, f1, f2, f3, act_ref, slope_ref, wh):
    load_hidden(pl.program_id(0), 0, own, (f0, f1, f2, f3), wh)
    rows = m0.shape[0]
    for half, m in enumerate((m0, m1)):
        saved = slice(half * rows, (half + 1) * rows)
        pre = dot(m[...], wh[...], NT)
        part, bell = gelu_parts(pre)
        act_ref[saved] = (pre * part).astype(BF16)
        slope_ref[saved] = (part + pre * bell).astype(BF16)


def feed_out(place, g0, g1, own, f0, f1, f2, f3, f4, act_ref, slope_ref,
             mlp0, mlp1, mid0, mid1, pre_ref, wh, wr, mlp, mid):
    j = pl.program_id(0)
    load_hidden(j, 0, own, (f0, f1, f2, f3, f4), wh)
    load_hidden(j, 1, own, (f0, f1, f2, f3, f4), wr)
    rows = g0.shape[0]

    @pl.when(j == 0)
    def _():
        mlp[...] = jnp.zeros_like(mlp)
        mid[...] = jnp.zeros_like(mid)

    for half, g in enumerate((g0, g1)):
        saved = slice(half * rows, (half + 1) * rows)
        back = dot(g[...], wr[...], NT)
        pre_ref[saved] = (back * slope_ref[saved].astype(F32)).astype(BF16)
        mlp[saved] += dot(act_ref[saved], wr[...], NN)
        mid[saved] += dot(pre_ref[saved], wh[...], NN)

    @pl.when(j == pl.num_programs(0) - 1)
    def _():
        mlp0[...] = mlp[0:rows].astype(mlp0.dtype)
        mlp1[...] = mlp[rows:].astype(mlp1.dtype)
        mid0[...] = mid[0:rows].astype(mid0.dtype)
        mid1[...] = mid[rows:].astype(mid1.dtype)


def feed_weights(keeps, place, a0, a1, b_ref, keep, send):
    rows = a0.shape[0]
    cut = keep.shape[2]
    sends = [p for p in range(4) if p not in keeps]
    grad = (dot(b_ref[0:rows], a0[...], TN) + dot(b_ref[rows:], a1[...], TN)).astype(BF16)
    for p in range(4):
        out, at = (keep, keeps.index(p)) if p in keeps else (send, sends.index(p))
        out[at, 0] = grad[p * cut : (p + 1) * cut]


def live_rows(place, count):
    at = place[0] * (count * pl.num_programs(0)) + pl.program_id(0) * count
    position = at + lax.broadcasted_iota(jnp.int32, (count, 1), 0)
    return (position < place[2]).astype(F32)


def middle(place, tokens, own, got, gain, residual, m_ref):
    value = tokens[0].astype(F32) + own[...] + got[...].astype(F32)
    residual[...] = value
    m_ref[...] = (normalize(value)[0] * gain[...]).astype(BF16)


def finish(place, residual, own, got, out):
    value = residual[...] + own[...] + got[...].astype(F32)
    out[...] = (value * live_rows(place, value.shape[0])).astype(BF16)


def middle_back(place, residual, own, got, cot, gain, grad, grad_b, sums):
    value = residual[...]
    normed, inverse = normalize(value)
    valid = live_rows(place, value.shape[0])
    back = own[...] + got[...].astype(F32)
    total = jnp.sum(back * normed, axis=0, keepdims=True)

    @pl.when(pl.program_id(0) == 0)
    def _():
        sums[...] = total

    @pl.when(pl.program_id(0) > 0)
    def _():
        sums[...] += total

    value = cot[0].astype(F32) * valid + norm_back(normed, inverse, back * gain[...])
    grad[...] = value
    grad_b[...] = value.astype(BF16)


def first_back(place, tokens, own, got, signal, grad, gain, out, sums):
    normed, inverse = normalize(tokens[0].astype(F32))
    valid = live_rows(place, out.shape[0])
    back = own[...] + got[...].astype(F32) + signal[...].astype(F32) * valid
    total = jnp.sum(back * normed, axis=0, keepdims=True)

    @pl.when(pl.program_id(0) == 0)
    def _():
        sums[...] = total

    @pl.when(pl.program_id(0) > 0)
    def _():
        sums[...] += total

    out[...] = (grad[...] + norm_back(normed, inverse, back * gain[...])).astype(BF16)


def unpack_heads(place, n0, n1, n2, n3, f0, f1, f2, f3, q, k, v, o, sk, sv, rows_ref):
    core, chip = place[0] & 1, place[0] >> 1
    cut = n0.shape[1]
    for w, out in ((0, q), (1, k), (2, v), (3, sk), (4, sv), (5, o)):
        for other, pieces in ((0, (n0, n1, n2, n3)), (1, (f0, f1, f2, f3))):
            for p, piece in enumerate(pieces):
                at = (core ^ other) * DH + (chip ^ p) * cut
                rows_ref[pl.ds(pl.multiple_of(at, cut), cut), :] = piece[w].astype(F32)
        out[...] = rows_ref[...] if out is o else rows_ref[...].T


def unpack_hidden(place, n0, n1, n2, n3, f0, f1, f2, f3, h, r):
    core, chip = place[0] & 1, place[0] >> 1
    cut = n0.shape[1]
    for other, pieces in ((0, (n0, n1, n2, n3)), (1, (f0, f1, f2, f3))):
        for p, piece in enumerate(pieces):
            at = pl.multiple_of((core ^ other) * 4 * cut + (chip ^ p) * cut, cut)
            r[pl.ds(at, cut), :] = piece[1].astype(F32)
            h[:, pl.ds(at, cut)] = piece[0].astype(F32).T


def add(a, b):
    return (a.astype(F32) + b.astype(F32)).astype(BF16)


def after(value, *earlier):
    return lax.optimization_barrier((value, *earlier))[0]


def powers(lengths, rate_ref, *outs):
    for length, out in zip(lengths, outs):
        out[...] = jnp.exp(-rate_ref[...] * float(length))


def states_around(local, power, sign, first, *earlier):
    group = local
    for m in (1, 2):
        group = group + power[m] * shifted(local, sign * m)
    group = after(group, *earlier)
    total = shifted(group, sign * first)
    for m in range(first + 3, 8, 3):
        total = total + power[m - first] * shifted(group, sign * m)
    return total


def scan_rows(decay_ref, gain_ref, late_ref, g_ref, y_ref, end_ref):
    decay, gain = decay_ref[...], gain_ref[...]
    rows, count = y_ref.shape[0], g_ref.shape[0]

    def full(t, lam):
        lam = lam + g_ref[count - 1 - t]
        y_ref[rows - 1 - t] = jnp.sum(gain * lam, axis=0)
        return decay * lam

    def empty(t, lam):
        y_ref[rows - count - 1 - t] = jnp.sum(gain * lam, axis=0)
        return decay * lam

    lam = lax.fori_loop(0, count, full, late_ref[...], unroll=8)
    end_ref[...] = lam
    lax.fori_loop(0, rows - count, empty, lam, unroll=8)


def scan_sums(decay_ref, start_ref, u_ref, g_ref, gh_ref, gm_ref):
    decay = decay_ref[...]

    def again(t, carry):
        h, m, gh, gm = carry
        h, m = decay * h + u_ref[t], decay * (m + h)
        g = g_ref[t]
        return h, m, gh + g * h, gm + g * m

    zero = jnp.zeros(decay.shape, F32)
    _, _, gh, gm = lax.fori_loop(0, u_ref.shape[0], again, (start_ref[...], zero, zero, zero))
    gh_ref[...] = gh
    gm_ref[...] = gm


def fast_body(
    tokens, lengths, attention_norm_gain, query_weight, key_weight, value_weight, output_weight,
    state_key_weight, state_value_weight, state_coefficient, state_rate, feedforward_norm_gain,
    hidden_weight, return_weight, cotangent,
):
    sequences, block_len, features = tokens.shape
    tp_count = lax.axis_size("tp")
    seq_index = lax.axis_index("seq")
    tp_index = lax.axis_index("tp")
    hidden_cols = hidden_weight.shape[1]
    cut = DH // 4
    wide = hidden_cols // 8
    length = lax.dynamic_index_in_dim(lengths, tp_index, 0, keepdims=False)
    place = jnp.stack([seq_index, tp_index, length]).astype(jnp.int32)

    column = pl.BlockSpec((features, DH), lambda i, place: (0, place[0] & 1))
    (own_w,) = timed(4)(
        pack_heads, place, (1,),
        [column] * 5 + [pl.BlockSpec((DH, features), lambda i, place: (place[0] & 1, 0))],
        [whole((4, 6, cut, features))],
        [like((4, 6, cut, features))],
        (query_weight, key_weight, value_weight, state_key_weight, state_value_weight, output_weight),
        [pltpu.VMEM((DH, features), F32)],
    )
    (own_m,) = timed(5)(
        pack_hidden, place, (1,),
        [
            pl.BlockSpec((features, hidden_cols // 2), lambda i, place: (0, place[0] & 1)),
            pl.BlockSpec((hidden_cols // 2, features), lambda i, place: (place[0] & 1, 0)),
        ],
        [whole((4, 2, wide, features))],
        [like((4, 2, wide, features))],
        (hidden_weight, return_weight),
        [pltpu.VMEM((hidden_cols // 2, features), F32)],
    )

    own_tokens = lax.dynamic_index_in_dim(tokens, tp_index, 0, keepdims=False)
    own_cot = lax.dynamic_index_in_dim(cotangent, tp_index, 0, keepdims=False)
    before = shifted(own_tokens[block_len - CTX :], 1)
    positions = seq_index * block_len - CTX + jnp.arange(block_len + CTX)
    live = ((positions < length) & (positions >= 0)).astype(F32)[:, None]
    x = (normalize(own_tokens.astype(F32))[0] * attention_norm_gain).astype(BF16)
    x_other = flip(x, 1)
    grad_out = (own_cot.astype(F32) * live[CTX:]).astype(BF16)
    grad_out_other = flip(grad_out, 1)
    early = (normalize(before.astype(F32))[0] * attention_norm_gain).astype(BF16)
    signal = tiles(
        jnp.concatenate([early, x[: block_len - CTX]]).astype(F32) * live[:block_len]
    )

    states = state_rate.shape[1]
    channels = state_rate.shape[0]
    both = jnp.stack([state_rate, state_coefficient]).reshape(1, -1, 128)
    devices = features // channels
    both = lax.all_to_all(
        jnp.broadcast_to(both, (devices,) + both.shape[1:]), ("seq", "tp"), 0, 0
    )
    both = jnp.transpose(both.reshape(devices, 2, channels, states), (1, 3, 0, 2))
    both = both.reshape(2, states, features // 128, 128)
    rate, gain = both[0], both[1]
    grid = rate.shape
    spans = [1, block_len - CTX] + [block_len * m for m in (1, 2, 3, 6)]
    decay, tail_power, *blocks = call(
        partial(powers, spans), [(grid, F32)] * len(spans), rate, us=1
    )
    block_power = dict(zip((1, 2, 3, 6), blocks))

    def line_of(own):
        return jnp.stack([cycle(own[0], j) for j in range(1, tp_count)])

    def plane_of(line, by_x, by_y, half):
        return [line, by_x, by_y, flip(by_y[:, :half], 2), flip(by_x[:, half:], 4)]

    line_w = line_of(own_w)
    near_w = flip(line_w, 2), flip(line_w, 4)
    far_w = plane_of(line_w, *near_w, 3)
    line_m = line_of(after(own_m, line_w))
    near_m = flip(line_m, 2), flip(line_m, 4)
    far_m = plane_of(line_m, *near_m, 1)
    far_m[3:] = [value[:, 0] for value in far_m[3:]]

    local_state, local_moment = call(
        scan_in, [(grid, F32)] * 2, decay, after(signal, line_w, own_m), us=8
    )
    start = states_around(after(local_state, *near_w), block_power, 1, 1)
    (context,) = call(scan_out, [((CTX,) + grid[1:], F32)], decay, gain, start, signal[:CTX], us=3)
    context = context.reshape(CTX, features).astype(BF16)
    context_other = flip(context, 1)

    rows = 2 * block_len
    slots = tp_count
    own_spec = whole((4, 6, cut, features))

    def slot_spec(*shape):
        return pl.BlockSpec(
            (1, *shape, features),
            lambda j, place: (jnp.maximum(j - 1, 0),) + (0,) * (len(shape) + 1),
        )

    weight_specs = [own_spec] + [slot_spec(6, cut)] * 3 + [slot_spec(3, cut)] * 2
    weights = (own_w, *far_w)
    full = whole((block_len, features))
    ctx_spec = whole((CTX, features))
    head = lambda n, width: pl.BlockSpec((n, width), lambda j, place: (0, j))
    lse_spec = pl.BlockSpec((1, rows, 1), lambda j, place: (j, 0, 0))
    q, k, v = timed(8)(
        project, place, (slots,),
        [full] * 2 + weight_specs,
        [head(rows, DH)] * 3,
        [like((rows, slots * DH))] * 3,
        (x, x_other, *weights),
        [pltpu.VMEM((3, DH, features), BF16)],
    )
    attended = timed(20)(
        attend, place, (slots,),
        [ctx_spec] * 2 + weight_specs + [head(rows, DH)] * 3,
        [full] * 2 + [head(2 * CTX, 2 * DH), head(rows, DH), lse_spec],
        [like((block_len, features), F32), like((block_len, features))]
        + [like((2 * CTX, slots * 2 * DH)), like((rows, slots * DH)), like((slots, rows, 1), F32)],
        (after(context, line_m), context_other, *weights, q, k, v),
        [
            pltpu.VMEM((3, DH, features), BF16),
            pltpu.VMEM((2, CTX + block_len, DH), BF16),
            pltpu.VMEM((2, CTX + block_len, DH), BF16),
            pltpu.VMEM((rows, features), F32),
        ],
    )
    part, part_other, state, mix, lse = attended
    group = 128
    steps = block_len // group
    row_spec = pl.BlockSpec((group, features), lambda i, place: (i, 0))
    seq_spec = pl.BlockSpec((1, group, features), lambda i, place: (place[1], i, 0))
    gain_spec = whole((1, features))
    mid_gain = feedforward_norm_gain.reshape(1, -1)
    residual, m = timed(4)(
        middle, place, (steps,),
        [seq_spec, row_spec, row_spec, gain_spec], [row_spec] * 2,
        [like((block_len, features), F32), like((block_len, features))],
        (tokens, part, after(flip(part_other, 1), *near_m), mid_gain),
    )
    m_other = flip(m, 1)

    hidden_own = whole((4, 2, wide, features))
    hidden_far = [slot_spec(2, wide)] * 3 + [slot_spec(wide)]
    chunk = 4 * wide
    act, slope = timed(14)(
        feed_in, place, (slots,),
        [full] * 2 + [hidden_own] + hidden_far,
        [head(rows, chunk)] * 2,
        [like((rows, slots * chunk))] * 2,
        (m, m_other, own_m, *far_m[:4]),
        [pltpu.VMEM((chunk, features), BF16)],
    )
    mlp, mlp_other, mid, mid_other, pre = timed(21)(
        feed_out, place, (slots,),
        [full] * 2 + [hidden_own] + hidden_far + hidden_far[3:] + [head(rows, chunk)] * 2,
        [full] * 4 + [head(rows, chunk)],
        [like((block_len, features), F32), like((block_len, features))] * 2
        + [like((rows, slots * chunk))],
        (grad_out, grad_out_other, own_m, *far_m, act, slope),
        [pltpu.VMEM((chunk, features), BF16)] * 2 + [pltpu.VMEM((rows, features), F32)] * 2,
    )
    mid_got, mlp_got = flip(mid_other, 1), flip(mlp_other, 1)
    grad_spec = pl.BlockSpec((2, 1, wide, features), lambda j, place: (0, j, 0, 0))
    hidden_grads = partial(
        launch, place=place, grid=(slots,), us=8,
        in_specs=[full] * 2 + [head(rows, chunk)], out_specs=[grad_spec] * 2,
        outs=[like((2, slots, wide, features))] * 2,
    )
    keep_r, send_r = hidden_grads(
        partial(feed_weights, (0, 1)), operands=(grad_out, grad_out_other, after(act, pre))
    )
    mlp_got = after(mlp_got, keep_r)
    mid_got = after(mid_got, keep_r)
    (output,) = timed(3)(
        finish, place, (steps,),
        [row_spec] * 3, [row_spec], [like((block_len, features))], (residual, mlp, mlp_got),
    )
    output_all = lax.all_gather(output, "tp")
    resid, resid_b, sums_mid = timed(5)(
        middle_back, place, (steps,),
        [row_spec] * 3 + [seq_spec, gain_spec], [row_spec] * 2 + [gain_spec],
        [
            like((block_len, features), F32), like((block_len, features)),
            like((1, features), F32),
        ],
        (after(residual, output), mid, mid_got, cotangent, mid_gain),
    )
    resid_other = flip(resid_b, 1)
    keep_h, send_h = hidden_grads(
        partial(feed_weights, (0, 2)), operands=(m, m_other, after(pre, resid_b))
    )

    grad_in, grad_in_other, grad_ctx, grad_ctx_other, d, ds = timed(27)(
        attend_back, place, (slots,),
        [full] * 2 + weight_specs + [head(rows, DH)] * 3 + [head(2 * CTX, 2 * DH), lse_spec],
        [full] * 2 + [ctx_spec] * 2 + [head(rows, 3 * DH), head(2 * CTX, 2 * DH)],
        [
            like((block_len, features), F32), like((block_len, features)),
            like((CTX, features), F32), like((CTX, features)),
            like((rows, slots * 3 * DH)), like((2 * CTX, slots * 2 * DH)),
        ],
        (after(resid_b, keep_h), resid_other, *weights, q, k, v, state, lse),
        [
            pltpu.VMEM((6, DH, features), BF16),
            pltpu.VMEM((2, CTX + block_len, DH), BF16),
            pltpu.VMEM((2, CTX + block_len, DH), BF16),
            pltpu.VMEM((2, block_len, DH), BF16),
            pltpu.VMEM((2, CTX + block_len, DH), F32),
            pltpu.VMEM((2, CTX + block_len, DH), F32),
            pltpu.VMEM((rows, features), F32),
            pltpu.VMEM((2 * CTX, features), F32),
        ],
    )
    grad_ctx_got = flip(grad_ctx_other, 1)
    grad_in_got = flip(grad_in_other, 1)
    part_spec = pl.BlockSpec((2, 1, 3, cut, features), lambda j, place: (0, j, 0, 0, 0))
    keep_a, send_a, keep_b, send_b = timed(10)(
        attend_weights, place, (slots,),
        [full] * 2 + [ctx_spec] * 2 + [full] * 2
        + [head(rows, 3 * DH), head(2 * CTX, 2 * DH), head(rows, DH)],
        [part_spec] * 4,
        [like((2, slots, 3, cut, features))] * 4,
        (x, x_other, context, context_other, resid_b, resid_other, d, ds, mix),
    )

    got_r = flip(after(send_r, resid_b), 4)
    got_h = flip(after(send_h, resid_b), 2)
    grad_context = (grad_ctx + grad_ctx_got.astype(F32)).astype(BF16)
    grad_conv = tiles(after(grad_context, got_r, got_h))
    grad_later = tiles(shifted(grad_context, -1))
    (local_back,) = call(scan_back_in, [(grid, F32)], decay, grad_conv)
    late = tail_power * states_around(local_back, block_power, -1, 2, keep_a)
    grad_signal, end = call(
        scan_rows, [((block_len,) + grid[1:], F32), (grid, F32)], decay, gain, late, grad_later
    )
    grad_signal = grad_signal.reshape(block_len, features).astype(BF16)
    grad_gain, grad_moment = call(
        scan_sums, [(grid, F32)] * 2, decay, start, signal[:CTX], grad_conv
    )
    end_moment = block_len * block_power[1] * start + local_moment
    grad_rate = -gain * (grad_moment + end * end_moment)
    grad_tokens, sums_in = timed(5)(
        first_back, place, (steps,),
        [seq_spec] + [row_spec] * 4 + [gain_spec], [row_spec, gain_spec],
        [like((block_len, features)), like((1, features), F32)],
        (tokens, grad_in, grad_in_got, grad_signal, after(resid, output_all), attention_norm_gain.reshape(1, -1)),
    )

    def plane_sum(keep_first, got_first, keep_second, got_second, then, end):
        got = after(got_first, *then)
        near, away = add(keep_first[0], got[0]), add(keep_first[1], got[1])
        first = (near, after(flip(away, 4), *end))
        got = after(got_second, *then)
        near, away = add(keep_second[0], got[0]), add(keep_second[1], got[1])
        second = (near, after(flip(away, 2), *end))
        return [
            jnp.stack([add(a[j], b[j]) for a, b in (first, second)]) for j in range(slots)
        ]

    def regather(total):
        held = [total, flip(total, 2), flip(total, 4), flip(total, 6)]
        return held + [flip(value, 1) for value in held]

    ready = (late, grad_later)
    got_a, got_b = flip(after(send_a, *ready), 2), flip(after(send_b, *ready), 4)
    total_m = line_reduce(plane_sum(keep_h, got_h, keep_r, got_r, ready, (grad_tokens,)))
    pieces_m = regather(total_m)
    total_a = line_reduce(plane_sum(keep_a, got_a, keep_b, got_b, (grad_tokens,), ()))
    pieces_a = regather(total_a.reshape(6, cut, features))
    grad_hidden, grad_return = timed(5)(
        unpack_hidden, place, (1,),
        [whole((2, wide, features))] * 8,
        [whole((features, hidden_cols)), whole((hidden_cols, features))],
        [like((features, hidden_cols), F32), like((hidden_cols, features), F32)],
        pieces_m,
    )
    grad_q, grad_k, grad_v, grad_o, grad_sk, grad_sv = timed(5)(
        unpack_heads, place, (1,),
        [whole((6, cut, features))] * 8,
        [whole((features, 2 * DH))] * 3 + [whole((2 * DH, features))] + [whole((features, 2 * DH))] * 2,
        [like((features, 2 * DH), F32)] * 3
        + [like((2 * DH, features), F32)]
        + [like((features, 2 * DH), F32)] * 2,
        pieces_a,
        [pltpu.VMEM((2 * DH, features), F32)],
    )

    small = jnp.stack([grad_gain, grad_rate]).reshape(2, states, devices, channels)
    small = jnp.transpose(small, (2, 3, 0, 1)).reshape(devices, -1, 128)
    sums = jnp.concatenate([sums_in, sums_mid]).reshape(1, -1, 128)
    sums = jnp.broadcast_to(sums, (devices,) + sums.shape[1:])
    count = small.shape[1]
    small = jnp.sum(
        lax.all_to_all(jnp.concatenate([small, sums], axis=1), ("seq", "tp"), 0, 0), axis=0
    )
    kernel_grads = small[:count].reshape(channels, 2, states)
    gains = small[count:].reshape(2, features)

    grad_tokens = lax.all_gather(grad_tokens, "tp").astype(F32)
    return (
        output_all, grad_tokens, gains[0], grad_q, grad_k, grad_v, grad_o, grad_sk, grad_sv,
        kernel_grads[:, 0], kernel_grads[:, 1], gains[1], grad_hidden, grad_return,
    )


def choose(tokens, *others):
    query_weight = others[2]
    fits = (
        lax.axis_size("seq") == 8
        and lax.axis_size("tp") == tokens.shape[0]
        and query_weight.shape[1] == 2 * DH
        and others[11].shape[1] % 1024 == 0
        and tokens.shape[1] % 512 == 0
        and tokens.shape[2] == 1024
    )
    return (fast_body if fits else body)(tokens, *others)


def solution(mesh):
    rows = P(None, "seq", None)
    columns = P(None, "tp")
    heads = P("tp", None)
    channels = P(("seq", "tp"), None)
    return jax.shard_map(
        choose,
        mesh=mesh,
        in_specs=(
            rows, P(), P(), columns, columns, columns, heads, columns, columns,
            channels, channels, P(), columns, heads, rows,
        ),
        out_specs=(
            rows, rows, P(), columns, columns, columns, heads, columns, columns,
            channels, channels, P(), columns, heads,
        ),
        check_vma=False,
    )
```

```python
from functools import partial
import math

import jax
import jax.numpy as jnp
from jax import lax
from jax.experimental import pallas as pl
from jax.experimental.pallas import tpu as pltpu
from jax.sharding import PartitionSpec as P

DH = 128
CTX = 128
EPS = 1e-05
NEGATIVE = -1e30
F32 = jnp.float32
BF16 = jnp.bfloat16


def normalize(values):
    center = values - jnp.mean(values, axis=-1, keepdims=True)
    inverse = lax.rsqrt(jnp.mean(center * center, axis=-1, keepdims=True) + EPS)
    return (center * inverse, inverse)


def norm_back(normed, inverse, grad_normed):
    mean_grad = jnp.mean(grad_normed, axis=-1, keepdims=True)
    mean_cross = jnp.mean(grad_normed * normed, axis=-1, keepdims=True)
    return inverse * (grad_normed - mean_grad - normed * mean_cross)


def flip(value, mask):
    count = lax.axis_size("seq")
    return lax.ppermute(value, "seq", [(i, i ^ mask) for i in range(count)])


def shifted(value, steps):
    count = lax.axis_size("seq")
    first, last = (max(0, -steps), min(count, count - steps))
    return lax.ppermute(value, "seq", [(i, i + steps) for i in range(first, last)])


def line_steps(value):
    count = lax.axis_size("tp")
    lefts, rights = [value], [value]
    for k in range(1, count):
        lefts.append(lax.ppermute(lefts[-1], "tp", [(i, i + 1) for i in range(k - 1, count - 1)]))
        rights.append(
            lax.ppermute(rights[-1], "tp", [(i, i - 1) for i in range(1, count - k + 1)])
        )
    return lefts, rights


def line_gather(value):
    count = lax.axis_size("tp")
    place = lax.axis_index("tp")
    lefts, rights = line_steps(value)
    return [value] + [
        jnp.where(place >= j, lefts[j], rights[count - j]) for j in range(1, count)
    ]


def line_reduce(chunks, pace=None):
    count = lax.axis_size("tp")

    def add(a, b, k):
        if pace:
            a = lax.optimization_barrier((a, *pace[k - 1]))[0]
        return a if b is None else (a.astype(F32) + b.astype(F32)).astype(BF16)

    going, coming = None, None
    for k in range(1, count):
        going = lax.ppermute(add(chunks[k], going, k), "tp", [(i, i + 1) for i in range(k)])
        coming = lax.ppermute(
            add(chunks[count - k], coming, k), "tp", [(i, i - 1) for i in range(count - k, count)]
        )
    return (chunks[0].astype(F32) + going.astype(F32) + coming.astype(F32)).astype(BF16)


def plane_bits(reverse):
    count = lax.axis_size("seq") // 2
    bits = [1 << b for b in range(count.bit_length() - 1)]
    return bits[::-1] if reverse else bits


def plane_gather(value, reverse):
    held = {0: value}
    for bit in plane_bits(reverse):
        held.update({p | bit: flip(v, 2 * bit) for p, v in list(held.items())})
    return held


def plane_reduce(pieces, reverse):
    held = dict(pieces)
    for bit in plane_bits(reverse):
        for p in [p for p in held if p & bit]:
            got = flip(held.pop(p), 2 * bit)
            held[p ^ bit] = (held[p ^ bit].astype(F32) + got.astype(F32)).astype(BF16)
    return held[0]


def scan_in(decay_ref, u_ref, state_ref, moment_ref):
    decay = decay_ref[...]

    def step(t, carry):
        h, m = carry
        return decay * h + u_ref[t], decay * (m + h)

    zero = jnp.zeros(decay.shape, F32)
    h, m = lax.fori_loop(0, u_ref.shape[0], step, (zero, zero))
    state_ref[...] = h
    moment_ref[...] = m


def scan_out(decay_ref, gain_ref, start_ref, u_ref, y_ref):
    decay, gain = decay_ref[...], gain_ref[...]

    def step(t, h):
        h = decay * h + u_ref[t]
        y_ref[t] = jnp.sum(gain * h, axis=0)
        return h

    lax.fori_loop(0, u_ref.shape[0], step, start_ref[...])


def scan_back_in(decay_ref, g_ref, state_ref):
    decay = decay_ref[...]
    last = g_ref.shape[0] - 1

    def step(t, lam):
        return decay * (lam + g_ref[last - t])

    state_ref[...] = lax.fori_loop(0, last + 1, step, jnp.zeros(decay.shape, F32))


def scan_back_out(decay_ref, gain_ref, end_ref, start_ref, u_ref, g_ref, y_ref, gh_ref, gm_ref):
    decay, gain = decay_ref[...], gain_ref[...]
    rows, count = y_ref.shape[0], g_ref.shape[0]

    def empty(t, lam):
        y_ref[rows - 1 - t] = jnp.sum(gain * lam, axis=0)
        return decay * lam

    def full(t, lam):
        lam = lam + g_ref[count - 1 - t]
        y_ref[count - 1 - t] = jnp.sum(gain * lam, axis=0)
        return decay * lam

    lam = lax.fori_loop(0, rows - count, empty, end_ref[...])
    lax.fori_loop(0, count, full, lam)

    def again(t, carry):
        h, m, gh, gm = carry
        h, m = decay * h + u_ref[t], decay * (m + h)
        g = g_ref[t]
        return h, m, gh + g * h, gm + g * m

    zero = jnp.zeros(decay.shape, F32)
    _, _, gh, gm = lax.fori_loop(0, count, again, (start_ref[...], zero, zero, zero))
    gh_ref[...] = gh
    gm_ref[...] = gm


def call(kernel, outs, *operands, us=5):
    return pl.pallas_call(
        kernel,
        out_shape=[jax.ShapeDtypeStruct(shape, dtype) for shape, dtype in outs],
        compiler_params=pltpu.CompilerParams(vmem_limit_bytes=42 * 2**20),
        cost_estimate=pl.CostEstimate(flops=int(us * 1.1e9), bytes_accessed=0, transcendentals=0),
    )(*operands)


def tiles(values):
    return values.astype(F32).reshape(values.shape[0], values.shape[1] // 128, 128)


def dot(a, b, dims):
    return lax.dot_general(a, b, (dims, ((), ())), preferred_element_type=F32)


NN = ((1,), (0,))
NT = ((1,), (1,))
TN = ((0,), (0,))


def body(
    tokens,
    lengths,
    attention_norm_gain,
    query_weight,
    key_weight,
    value_weight,
    output_weight,
    state_key_weight,
    state_value_weight,
    state_coefficient,
    state_rate,
    feedforward_norm_gain,
    hidden_weight,
    return_weight,
    cotangent,
):
    sequences, block_len, features = tokens.shape
    seq_count = lax.axis_size("seq")
    tp_count = lax.axis_size("tp")
    seq_index = lax.axis_index("seq")
    tp_index = lax.axis_index("tp")
    planes = seq_count // 2
    copies = tp_count // sequences
    sequence = tp_index // copies
    head_cols = query_weight.shape[1]
    hidden_cols = hidden_weight.shape[1]
    heads = head_cols * tp_count // DH
    head_rows = head_cols // seq_count
    hidden_rows = hidden_cols // seq_count
    scale = DH ** (-0.5)

    shard_a = [query_weight.T, key_weight.T, value_weight.T]
    shard_b = [state_key_weight.T, state_value_weight.T, output_weight]
    shard_m = [hidden_weight.T, return_weight]

    def head_slice(shard, relative):
        other = seq_index ^ relative
        at = (other & 1) * planes + (other >> 1)
        return lax.dynamic_slice_in_dim(shard, at * head_rows, head_rows, 0)

    def hidden_slice(shard, relative):
        return lax.dynamic_slice_in_dim(
            shard, (seq_index ^ relative) * hidden_rows, hidden_rows, 0
        )

    def gather_heads(shards, reverse):
        mine = jnp.stack([head_slice(w, 0) for w in shards])
        line = jnp.stack(line_gather(mine)[1:])
        plane = plane_gather(line, reverse)
        other = {p: flip(v, 1) for p, v in plane.items()}
        far = jnp.stack(
            [jnp.stack([group[p] for p in range(planes)]) for group in (plane, other)]
        )
        far = jnp.transpose(far, (3, 2, 0, 1, 4, 5))
        own = jnp.stack(
            [
                jnp.concatenate([head_slice(w, 2 * p + c) for c in range(2) for p in range(planes)])
                for w in shards
            ]
        )
        far = far.reshape(len(shards), (tp_count - 1) * head_cols, features)
        return jnp.concatenate([own, far], axis=1)

    def gather_hidden(shard, reverse):
        line = line_gather(hidden_slice(shard, 0))
        plane = plane_gather(jnp.concatenate(line[1:]), reverse)
        return jnp.concatenate(
            [
                piece
                for p in range(planes)
                for piece in (hidden_slice(shard, 2 * p), plane[p])
            ]
        )

    wq, wk, wv = gather_heads(shard_a, False)
    wsk, wsv, wo = gather_heads(shard_b, True)
    wh = gather_hidden(shard_m[0], False)
    wr = gather_hidden(shard_m[1], True)

    own_tokens = lax.dynamic_index_in_dim(tokens, sequence, 0, keepdims=False)
    own_cot = lax.dynamic_index_in_dim(cotangent, sequence, 0, keepdims=False)
    length = lax.dynamic_index_in_dim(lengths, sequence, 0, keepdims=False)
    before = shifted(own_tokens[block_len - CTX :], 1)
    positions = seq_index * block_len - CTX + jnp.arange(block_len + CTX)
    live = ((positions < length) & (positions >= 0)).astype(F32)[:, None]
    valid = live[CTX:]
    inputs = own_tokens.astype(F32)
    normed_in, inverse_in = normalize(inputs)
    attn_input = (normed_in * attention_norm_gain).astype(BF16)
    early = (normalize(before.astype(F32))[0] * attention_norm_gain).astype(BF16)
    window = jnp.concatenate([early, attn_input[: block_len - CTX]]).astype(F32) * live[:block_len]
    signal = tiles(window)

    both = jnp.stack([state_rate, state_coefficient])
    both = lax.all_gather(both, ("seq", "tp"), axis=1, tiled=True)
    states = both.shape[2]
    both = jnp.transpose(both, (0, 2, 1)).reshape(2, states, features // 128, 128)
    rate, gain = both[0], both[1]
    decay = jnp.exp(-rate)
    grid = rate.shape
    local_state, local_moment = call(scan_in, [(grid, F32)] * 2, decay, signal)
    start = 0.0
    for m in range(1, seq_count):
        start = start + jnp.exp(-rate * (block_len * (m - 1))) * shifted(local_state, m)
    (context,) = call(
        scan_out, [((CTX,) + grid[1:], F32)], decay, gain, start, signal[:CTX]
    )
    context = context.reshape(CTX, features).astype(BF16)

    queries = dot(attn_input, wq, NT).astype(BF16)
    token_keys = dot(attn_input, wk, NT).astype(BF16)
    token_values = dot(attn_input, wv, NT).astype(BF16)
    state_keys = dot(context, wsk, NT).astype(BF16)
    state_values = dot(context, wsv, NT).astype(BF16)
    query_heads = queries.reshape(block_len, heads, DH)
    key_heads = jnp.concatenate([token_keys, state_keys]).reshape(-1, heads, DH)
    value_heads = jnp.concatenate([token_values, state_values]).reshape(-1, heads, DH)
    causal = jnp.arange(block_len)[:, None] >= jnp.arange(block_len)[None, :]
    allowed = jnp.concatenate([causal, jnp.broadcast_to(seq_index > 0, (block_len, CTX))], axis=1)
    raw = jnp.einsum("qhd,khd->hqk", query_heads, key_heads, preferred_element_type=F32) * scale
    scores = jnp.where(allowed, raw, NEGATIVE)
    row_max = jnp.max(scores, axis=-1, keepdims=True)
    exp_scores = jnp.exp(scores - row_max)
    row_total = jnp.sum(exp_scores, axis=-1, keepdims=True)
    probs_full = exp_scores / row_total
    attn_probs = probs_full.astype(BF16)
    head_mix = jnp.einsum("hqk,khd->qhd", attn_probs, value_heads, preferred_element_type=F32)
    head_mix = head_mix.reshape(block_len, heads * DH).astype(BF16)
    residual = inputs + dot(head_mix, wo, NN)
    normed_mid, inverse_mid = normalize(residual)
    mlp_input = (normed_mid * feedforward_norm_gain).astype(BF16)

    grad_out = own_cot.astype(F32) * valid
    grad_out_b = grad_out.astype(BF16)
    mlp_rows = jnp.concatenate([mlp_input, flip(mlp_input, 1)])
    out_rows = jnp.concatenate([grad_out_b, flip(grad_out_b, 1)])
    pre_act = dot(mlp_rows, wh, NT)
    activated, gelu_back = jax.vjp(partial(jax.nn.gelu, approximate=False), pre_act)
    activated = activated.astype(BF16)
    mlp_part = dot(activated, wr, NN)
    grad_act = dot(out_rows, wr, NT)
    grad_pre = gelu_back(grad_act)[0].astype(BF16)
    mid_part = dot(grad_pre, wh, NN)
    grad_mid = mid_part[:block_len] + flip(mid_part[block_len:].astype(BF16), 1).astype(F32)
    mlp_out = mlp_part[:block_len] + flip(mlp_part[block_len:].astype(BF16), 1).astype(F32)
    output = ((residual + mlp_out) * valid).astype(BF16)
    output_line = line_gather(output)
    grad_return = dot(activated, out_rows, TN).astype(BF16)
    grad_hidden = dot(grad_pre, mlp_rows, TN).astype(BF16)

    def reduce_hidden(grad, reverse):
        grad = grad.reshape(planes, tp_count * hidden_rows, features)
        mine = plane_reduce({p: grad[p] for p in range(planes)}, reverse)
        mine = mine.reshape(tp_count, hidden_rows, features)
        return line_reduce([mine[j] for j in range(tp_count)])

    sum_hidden = reduce_hidden(grad_hidden, False)
    sum_return = reduce_hidden(grad_return, True)

    grad_mlp_gain = jnp.sum(grad_mid * normed_mid, axis=0)
    grad_resid = grad_out + norm_back(normed_mid, inverse_mid, grad_mid * feedforward_norm_gain)
    grad_resid_b = grad_resid.astype(BF16)
    grad_heads = dot(grad_resid_b, wo, NT).astype(BF16).reshape(block_len, heads, DH)
    grad_probs = jnp.einsum("qhd,khd->hqk", grad_heads, value_heads, preferred_element_type=F32)
    delta = jnp.sum(probs_full * grad_probs, axis=-1, keepdims=True)
    grad_scores = (probs_full * (grad_probs - delta)).astype(BF16)
    grad_queries = (
        jnp.einsum("hqk,khd->qhd", grad_scores, key_heads, preferred_element_type=F32) * scale
    )
    grad_keys_all = (
        jnp.einsum("hqk,qhd->khd", grad_scores, query_heads, preferred_element_type=F32) * scale
    )
    grad_values_all = jnp.einsum(
        "hqk,qhd->khd", attn_probs, grad_heads, preferred_element_type=F32
    )
    wide = heads * DH
    grad_queries = grad_queries.reshape(block_len, wide).astype(BF16)
    grad_keys_all = grad_keys_all.reshape(block_len + CTX, wide).astype(BF16)
    grad_values_all = grad_values_all.reshape(block_len + CTX, wide).astype(BF16)
    grad_token_keys, grad_state_keys = grad_keys_all[:block_len], grad_keys_all[block_len:]
    grad_token_values, grad_state_values = grad_values_all[:block_len], grad_values_all[block_len:]
    grad_context = (
        dot(grad_state_keys, wsk, NN) + dot(grad_state_values, wsv, NN)
    ).astype(BF16)

    grad_conv = tiles(grad_context)
    (local_back,) = call(scan_back_in, [(grid, F32)], decay, grad_conv)
    end = 0.0
    for m in range(1, seq_count):
        end = end + jnp.exp(-rate * (block_len * (m - 1))) * shifted(local_back, -m)
    grad_signal, grad_gain, grad_moment = call(
        scan_back_out,
        [((block_len,) + grid[1:], F32), (grid, F32), (grid, F32)],
        decay,
        gain,
        end,
        start,
        signal[:CTX],
        grad_conv,
    )
    end_moment = block_len * jnp.exp(-rate * block_len) * start + local_moment
    grad_rate = -gain * (grad_moment + end * end_moment)
    grad_signal = grad_signal.reshape(block_len, features).astype(BF16)
    grad_signal = jnp.concatenate([grad_signal[CTX:], shifted(grad_signal[:CTX], -1)])

    grad_in = (
        dot(grad_queries, wq, NN)
        + dot(grad_token_keys, wk, NN)
        + dot(grad_token_values, wv, NN)
        + grad_signal.astype(F32) * valid
    )
    grad_attn_gain = jnp.sum(grad_in * normed_in, axis=0)
    grad_tokens = grad_resid + norm_back(normed_in, inverse_in, grad_in * attention_norm_gain)
    tokens_line = line_gather(grad_tokens.astype(BF16))

    def split(values):
        return values.reshape(values.shape[0], tp_count, 2, head_cols // 2)

    def both_rows(values):
        values = split(values)
        mine, other = values[:, :, 0], values[:, :, 1]
        joined = jnp.concatenate([mine, flip(other, 1)])
        return joined.reshape(joined.shape[0], -1)

    def both_full(values):
        return jnp.concatenate([values, flip(values, 1)])

    x_rows, c_rows, r_rows = both_full(attn_input), both_full(context), both_full(grad_resid_b)
    grads_a = [
        dot(both_rows(grad_queries), x_rows, TN),
        dot(both_rows(grad_token_keys), x_rows, TN),
        dot(both_rows(grad_token_values), x_rows, TN),
    ]
    grads_b = [
        dot(both_rows(grad_state_keys), c_rows, TN),
        dot(both_rows(grad_state_values), c_rows, TN),
        dot(both_rows(head_mix), r_rows, TN),
    ]

    def reduce_heads(grads, reverse):
        stack = jnp.stack([g.astype(BF16) for g in grads]).reshape(
            len(grads), tp_count, planes, head_rows, features
        )
        mine = plane_reduce(
            {p: jnp.transpose(stack[:, :, p], (1, 0, 2, 3)) for p in range(planes)}, reverse
        )
        return line_reduce([mine[j] for j in range(tp_count)])

    sum_a = reduce_heads(grads_a, False)
    sum_b = reduce_heads(grads_b, True)

    def spread(value, reverse):
        plane = plane_gather(value, reverse)
        other = {p: flip(v, 1) for p, v in plane.items()}
        return jnp.stack([(plane, other)[i & 1][i >> 1] for i in range(seq_count)])

    def ordered(stack):
        return [
            lax.dynamic_index_in_dim(stack, seq_index ^ i, 0, keepdims=False)
            for i in range(seq_count)
        ]

    fix = 1.0 / copies

    def head_grads(value, reverse):
        parts = ordered(spread(value, reverse))
        parts = [parts[2 * p + c] for c in range(2) for p in range(planes)]
        return jnp.concatenate(parts, axis=1).astype(F32) * fix

    def hidden_grads(value, reverse):
        return jnp.concatenate(ordered(spread(value, reverse))).astype(F32) * fix

    full_a = head_grads(sum_a, False)
    full_b = head_grads(sum_b, True)
    full_hidden = hidden_grads(sum_hidden, False)
    full_return = hidden_grads(sum_return, True)

    gains = lax.psum(jnp.stack([grad_attn_gain, grad_mlp_gain]), ("seq", "tp")) * fix
    kernel_grads = jnp.stack([grad_gain, grad_rate]).reshape(2, states, features)
    kernel_grads = lax.psum_scatter(
        jnp.transpose(kernel_grads, (2, 0, 1)).reshape(features, 2 * states),
        ("seq", "tp"),
        scatter_dimension=0,
        tiled=True,
    )
    kernel_grads = kernel_grads * fix

    def lined(line, dtype):
        stack = jnp.stack(line)
        return jnp.stack(
            [
                lax.dynamic_index_in_dim(
                    stack, (tp_index - b * copies) % tp_count, 0, keepdims=False
                )
                for b in range(sequences)
            ]
        ).astype(dtype)

    return (
        lined(output_line, BF16),
        lined(tokens_line, F32),
        gains[0],
        full_a[0].T,
        full_a[1].T,
        full_a[2].T,
        full_b[2],
        full_b[0].T,
        full_b[1].T,
        kernel_grads[:, :states],
        kernel_grads[:, states:],
        gains[1],
        full_hidden.T,
        full_return,
    )


LOG2E = math.log2(math.e)
SCALE = DH ** (-0.5)


def cost(us):
    return pl.CostEstimate(flops=int(us * 1.1e9), bytes_accessed=0, transcendentals=0)


def params(limit=42):
    return pltpu.CompilerParams(vmem_limit_bytes=limit * 2**20)


def like(shape, dtype=BF16):
    return jax.ShapeDtypeStruct(shape, dtype)


def whole(shape):
    return pl.BlockSpec(shape, lambda *_: (0,) * len(shape))


def launch(kernel, place, grid, in_specs, out_specs, outs, operands, scratch=(), us=5):
    return pl.pallas_call(
        kernel,
        grid_spec=pltpu.PrefetchScalarGridSpec(
            num_scalar_prefetch=1,
            grid=grid,
            in_specs=in_specs,
            out_specs=out_specs,
            scratch_shapes=list(scratch),
        ),
        out_shape=outs,
        compiler_params=params(),
        cost_estimate=cost(us),
    )(place, *operands)


def timed(us):
    return partial(launch, us=us)


def cycle(value, steps):
    count = lax.axis_size("tp")
    return lax.ppermute(value, "tp", [(i, (i + steps) % count) for i in range(count)])


def pack_heads(place, wq, wk, wv, wsk, wsv, wo, out, turned):
    chip = place[0] >> 1
    rows = out.shape[2]
    for w, ref in enumerate((wq, wk, wv, wsk, wsv, wo)):
        turned[...] = ref[...].astype(F32) if ref is wo else ref[...].astype(F32).T
        for p in range(4):
            cut = pl.ds(pl.multiple_of((chip ^ p) * rows, rows), rows)
            out[p, w] = turned[cut, :].astype(BF16)


def pack_hidden(place, wh, wr, out, turned):
    chip = place[0] >> 1
    rows = out.shape[2]
    for w, ref in enumerate((wh, wr)):
        turned[...] = ref[...].astype(F32).T if ref is wh else ref[...].astype(F32)
        for p in range(4):
            cut = pl.ds(pl.multiple_of((chip ^ p) * rows, rows), rows)
            out[p, w] = turned[cut, :].astype(BF16)


def load_heads(j, own, far, into, first, count):
    rows = own.shape[2]

    @pl.when(j == 0)
    def _():
        for p in range(4):
            for w in range(count):
                into[w, p * rows : (p + 1) * rows] = own[p, first + w]

    @pl.when(j > 0)
    def _():
        for p in range(4):
            for w in range(count):
                if p < 3:
                    into[w, p * rows : (p + 1) * rows] = far[p][0, first + w]
                else:
                    into[w, p * rows : (p + 1) * rows] = far[3 + (first + w) // 3][0, (first + w) % 3]


def masked(raw, r, block):
    n = raw.shape[1]
    column = lax.broadcasted_iota(jnp.int32, raw.shape, 1)
    row = lax.broadcasted_iota(jnp.int32, raw.shape, 0)
    keep = (column - (n - 128) <= row) & ((column >= CTX) | (block > 0))
    return jnp.where(keep, raw * (SCALE * LOG2E), NEGATIVE)


def project(place, x0, x1, own, f0, f1, f2, f3, f4, q_ref, k_ref, v_ref, weight):
    j = pl.program_id(0)
    load_heads(j, own, (f0, f1, f2, f3, f4), weight, 0, 3)
    rows = x0.shape[0]
    qkv_w = weight[0:3].reshape(3 * DH, -1)
    for half, x in enumerate((x0, x1)):
        saved = slice(half * rows, (half + 1) * rows)
        qkv = dot(x[...], qkv_w, NT).astype(BF16)
        q_ref[saved] = qkv[:, :DH]
        k_ref[saved] = qkv[:, DH : 2 * DH]
        v_ref[saved] = qkv[:, 2 * DH :]


def attend(place, c0, c1, own, f0, f1, f2, f3, f4, q_ref, k_ref, v_ref,
           part0, part1, s_ref, o_ref, lse_ref, weight, keys, values, total):
    j = pl.program_id(0)
    load_heads(j, own, (f0, f1, f2, f3, f4), weight, 3, 3)
    rows = part0.shape[0]

    @pl.when(j == 0)
    def _():
        total[...] = jnp.zeros_like(total)

    st_w = weight[0:2].reshape(2 * DH, -1)
    for half, c in enumerate((c0, c1)):
        base = half * rows
        state = dot(c[...], st_w, NT).astype(BF16)
        s_ref[half * CTX : (half + 1) * CTX] = state
        keys[half, 0:CTX] = state[:, :DH]
        values[half, 0:CTX] = state[:, DH:]
        keys[half, CTX:] = k_ref[base : base + rows]
        values[half, CTX:] = v_ref[base : base + rows]
    for half in range(2):
        block = place[0] ^ half
        base = half * rows
        for r in range(rows // 128):
            saved = slice(base + r * 128, base + (r + 1) * 128)
            n = CTX + (r + 1) * 128
            scores = masked(dot(q_ref[saved], keys[half, 0:n], NT), r, block)
            top = jnp.max(scores, axis=1, keepdims=True)
            power = jnp.exp2(scores - top)
            summed = jnp.sum(power, axis=1, keepdims=True)
            lse_ref[0, saved] = top + jnp.log2(summed)
            probs = (power * (1.0 / summed)).astype(BF16)
            o_ref[saved] = dot(probs, values[half, 0:n], NN).astype(BF16)
    for half in range(2):
        base = half * rows
        total[base : base + rows] += dot(o_ref[base : base + rows], weight[2], NN)

    @pl.when(j == pl.num_programs(0) - 1)
    def _():
        part0[...] = total[0:rows].astype(part0.dtype)
        part1[...] = total[rows:].astype(part1.dtype)


def attend_back(place, g0, g1, own, f0, f1, f2, f3, f4,
                q_ref, k_ref, v_ref, s_ref, lse_ref,
                in0, in1, ctx0, ctx1, d_ref, ds_ref,
                weight, keys, values, heads, grad_k, grad_v, total, ctx_total):
    j = pl.program_id(0)
    load_heads(j, own, (f0, f1, f2, f3, f4), weight, 0, 6)
    rows = g0.shape[0]

    @pl.when(j == 0)
    def _():
        total[...] = jnp.zeros_like(total)
        ctx_total[...] = jnp.zeros_like(ctx_total)

    qkv_w = weight[0:3].reshape(3 * DH, -1)
    st_w = weight[3:5].reshape(2 * DH, -1)
    for half, g in enumerate((g0, g1)):
        base = half * rows
        keys[half, 0:CTX] = s_ref[half * CTX : (half + 1) * CTX, :DH]
        values[half, 0:CTX] = s_ref[half * CTX : (half + 1) * CTX, DH:]
        keys[half, CTX:] = k_ref[base : base + rows]
        values[half, CTX:] = v_ref[base : base + rows]
        heads[half] = dot(g[...], weight[5], NT).astype(BF16)
    for half in range(2):
        block = place[0] ^ half
        base = half * rows
        for r in reversed(range(rows // 128)):
            saved = slice(base + r * 128, base + (r + 1) * 128)
            n = CTX + (r + 1) * 128
            q = q_ref[saved]
            own = heads[half, r * 128 : (r + 1) * 128]
            probs = jnp.exp2(masked(dot(q, keys[half, 0:n], NT), r, block) - lse_ref[0, saved])
            grad = dot(own, values[half, 0:n], NT)
            delta = jnp.sum(probs * grad, axis=1, keepdims=True)
            scores = (probs * (grad - delta)).astype(BF16)
            d_ref[saved, 0:DH] = (dot(scores, keys[half, 0:n], NN) * SCALE).astype(BF16)
            to_k = dot(scores, q, TN)
            to_v = dot(probs.astype(BF16), own, TN)
            if r == rows // 128 - 1:
                grad_k[half, 0:n] = to_k
                grad_v[half, 0:n] = to_v
            else:
                grad_k[half, 0:n] += to_k
                grad_v[half, 0:n] += to_v
    for half in range(2):
        base = half * rows
        d_ref[base : base + rows, DH : 2 * DH] = (grad_k[half, CTX:] * SCALE).astype(BF16)
        d_ref[base : base + rows, 2 * DH :] = grad_v[half, CTX:].astype(BF16)
        state = slice(half * CTX, (half + 1) * CTX)
        ds_ref[state, :DH] = (grad_k[half, 0:CTX] * SCALE).astype(BF16)
        ds_ref[state, DH:] = grad_v[half, 0:CTX].astype(BF16)
        ctx_total[state] += dot(ds_ref[state], st_w, NN)
        total[base : base + rows] += dot(d_ref[base : base + rows], qkv_w, NN)

    @pl.when(j == pl.num_programs(0) - 1)
    def _():
        in0[...] = total[0:rows].astype(in0.dtype)
        in1[...] = total[rows:].astype(in1.dtype)
        ctx0[...] = ctx_total[0:CTX].astype(ctx0.dtype)
        ctx1[...] = ctx_total[CTX:].astype(ctx1.dtype)


def attend_weights(place, x0, x1, c0, c1, g0, g1, d_ref, ds_ref, o_ref, keep_a, send_a, keep_b, send_b):
    rows = x0.shape[0]
    cut = keep_a.shape[3]
    to_qkv = (dot(d_ref[0:rows], x0[...], TN) + dot(d_ref[rows:], x1[...], TN)).astype(BF16)
    to_state = (dot(ds_ref[0:CTX], c0[...], TN) + dot(ds_ref[CTX:], c1[...], TN)).astype(BF16)
    to_out = (dot(o_ref[0:rows], g0[...], TN) + dot(o_ref[rows:], g1[...], TN)).astype(BF16)
    spots_a = {0: (keep_a, 0), 2: (keep_a, 1), 1: (send_a, 0), 3: (send_a, 1)}
    spots_b = {0: (keep_b, 0), 1: (keep_b, 1), 2: (send_b, 0), 3: (send_b, 1)}
    for p in range(4):
        out, at = spots_a[p]
        for w in range(3):
            out[at, 0, w] = to_qkv[w * DH + p * cut : w * DH + (p + 1) * cut]
        out, at = spots_b[p]
        for w in range(2):
            out[at, 0, w] = to_state[w * DH + p * cut : w * DH + (p + 1) * cut]
        out[at, 0, 2] = to_out[p * cut : (p + 1) * cut]


def gelu_parts(x):
    size = jnp.abs(x) * math.sqrt(0.5)
    bell = jnp.exp2(x * x * (-0.5 * LOG2E))
    t = 1.0 / (1.0 + 0.3275911 * size)
    poly = 1.061405429 * t - 1.453152027
    poly = poly * t + 1.421413741
    poly = poly * t - 0.284496736
    poly = poly * t + 0.254829592
    tail = 0.5 * poly * t * bell
    return jnp.where(x >= 0, 1.0 - tail, tail), bell * (1.0 / math.sqrt(2.0 * math.pi))


def load_hidden(j, w, own, far, into):
    rows = own.shape[2]

    @pl.when(j == 0)
    def _():
        for p in range(4):
            into[p * rows : (p + 1) * rows] = own[p, w]

    @pl.when(j > 0)
    def _():
        for p in range(3):
            into[p * rows : (p + 1) * rows] = far[p][0, w]
        into[3 * rows :] = far[3 + w][0]


def feed_in(place, m0, m1, own, f0, f1, f2, f3, act_ref, slope_ref, wh):
    load_hidden(pl.program_id(0), 0, own, (f0, f1, f2, f3), wh)
    rows = m0.shape[0]
    for half, m in enumerate((m0, m1)):
        saved = slice(half * rows, (half + 1) * rows)
        pre = dot(m[...], wh[...], NT)
        part, bell = gelu_parts(pre)
        act_ref[saved] = (pre * part).astype(BF16)
        slope_ref[saved] = (part + pre * bell).astype(BF16)


def feed_out(place, g0, g1, own, f0, f1, f2, f3, f4, act_ref, slope_ref,
             mlp0, mlp1, mid0, mid1, pre_ref, wh, wr, mlp, mid):
    j = pl.program_id(0)
    load_hidden(j, 0, own, (f0, f1, f2, f3, f4), wh)
    load_hidden(j, 1, own, (f0, f1, f2, f3, f4), wr)
    rows = g0.shape[0]

    @pl.when(j == 0)
    def _():
        mlp[...] = jnp.zeros_like(mlp)
        mid[...] = jnp.zeros_like(mid)

    for half, g in enumerate((g0, g1)):
        saved = slice(half * rows, (half + 1) * rows)
        back = dot(g[...], wr[...], NT)
        pre_ref[saved] = (back * slope_ref[saved].astype(F32)).astype(BF16)
        mlp[saved] += dot(act_ref[saved], wr[...], NN)
        mid[saved] += dot(pre_ref[saved], wh[...], NN)

    @pl.when(j == pl.num_programs(0) - 1)
    def _():
        mlp0[...] = mlp[0:rows].astype(mlp0.dtype)
        mlp1[...] = mlp[rows:].astype(mlp1.dtype)
        mid0[...] = mid[0:rows].astype(mid0.dtype)
        mid1[...] = mid[rows:].astype(mid1.dtype)


def feed_weights(keeps, place, a0, a1, b_ref, keep, send):
    rows = a0.shape[0]
    cut = keep.shape[2]
    sends = [p for p in range(4) if p not in keeps]
    grad = (dot(b_ref[0:rows], a0[...], TN) + dot(b_ref[rows:], a1[...], TN)).astype(BF16)
    for p in range(4):
        out, at = (keep, keeps.index(p)) if p in keeps else (send, sends.index(p))
        out[at, 0] = grad[p * cut : (p + 1) * cut]


def live_rows(place, count):
    at = place[0] * (count * pl.num_programs(0)) + pl.program_id(0) * count
    position = at + lax.broadcasted_iota(jnp.int32, (count, 1), 0)
    return (position < place[2]).astype(F32)


def middle(place, tokens, own, got, gain, residual, m_ref):
    value = tokens[0].astype(F32) + own[...] + got[...].astype(F32)
    residual[...] = value
    m_ref[...] = (normalize(value)[0] * gain[...]).astype(BF16)


def finish(place, residual, own, got, out):
    value = residual[...] + own[...] + got[...].astype(F32)
    out[...] = (value * live_rows(place, value.shape[0])).astype(BF16)


def middle_back(place, residual, own, got, cot, gain, grad, grad_b, sums):
    value = residual[...]
    normed, inverse = normalize(value)
    valid = live_rows(place, value.shape[0])
    back = own[...] + got[...].astype(F32)
    total = jnp.sum(back * normed, axis=0, keepdims=True)

    @pl.when(pl.program_id(0) == 0)
    def _():
        sums[...] = total

    @pl.when(pl.program_id(0) > 0)
    def _():
        sums[...] += total

    value = cot[0].astype(F32) * valid + norm_back(normed, inverse, back * gain[...])
    grad[...] = value
    grad_b[...] = value.astype(BF16)


def first_back(place, tokens, own, got, signal, grad, gain, out, sums):
    normed, inverse = normalize(tokens[0].astype(F32))
    valid = live_rows(place, out.shape[0])
    back = own[...] + got[...].astype(F32) + signal[...].astype(F32) * valid
    total = jnp.sum(back * normed, axis=0, keepdims=True)

    @pl.when(pl.program_id(0) == 0)
    def _():
        sums[...] = total

    @pl.when(pl.program_id(0) > 0)
    def _():
        sums[...] += total

    out[...] = (grad[...] + norm_back(normed, inverse, back * gain[...])).astype(BF16)


def unpack_heads(place, n0, n1, n2, n3, f0, f1, f2, f3, q, k, v, o, sk, sv, rows_ref):
    core, chip = place[0] & 1, place[0] >> 1
    cut = n0.shape[1]
    for w, out in ((0, q), (1, k), (2, v), (3, sk), (4, sv), (5, o)):
        for other, pieces in ((0, (n0, n1, n2, n3)), (1, (f0, f1, f2, f3))):
            for p, piece in enumerate(pieces):
                at = (core ^ other) * DH + (chip ^ p) * cut
                rows_ref[pl.ds(pl.multiple_of(at, cut), cut), :] = piece[w].astype(F32)
        out[...] = rows_ref[...] if out is o else rows_ref[...].T


def unpack_hidden(place, n0, n1, n2, n3, f0, f1, f2, f3, h, r):
    core, chip = place[0] & 1, place[0] >> 1
    cut = n0.shape[1]
    for other, pieces in ((0, (n0, n1, n2, n3)), (1, (f0, f1, f2, f3))):
        for p, piece in enumerate(pieces):
            at = pl.multiple_of((core ^ other) * 4 * cut + (chip ^ p) * cut, cut)
            r[pl.ds(at, cut), :] = piece[1].astype(F32)
            h[:, pl.ds(at, cut)] = piece[0].astype(F32).T


def add(a, b):
    return (a.astype(F32) + b.astype(F32)).astype(BF16)


def after(value, *earlier):
    return lax.optimization_barrier((value, *earlier))[0]


def powers(lengths, rate_ref, *outs):
    for length, out in zip(lengths, outs):
        out[...] = jnp.exp(-rate_ref[...] * float(length))


def states_around(local, power, sign, first, *earlier):
    group = local
    for m in (1, 2):
        group = group + power[m] * shifted(local, sign * m)
    group = after(group, *earlier)
    total = shifted(group, sign * first)
    for m in range(first + 3, 8, 3):
        total = total + power[m - first] * shifted(group, sign * m)
    return total


def scan_rows(decay_ref, gain_ref, late_ref, g_ref, y_ref, end_ref):
    decay, gain = decay_ref[...], gain_ref[...]
    rows, count = y_ref.shape[0], g_ref.shape[0]

    def full(t, lam):
        lam = lam + g_ref[count - 1 - t]
        y_ref[rows - 1 - t] = jnp.sum(gain * lam, axis=0)
        return decay * lam

    def empty(t, lam):
        y_ref[rows - count - 1 - t] = jnp.sum(gain * lam, axis=0)
        return decay * lam

    lam = lax.fori_loop(0, count, full, late_ref[...], unroll=8)
    end_ref[...] = lam
    lax.fori_loop(0, rows - count, empty, lam, unroll=8)


def scan_sums(decay_ref, start_ref, u_ref, g_ref, gh_ref, gm_ref):
    decay = decay_ref[...]

    def again(t, carry):
        h, m, gh, gm = carry
        h, m = decay * h + u_ref[t], decay * (m + h)
        g = g_ref[t]
        return h, m, gh + g * h, gm + g * m

    zero = jnp.zeros(decay.shape, F32)
    _, _, gh, gm = lax.fori_loop(0, u_ref.shape[0], again, (start_ref[...], zero, zero, zero))
    gh_ref[...] = gh
    gm_ref[...] = gm


def fast_body(
    tokens, lengths, attention_norm_gain, query_weight, key_weight, value_weight, output_weight,
    state_key_weight, state_value_weight, state_coefficient, state_rate, feedforward_norm_gain,
    hidden_weight, return_weight, cotangent,
):
    sequences, block_len, features = tokens.shape
    tp_count = lax.axis_size("tp")
    seq_index = lax.axis_index("seq")
    tp_index = lax.axis_index("tp")
    hidden_cols = hidden_weight.shape[1]
    cut = DH // 4
    wide = hidden_cols // 8
    length = lax.dynamic_index_in_dim(lengths, tp_index, 0, keepdims=False)
    place = jnp.stack([seq_index, tp_index, length]).astype(jnp.int32)

    column = pl.BlockSpec((features, DH), lambda i, place: (0, place[0] & 1))
    (own_w,) = timed(4)(
        pack_heads, place, (1,),
        [column] * 5 + [pl.BlockSpec((DH, features), lambda i, place: (place[0] & 1, 0))],
        [whole((4, 6, cut, features))],
        [like((4, 6, cut, features))],
        (query_weight, key_weight, value_weight, state_key_weight, state_value_weight, output_weight),
        [pltpu.VMEM((DH, features), F32)],
    )
    (own_m,) = timed(5)(
        pack_hidden, place, (1,),
        [
            pl.BlockSpec((features, hidden_cols // 2), lambda i, place: (0, place[0] & 1)),
            pl.BlockSpec((hidden_cols // 2, features), lambda i, place: (place[0] & 1, 0)),
        ],
        [whole((4, 2, wide, features))],
        [like((4, 2, wide, features))],
        (hidden_weight, return_weight),
        [pltpu.VMEM((hidden_cols // 2, features), F32)],
    )

    own_tokens = lax.dynamic_index_in_dim(tokens, tp_index, 0, keepdims=False)
    own_cot = lax.dynamic_index_in_dim(cotangent, tp_index, 0, keepdims=False)
    before = shifted(own_tokens[block_len - CTX :], 1)
    positions = seq_index * block_len - CTX + jnp.arange(block_len + CTX)
    live = ((positions < length) & (positions >= 0)).astype(F32)[:, None]
    x = (normalize(own_tokens.astype(F32))[0] * attention_norm_gain).astype(BF16)
    x_other = flip(x, 1)
    grad_out = (own_cot.astype(F32) * live[CTX:]).astype(BF16)
    grad_out_other = flip(grad_out, 1)
    early = (normalize(before.astype(F32))[0] * attention_norm_gain).astype(BF16)
    signal = tiles(
        jnp.concatenate([early, x[: block_len - CTX]]).astype(F32) * live[:block_len]
    )

    states = state_rate.shape[1]
    channels = state_rate.shape[0]
    both = jnp.stack([state_rate, state_coefficient]).reshape(1, -1, 128)
    devices = features // channels
    both = lax.all_to_all(
        jnp.broadcast_to(both, (devices,) + both.shape[1:]), ("seq", "tp"), 0, 0
    )
    both = jnp.transpose(both.reshape(devices, 2, channels, states), (1, 3, 0, 2))
    both = both.reshape(2, states, features // 128, 128)
    rate, gain = both[0], both[1]
    grid = rate.shape
    spans = [1, block_len - CTX] + [block_len * m for m in (1, 2, 3, 6)]
    decay, tail_power, *blocks = call(
        partial(powers, spans), [(grid, F32)] * len(spans), rate, us=1
    )
    block_power = dict(zip((1, 2, 3, 6), blocks))

    def line_of(own):
        return jnp.stack([cycle(own, j) for j in range(1, tp_count)])

    def plane_of(line, by_x, by_y, half):
        return [line, by_x, by_y, flip(by_y[:, :half], 2), flip(by_x[:, half:], 4)]

    line_w = line_of(own_w[0])
    near_w = flip(line_w, 2), flip(line_w, 4)
    far_w = plane_of(line_w, *near_w, 3)
    line_m = line_of(after(own_m[0], line_w))
    near_m = flip(after(line_m, *near_w), 2), flip(after(line_m, *near_w), 4)
    far_m = plane_of(line_m, *near_m, 1)
    far_m[3:] = [value[:, 0] for value in far_m[3:]]

    local_state, local_moment = call(
        scan_in, [(grid, F32)] * 2, decay, after(signal, line_w, own_m, x_other, grad_out_other), us=8
    )
    start = states_around(after(local_state, *near_w), block_power, 1, 1)
    (context,) = call(scan_out, [((CTX,) + grid[1:], F32)], decay, gain, start, signal[:CTX], us=3)
    context = context.reshape(CTX, features).astype(BF16)
    context_other = flip(context, 1)
    rows = 2 * block_len
    slots = tp_count
    own_spec = whole((4, 6, cut, features))

    def slot_spec(*shape):
        return pl.BlockSpec(
            (1, *shape, features),
            lambda j, place: (jnp.maximum(j - 1, 0),) + (0,) * (len(shape) + 1),
        )

    weight_specs = [own_spec] + [slot_spec(6, cut)] * 3 + [slot_spec(3, cut)] * 2
    weights = (own_w, *far_w)
    full = whole((block_len, features))
    ctx_spec = whole((CTX, features))
    head = lambda n, width: pl.BlockSpec((n, width), lambda j, place: (0, j))
    lse_spec = pl.BlockSpec((1, rows, 1), lambda j, place: (j, 0, 0))
    q, k, v = timed(8)(
        project, place, (slots,),
        [full] * 2 + weight_specs,
        [head(rows, DH)] * 3,
        [like((rows, slots * DH))] * 3,
        (x, x_other, *weights),
        [pltpu.VMEM((3, DH, features), BF16)],
    )
    attended = timed(20)(
        attend, place, (slots,),
        [ctx_spec] * 2 + weight_specs + [head(rows, DH)] * 3,
        [full] * 2 + [head(2 * CTX, 2 * DH), head(rows, DH), lse_spec],
        [like((block_len, features), F32), like((block_len, features))]
        + [like((2 * CTX, slots * 2 * DH)), like((rows, slots * DH)), like((slots, rows, 1), F32)],
        (after(context, line_m), context_other, *weights, q, k, v),
        [
            pltpu.VMEM((3, DH, features), BF16),
            pltpu.VMEM((2, CTX + block_len, DH), BF16),
            pltpu.VMEM((2, CTX + block_len, DH), BF16),
            pltpu.VMEM((rows, features), F32),
        ],
    )
    part, part_other, state, mix, lse = attended
    group = 128
    steps = block_len // group
    row_spec = pl.BlockSpec((group, features), lambda i, place: (i, 0))
    seq_spec = pl.BlockSpec((1, group, features), lambda i, place: (place[1], i, 0))
    gain_spec = whole((1, features))
    mid_gain = feedforward_norm_gain.reshape(1, -1)
    residual, m = timed(4)(
        middle, place, (steps,),
        [seq_spec, row_spec, row_spec, gain_spec], [row_spec] * 2,
        [like((block_len, features), F32), like((block_len, features))],
        (tokens, part, after(flip(part_other, 1), *near_m), mid_gain),
    )
    m_other = flip(m, 1)

    hidden_own = whole((4, 2, wide, features))
    hidden_far = [slot_spec(2, wide)] * 3 + [slot_spec(wide)]
    chunk = 4 * wide
    act, slope = timed(14)(
        feed_in, place, (slots,),
        [full] * 2 + [hidden_own] + hidden_far,
        [head(rows, chunk)] * 2,
        [like((rows, slots * chunk))] * 2,
        (m, m_other, own_m, *far_m[:4]),
        [pltpu.VMEM((chunk, features), BF16)],
    )
    mlp, mlp_other, mid, mid_other, pre = timed(21)(
        feed_out, place, (slots,),
        [full] * 2 + [hidden_own] + hidden_far + hidden_far[3:] + [head(rows, chunk)] * 2,
        [full] * 4 + [head(rows, chunk)],
        [like((block_len, features), F32), like((block_len, features))] * 2
        + [like((rows, slots * chunk))],
        (grad_out, grad_out_other, own_m, *far_m, act, slope),
        [pltpu.VMEM((chunk, features), BF16)] * 2 + [pltpu.VMEM((rows, features), F32)] * 2,
    )
    mid_got, mlp_got = flip(mid_other, 1), flip(mlp_other, 1)
    grad_spec = pl.BlockSpec((2, 1, wide, features), lambda j, place: (0, j, 0, 0))
    hidden_grads = partial(
        launch, place=place, grid=(slots,), us=8,
        in_specs=[full] * 2 + [head(rows, chunk)], out_specs=[grad_spec] * 2,
        outs=[like((2, slots, wide, features))] * 2,
    )
    keep_r, send_r = hidden_grads(
        partial(feed_weights, (0, 1)), operands=(grad_out, grad_out_other, after(act, pre))
    )
    mlp_got = after(mlp_got, keep_r)
    mid_got = after(mid_got, keep_r)
    (output,) = timed(3)(
        finish, place, (steps,),
        [row_spec] * 3, [row_spec], [like((block_len, features))], (residual, mlp, mlp_got),
    )
    output_all = lax.all_gather(output, "tp")
    resid, resid_b, sums_mid = timed(5)(
        middle_back, place, (steps,),
        [row_spec] * 3 + [seq_spec, gain_spec], [row_spec] * 2 + [gain_spec],
        [
            like((block_len, features), F32), like((block_len, features)),
            like((1, features), F32),
        ],
        (after(residual, output), mid, mid_got, cotangent, mid_gain),
    )
    resid_other = flip(resid_b, 1)
    keep_h, send_h = hidden_grads(
        partial(feed_weights, (0, 2)), operands=(m, m_other, after(pre, resid_b))
    )

    grad_in, grad_in_other, grad_ctx, grad_ctx_other, d, ds = timed(27)(
        attend_back, place, (slots,),
        [full] * 2 + weight_specs + [head(rows, DH)] * 3 + [head(2 * CTX, 2 * DH), lse_spec],
        [full] * 2 + [ctx_spec] * 2 + [head(rows, 3 * DH), head(2 * CTX, 2 * DH)],
        [
            like((block_len, features), F32), like((block_len, features)),
            like((CTX, features), F32), like((CTX, features)),
            like((rows, slots * 3 * DH)), like((2 * CTX, slots * 2 * DH)),
        ],
        (after(resid_b, keep_h), resid_other, *weights, q, k, v, state, lse),
        [
            pltpu.VMEM((6, DH, features), BF16),
            pltpu.VMEM((2, CTX + block_len, DH), BF16),
            pltpu.VMEM((2, CTX + block_len, DH), BF16),
            pltpu.VMEM((2, block_len, DH), BF16),
            pltpu.VMEM((2, CTX + block_len, DH), F32),
            pltpu.VMEM((2, CTX + block_len, DH), F32),
            pltpu.VMEM((rows, features), F32),
            pltpu.VMEM((2 * CTX, features), F32),
        ],
    )
    grad_ctx_got = flip(grad_ctx_other, 1)
    grad_in_got = flip(grad_in_other, 1)
    part_spec = pl.BlockSpec((2, 1, 3, cut, features), lambda j, place: (0, j, 0, 0, 0))
    keep_a, send_a, keep_b, send_b = timed(10)(
        attend_weights, place, (slots,),
        [full] * 2 + [ctx_spec] * 2 + [full] * 2
        + [head(rows, 3 * DH), head(2 * CTX, 2 * DH), head(rows, DH)],
        [part_spec] * 4,
        [like((2, slots, 3, cut, features))] * 4,
        (x, x_other, context, context_other, resid_b, resid_other, d, ds, mix),
    )

    got_r = flip(after(send_r, resid_b), 4)
    got_h = flip(after(send_h, resid_b), 2)
    near_h, away_h = add(keep_h[0], got_h[0]), add(keep_h[1], got_h[1])
    near_r, away_r = add(keep_r[0], got_r[0]), add(keep_r[1], got_r[1])
    grad_context = (grad_ctx + grad_ctx_got.astype(F32)).astype(BF16)
    grad_conv = tiles(after(grad_context, got_r, got_h))
    grad_later = tiles(shifted(grad_context, -1))
    (local_back,) = call(scan_back_in, [(grid, F32)], decay, grad_conv)
    late = tail_power * states_around(local_back, block_power, -1, 2, keep_a, away_h, away_r)
    grad_signal, end = call(
        scan_rows, [((block_len,) + grid[1:], F32), (grid, F32)], decay, gain, late, grad_later
    )
    grad_signal = grad_signal.reshape(block_len, features).astype(BF16)
    grad_tokens, sums_in = timed(5)(
        first_back, place, (steps,),
        [seq_spec] + [row_spec] * 4 + [gain_spec], [row_spec, gain_spec],
        [like((block_len, features)), like((1, features), F32)],
        (tokens, grad_in, grad_in_got, grad_signal, after(resid, output_all), attention_norm_gain.reshape(1, -1)),
    )

    lefts, rights = line_steps(grad_tokens)
    line = [grad_tokens] + [
        jnp.where(tp_index >= j, lefts[j], rights[slots - j]) for j in range(1, slots)
    ]
    line = jnp.stack(line)
    tokens_all = jnp.stack(
        [
            lax.dynamic_index_in_dim(line, (tp_index - b) % slots, 0, keepdims=False)
            for b in range(sequences)
        ]
    ).astype(F32)
    grad_gain, grad_moment = call(
        scan_sums, [(grid, F32)] * 2, decay, after(start, grad_tokens), signal[:CTX], grad_conv
    )
    end_moment = block_len * block_power[1] * start + local_moment
    grad_rate = -gain * (grad_moment + end * end_moment)

    def regather(total):
        held = [total, flip(total, 2), flip(total, 4), flip(total, 6)]
        return held + [flip(value, 1) for value in held]

    ready = (late, grad_later)
    more_h, more_r = flip(after(away_h, *ready), 4), flip(after(away_r, *ready), 2)
    more_h, more_r = after(more_h, grad_tokens), after(more_r, grad_tokens)
    got_a = flip(after(send_a, more_h, more_r), 2)
    got_b = flip(after(send_b, more_h, more_r), 4)
    pairs = (near_h, more_h), (near_r, more_r)
    total_m = line_reduce(
        [jnp.stack([add(a[j], b[j]) for a, b in pairs]) for j in range(slots)],
        list(zip(lefts[1:], rights[1:])),
    )
    near_a, away_a = add(keep_a[0], got_a[0]), add(keep_a[1], got_a[1])
    near_b, away_b = add(keep_b[0], got_b[0]), add(keep_b[1], got_b[1])
    pairs = (near_a, flip(away_a, 4)), (near_b, flip(away_b, 2))
    total_a = line_reduce(
        [jnp.stack([add(a[j], b[j]) for a, b in pairs]) for j in range(slots)]
    )
    pieces_m = regather(total_m)
    pieces_a = regather(total_a.reshape(6, cut, features))
    grad_hidden, grad_return = timed(5)(
        unpack_hidden, place, (1,),
        [whole((2, wide, features))] * 8,
        [whole((features, hidden_cols)), whole((hidden_cols, features))],
        [like((features, hidden_cols), F32), like((hidden_cols, features), F32)],
        pieces_m,
    )
    grad_q, grad_k, grad_v, grad_o, grad_sk, grad_sv = timed(5)(
        unpack_heads, place, (1,),
        [whole((6, cut, features))] * 8,
        [whole((features, 2 * DH))] * 3 + [whole((2 * DH, features))] + [whole((features, 2 * DH))] * 2,
        [like((features, 2 * DH), F32)] * 3
        + [like((2 * DH, features), F32)]
        + [like((features, 2 * DH), F32)] * 2,
        pieces_a,
        [pltpu.VMEM((2 * DH, features), F32)],
    )

    small = jnp.stack([grad_gain, grad_rate]).reshape(2, states, devices, channels)
    small = jnp.transpose(small, (2, 3, 0, 1)).reshape(devices, -1, 128)
    sums = jnp.concatenate([sums_in, sums_mid]).reshape(1, -1, 128)
    sums = jnp.broadcast_to(sums, (devices,) + sums.shape[1:])
    count = small.shape[1]
    small = jnp.sum(
        lax.all_to_all(
            after(jnp.concatenate([small, sums], axis=1), total_a), ("seq", "tp"), 0, 0
        ),
        axis=0,
    )
    kernel_grads = small[:count].reshape(channels, 2, states)
    gains = small[count:].reshape(2, features)

    return (
        output_all, tokens_all, gains[0], grad_q, grad_k, grad_v, grad_o, grad_sk, grad_sv,
        kernel_grads[:, 0], kernel_grads[:, 1], gains[1], grad_hidden, grad_return,
    )


def choose(tokens, *others):
    query_weight = others[2]
    fits = (
        lax.axis_size("seq") == 8
        and lax.axis_size("tp") == tokens.shape[0]
        and query_weight.shape[1] == 2 * DH
        and others[11].shape[1] % 1024 == 0
        and tokens.shape[1] % 512 == 0
        and tokens.shape[2] == 1024
    )
    return (fast_body if fits else body)(tokens, *others)


def solution(mesh):
    rows = P(None, "seq", None)
    columns = P(None, "tp")
    heads = P("tp", None)
    channels = P(("seq", "tp"), None)
    return jax.shard_map(
        choose,
        mesh=mesh,
        in_specs=(
            rows, P(), P(), columns, columns, columns, heads, columns, columns,
            channels, channels, P(), columns, heads, rows,
        ),
        out_specs=(
            rows, rows, P(), columns, columns, columns, heads, columns, columns,
            channels, channels, P(), columns, heads,
        ),
        check_vma=False,
    )
```

```python
from functools import partial
import math

import jax
import jax.numpy as jnp
from jax import lax
from jax.experimental import pallas as pl
from jax.experimental.pallas import tpu as pltpu
from jax.sharding import PartitionSpec as P

DH = 128
CTX = 128
EPS = 1e-05
NEGATIVE = -1e30
F32 = jnp.float32
BF16 = jnp.bfloat16


def normalize(values):
    center = values - jnp.mean(values, axis=-1, keepdims=True)
    inverse = lax.rsqrt(jnp.mean(center * center, axis=-1, keepdims=True) + EPS)
    return (center * inverse, inverse)


def norm_back(normed, inverse, grad_normed):
    mean_grad = jnp.mean(grad_normed, axis=-1, keepdims=True)
    mean_cross = jnp.mean(grad_normed * normed, axis=-1, keepdims=True)
    return inverse * (grad_normed - mean_grad - normed * mean_cross)


def flip(value, mask):
    count = lax.axis_size("seq")
    return lax.ppermute(value, "seq", [(i, i ^ mask) for i in range(count)])


def shifted(value, steps):
    count = lax.axis_size("seq")
    first, last = (max(0, -steps), min(count, count - steps))
    return lax.ppermute(value, "seq", [(i, i + steps) for i in range(first, last)])


def line_steps(value):
    count = lax.axis_size("tp")
    lefts, rights = [value], [value]
    for k in range(1, count):
        lefts.append(lax.ppermute(lefts[-1], "tp", [(i, i + 1) for i in range(k - 1, count - 1)]))
        rights.append(
            lax.ppermute(rights[-1], "tp", [(i, i - 1) for i in range(1, count - k + 1)])
        )
    return lefts, rights


def line_gather(value):
    count = lax.axis_size("tp")
    place = lax.axis_index("tp")
    lefts, rights = line_steps(value)
    return [value] + [
        jnp.where(place >= j, lefts[j], rights[count - j]) for j in range(1, count)
    ]


def line_reduce(chunks, pace=None):
    count = lax.axis_size("tp")

    def add(a, b, k):
        if pace:
            a = lax.optimization_barrier((a, *pace[k - 1]))[0]
        return a if b is None else (a.astype(F32) + b.astype(F32)).astype(BF16)

    going, coming = None, None
    for k in range(1, count):
        going = lax.ppermute(add(chunks[k], going, k), "tp", [(i, i + 1) for i in range(k)])
        coming = lax.ppermute(
            add(chunks[count - k], coming, k), "tp", [(i, i - 1) for i in range(count - k, count)]
        )
    return (chunks[0].astype(F32) + going.astype(F32) + coming.astype(F32)).astype(BF16)


def plane_bits(reverse):
    count = lax.axis_size("seq") // 2
    bits = [1 << b for b in range(count.bit_length() - 1)]
    return bits[::-1] if reverse else bits


def plane_gather(value, reverse):
    held = {0: value}
    for bit in plane_bits(reverse):
        held.update({p | bit: flip(v, 2 * bit) for p, v in list(held.items())})
    return held


def plane_reduce(pieces, reverse):
    held = dict(pieces)
    for bit in plane_bits(reverse):
        for p in [p for p in held if p & bit]:
            got = flip(held.pop(p), 2 * bit)
            held[p ^ bit] = (held[p ^ bit].astype(F32) + got.astype(F32)).astype(BF16)
    return held[0]


def scan_in(decay_ref, u_ref, state_ref, moment_ref):
    decay = decay_ref[...]

    def step(t, carry):
        h, m = carry
        return decay * h + u_ref[t], decay * (m + h)

    zero = jnp.zeros(decay.shape, F32)
    h, m = lax.fori_loop(0, u_ref.shape[0], step, (zero, zero))
    state_ref[...] = h
    moment_ref[...] = m


def scan_out(decay_ref, gain_ref, start_ref, u_ref, y_ref):
    decay, gain = decay_ref[...], gain_ref[...]

    def step(t, h):
        h = decay * h + u_ref[t]
        y_ref[t] = jnp.sum(gain * h, axis=0)
        return h

    lax.fori_loop(0, u_ref.shape[0], step, start_ref[...])


def scan_back_in(decay_ref, g_ref, state_ref):
    decay = decay_ref[...]
    last = g_ref.shape[0] - 1

    def step(t, lam):
        return decay * (lam + g_ref[last - t])

    state_ref[...] = lax.fori_loop(0, last + 1, step, jnp.zeros(decay.shape, F32))


def scan_back_out(decay_ref, gain_ref, end_ref, start_ref, u_ref, g_ref, y_ref, gh_ref, gm_ref):
    decay, gain = decay_ref[...], gain_ref[...]
    rows, count = y_ref.shape[0], g_ref.shape[0]

    def empty(t, lam):
        y_ref[rows - 1 - t] = jnp.sum(gain * lam, axis=0)
        return decay * lam

    def full(t, lam):
        lam = lam + g_ref[count - 1 - t]
        y_ref[count - 1 - t] = jnp.sum(gain * lam, axis=0)
        return decay * lam

    lam = lax.fori_loop(0, rows - count, empty, end_ref[...])
    lax.fori_loop(0, count, full, lam)

    def again(t, carry):
        h, m, gh, gm = carry
        h, m = decay * h + u_ref[t], decay * (m + h)
        g = g_ref[t]
        return h, m, gh + g * h, gm + g * m

    zero = jnp.zeros(decay.shape, F32)
    _, _, gh, gm = lax.fori_loop(0, count, again, (start_ref[...], zero, zero, zero))
    gh_ref[...] = gh
    gm_ref[...] = gm


def call(kernel, outs, *operands, us=5):
    return pl.pallas_call(
        kernel,
        out_shape=[jax.ShapeDtypeStruct(shape, dtype) for shape, dtype in outs],
        compiler_params=pltpu.CompilerParams(vmem_limit_bytes=42 * 2**20),
        cost_estimate=pl.CostEstimate(flops=int(us * 1.1e9), bytes_accessed=0, transcendentals=0),
    )(*operands)


def tiles(values):
    return values.astype(F32).reshape(values.shape[0], values.shape[1] // 128, 128)


def dot(a, b, dims):
    return lax.dot_general(a, b, (dims, ((), ())), preferred_element_type=F32)


NN = ((1,), (0,))
NT = ((1,), (1,))
TN = ((0,), (0,))


def body(
    tokens,
    lengths,
    attention_norm_gain,
    query_weight,
    key_weight,
    value_weight,
    output_weight,
    state_key_weight,
    state_value_weight,
    state_coefficient,
    state_rate,
    feedforward_norm_gain,
    hidden_weight,
    return_weight,
    cotangent,
):
    sequences, block_len, features = tokens.shape
    seq_count = lax.axis_size("seq")
    tp_count = lax.axis_size("tp")
    seq_index = lax.axis_index("seq")
    tp_index = lax.axis_index("tp")
    planes = seq_count // 2
    copies = tp_count // sequences
    sequence = tp_index // copies
    head_cols = query_weight.shape[1]
    hidden_cols = hidden_weight.shape[1]
    heads = head_cols * tp_count // DH
    head_rows = head_cols // seq_count
    hidden_rows = hidden_cols // seq_count
    scale = DH ** (-0.5)

    shard_a = [query_weight.T, key_weight.T, value_weight.T]
    shard_b = [state_key_weight.T, state_value_weight.T, output_weight]
    shard_m = [hidden_weight.T, return_weight]

    def head_slice(shard, relative):
        other = seq_index ^ relative
        at = (other & 1) * planes + (other >> 1)
        return lax.dynamic_slice_in_dim(shard, at * head_rows, head_rows, 0)

    def hidden_slice(shard, relative):
        return lax.dynamic_slice_in_dim(
            shard, (seq_index ^ relative) * hidden_rows, hidden_rows, 0
        )

    def gather_heads(shards, reverse):
        mine = jnp.stack([head_slice(w, 0) for w in shards])
        line = jnp.stack(line_gather(mine)[1:])
        plane = plane_gather(line, reverse)
        other = {p: flip(v, 1) for p, v in plane.items()}
        far = jnp.stack(
            [jnp.stack([group[p] for p in range(planes)]) for group in (plane, other)]
        )
        far = jnp.transpose(far, (3, 2, 0, 1, 4, 5))
        own = jnp.stack(
            [
                jnp.concatenate([head_slice(w, 2 * p + c) for c in range(2) for p in range(planes)])
                for w in shards
            ]
        )
        far = far.reshape(len(shards), (tp_count - 1) * head_cols, features)
        return jnp.concatenate([own, far], axis=1)

    def gather_hidden(shard, reverse):
        line = line_gather(hidden_slice(shard, 0))
        plane = plane_gather(jnp.concatenate(line[1:]), reverse)
        return jnp.concatenate(
            [
                piece
                for p in range(planes)
                for piece in (hidden_slice(shard, 2 * p), plane[p])
            ]
        )

    wq, wk, wv = gather_heads(shard_a, False)
    wsk, wsv, wo = gather_heads(shard_b, True)
    wh = gather_hidden(shard_m[0], False)
    wr = gather_hidden(shard_m[1], True)

    own_tokens = lax.dynamic_index_in_dim(tokens, sequence, 0, keepdims=False)
    own_cot = lax.dynamic_index_in_dim(cotangent, sequence, 0, keepdims=False)
    length = lax.dynamic_index_in_dim(lengths, sequence, 0, keepdims=False)
    before = shifted(own_tokens[block_len - CTX :], 1)
    positions = seq_index * block_len - CTX + jnp.arange(block_len + CTX)
    live = ((positions < length) & (positions >= 0)).astype(F32)[:, None]
    valid = live[CTX:]
    inputs = own_tokens.astype(F32)
    normed_in, inverse_in = normalize(inputs)
    attn_input = (normed_in * attention_norm_gain).astype(BF16)
    early = (normalize(before.astype(F32))[0] * attention_norm_gain).astype(BF16)
    window = jnp.concatenate([early, attn_input[: block_len - CTX]]).astype(F32) * live[:block_len]
    signal = tiles(window)

    both = jnp.stack([state_rate, state_coefficient])
    both = lax.all_gather(both, ("seq", "tp"), axis=1, tiled=True)
    states = both.shape[2]
    both = jnp.transpose(both, (0, 2, 1)).reshape(2, states, features // 128, 128)
    rate, gain = both[0], both[1]
    decay = jnp.exp(-rate)
    grid = rate.shape
    local_state, local_moment = call(scan_in, [(grid, F32)] * 2, decay, signal)
    start = 0.0
    for m in range(1, seq_count):
        start = start + jnp.exp(-rate * (block_len * (m - 1))) * shifted(local_state, m)
    (context,) = call(
        scan_out, [((CTX,) + grid[1:], F32)], decay, gain, start, signal[:CTX]
    )
    context = context.reshape(CTX, features).astype(BF16)

    queries = dot(attn_input, wq, NT).astype(BF16)
    token_keys = dot(attn_input, wk, NT).astype(BF16)
    token_values = dot(attn_input, wv, NT).astype(BF16)
    state_keys = dot(context, wsk, NT).astype(BF16)
    state_values = dot(context, wsv, NT).astype(BF16)
    query_heads = queries.reshape(block_len, heads, DH)
    key_heads = jnp.concatenate([token_keys, state_keys]).reshape(-1, heads, DH)
    value_heads = jnp.concatenate([token_values, state_values]).reshape(-1, heads, DH)
    causal = jnp.arange(block_len)[:, None] >= jnp.arange(block_len)[None, :]
    allowed = jnp.concatenate([causal, jnp.broadcast_to(seq_index > 0, (block_len, CTX))], axis=1)
    raw = jnp.einsum("qhd,khd->hqk", query_heads, key_heads, preferred_element_type=F32) * scale
    scores = jnp.where(allowed, raw, NEGATIVE)
    row_max = jnp.max(scores, axis=-1, keepdims=True)
    exp_scores = jnp.exp(scores - row_max)
    row_total = jnp.sum(exp_scores, axis=-1, keepdims=True)
    probs_full = exp_scores / row_total
    attn_probs = probs_full.astype(BF16)
    head_mix = jnp.einsum("hqk,khd->qhd", attn_probs, value_heads, preferred_element_type=F32)
    head_mix = head_mix.reshape(block_len, heads * DH).astype(BF16)
    residual = inputs + dot(head_mix, wo, NN)
    normed_mid, inverse_mid = normalize(residual)
    mlp_input = (normed_mid * feedforward_norm_gain).astype(BF16)

    grad_out = own_cot.astype(F32) * valid
    grad_out_b = grad_out.astype(BF16)
    mlp_rows = jnp.concatenate([mlp_input, flip(mlp_input, 1)])
    out_rows = jnp.concatenate([grad_out_b, flip(grad_out_b, 1)])
    pre_act = dot(mlp_rows, wh, NT)
    activated, gelu_back = jax.vjp(partial(jax.nn.gelu, approximate=False), pre_act)
    activated = activated.astype(BF16)
    mlp_part = dot(activated, wr, NN)
    grad_act = dot(out_rows, wr, NT)
    grad_pre = gelu_back(grad_act)[0].astype(BF16)
    mid_part = dot(grad_pre, wh, NN)
    grad_mid = mid_part[:block_len] + flip(mid_part[block_len:].astype(BF16), 1).astype(F32)
    mlp_out = mlp_part[:block_len] + flip(mlp_part[block_len:].astype(BF16), 1).astype(F32)
    output = ((residual + mlp_out) * valid).astype(BF16)
    output_line = line_gather(output)
    grad_return = dot(activated, out_rows, TN).astype(BF16)
    grad_hidden = dot(grad_pre, mlp_rows, TN).astype(BF16)

    def reduce_hidden(grad, reverse):
        grad = grad.reshape(planes, tp_count * hidden_rows, features)
        mine = plane_reduce({p: grad[p] for p in range(planes)}, reverse)
        mine = mine.reshape(tp_count, hidden_rows, features)
        return line_reduce([mine[j] for j in range(tp_count)])

    sum_hidden = reduce_hidden(grad_hidden, False)
    sum_return = reduce_hidden(grad_return, True)

    grad_mlp_gain = jnp.sum(grad_mid * normed_mid, axis=0)
    grad_resid = grad_out + norm_back(normed_mid, inverse_mid, grad_mid * feedforward_norm_gain)
    grad_resid_b = grad_resid.astype(BF16)
    grad_heads = dot(grad_resid_b, wo, NT).astype(BF16).reshape(block_len, heads, DH)
    grad_probs = jnp.einsum("qhd,khd->hqk", grad_heads, value_heads, preferred_element_type=F32)
    delta = jnp.sum(probs_full * grad_probs, axis=-1, keepdims=True)
    grad_scores = (probs_full * (grad_probs - delta)).astype(BF16)
    grad_queries = (
        jnp.einsum("hqk,khd->qhd", grad_scores, key_heads, preferred_element_type=F32) * scale
    )
    grad_keys_all = (
        jnp.einsum("hqk,qhd->khd", grad_scores, query_heads, preferred_element_type=F32) * scale
    )
    grad_values_all = jnp.einsum(
        "hqk,qhd->khd", attn_probs, grad_heads, preferred_element_type=F32
    )
    wide = heads * DH
    grad_queries = grad_queries.reshape(block_len, wide).astype(BF16)
    grad_keys_all = grad_keys_all.reshape(block_len + CTX, wide).astype(BF16)
    grad_values_all = grad_values_all.reshape(block_len + CTX, wide).astype(BF16)
    grad_token_keys, grad_state_keys = grad_keys_all[:block_len], grad_keys_all[block_len:]
    grad_token_values, grad_state_values = grad_values_all[:block_len], grad_values_all[block_len:]
    grad_context = (
        dot(grad_state_keys, wsk, NN) + dot(grad_state_values, wsv, NN)
    ).astype(BF16)

    grad_conv = tiles(grad_context)
    (local_back,) = call(scan_back_in, [(grid, F32)], decay, grad_conv)
    end = 0.0
    for m in range(1, seq_count):
        end = end + jnp.exp(-rate * (block_len * (m - 1))) * shifted(local_back, -m)
    grad_signal, grad_gain, grad_moment = call(
        scan_back_out,
        [((block_len,) + grid[1:], F32), (grid, F32), (grid, F32)],
        decay,
        gain,
        end,
        start,
        signal[:CTX],
        grad_conv,
    )
    end_moment = block_len * jnp.exp(-rate * block_len) * start + local_moment
    grad_rate = -gain * (grad_moment + end * end_moment)
    grad_signal = grad_signal.reshape(block_len, features).astype(BF16)
    grad_signal = jnp.concatenate([grad_signal[CTX:], shifted(grad_signal[:CTX], -1)])

    grad_in = (
        dot(grad_queries, wq, NN)
        + dot(grad_token_keys, wk, NN)
        + dot(grad_token_values, wv, NN)
        + grad_signal.astype(F32) * valid
    )
    grad_attn_gain = jnp.sum(grad_in * normed_in, axis=0)
    grad_tokens = grad_resid + norm_back(normed_in, inverse_in, grad_in * attention_norm_gain)
    tokens_line = line_gather(grad_tokens.astype(BF16))

    def split(values):
        return values.reshape(values.shape[0], tp_count, 2, head_cols // 2)

    def both_rows(values):
        values = split(values)
        mine, other = values[:, :, 0], values[:, :, 1]
        joined = jnp.concatenate([mine, flip(other, 1)])
        return joined.reshape(joined.shape[0], -1)

    def both_full(values):
        return jnp.concatenate([values, flip(values, 1)])

    x_rows, c_rows, r_rows = both_full(attn_input), both_full(context), both_full(grad_resid_b)
    grads_a = [
        dot(both_rows(grad_queries), x_rows, TN),
        dot(both_rows(grad_token_keys), x_rows, TN),
        dot(both_rows(grad_token_values), x_rows, TN),
    ]
    grads_b = [
        dot(both_rows(grad_state_keys), c_rows, TN),
        dot(both_rows(grad_state_values), c_rows, TN),
        dot(both_rows(head_mix), r_rows, TN),
    ]

    def reduce_heads(grads, reverse):
        stack = jnp.stack([g.astype(BF16) for g in grads]).reshape(
            len(grads), tp_count, planes, head_rows, features
        )
        mine = plane_reduce(
            {p: jnp.transpose(stack[:, :, p], (1, 0, 2, 3)) for p in range(planes)}, reverse
        )
        return line_reduce([mine[j] for j in range(tp_count)])

    sum_a = reduce_heads(grads_a, False)
    sum_b = reduce_heads(grads_b, True)

    def spread(value, reverse):
        plane = plane_gather(value, reverse)
        other = {p: flip(v, 1) for p, v in plane.items()}
        return jnp.stack([(plane, other)[i & 1][i >> 1] for i in range(seq_count)])

    def ordered(stack):
        return [
            lax.dynamic_index_in_dim(stack, seq_index ^ i, 0, keepdims=False)
            for i in range(seq_count)
        ]

    fix = 1.0 / copies

    def head_grads(value, reverse):
        parts = ordered(spread(value, reverse))
        parts = [parts[2 * p + c] for c in range(2) for p in range(planes)]
        return jnp.concatenate(parts, axis=1).astype(F32) * fix

    def hidden_grads(value, reverse):
        return jnp.concatenate(ordered(spread(value, reverse))).astype(F32) * fix

    full_a = head_grads(sum_a, False)
    full_b = head_grads(sum_b, True)
    full_hidden = hidden_grads(sum_hidden, False)
    full_return = hidden_grads(sum_return, True)

    gains = lax.psum(jnp.stack([grad_attn_gain, grad_mlp_gain]), ("seq", "tp")) * fix
    kernel_grads = jnp.stack([grad_gain, grad_rate]).reshape(2, states, features)
    kernel_grads = lax.psum_scatter(
        jnp.transpose(kernel_grads, (2, 0, 1)).reshape(features, 2 * states),
        ("seq", "tp"),
        scatter_dimension=0,
        tiled=True,
    )
    kernel_grads = kernel_grads * fix

    def lined(line, dtype):
        stack = jnp.stack(line)
        return jnp.stack(
            [
                lax.dynamic_index_in_dim(
                    stack, (tp_index - b * copies) % tp_count, 0, keepdims=False
                )
                for b in range(sequences)
            ]
        ).astype(dtype)

    return (
        lined(output_line, BF16),
        lined(tokens_line, F32),
        gains[0],
        full_a[0].T,
        full_a[1].T,
        full_a[2].T,
        full_b[2],
        full_b[0].T,
        full_b[1].T,
        kernel_grads[:, :states],
        kernel_grads[:, states:],
        gains[1],
        full_hidden.T,
        full_return,
    )


LOG2E = math.log2(math.e)
SCALE = DH ** (-0.5)


def cost(us):
    return pl.CostEstimate(flops=int(us * 1.1e9), bytes_accessed=0, transcendentals=0)


def params(limit=50):
    return pltpu.CompilerParams(vmem_limit_bytes=limit * 2**20)


def like(shape, dtype=BF16):
    return jax.ShapeDtypeStruct(shape, dtype)


def whole(shape):
    return pl.BlockSpec(shape, lambda *_: (0,) * len(shape))


def launch(kernel, place, grid, in_specs, out_specs, outs, operands, scratch=(), us=5):
    return pl.pallas_call(
        kernel,
        grid_spec=pltpu.PrefetchScalarGridSpec(
            num_scalar_prefetch=1,
            grid=grid,
            in_specs=in_specs,
            out_specs=out_specs,
            scratch_shapes=list(scratch),
        ),
        out_shape=outs,
        compiler_params=params(),
        cost_estimate=cost(us),
    )(place, *operands)


def timed(us):
    return partial(launch, us=us)


def cycle(value, steps):
    count = lax.axis_size("tp")
    return lax.ppermute(value, "tp", [(i, (i + steps) % count) for i in range(count)])


def pack_heads(place, wq, wk, wv, wsk, wsv, wo, out, turned):
    chip = place[0] >> 1
    rows = out.shape[2]
    for w, ref in enumerate((wq, wk, wv, wsk, wsv, wo)):
        turned[...] = ref[...].astype(F32) if ref is wo else ref[...].astype(F32).T
        for p in range(4):
            cut = pl.ds(pl.multiple_of((chip ^ p) * rows, rows), rows)
            out[p, w] = turned[cut, :].astype(BF16)


def pack_hidden(place, wh, wr, out, turned):
    chip = place[0] >> 1
    rows = out.shape[2]
    for w, ref in enumerate((wh, wr)):
        turned[...] = ref[...].astype(F32).T if ref is wh else ref[...].astype(F32)
        for p in range(4):
            cut = pl.ds(pl.multiple_of((chip ^ p) * rows, rows), rows)
            out[p, w] = turned[cut, :].astype(BF16)


def load_heads(j, own, far, into, first, count):
    rows = own.shape[2]

    @pl.when(j == 0)
    def _():
        for p in range(4):
            for w in range(count):
                into[w, p * rows : (p + 1) * rows] = own[p, first + w]

    @pl.when(j > 0)
    def _():
        for p in range(4):
            for w in range(count):
                if p < 3:
                    into[w, p * rows : (p + 1) * rows] = far[p][0, first + w]
                else:
                    into[w, p * rows : (p + 1) * rows] = far[3 + (first + w) // 3][0, (first + w) % 3]


def masked(raw, r, block):
    n = raw.shape[1]
    column = lax.broadcasted_iota(jnp.int32, raw.shape, 1)
    row = lax.broadcasted_iota(jnp.int32, raw.shape, 0)
    keep = (column - (n - 128) <= row) & ((column >= CTX) | (block > 0))
    return jnp.where(keep, raw * (SCALE * LOG2E), NEGATIVE)


def project(place, x0, x1, own, f0, f1, f2, f3, f4, q_ref, k_ref, v_ref, weight):
    j = pl.program_id(0)
    load_heads(j, own, (f0, f1, f2, f3, f4), weight, 0, 3)
    rows = x0.shape[0]
    qkv_w = weight[0:3].reshape(3 * DH, -1)
    for half, x in enumerate((x0, x1)):
        saved = slice(half * rows, (half + 1) * rows)
        qkv = dot(x[...], qkv_w, NT).astype(BF16)
        q_ref[saved] = qkv[:, :DH]
        k_ref[saved] = qkv[:, DH : 2 * DH]
        v_ref[saved] = qkv[:, 2 * DH :]


def attend(place, c0, c1, own, f0, f1, f2, f3, f4, q_ref, k_ref, v_ref,
           part0, part1, s_ref, o_ref, lse_ref, weight, keys, values, total):
    j = pl.program_id(0)
    load_heads(j, own, (f0, f1, f2, f3, f4), weight, 3, 3)
    rows = part0.shape[0]

    @pl.when(j == 0)
    def _():
        total[...] = jnp.zeros_like(total)

    st_w = weight[0:2].reshape(2 * DH, -1)
    for half, c in enumerate((c0, c1)):
        base = half * rows
        state = dot(c[...], st_w, NT).astype(BF16)
        s_ref[half * CTX : (half + 1) * CTX] = state
        keys[half, 0:CTX] = state[:, :DH]
        values[half, 0:CTX] = state[:, DH:]
        keys[half, CTX:] = k_ref[base : base + rows]
        values[half, CTX:] = v_ref[base : base + rows]
    for half in range(2):
        block = place[0] ^ half
        base = half * rows
        for r in range(rows // 128):
            saved = slice(base + r * 128, base + (r + 1) * 128)
            n = CTX + (r + 1) * 128
            scores = masked(dot(q_ref[saved], keys[half, 0:n], NT), r, block)
            top = jnp.max(scores, axis=1, keepdims=True)
            power = jnp.exp2(scores - top)
            summed = jnp.sum(power, axis=1, keepdims=True)
            lse_ref[0, saved] = top + jnp.log2(summed)
            probs = (power * (1.0 / summed)).astype(BF16)
            o_ref[saved] = dot(probs, values[half, 0:n], NN).astype(BF16)
    for half in range(2):
        base = half * rows
        total[base : base + rows] += dot(o_ref[base : base + rows], weight[2], NN)

    @pl.when(j == pl.num_programs(0) - 1)
    def _():
        part0[...] = total[0:rows].astype(part0.dtype)
        part1[...] = total[rows:].astype(part1.dtype)


def attend_back(place, g0, g1, own, f0, f1, f2, f3, f4,
                q_ref, k_ref, v_ref, s_ref, lse_ref,
                in0, in1, ctx0, ctx1, d_ref, ds_ref,
                weight, keys, values, heads, grad_k, grad_v, total, ctx_total):
    j = pl.program_id(0)
    load_heads(j, own, (f0, f1, f2, f3, f4), weight, 0, 6)
    rows = g0.shape[0]

    @pl.when(j == 0)
    def _():
        total[...] = jnp.zeros_like(total)
        ctx_total[...] = jnp.zeros_like(ctx_total)

    qkv_w = weight[0:3].reshape(3 * DH, -1)
    st_w = weight[3:5].reshape(2 * DH, -1)
    for half, g in enumerate((g0, g1)):
        base = half * rows
        keys[half, 0:CTX] = s_ref[half * CTX : (half + 1) * CTX, :DH]
        values[half, 0:CTX] = s_ref[half * CTX : (half + 1) * CTX, DH:]
        keys[half, CTX:] = k_ref[base : base + rows]
        values[half, CTX:] = v_ref[base : base + rows]
        heads[half] = dot(g[...], weight[5], NT).astype(BF16)
    for half in range(2):
        block = place[0] ^ half
        base = half * rows
        for r in reversed(range(rows // 128)):
            saved = slice(base + r * 128, base + (r + 1) * 128)
            n = CTX + (r + 1) * 128
            q = q_ref[saved]
            own = heads[half, r * 128 : (r + 1) * 128]
            probs = jnp.exp2(masked(dot(q, keys[half, 0:n], NT), r, block) - lse_ref[0, saved])
            grad = dot(own, values[half, 0:n], NT)
            delta = jnp.sum(probs * grad, axis=1, keepdims=True)
            scores = (probs * (grad - delta)).astype(BF16)
            d_ref[saved, 0:DH] = (dot(scores, keys[half, 0:n], NN) * SCALE).astype(BF16)
            to_k = dot(scores, q, TN)
            to_v = dot(probs.astype(BF16), own, TN)
            if r == rows // 128 - 1:
                grad_k[half, 0:n] = to_k
                grad_v[half, 0:n] = to_v
            else:
                grad_k[half, 0:n] += to_k
                grad_v[half, 0:n] += to_v
    for half in range(2):
        base = half * rows
        d_ref[base : base + rows, DH : 2 * DH] = (grad_k[half, CTX:] * SCALE).astype(BF16)
        d_ref[base : base + rows, 2 * DH :] = grad_v[half, CTX:].astype(BF16)
        state = slice(half * CTX, (half + 1) * CTX)
        ds_ref[state, :DH] = (grad_k[half, 0:CTX] * SCALE).astype(BF16)
        ds_ref[state, DH:] = grad_v[half, 0:CTX].astype(BF16)
        ctx_total[state] += dot(ds_ref[state], st_w, NN)
        total[base : base + rows] += dot(d_ref[base : base + rows], qkv_w, NN)

    @pl.when(j == pl.num_programs(0) - 1)
    def _():
        in0[...] = total[0:rows].astype(in0.dtype)
        in1[...] = total[rows:].astype(in1.dtype)
        ctx0[...] = ctx_total[0:CTX].astype(ctx0.dtype)
        ctx1[...] = ctx_total[CTX:].astype(ctx1.dtype)


def attend_weights(place, x0, x1, c0, c1, g0, g1, d_ref, ds_ref, o_ref, keep_a, send_a, keep_b, send_b):
    rows = x0.shape[0]
    cut = keep_a.shape[3]
    to_qkv = (dot(d_ref[0:rows], x0[...], TN) + dot(d_ref[rows:], x1[...], TN)).astype(BF16)
    to_state = (dot(ds_ref[0:CTX], c0[...], TN) + dot(ds_ref[CTX:], c1[...], TN)).astype(BF16)
    to_out = (dot(o_ref[0:rows], g0[...], TN) + dot(o_ref[rows:], g1[...], TN)).astype(BF16)
    spots_a = {0: (keep_a, 0), 2: (keep_a, 1), 1: (send_a, 0), 3: (send_a, 1)}
    spots_b = {0: (keep_b, 0), 1: (keep_b, 1), 2: (send_b, 0), 3: (send_b, 1)}
    for p in range(4):
        out, at = spots_a[p]
        for w in range(3):
            out[at, 0, w] = to_qkv[w * DH + p * cut : w * DH + (p + 1) * cut]
        out, at = spots_b[p]
        for w in range(2):
            out[at, 0, w] = to_state[w * DH + p * cut : w * DH + (p + 1) * cut]
        out[at, 0, 2] = to_out[p * cut : (p + 1) * cut]


def gelu_parts(x):
    size = jnp.abs(x) * math.sqrt(0.5)
    bell = jnp.exp2(x * x * (-0.5 * LOG2E))
    t = 1.0 / (1.0 + 0.3275911 * size)
    poly = 1.061405429 * t - 1.453152027
    poly = poly * t + 1.421413741
    poly = poly * t - 0.284496736
    poly = poly * t + 0.254829592
    tail = 0.5 * poly * t * bell
    return jnp.where(x >= 0, 1.0 - tail, tail), bell * (1.0 / math.sqrt(2.0 * math.pi))


def load_hidden(j, w, own, far, into):
    rows = own.shape[2]

    @pl.when(j == 0)
    def _():
        for p in range(4):
            into[p * rows : (p + 1) * rows] = own[p, w]

    @pl.when(j > 0)
    def _():
        for p in range(3):
            into[p * rows : (p + 1) * rows] = far[p][0, w]
        into[3 * rows :] = far[3 + w][0]


def feed_in(place, m0, m1, own, f0, f1, f2, f3, act_ref, slope_ref, wh):
    load_hidden(pl.program_id(0), 0, own, (f0, f1, f2, f3), wh)
    rows = m0.shape[0]
    for half, m in enumerate((m0, m1)):
        saved = slice(half * rows, (half + 1) * rows)
        pre = dot(m[...], wh[...], NT)
        part, bell = gelu_parts(pre)
        act_ref[saved] = (pre * part).astype(BF16)
        slope_ref[saved] = (part + pre * bell).astype(BF16)


def feed_out(place, g0, g1, own, f0, f1, f2, f3, f4, act_ref, slope_ref,
             mlp0, mlp1, mid0, mid1, pre_ref, wh, wr, mlp, mid):
    j = pl.program_id(0)
    load_hidden(j, 0, own, (f0, f1, f2, f3, f4), wh)
    load_hidden(j, 1, own, (f0, f1, f2, f3, f4), wr)
    rows = g0.shape[0]

    @pl.when(j == 0)
    def _():
        mlp[...] = jnp.zeros_like(mlp)
        mid[...] = jnp.zeros_like(mid)

    for half, g in enumerate((g0, g1)):
        saved = slice(half * rows, (half + 1) * rows)
        back = dot(g[...], wr[...], NT)
        pre_ref[saved] = (back * slope_ref[saved].astype(F32)).astype(BF16)
        mlp[saved] += dot(act_ref[saved], wr[...], NN)
        mid[saved] += dot(pre_ref[saved], wh[...], NN)

    @pl.when(j == pl.num_programs(0) - 1)
    def _():
        mlp0[...] = mlp[0:rows].astype(mlp0.dtype)
        mlp1[...] = mlp[rows:].astype(mlp1.dtype)
        mid0[...] = mid[0:rows].astype(mid0.dtype)
        mid1[...] = mid[rows:].astype(mid1.dtype)


def feed_weights(keeps, place, a0, a1, b_ref, keep, send):
    rows = a0.shape[0]
    cut = keep.shape[2]
    sends = [p for p in range(4) if p not in keeps]
    grad = (dot(b_ref[0:rows], a0[...], TN) + dot(b_ref[rows:], a1[...], TN)).astype(BF16)
    for p in range(4):
        out, at = (keep, keeps.index(p)) if p in keeps else (send, sends.index(p))
        out[at, 0] = grad[p * cut : (p + 1) * cut]


def live_rows(place, count):
    at = place[0] * (count * pl.num_programs(0)) + pl.program_id(0) * count
    position = at + lax.broadcasted_iota(jnp.int32, (count, 1), 0)
    return (position < place[2]).astype(F32)


def middle(place, tokens, own, got, gain, residual, m_ref):
    value = tokens[0].astype(F32) + own[...] + got[...].astype(F32)
    residual[...] = value
    m_ref[...] = (normalize(value)[0] * gain[...]).astype(BF16)


def finish(place, residual, own, got, out):
    value = residual[...] + own[...] + got[...].astype(F32)
    out[...] = (value * live_rows(place, value.shape[0])).astype(BF16)


def middle_back(place, residual, own, got, cot, gain, grad, grad_b, sums):
    value = residual[...]
    normed, inverse = normalize(value)
    valid = live_rows(place, value.shape[0])
    back = own[...] + got[...].astype(F32)
    total = jnp.sum(back * normed, axis=0, keepdims=True)

    @pl.when(pl.program_id(0) == 0)
    def _():
        sums[...] = total

    @pl.when(pl.program_id(0) > 0)
    def _():
        sums[...] += total

    value = cot[0].astype(F32) * valid + norm_back(normed, inverse, back * gain[...])
    grad[...] = value
    grad_b[...] = value.astype(BF16)


def first_back(place, tokens, own, got, signal, grad, gain, out, sums):
    normed, inverse = normalize(tokens[0].astype(F32))
    valid = live_rows(place, out.shape[0])
    back = own[...] + got[...].astype(F32) + signal[...].astype(F32) * valid
    total = jnp.sum(back * normed, axis=0, keepdims=True)

    @pl.when(pl.program_id(0) == 0)
    def _():
        sums[...] = total

    @pl.when(pl.program_id(0) > 0)
    def _():
        sums[...] += total

    out[...] = (grad[...] + norm_back(normed, inverse, back * gain[...])).astype(BF16)


def unpack_heads(place, n0, n1, n2, n3, f0, f1, f2, f3, q, k, v, o, sk, sv, rows_ref):
    core, chip = place[0] & 1, place[0] >> 1
    cut = n0.shape[1]
    for w, out in ((0, q), (1, k), (2, v), (3, sk), (4, sv), (5, o)):
        for other, pieces in ((0, (n0, n1, n2, n3)), (1, (f0, f1, f2, f3))):
            for p, piece in enumerate(pieces):
                at = (core ^ other) * DH + (chip ^ p) * cut
                rows_ref[pl.ds(pl.multiple_of(at, cut), cut), :] = piece[w].astype(F32)
        out[...] = rows_ref[...] if out is o else rows_ref[...].T


def unpack_hidden(place, n0, n1, n2, n3, f0, f1, f2, f3, h, r):
    core, chip = place[0] & 1, place[0] >> 1
    cut = n0.shape[1]
    for other, pieces in ((0, (n0, n1, n2, n3)), (1, (f0, f1, f2, f3))):
        for p, piece in enumerate(pieces):
            at = pl.multiple_of((core ^ other) * 4 * cut + (chip ^ p) * cut, cut)
            r[pl.ds(at, cut), :] = piece[1].astype(F32)
            h[:, pl.ds(at, cut)] = piece[0].astype(F32).T


def far_away(value):
    return pltpu.with_memory_space_constraint(value, pltpu.HBM)


def add(a, b):
    return (a.astype(F32) + b.astype(F32)).astype(BF16)


def after(value, *earlier):
    return lax.optimization_barrier((value, *earlier))[0]


def powers(lengths, rate_ref, *outs):
    for length, out in zip(lengths, outs):
        out[...] = jnp.exp(-rate_ref[...] * float(length))


def states_around(local, power, sign, first, *earlier):
    group = local
    for m in (1, 2):
        group = group + power[m] * shifted(local, sign * m)
    group = after(group, *earlier)
    total = shifted(group, sign * first)
    for m in range(first + 3, 8, 3):
        total = total + power[m - first] * shifted(group, sign * m)
    return total


def scan_rows(decay_ref, gain_ref, late_ref, g_ref, y_ref, end_ref):
    decay, gain = decay_ref[...], gain_ref[...]
    rows, count = y_ref.shape[0], g_ref.shape[0]

    def full(t, lam):
        lam = lam + g_ref[count - 1 - t]
        y_ref[rows - 1 - t] = jnp.sum(gain * lam, axis=0)
        return decay * lam

    def empty(t, lam):
        y_ref[rows - count - 1 - t] = jnp.sum(gain * lam, axis=0)
        return decay * lam

    lam = lax.fori_loop(0, count, full, late_ref[...], unroll=8)
    end_ref[...] = lam
    lax.fori_loop(0, rows - count, empty, lam, unroll=8)


def scan_sums(decay_ref, start_ref, u_ref, g_ref, gh_ref, gm_ref):
    decay = decay_ref[...]

    def again(t, carry):
        h, m, gh, gm = carry
        h, m = decay * h + u_ref[t], decay * (m + h)
        g = g_ref[t]
        return h, m, gh + g * h, gm + g * m

    zero = jnp.zeros(decay.shape, F32)
    _, _, gh, gm = lax.fori_loop(0, u_ref.shape[0], again, (start_ref[...], zero, zero, zero))
    gh_ref[...] = gh
    gm_ref[...] = gm


def fast_body(
    tokens, lengths, attention_norm_gain, query_weight, key_weight, value_weight, output_weight,
    state_key_weight, state_value_weight, state_coefficient, state_rate, feedforward_norm_gain,
    hidden_weight, return_weight, cotangent,
):
    sequences, block_len, features = tokens.shape
    tp_count = lax.axis_size("tp")
    seq_index = lax.axis_index("seq")
    tp_index = lax.axis_index("tp")
    hidden_cols = hidden_weight.shape[1]
    cut = DH // 4
    wide = hidden_cols // 8
    length = lax.dynamic_index_in_dim(lengths, tp_index, 0, keepdims=False)
    place = jnp.stack([seq_index, tp_index, length]).astype(jnp.int32)

    column = pl.BlockSpec((features, DH), lambda i, place: (0, place[0] & 1))
    (own_w,) = timed(4)(
        pack_heads, place, (1,),
        [column] * 5 + [pl.BlockSpec((DH, features), lambda i, place: (place[0] & 1, 0))],
        [whole((4, 6, cut, features))],
        [like((4, 6, cut, features))],
        tuple(map(far_away, (
            query_weight, key_weight, value_weight, state_key_weight, state_value_weight, output_weight
        ))),
        [pltpu.VMEM((DH, features), F32)],
    )
    (own_m,) = timed(5)(
        pack_hidden, place, (1,),
        [
            pl.BlockSpec((features, hidden_cols // 2), lambda i, place: (0, place[0] & 1)),
            pl.BlockSpec((hidden_cols // 2, features), lambda i, place: (place[0] & 1, 0)),
        ],
        [whole((4, 2, wide, features))],
        [like((4, 2, wide, features))],
        (far_away(hidden_weight), far_away(return_weight)),
        [pltpu.VMEM((hidden_cols // 2, features), F32)],
    )

    own_tokens = lax.dynamic_index_in_dim(tokens, tp_index, 0, keepdims=False)
    own_cot = lax.dynamic_index_in_dim(cotangent, tp_index, 0, keepdims=False)
    before = shifted(own_tokens[block_len - CTX :], 1)
    positions = seq_index * block_len - CTX + jnp.arange(block_len + CTX)
    live = ((positions < length) & (positions >= 0)).astype(F32)[:, None]
    x = (normalize(own_tokens.astype(F32))[0] * attention_norm_gain).astype(BF16)
    x_other = flip(x, 1)
    grad_out = (own_cot.astype(F32) * live[CTX:]).astype(BF16)
    grad_out_other = flip(grad_out, 1)
    early = (normalize(before.astype(F32))[0] * attention_norm_gain).astype(BF16)
    signal = tiles(
        jnp.concatenate([early, x[: block_len - CTX]]).astype(F32) * live[:block_len]
    )

    states = state_rate.shape[1]
    channels = state_rate.shape[0]
    both = jnp.stack([state_rate, state_coefficient]).reshape(1, -1, 128)
    devices = features // channels
    both = lax.all_to_all(
        jnp.broadcast_to(both, (devices,) + both.shape[1:]), ("seq", "tp"), 0, 0
    )
    both = jnp.transpose(both.reshape(devices, 2, channels, states), (1, 3, 0, 2))
    both = both.reshape(2, states, features // 128, 128)
    rate, gain = both[0], both[1]
    grid = rate.shape
    spans = [1, block_len - CTX] + [block_len * m for m in (1, 2, 3, 6)]
    decay, tail_power, *blocks = call(
        partial(powers, spans), [(grid, F32)] * len(spans), rate, us=1
    )
    block_power = dict(zip((1, 2, 3, 6), blocks))

    def line_of(own):
        return jnp.stack([cycle(own, j) for j in range(1, tp_count)])

    def plane_of(line, by_x, by_y, half):
        return [line, by_x, by_y, flip(by_y[:, :half], 2), flip(by_x[:, half:], 4)]

    line_w = line_of(own_w[0])
    near_w = flip(line_w, 2), flip(line_w, 4)
    far_w = plane_of(line_w, *near_w, 3)
    line_m = line_of(after(own_m[0], line_w))
    near_m = flip(after(line_m, *near_w), 2), flip(after(line_m, *near_w), 4)
    far_m = plane_of(line_m, *near_m, 1)
    far_m[3:] = [value[:, 0] for value in far_m[3:]]

    local_state, local_moment = call(
        scan_in, [(grid, F32)] * 2, decay, after(signal, line_w, own_m, x_other, grad_out_other), us=8
    )
    start = states_around(after(local_state, *near_w), block_power, 1, 1)
    (context,) = call(scan_out, [((CTX,) + grid[1:], F32)], decay, gain, start, signal[:CTX], us=3)
    context = context.reshape(CTX, features).astype(BF16)
    context_other = flip(context, 1)
    rows = 2 * block_len
    slots = tp_count
    own_spec = whole((4, 6, cut, features))

    def slot_spec(*shape):
        return pl.BlockSpec(
            (1, *shape, features),
            lambda j, place: (jnp.maximum(j - 1, 0),) + (0,) * (len(shape) + 1),
        )

    weight_specs = [own_spec] + [slot_spec(6, cut)] * 3 + [slot_spec(3, cut)] * 2
    weights = (own_w, *far_w)
    full = whole((block_len, features))
    ctx_spec = whole((CTX, features))
    head = lambda n, width: pl.BlockSpec((n, width), lambda j, place: (0, j))
    lse_spec = pl.BlockSpec((1, rows, 1), lambda j, place: (j, 0, 0))
    q, k, v = timed(8)(
        project, place, (slots,),
        [full] * 2 + weight_specs,
        [head(rows, DH)] * 3,
        [like((rows, slots * DH))] * 3,
        (x, x_other, *weights),
        [pltpu.VMEM((3, DH, features), BF16)],
    )
    attended = timed(20)(
        attend, place, (slots,),
        [ctx_spec] * 2 + weight_specs + [head(rows, DH)] * 3,
        [full] * 2 + [head(2 * CTX, 2 * DH), head(rows, DH), lse_spec],
        [like((block_len, features), F32), like((block_len, features))]
        + [like((2 * CTX, slots * 2 * DH)), like((rows, slots * DH)), like((slots, rows, 1), F32)],
        (after(context, line_m), context_other, *weights, q, k, v),
        [
            pltpu.VMEM((3, DH, features), BF16),
            pltpu.VMEM((2, CTX + block_len, DH), BF16),
            pltpu.VMEM((2, CTX + block_len, DH), BF16),
            pltpu.VMEM((rows, features), F32),
        ],
    )
    part, part_other, state, mix, lse = attended
    group = 128
    steps = block_len // group
    row_spec = pl.BlockSpec((group, features), lambda i, place: (i, 0))
    seq_spec = pl.BlockSpec((1, group, features), lambda i, place: (place[1], i, 0))
    gain_spec = whole((1, features))
    mid_gain = feedforward_norm_gain.reshape(1, -1)
    residual, m = timed(4)(
        middle, place, (steps,),
        [seq_spec, row_spec, row_spec, gain_spec], [row_spec] * 2,
        [like((block_len, features), F32), like((block_len, features))],
        (tokens, part, after(flip(part_other, 1), *near_m), mid_gain),
    )
    m_other = flip(m, 1)

    hidden_own = whole((4, 2, wide, features))
    hidden_far = [slot_spec(2, wide)] * 3 + [slot_spec(wide)]
    chunk = 4 * wide
    act, slope = timed(14)(
        feed_in, place, (slots,),
        [full] * 2 + [hidden_own] + hidden_far,
        [head(rows, chunk)] * 2,
        [like((rows, slots * chunk))] * 2,
        (m, m_other, own_m, *far_m[:4]),
        [pltpu.VMEM((chunk, features), BF16)],
    )
    mlp, mlp_other, mid, mid_other, pre = timed(21)(
        feed_out, place, (slots,),
        [full] * 2 + [hidden_own] + hidden_far + hidden_far[3:] + [head(rows, chunk)] * 2,
        [full] * 4 + [head(rows, chunk)],
        [like((block_len, features), F32), like((block_len, features))] * 2
        + [like((rows, slots * chunk))],
        (grad_out, grad_out_other, own_m, *far_m, act, slope),
        [pltpu.VMEM((chunk, features), BF16)] * 2 + [pltpu.VMEM((rows, features), F32)] * 2,
    )
    mid_got, mlp_got = flip(mid_other, 1), flip(mlp_other, 1)
    grad_spec = pl.BlockSpec((2, 1, wide, features), lambda j, place: (0, j, 0, 0))
    hidden_grads = partial(
        launch, place=place, grid=(slots,), us=8,
        in_specs=[full] * 2 + [head(rows, chunk)], out_specs=[grad_spec] * 2,
        outs=[like((2, slots, wide, features))] * 2,
    )
    keep_r, send_r = hidden_grads(
        partial(feed_weights, (0, 1)), operands=(grad_out, grad_out_other, far_away(after(act, pre)))
    )
    mlp_got = after(mlp_got, keep_r)
    mid_got = after(mid_got, keep_r)
    (output,) = timed(3)(
        finish, place, (steps,),
        [row_spec] * 3, [row_spec], [like((block_len, features))], (residual, mlp, mlp_got),
    )
    output_all = lax.all_gather(output, "tp")
    resid, resid_b, sums_mid = timed(5)(
        middle_back, place, (steps,),
        [row_spec] * 3 + [seq_spec, gain_spec], [row_spec] * 2 + [gain_spec],
        [
            like((block_len, features), F32), like((block_len, features)),
            like((1, features), F32),
        ],
        (after(residual, output), mid, mid_got, cotangent, mid_gain),
    )
    resid_other = flip(resid_b, 1)
    keep_h, send_h = hidden_grads(
        partial(feed_weights, (0, 2)), operands=(m, m_other, far_away(after(pre, resid_b)))
    )

    grad_in, grad_in_other, grad_ctx, grad_ctx_other, d, ds = timed(27)(
        attend_back, place, (slots,),
        [full] * 2 + weight_specs + [head(rows, DH)] * 3 + [head(2 * CTX, 2 * DH), lse_spec],
        [full] * 2 + [ctx_spec] * 2 + [head(rows, 3 * DH), head(2 * CTX, 2 * DH)],
        [
            like((block_len, features), F32), like((block_len, features)),
            like((CTX, features), F32), like((CTX, features)),
            like((rows, slots * 3 * DH)), like((2 * CTX, slots * 2 * DH)),
        ],
        (after(resid_b, keep_h), resid_other, *map(far_away, weights), q, k, v, state, lse),
        [
            pltpu.VMEM((6, DH, features), BF16),
            pltpu.VMEM((2, CTX + block_len, DH), BF16),
            pltpu.VMEM((2, CTX + block_len, DH), BF16),
            pltpu.VMEM((2, block_len, DH), BF16),
            pltpu.VMEM((2, CTX + block_len, DH), F32),
            pltpu.VMEM((2, CTX + block_len, DH), F32),
            pltpu.VMEM((rows, features), F32),
            pltpu.VMEM((2 * CTX, features), F32),
        ],
    )
    grad_ctx_got = flip(grad_ctx_other, 1)
    grad_in_got = flip(grad_in_other, 1)
    part_spec = pl.BlockSpec((2, 1, 3, cut, features), lambda j, place: (0, j, 0, 0, 0))
    keep_a, send_a, keep_b, send_b = timed(10)(
        attend_weights, place, (slots,),
        [full] * 2 + [ctx_spec] * 2 + [full] * 2
        + [head(rows, 3 * DH), head(2 * CTX, 2 * DH), head(rows, DH)],
        [part_spec] * 4,
        [like((2, slots, 3, cut, features))] * 4,
        (x, x_other, context, context_other, resid_b, resid_other, d, ds, mix),
    )

    got_r = flip(after(send_r, resid_b), 4)
    got_h = flip(after(send_h, resid_b), 2)
    near_h, away_h = add(keep_h[0], got_h[0]), add(keep_h[1], got_h[1])
    near_r, away_r = add(keep_r[0], got_r[0]), add(keep_r[1], got_r[1])
    grad_context = (grad_ctx + grad_ctx_got.astype(F32)).astype(BF16)
    grad_conv = tiles(after(grad_context, got_r, got_h))
    grad_later = tiles(shifted(grad_context, -1))
    (local_back,) = call(scan_back_in, [(grid, F32)], decay, grad_conv)
    late = tail_power * states_around(local_back, block_power, -1, 2, keep_a, away_h, away_r)
    grad_signal, end = call(
        scan_rows, [((block_len,) + grid[1:], F32), (grid, F32)], decay, gain, late, grad_later
    )
    grad_signal = grad_signal.reshape(block_len, features).astype(BF16)
    grad_tokens, sums_in = timed(5)(
        first_back, place, (steps,),
        [seq_spec] + [row_spec] * 4 + [gain_spec], [row_spec, gain_spec],
        [like((block_len, features)), like((1, features), F32)],
        (tokens, grad_in, grad_in_got, grad_signal, after(resid, output_all), attention_norm_gain.reshape(1, -1)),
    )

    lefts, rights = line_steps(grad_tokens)
    line = [grad_tokens] + [
        jnp.where(tp_index >= j, lefts[j], rights[slots - j]) for j in range(1, slots)
    ]
    line = jnp.stack(line)
    tokens_all = jnp.stack(
        [
            lax.dynamic_index_in_dim(line, (tp_index - b) % slots, 0, keepdims=False)
            for b in range(sequences)
        ]
    ).astype(F32)
    grad_gain, grad_moment = call(
        scan_sums, [(grid, F32)] * 2, decay, after(start, grad_tokens), signal[:CTX], grad_conv
    )
    end_moment = block_len * block_power[1] * start + local_moment
    grad_rate = -gain * (grad_moment + end * end_moment)

    def regather(total):
        held = [total, flip(total, 2), flip(total, 4), flip(total, 6)]
        return held + [flip(value, 1) for value in held]

    ready = (late, grad_later)
    more_h, more_r = flip(after(away_h, *ready), 4), flip(after(away_r, *ready), 2)
    more_h, more_r = after(more_h, grad_tokens), after(more_r, grad_tokens)
    got_a = flip(after(send_a, more_h, more_r), 2)
    got_b = flip(after(send_b, more_h, more_r), 4)
    pairs = (near_h, more_h), (near_r, more_r)
    total_m = line_reduce(
        [jnp.stack([add(a[j], b[j]) for a, b in pairs]) for j in range(slots)],
        list(zip(lefts[1:], rights[1:])),
    )
    near_a, away_a = add(keep_a[0], got_a[0]), add(keep_a[1], got_a[1])
    near_b, away_b = add(keep_b[0], got_b[0]), add(keep_b[1], got_b[1])
    pairs = (near_a, flip(away_a, 4)), (near_b, flip(away_b, 2))
    total_a = line_reduce(
        [jnp.stack([add(a[j], b[j]) for a, b in pairs]) for j in range(slots)]
    )
    pieces_m = regather(total_m)
    pieces_a = regather(total_a.reshape(6, cut, features))
    grad_hidden, grad_return = timed(5)(
        unpack_hidden, place, (1,),
        [whole((2, wide, features))] * 8,
        [whole((features, hidden_cols)), whole((hidden_cols, features))],
        [like((features, hidden_cols), F32), like((hidden_cols, features), F32)],
        pieces_m,
    )
    grad_q, grad_k, grad_v, grad_o, grad_sk, grad_sv = timed(5)(
        unpack_heads, place, (1,),
        [whole((6, cut, features))] * 8,
        [whole((features, 2 * DH))] * 3 + [whole((2 * DH, features))] + [whole((features, 2 * DH))] * 2,
        [like((features, 2 * DH), F32)] * 3
        + [like((2 * DH, features), F32)]
        + [like((features, 2 * DH), F32)] * 2,
        pieces_a,
        [pltpu.VMEM((2 * DH, features), F32)],
    )

    small = jnp.stack([grad_gain, grad_rate]).reshape(2, states, devices, channels)
    small = jnp.transpose(small, (2, 3, 0, 1)).reshape(devices, -1, 128)
    sums = jnp.concatenate([sums_in, sums_mid]).reshape(1, -1, 128)
    sums = jnp.broadcast_to(sums, (devices,) + sums.shape[1:])
    count = small.shape[1]
    small = jnp.sum(
        lax.all_to_all(
            after(jnp.concatenate([small, sums], axis=1), total_a), ("seq", "tp"), 0, 0
        ),
        axis=0,
    )
    kernel_grads = small[:count].reshape(channels, 2, states)
    gains = small[count:].reshape(2, features)

    return (
        output_all, tokens_all, gains[0], grad_q, grad_k, grad_v, grad_o, grad_sk, grad_sv,
        kernel_grads[:, 0], kernel_grads[:, 1], gains[1], grad_hidden, grad_return,
    )


def choose(tokens, *others):
    query_weight = others[2]
    fits = (
        lax.axis_size("seq") == 8
        and lax.axis_size("tp") == tokens.shape[0]
        and query_weight.shape[1] == 2 * DH
        and others[11].shape[1] % 1024 == 0
        and tokens.shape[1] % 512 == 0
        and tokens.shape[2] == 1024
    )
    return (fast_body if fits else body)(tokens, *others)


def solution(mesh):
    rows = P(None, "seq", None)
    columns = P(None, "tp")
    heads = P("tp", None)
    channels = P(("seq", "tp"), None)
    return jax.shard_map(
        choose,
        mesh=mesh,
        in_specs=(
            rows, P(), P(), columns, columns, columns, heads, columns, columns,
            channels, channels, P(), columns, heads, rows,
        ),
        out_specs=(
            rows, rows, P(), columns, columns, columns, heads, columns, columns,
            channels, channels, P(), columns, heads,
        ),
        check_vma=False,
    )
```

```python
from functools import partial
import math

import jax
import jax.numpy as jnp
from jax import lax
from jax.experimental import pallas as pl
from jax.experimental.pallas import tpu as pltpu
from jax.sharding import PartitionSpec as P

DH = 128
CTX = 128
EPS = 1e-05
NEGATIVE = -1e30
F32 = jnp.float32
BF16 = jnp.bfloat16


def normalize(values):
    center = values - jnp.mean(values, axis=-1, keepdims=True)
    inverse = lax.rsqrt(jnp.mean(center * center, axis=-1, keepdims=True) + EPS)
    return (center * inverse, inverse)


def norm_back(normed, inverse, grad_normed):
    mean_grad = jnp.mean(grad_normed, axis=-1, keepdims=True)
    mean_cross = jnp.mean(grad_normed * normed, axis=-1, keepdims=True)
    return inverse * (grad_normed - mean_grad - normed * mean_cross)


def flip(value, mask):
    count = lax.axis_size("seq")
    return lax.ppermute(value, "seq", [(i, i ^ mask) for i in range(count)])


def shifted(value, steps):
    count = lax.axis_size("seq")
    first, last = (max(0, -steps), min(count, count - steps))
    return lax.ppermute(value, "seq", [(i, i + steps) for i in range(first, last)])


def line_steps(value):
    count = lax.axis_size("tp")
    lefts, rights = [value], [value]
    for k in range(1, count):
        lefts.append(lax.ppermute(lefts[-1], "tp", [(i, i + 1) for i in range(k - 1, count - 1)]))
        rights.append(
            lax.ppermute(rights[-1], "tp", [(i, i - 1) for i in range(1, count - k + 1)])
        )
    return lefts, rights


def line_gather(value):
    count = lax.axis_size("tp")
    place = lax.axis_index("tp")
    lefts, rights = line_steps(value)
    return [value] + [
        jnp.where(place >= j, lefts[j], rights[count - j]) for j in range(1, count)
    ]


def line_reduce(chunks, pace=None):
    count = lax.axis_size("tp")

    def add(a, b, k):
        if pace:
            a = lax.optimization_barrier((a, *pace[k - 1]))[0]
        return a if b is None else (a.astype(F32) + b.astype(F32)).astype(BF16)

    going, coming = None, None
    for k in range(1, count):
        going = lax.ppermute(add(chunks[k], going, k), "tp", [(i, i + 1) for i in range(k)])
        coming = lax.ppermute(
            add(chunks[count - k], coming, k), "tp", [(i, i - 1) for i in range(count - k, count)]
        )
    return (chunks[0].astype(F32) + going.astype(F32) + coming.astype(F32)).astype(BF16)


def plane_bits(reverse):
    count = lax.axis_size("seq") // 2
    bits = [1 << b for b in range(count.bit_length() - 1)]
    return bits[::-1] if reverse else bits


def plane_gather(value, reverse):
    held = {0: value}
    for bit in plane_bits(reverse):
        held.update({p | bit: flip(v, 2 * bit) for p, v in list(held.items())})
    return held


def plane_reduce(pieces, reverse):
    held = dict(pieces)
    for bit in plane_bits(reverse):
        for p in [p for p in held if p & bit]:
            got = flip(held.pop(p), 2 * bit)
            held[p ^ bit] = (held[p ^ bit].astype(F32) + got.astype(F32)).astype(BF16)
    return held[0]


def scan_in(decay_ref, u_ref, state_ref, moment_ref):
    decay = decay_ref[...]

    def step(t, carry):
        h, m = carry
        return decay * h + u_ref[t], decay * (m + h)

    zero = jnp.zeros(decay.shape, F32)
    h, m = lax.fori_loop(0, u_ref.shape[0], step, (zero, zero))
    state_ref[...] = h
    moment_ref[...] = m


def scan_out(decay_ref, gain_ref, start_ref, u_ref, y_ref):
    decay, gain = decay_ref[...], gain_ref[...]

    def step(t, h):
        h = decay * h + u_ref[t]
        y_ref[t] = jnp.sum(gain * h, axis=0)
        return h

    lax.fori_loop(0, u_ref.shape[0], step, start_ref[...])


def scan_back_in(decay_ref, g_ref, state_ref):
    decay = decay_ref[...]
    last = g_ref.shape[0] - 1

    def step(t, lam):
        return decay * (lam + g_ref[last - t])

    state_ref[...] = lax.fori_loop(0, last + 1, step, jnp.zeros(decay.shape, F32))


def scan_back_out(decay_ref, gain_ref, end_ref, start_ref, u_ref, g_ref, y_ref, gh_ref, gm_ref):
    decay, gain = decay_ref[...], gain_ref[...]
    rows, count = y_ref.shape[0], g_ref.shape[0]

    def empty(t, lam):
        y_ref[rows - 1 - t] = jnp.sum(gain * lam, axis=0)
        return decay * lam

    def full(t, lam):
        lam = lam + g_ref[count - 1 - t]
        y_ref[count - 1 - t] = jnp.sum(gain * lam, axis=0)
        return decay * lam

    lam = lax.fori_loop(0, rows - count, empty, end_ref[...])
    lax.fori_loop(0, count, full, lam)

    def again(t, carry):
        h, m, gh, gm = carry
        h, m = decay * h + u_ref[t], decay * (m + h)
        g = g_ref[t]
        return h, m, gh + g * h, gm + g * m

    zero = jnp.zeros(decay.shape, F32)
    _, _, gh, gm = lax.fori_loop(0, count, again, (start_ref[...], zero, zero, zero))
    gh_ref[...] = gh
    gm_ref[...] = gm


def call(kernel, outs, *operands, us=5):
    return pl.pallas_call(
        kernel,
        out_shape=[jax.ShapeDtypeStruct(shape, dtype) for shape, dtype in outs],
        compiler_params=pltpu.CompilerParams(vmem_limit_bytes=42 * 2**20),
        cost_estimate=pl.CostEstimate(flops=int(us * 1.1e9), bytes_accessed=0, transcendentals=0),
    )(*operands)


def tiles(values):
    return values.astype(F32).reshape(values.shape[0], values.shape[1] // 128, 128)


def dot(a, b, dims):
    return lax.dot_general(a, b, (dims, ((), ())), preferred_element_type=F32)


NN = ((1,), (0,))
NT = ((1,), (1,))
TN = ((0,), (0,))


def body(
    tokens,
    lengths,
    attention_norm_gain,
    query_weight,
    key_weight,
    value_weight,
    output_weight,
    state_key_weight,
    state_value_weight,
    state_coefficient,
    state_rate,
    feedforward_norm_gain,
    hidden_weight,
    return_weight,
    cotangent,
):
    sequences, block_len, features = tokens.shape
    seq_count = lax.axis_size("seq")
    tp_count = lax.axis_size("tp")
    seq_index = lax.axis_index("seq")
    tp_index = lax.axis_index("tp")
    planes = seq_count // 2
    copies = tp_count // sequences
    sequence = tp_index // copies
    head_cols = query_weight.shape[1]
    hidden_cols = hidden_weight.shape[1]
    heads = head_cols * tp_count // DH
    head_rows = head_cols // seq_count
    hidden_rows = hidden_cols // seq_count
    scale = DH ** (-0.5)

    shard_a = [query_weight.T, key_weight.T, value_weight.T]
    shard_b = [state_key_weight.T, state_value_weight.T, output_weight]
    shard_m = [hidden_weight.T, return_weight]

    def head_slice(shard, relative):
        other = seq_index ^ relative
        at = (other & 1) * planes + (other >> 1)
        return lax.dynamic_slice_in_dim(shard, at * head_rows, head_rows, 0)

    def hidden_slice(shard, relative):
        return lax.dynamic_slice_in_dim(
            shard, (seq_index ^ relative) * hidden_rows, hidden_rows, 0
        )

    def gather_heads(shards, reverse):
        mine = jnp.stack([head_slice(w, 0) for w in shards])
        line = jnp.stack(line_gather(mine)[1:])
        plane = plane_gather(line, reverse)
        other = {p: flip(v, 1) for p, v in plane.items()}
        far = jnp.stack(
            [jnp.stack([group[p] for p in range(planes)]) for group in (plane, other)]
        )
        far = jnp.transpose(far, (3, 2, 0, 1, 4, 5))
        own = jnp.stack(
            [
                jnp.concatenate([head_slice(w, 2 * p + c) for c in range(2) for p in range(planes)])
                for w in shards
            ]
        )
        far = far.reshape(len(shards), (tp_count - 1) * head_cols, features)
        return jnp.concatenate([own, far], axis=1)

    def gather_hidden(shard, reverse):
        line = line_gather(hidden_slice(shard, 0))
        plane = plane_gather(jnp.concatenate(line[1:]), reverse)
        return jnp.concatenate(
            [
                piece
                for p in range(planes)
                for piece in (hidden_slice(shard, 2 * p), plane[p])
            ]
        )

    wq, wk, wv = gather_heads(shard_a, False)
    wsk, wsv, wo = gather_heads(shard_b, True)
    wh = gather_hidden(shard_m[0], False)
    wr = gather_hidden(shard_m[1], True)

    own_tokens = lax.dynamic_index_in_dim(tokens, sequence, 0, keepdims=False)
    own_cot = lax.dynamic_index_in_dim(cotangent, sequence, 0, keepdims=False)
    length = lax.dynamic_index_in_dim(lengths, sequence, 0, keepdims=False)
    before = shifted(own_tokens[block_len - CTX :], 1)
    positions = seq_index * block_len - CTX + jnp.arange(block_len + CTX)
    live = ((positions < length) & (positions >= 0)).astype(F32)[:, None]
    valid = live[CTX:]
    inputs = own_tokens.astype(F32)
    normed_in, inverse_in = normalize(inputs)
    attn_input = (normed_in * attention_norm_gain).astype(BF16)
    early = (normalize(before.astype(F32))[0] * attention_norm_gain).astype(BF16)
    window = jnp.concatenate([early, attn_input[: block_len - CTX]]).astype(F32) * live[:block_len]
    signal = tiles(window)

    both = jnp.stack([state_rate, state_coefficient])
    both = lax.all_gather(both, ("seq", "tp"), axis=1, tiled=True)
    states = both.shape[2]
    both = jnp.transpose(both, (0, 2, 1)).reshape(2, states, features // 128, 128)
    rate, gain = both[0], both[1]
    decay = jnp.exp(-rate)
    grid = rate.shape
    local_state, local_moment = call(scan_in, [(grid, F32)] * 2, decay, signal)
    start = 0.0
    for m in range(1, seq_count):
        start = start + jnp.exp(-rate * (block_len * (m - 1))) * shifted(local_state, m)
    (context,) = call(
        scan_out, [((CTX,) + grid[1:], F32)], decay, gain, start, signal[:CTX]
    )
    context = context.reshape(CTX, features).astype(BF16)

    queries = dot(attn_input, wq, NT).astype(BF16)
    token_keys = dot(attn_input, wk, NT).astype(BF16)
    token_values = dot(attn_input, wv, NT).astype(BF16)
    state_keys = dot(context, wsk, NT).astype(BF16)
    state_values = dot(context, wsv, NT).astype(BF16)
    query_heads = queries.reshape(block_len, heads, DH)
    key_heads = jnp.concatenate([token_keys, state_keys]).reshape(-1, heads, DH)
    value_heads = jnp.concatenate([token_values, state_values]).reshape(-1, heads, DH)
    causal = jnp.arange(block_len)[:, None] >= jnp.arange(block_len)[None, :]
    allowed = jnp.concatenate([causal, jnp.broadcast_to(seq_index > 0, (block_len, CTX))], axis=1)
    raw = jnp.einsum("qhd,khd->hqk", query_heads, key_heads, preferred_element_type=F32) * scale
    scores = jnp.where(allowed, raw, NEGATIVE)
    row_max = jnp.max(scores, axis=-1, keepdims=True)
    exp_scores = jnp.exp(scores - row_max)
    row_total = jnp.sum(exp_scores, axis=-1, keepdims=True)
    probs_full = exp_scores / row_total
    attn_probs = probs_full.astype(BF16)
    head_mix = jnp.einsum("hqk,khd->qhd", attn_probs, value_heads, preferred_element_type=F32)
    head_mix = head_mix.reshape(block_len, heads * DH).astype(BF16)
    residual = inputs + dot(head_mix, wo, NN)
    normed_mid, inverse_mid = normalize(residual)
    mlp_input = (normed_mid * feedforward_norm_gain).astype(BF16)

    grad_out = own_cot.astype(F32) * valid
    grad_out_b = grad_out.astype(BF16)
    mlp_rows = jnp.concatenate([mlp_input, flip(mlp_input, 1)])
    out_rows = jnp.concatenate([grad_out_b, flip(grad_out_b, 1)])
    pre_act = dot(mlp_rows, wh, NT)
    activated, gelu_back = jax.vjp(partial(jax.nn.gelu, approximate=False), pre_act)
    activated = activated.astype(BF16)
    mlp_part = dot(activated, wr, NN)
    grad_act = dot(out_rows, wr, NT)
    grad_pre = gelu_back(grad_act)[0].astype(BF16)
    mid_part = dot(grad_pre, wh, NN)
    grad_mid = mid_part[:block_len] + flip(mid_part[block_len:].astype(BF16), 1).astype(F32)
    mlp_out = mlp_part[:block_len] + flip(mlp_part[block_len:].astype(BF16), 1).astype(F32)
    output = ((residual + mlp_out) * valid).astype(BF16)
    output_line = line_gather(output)
    grad_return = dot(activated, out_rows, TN).astype(BF16)
    grad_hidden = dot(grad_pre, mlp_rows, TN).astype(BF16)

    def reduce_hidden(grad, reverse):
        grad = grad.reshape(planes, tp_count * hidden_rows, features)
        mine = plane_reduce({p: grad[p] for p in range(planes)}, reverse)
        mine = mine.reshape(tp_count, hidden_rows, features)
        return line_reduce([mine[j] for j in range(tp_count)])

    sum_hidden = reduce_hidden(grad_hidden, False)
    sum_return = reduce_hidden(grad_return, True)

    grad_mlp_gain = jnp.sum(grad_mid * normed_mid, axis=0)
    grad_resid = grad_out + norm_back(normed_mid, inverse_mid, grad_mid * feedforward_norm_gain)
    grad_resid_b = grad_resid.astype(BF16)
    grad_heads = dot(grad_resid_b, wo, NT).astype(BF16).reshape(block_len, heads, DH)
    grad_probs = jnp.einsum("qhd,khd->hqk", grad_heads, value_heads, preferred_element_type=F32)
    delta = jnp.sum(probs_full * grad_probs, axis=-1, keepdims=True)
    grad_scores = (probs_full * (grad_probs - delta)).astype(BF16)
    grad_queries = (
        jnp.einsum("hqk,khd->qhd", grad_scores, key_heads, preferred_element_type=F32) * scale
    )
    grad_keys_all = (
        jnp.einsum("hqk,qhd->khd", grad_scores, query_heads, preferred_element_type=F32) * scale
    )
    grad_values_all = jnp.einsum(
        "hqk,qhd->khd", attn_probs, grad_heads, preferred_element_type=F32
    )
    wide = heads * DH
    grad_queries = grad_queries.reshape(block_len, wide).astype(BF16)
    grad_keys_all = grad_keys_all.reshape(block_len + CTX, wide).astype(BF16)
    grad_values_all = grad_values_all.reshape(block_len + CTX, wide).astype(BF16)
    grad_token_keys, grad_state_keys = grad_keys_all[:block_len], grad_keys_all[block_len:]
    grad_token_values, grad_state_values = grad_values_all[:block_len], grad_values_all[block_len:]
    grad_context = (
        dot(grad_state_keys, wsk, NN) + dot(grad_state_values, wsv, NN)
    ).astype(BF16)

    grad_conv = tiles(grad_context)
    (local_back,) = call(scan_back_in, [(grid, F32)], decay, grad_conv)
    end = 0.0
    for m in range(1, seq_count):
        end = end + jnp.exp(-rate * (block_len * (m - 1))) * shifted(local_back, -m)
    grad_signal, grad_gain, grad_moment = call(
        scan_back_out,
        [((block_len,) + grid[1:], F32), (grid, F32), (grid, F32)],
        decay,
        gain,
        end,
        start,
        signal[:CTX],
        grad_conv,
    )
    end_moment = block_len * jnp.exp(-rate * block_len) * start + local_moment
    grad_rate = -gain * (grad_moment + end * end_moment)
    grad_signal = grad_signal.reshape(block_len, features).astype(BF16)
    grad_signal = jnp.concatenate([grad_signal[CTX:], shifted(grad_signal[:CTX], -1)])

    grad_in = (
        dot(grad_queries, wq, NN)
        + dot(grad_token_keys, wk, NN)
        + dot(grad_token_values, wv, NN)
        + grad_signal.astype(F32) * valid
    )
    grad_attn_gain = jnp.sum(grad_in * normed_in, axis=0)
    grad_tokens = grad_resid + norm_back(normed_in, inverse_in, grad_in * attention_norm_gain)
    tokens_line = line_gather(grad_tokens.astype(BF16))

    def split(values):
        return values.reshape(values.shape[0], tp_count, 2, head_cols // 2)

    def both_rows(values):
        values = split(values)
        mine, other = values[:, :, 0], values[:, :, 1]
        joined = jnp.concatenate([mine, flip(other, 1)])
        return joined.reshape(joined.shape[0], -1)

    def both_full(values):
        return jnp.concatenate([values, flip(values, 1)])

    x_rows, c_rows, r_rows = both_full(attn_input), both_full(context), both_full(grad_resid_b)
    grads_a = [
        dot(both_rows(grad_queries), x_rows, TN),
        dot(both_rows(grad_token_keys), x_rows, TN),
        dot(both_rows(grad_token_values), x_rows, TN),
    ]
    grads_b = [
        dot(both_rows(grad_state_keys), c_rows, TN),
        dot(both_rows(grad_state_values), c_rows, TN),
        dot(both_rows(head_mix), r_rows, TN),
    ]

    def reduce_heads(grads, reverse):
        stack = jnp.stack([g.astype(BF16) for g in grads]).reshape(
            len(grads), tp_count, planes, head_rows, features
        )
        mine = plane_reduce(
            {p: jnp.transpose(stack[:, :, p], (1, 0, 2, 3)) for p in range(planes)}, reverse
        )
        return line_reduce([mine[j] for j in range(tp_count)])

    sum_a = reduce_heads(grads_a, False)
    sum_b = reduce_heads(grads_b, True)

    def spread(value, reverse):
        plane = plane_gather(value, reverse)
        other = {p: flip(v, 1) for p, v in plane.items()}
        return jnp.stack([(plane, other)[i & 1][i >> 1] for i in range(seq_count)])

    def ordered(stack):
        return [
            lax.dynamic_index_in_dim(stack, seq_index ^ i, 0, keepdims=False)
            for i in range(seq_count)
        ]

    fix = 1.0 / copies

    def head_grads(value, reverse):
        parts = ordered(spread(value, reverse))
        parts = [parts[2 * p + c] for c in range(2) for p in range(planes)]
        return jnp.concatenate(parts, axis=1).astype(F32) * fix

    def hidden_grads(value, reverse):
        return jnp.concatenate(ordered(spread(value, reverse))).astype(F32) * fix

    full_a = head_grads(sum_a, False)
    full_b = head_grads(sum_b, True)
    full_hidden = hidden_grads(sum_hidden, False)
    full_return = hidden_grads(sum_return, True)

    gains = lax.psum(jnp.stack([grad_attn_gain, grad_mlp_gain]), ("seq", "tp")) * fix
    kernel_grads = jnp.stack([grad_gain, grad_rate]).reshape(2, states, features)
    kernel_grads = lax.psum_scatter(
        jnp.transpose(kernel_grads, (2, 0, 1)).reshape(features, 2 * states),
        ("seq", "tp"),
        scatter_dimension=0,
        tiled=True,
    )
    kernel_grads = kernel_grads * fix

    def lined(line, dtype):
        stack = jnp.stack(line)
        return jnp.stack(
            [
                lax.dynamic_index_in_dim(
                    stack, (tp_index - b * copies) % tp_count, 0, keepdims=False
                )
                for b in range(sequences)
            ]
        ).astype(dtype)

    return (
        lined(output_line, BF16),
        lined(tokens_line, F32),
        gains[0],
        full_a[0].T,
        full_a[1].T,
        full_a[2].T,
        full_b[2],
        full_b[0].T,
        full_b[1].T,
        kernel_grads[:, :states],
        kernel_grads[:, states:],
        gains[1],
        full_hidden.T,
        full_return,
    )


LOG2E = math.log2(math.e)
SCALE = DH ** (-0.5)


def cost(us):
    return pl.CostEstimate(flops=int(us * 1.1e9), bytes_accessed=0, transcendentals=0)


def params(limit=50):
    return pltpu.CompilerParams(vmem_limit_bytes=limit * 2**20)


def like(shape, dtype=BF16):
    return jax.ShapeDtypeStruct(shape, dtype)


def whole(shape):
    return pl.BlockSpec(shape, lambda *_: (0,) * len(shape))


def launch(kernel, place, grid, in_specs, out_specs, outs, operands, scratch=(), us=5):
    return pl.pallas_call(
        kernel,
        grid_spec=pltpu.PrefetchScalarGridSpec(
            num_scalar_prefetch=1,
            grid=grid,
            in_specs=in_specs,
            out_specs=out_specs,
            scratch_shapes=list(scratch),
        ),
        out_shape=outs,
        compiler_params=params(),
        cost_estimate=cost(us),
    )(place, *operands)


def timed(us):
    return partial(launch, us=us)


def cycle(value, steps):
    count = lax.axis_size("tp")
    return lax.ppermute(value, "tp", [(i, (i + steps) % count) for i in range(count)])


def pack_heads(place, wq, wk, wv, wsk, wsv, wo, out, turned):
    chip = place[0] >> 1
    rows = out.shape[2]
    for w, ref in enumerate((wq, wk, wv, wsk, wsv, wo)):
        turned[...] = ref[...].astype(F32) if ref is wo else ref[...].astype(F32).T
        for p in range(4):
            cut = pl.ds(pl.multiple_of((chip ^ p) * rows, rows), rows)
            out[p, w] = turned[cut, :].astype(BF16)


def pack_hidden(place, wh, wr, out, turned):
    chip = place[0] >> 1
    rows = out.shape[2]
    for w, ref in enumerate((wh, wr)):
        turned[...] = ref[...].astype(F32).T if ref is wh else ref[...].astype(F32)
        for p in range(4):
            cut = pl.ds(pl.multiple_of((chip ^ p) * rows, rows), rows)
            out[p, w] = turned[cut, :].astype(BF16)


def load_heads(j, own, far, into, first, count):
    rows = own.shape[2]

    @pl.when(j == 0)
    def _():
        for p in range(4):
            for w in range(count):
                into[w, p * rows : (p + 1) * rows] = own[p, first + w]

    @pl.when(j > 0)
    def _():
        for p in range(4):
            for w in range(count):
                if p < 3:
                    into[w, p * rows : (p + 1) * rows] = far[p][0, first + w]
                else:
                    into[w, p * rows : (p + 1) * rows] = far[3 + (first + w) // 3][0, (first + w) % 3]


def masked(raw, r, block):
    n = raw.shape[1]
    column = lax.broadcasted_iota(jnp.int32, raw.shape, 1)
    row = lax.broadcasted_iota(jnp.int32, raw.shape, 0)
    keep = (column - (n - 128) <= row) & ((column >= CTX) | (block > 0))
    return jnp.where(keep, raw * (SCALE * LOG2E), NEGATIVE)


def project(place, x0, x1, own, f0, f1, f2, f3, f4, q_ref, k_ref, v_ref, weight):
    j = pl.program_id(0)
    load_heads(j, own, (f0, f1, f2, f3, f4), weight, 0, 3)
    rows = x0.shape[0]
    qkv_w = weight[0:3].reshape(3 * DH, -1)
    for half, x in enumerate((x0, x1)):
        saved = slice(half * rows, (half + 1) * rows)
        qkv = dot(x[...], qkv_w, NT).astype(BF16)
        q_ref[saved] = qkv[:, :DH]
        k_ref[saved] = qkv[:, DH : 2 * DH]
        v_ref[saved] = qkv[:, 2 * DH :]


def attend(place, c0, c1, own, f0, f1, f2, f3, f4, q_ref, k_ref, v_ref,
           part0, part1, s_ref, o_ref, lse_ref, weight, keys, values, total):
    j = pl.program_id(0)
    load_heads(j, own, (f0, f1, f2, f3, f4), weight, 3, 3)
    rows = part0.shape[0]

    @pl.when(j == 0)
    def _():
        total[...] = jnp.zeros_like(total)

    st_w = weight[0:2].reshape(2 * DH, -1)
    for half, c in enumerate((c0, c1)):
        base = half * rows
        state = dot(c[...], st_w, NT).astype(BF16)
        s_ref[half * CTX : (half + 1) * CTX] = state
        keys[half, 0:CTX] = state[:, :DH]
        values[half, 0:CTX] = state[:, DH:]
        keys[half, CTX:] = k_ref[base : base + rows]
        values[half, CTX:] = v_ref[base : base + rows]
    for half in range(2):
        block = place[0] ^ half
        base = half * rows
        for r in range(rows // 128):
            saved = slice(base + r * 128, base + (r + 1) * 128)
            n = CTX + (r + 1) * 128
            scores = masked(dot(q_ref[saved], keys[half, 0:n], NT), r, block)
            top = jnp.max(scores, axis=1, keepdims=True)
            power = jnp.exp2(scores - top)
            summed = jnp.sum(power, axis=1, keepdims=True)
            lse_ref[0, saved] = top + jnp.log2(summed)
            probs = (power * (1.0 / summed)).astype(BF16)
            o_ref[saved] = dot(probs, values[half, 0:n], NN).astype(BF16)
    for half in range(2):
        base = half * rows
        total[base : base + rows] += dot(o_ref[base : base + rows], weight[2], NN)

    @pl.when(j == pl.num_programs(0) - 1)
    def _():
        part0[...] = total[0:rows].astype(part0.dtype)
        part1[...] = total[rows:].astype(part1.dtype)


def attend_back(place, g0, g1, own, f0, f1, f2, f3, f4,
                q_ref, k_ref, v_ref, s_ref, lse_ref,
                in0, in1, ctx0, ctx1, d_ref, ds_ref,
                weight, keys, values, heads, grad_k, grad_v, total, ctx_total):
    j = pl.program_id(0)
    load_heads(j, own, (f0, f1, f2, f3, f4), weight, 0, 6)
    rows = g0.shape[0]

    @pl.when(j == 0)
    def _():
        total[...] = jnp.zeros_like(total)
        ctx_total[...] = jnp.zeros_like(ctx_total)

    qkv_w = weight[0:3].reshape(3 * DH, -1)
    st_w = weight[3:5].reshape(2 * DH, -1)
    for half, g in enumerate((g0, g1)):
        base = half * rows
        keys[half, 0:CTX] = s_ref[half * CTX : (half + 1) * CTX, :DH]
        values[half, 0:CTX] = s_ref[half * CTX : (half + 1) * CTX, DH:]
        keys[half, CTX:] = k_ref[base : base + rows]
        values[half, CTX:] = v_ref[base : base + rows]
        heads[half] = dot(g[...], weight[5], NT).astype(BF16)
    for half in range(2):
        block = place[0] ^ half
        base = half * rows
        for r in reversed(range(rows // 128)):
            saved = slice(base + r * 128, base + (r + 1) * 128)
            n = CTX + (r + 1) * 128
            q = q_ref[saved]
            own = heads[half, r * 128 : (r + 1) * 128]
            probs = jnp.exp2(masked(dot(q, keys[half, 0:n], NT), r, block) - lse_ref[0, saved])
            grad = dot(own, values[half, 0:n], NT)
            delta = jnp.sum(probs * grad, axis=1, keepdims=True)
            scores = (probs * (grad - delta)).astype(BF16)
            d_ref[saved, 0:DH] = (dot(scores, keys[half, 0:n], NN) * SCALE).astype(BF16)
            to_k = dot(scores, q, TN)
            to_v = dot(probs.astype(BF16), own, TN)
            if r == rows // 128 - 1:
                grad_k[half, 0:n] = to_k
                grad_v[half, 0:n] = to_v
            else:
                grad_k[half, 0:n] += to_k
                grad_v[half, 0:n] += to_v
    for half in range(2):
        base = half * rows
        d_ref[base : base + rows, DH : 2 * DH] = (grad_k[half, CTX:] * SCALE).astype(BF16)
        d_ref[base : base + rows, 2 * DH :] = grad_v[half, CTX:].astype(BF16)
        state = slice(half * CTX, (half + 1) * CTX)
        ds_ref[state, :DH] = (grad_k[half, 0:CTX] * SCALE).astype(BF16)
        ds_ref[state, DH:] = grad_v[half, 0:CTX].astype(BF16)
        ctx_total[state] += dot(ds_ref[state], st_w, NN)
        total[base : base + rows] += dot(d_ref[base : base + rows], qkv_w, NN)

    @pl.when(j == pl.num_programs(0) - 1)
    def _():
        in0[...] = total[0:rows].astype(in0.dtype)
        in1[...] = total[rows:].astype(in1.dtype)
        ctx0[...] = ctx_total[0:CTX].astype(ctx0.dtype)
        ctx1[...] = ctx_total[CTX:].astype(ctx1.dtype)


def attend_weights(place, x0, x1, c0, c1, g0, g1, d_ref, ds_ref, o_ref, keep_a, send_a, keep_b, send_b):
    rows = x0.shape[0]
    cut = keep_a.shape[3]
    to_qkv = (dot(d_ref[0:rows], x0[...], TN) + dot(d_ref[rows:], x1[...], TN)).astype(BF16)
    to_state = (dot(ds_ref[0:CTX], c0[...], TN) + dot(ds_ref[CTX:], c1[...], TN)).astype(BF16)
    to_out = (dot(o_ref[0:rows], g0[...], TN) + dot(o_ref[rows:], g1[...], TN)).astype(BF16)
    spots_a = {0: (keep_a, 0), 2: (keep_a, 1), 1: (send_a, 0), 3: (send_a, 1)}
    spots_b = {0: (keep_b, 0), 1: (keep_b, 1), 2: (send_b, 0), 3: (send_b, 1)}
    for p in range(4):
        out, at = spots_a[p]
        for w in range(3):
            out[at, 0, w] = to_qkv[w * DH + p * cut : w * DH + (p + 1) * cut]
        out, at = spots_b[p]
        for w in range(2):
            out[at, 0, w] = to_state[w * DH + p * cut : w * DH + (p + 1) * cut]
        out[at, 0, 2] = to_out[p * cut : (p + 1) * cut]


def gelu_parts(x):
    size = jnp.abs(x) * math.sqrt(0.5)
    bell = jnp.exp2(x * x * (-0.5 * LOG2E))
    t = 1.0 / (1.0 + 0.3275911 * size)
    poly = 1.061405429 * t - 1.453152027
    poly = poly * t + 1.421413741
    poly = poly * t - 0.284496736
    poly = poly * t + 0.254829592
    tail = 0.5 * poly * t * bell
    return jnp.where(x >= 0, 1.0 - tail, tail), bell * (1.0 / math.sqrt(2.0 * math.pi))


def load_hidden(p, w, own, far, first, into):
    rows = into.shape[0] // 4
    into[0:rows] = own[0, w]
    for i, piece in enumerate(far):
        @pl.when(p == first + i)
        def _():
            for slot in range(3):
                held = piece[slot, w] if len(piece.shape) == 4 else piece[slot]
                into[(1 + slot) * rows : (2 + slot) * rows] = held


def feed_in(first, place, m0, m1, own, *rest):
    *far, act_ref, slope_ref, wh = rest
    load_hidden(pl.program_id(0) + first, 0, own, far, first, wh)
    rows = m0.shape[0]
    for half, m in enumerate((m0, m1)):
        saved = slice(half * rows, (half + 1) * rows)
        pre = dot(m[...], wh[...], NT)
        part, bell = gelu_parts(pre)
        act_ref[saved] = (pre * part).astype(BF16)
        slope_ref[saved] = (part + pre * bell).astype(BF16)


def feed_out(place, g0, g1, own, f0, f1, f2, h3, r3, act_a, slope_a, act_b, slope_b,
             mlp0, mlp1, mid0, mid1, pre_ref, wh, wr, mlp, mid):
    p = pl.program_id(0)
    load_hidden(p, 0, own, (f0, f1, f2, h3), 0, wh)
    load_hidden(p, 1, own, (f0, f1, f2, r3), 0, wr)
    rows = g0.shape[0]

    @pl.when(p == 0)
    def _():
        mlp[...] = jnp.zeros_like(mlp)
        mid[...] = jnp.zeros_like(mid)

    def step(act, slope):
        for half, g in enumerate((g0, g1)):
            saved = slice(half * rows, (half + 1) * rows)
            back = dot(g[...], wr[...], NT)
            pre_ref[saved] = (back * slope[saved].astype(F32)).astype(BF16)
            mlp[saved] += dot(act[saved], wr[...], NN)
            mid[saved] += dot(pre_ref[saved], wh[...], NN)

    @pl.when(p < 3)
    def _():
        step(act_a, slope_a)

    @pl.when(p == 3)
    def _():
        step(act_b, slope_b)

    @pl.when(p == 3)
    def _():
        mlp0[...] = mlp[0:rows].astype(mlp0.dtype)
        mlp1[...] = mlp[rows:].astype(mlp1.dtype)
        mid0[...] = mid[0:rows].astype(mid0.dtype)
        mid1[...] = mid[rows:].astype(mid1.dtype)


def feed_weights(keeps, place, a0, a1, *rest):
    *parts, keep, send = rest
    p = pl.program_id(0)
    rows = a0.shape[0]
    cut = keep.shape[2]

    def step(b, out):
        grad = (dot(b[0:rows], a0[...], TN) + dot(b[rows:], a1[...], TN)).astype(BF16)
        for slot in range(4):
            out[0, slot] = grad[slot * cut : (slot + 1) * cut]

    for i in range(4):
        @pl.when(p == i)
        def _():
            step(parts[-1] if i == 3 else parts[0], keep if i in keeps else send)


def live_rows(place, count):
    at = place[0] * (count * pl.num_programs(0)) + pl.program_id(0) * count
    position = at + lax.broadcasted_iota(jnp.int32, (count, 1), 0)
    return (position < place[2]).astype(F32)


def middle(place, tokens, own, got, gain, residual, m_ref):
    value = tokens[0].astype(F32) + own[...] + got[...].astype(F32)
    residual[...] = value
    m_ref[...] = (normalize(value)[0] * gain[...]).astype(BF16)


def finish(place, residual, own, got, out):
    value = residual[...] + own[...] + got[...].astype(F32)
    out[...] = (value * live_rows(place, value.shape[0])).astype(BF16)


def middle_back(place, residual, own, got, cot, gain, grad, grad_b, sums):
    value = residual[...]
    normed, inverse = normalize(value)
    valid = live_rows(place, value.shape[0])
    back = own[...] + got[...].astype(F32)
    total = jnp.sum(back * normed, axis=0, keepdims=True)

    @pl.when(pl.program_id(0) == 0)
    def _():
        sums[...] = total

    @pl.when(pl.program_id(0) > 0)
    def _():
        sums[...] += total

    value = cot[0].astype(F32) * valid + norm_back(normed, inverse, back * gain[...])
    grad[...] = value
    grad_b[...] = value.astype(BF16)


def first_back(place, tokens, own, got, signal, grad, gain, out, sums):
    normed, inverse = normalize(tokens[0].astype(F32))
    valid = live_rows(place, out.shape[0])
    back = own[...] + got[...].astype(F32) + signal[...].astype(F32) * valid
    total = jnp.sum(back * normed, axis=0, keepdims=True)

    @pl.when(pl.program_id(0) == 0)
    def _():
        sums[...] = total

    @pl.when(pl.program_id(0) > 0)
    def _():
        sums[...] += total

    out[...] = (grad[...] + norm_back(normed, inverse, back * gain[...])).astype(BF16)


def unpack_heads(place, n0, n1, n2, n3, f0, f1, f2, f3, q, k, v, o, sk, sv, rows_ref):
    core, chip = place[0] & 1, place[0] >> 1
    cut = n0.shape[1]
    for w, out in ((0, q), (1, k), (2, v), (3, sk), (4, sv), (5, o)):
        for other, pieces in ((0, (n0, n1, n2, n3)), (1, (f0, f1, f2, f3))):
            for p, piece in enumerate(pieces):
                at = (core ^ other) * DH + (chip ^ p) * cut
                rows_ref[pl.ds(pl.multiple_of(at, cut), cut), :] = piece[w].astype(F32)
        out[...] = rows_ref[...] if out is o else rows_ref[...].T


def unpack_hidden(place, n0, n1, n2, n3, f0, f1, f2, f3, h, r):
    core, chip = place[0] & 1, place[0] >> 1
    cut = n0.shape[1]
    for other, pieces in ((0, (n0, n1, n2, n3)), (1, (f0, f1, f2, f3))):
        for p, piece in enumerate(pieces):
            at = pl.multiple_of((core ^ other) * 4 * cut + (chip ^ p) * cut, cut)
            r[pl.ds(at, cut), :] = piece[1].astype(F32)
            h[:, pl.ds(at, cut)] = piece[0].astype(F32).T


def far_away(value):
    return pltpu.with_memory_space_constraint(value, pltpu.HBM)


def add(a, b):
    return (a.astype(F32) + b.astype(F32)).astype(BF16)


def after(value, *earlier):
    return lax.optimization_barrier((value, *earlier))[0]


def powers(lengths, rate_ref, *outs):
    for length, out in zip(lengths, outs):
        out[...] = jnp.exp(-rate_ref[...] * float(length))


def states_around(local, power, sign, first, *earlier):
    group = local
    for m in (1, 2):
        group = group + power[m] * shifted(local, sign * m)
    group = after(group, *earlier)
    total = shifted(group, sign * first)
    for m in range(first + 3, 8, 3):
        total = total + power[m - first] * shifted(group, sign * m)
    return total


def scan_rows(decay_ref, gain_ref, late_ref, g_ref, y_ref, end_ref):
    decay, gain = decay_ref[...], gain_ref[...]
    rows, count = y_ref.shape[0], g_ref.shape[0]

    def full(t, lam):
        lam = lam + g_ref[count - 1 - t]
        y_ref[rows - 1 - t] = jnp.sum(gain * lam, axis=0)
        return decay * lam

    def empty(t, lam):
        y_ref[rows - count - 1 - t] = jnp.sum(gain * lam, axis=0)
        return decay * lam

    lam = lax.fori_loop(0, count, full, late_ref[...], unroll=8)
    end_ref[...] = lam
    lax.fori_loop(0, rows - count, empty, lam, unroll=8)


def scan_sums(decay_ref, start_ref, u_ref, g_ref, gh_ref, gm_ref):
    decay = decay_ref[...]

    def again(t, carry):
        h, m, gh, gm = carry
        h, m = decay * h + u_ref[t], decay * (m + h)
        g = g_ref[t]
        return h, m, gh + g * h, gm + g * m

    zero = jnp.zeros(decay.shape, F32)
    _, _, gh, gm = lax.fori_loop(0, u_ref.shape[0], again, (start_ref[...], zero, zero, zero))
    gh_ref[...] = gh
    gm_ref[...] = gm


def fast_body(
    tokens, lengths, attention_norm_gain, query_weight, key_weight, value_weight, output_weight,
    state_key_weight, state_value_weight, state_coefficient, state_rate, feedforward_norm_gain,
    hidden_weight, return_weight, cotangent,
):
    sequences, block_len, features = tokens.shape
    tp_count = lax.axis_size("tp")
    seq_index = lax.axis_index("seq")
    tp_index = lax.axis_index("tp")
    hidden_cols = hidden_weight.shape[1]
    cut = DH // 4
    wide = hidden_cols // 8
    length = lax.dynamic_index_in_dim(lengths, tp_index, 0, keepdims=False)
    place = jnp.stack([seq_index, tp_index, length]).astype(jnp.int32)

    column = pl.BlockSpec((features, DH), lambda i, place: (0, place[0] & 1))
    (own_w,) = timed(4)(
        pack_heads, place, (1,),
        [column] * 5 + [pl.BlockSpec((DH, features), lambda i, place: (place[0] & 1, 0))],
        [whole((4, 6, cut, features))],
        [like((4, 6, cut, features))],
        tuple(map(far_away, (
            query_weight, key_weight, value_weight, state_key_weight, state_value_weight, output_weight
        ))),
        [pltpu.VMEM((DH, features), F32)],
    )
    (own_m,) = timed(5)(
        pack_hidden, place, (1,),
        [
            pl.BlockSpec((features, hidden_cols // 2), lambda i, place: (0, place[0] & 1)),
            pl.BlockSpec((hidden_cols // 2, features), lambda i, place: (place[0] & 1, 0)),
        ],
        [whole((4, 2, wide, features))],
        [like((4, 2, wide, features))],
        (far_away(hidden_weight), far_away(return_weight)),
        [pltpu.VMEM((hidden_cols // 2, features), F32)],
    )

    own_tokens = lax.dynamic_index_in_dim(tokens, tp_index, 0, keepdims=False)
    own_cot = lax.dynamic_index_in_dim(cotangent, tp_index, 0, keepdims=False)
    before = shifted(own_tokens[block_len - CTX :], 1)
    positions = seq_index * block_len - CTX + jnp.arange(block_len + CTX)
    live = ((positions < length) & (positions >= 0)).astype(F32)[:, None]
    x = (normalize(own_tokens.astype(F32))[0] * attention_norm_gain).astype(BF16)
    x_other = flip(x, 1)
    grad_out = (own_cot.astype(F32) * live[CTX:]).astype(BF16)
    grad_out_other = flip(grad_out, 1)
    early = (normalize(before.astype(F32))[0] * attention_norm_gain).astype(BF16)
    signal = tiles(
        jnp.concatenate([early, x[: block_len - CTX]]).astype(F32) * live[:block_len]
    )

    states = state_rate.shape[1]
    channels = state_rate.shape[0]
    both = jnp.stack([state_rate, state_coefficient]).reshape(1, -1, 128)
    devices = features // channels
    both = lax.all_to_all(
        jnp.broadcast_to(both, (devices,) + both.shape[1:]), ("seq", "tp"), 0, 0
    )
    both = jnp.transpose(both.reshape(devices, 2, channels, states), (1, 3, 0, 2))
    both = both.reshape(2, states, features // 128, 128)
    rate, gain = both[0], both[1]
    grid = rate.shape
    spans = [1, block_len - CTX] + [block_len * m for m in (1, 2, 3, 6)]
    decay, tail_power, *blocks = call(
        partial(powers, spans), [(grid, F32)] * len(spans), rate, us=1
    )
    block_power = dict(zip((1, 2, 3, 6), blocks))

    def line_of(own):
        return jnp.stack([cycle(own, j) for j in range(1, tp_count)])

    def plane_of(line, by_x, by_y, half):
        return [line, by_x, by_y, flip(by_y[:, :half], 2), flip(by_x[:, half:], 4)]

    line_w = line_of(own_w[0])
    near_w = flip(line_w, 2), flip(line_w, 4)
    far_w = plane_of(line_w, *near_w, 3)
    line_m = line_of(after(own_m[0], line_w))
    near_m = flip(after(line_m, *near_w), 2), flip(after(line_m, *near_w), 4)
    far_m = plane_of(line_m, *near_m, 1)
    far_m[3:] = [value[:, 0] for value in far_m[3:]]

    local_state, local_moment = call(
        scan_in, [(grid, F32)] * 2, decay, after(signal, line_w, own_m, x_other, grad_out_other), us=8
    )
    start = states_around(after(local_state, *near_w), block_power, 1, 1)
    (context,) = call(scan_out, [((CTX,) + grid[1:], F32)], decay, gain, start, signal[:CTX], us=3)
    context = context.reshape(CTX, features).astype(BF16)
    context_other = flip(context, 1)
    rows = 2 * block_len
    slots = tp_count
    own_spec = whole((4, 6, cut, features))

    def slot_spec(*shape):
        return pl.BlockSpec(
            (1, *shape, features),
            lambda j, place: (jnp.maximum(j - 1, 0),) + (0,) * (len(shape) + 1),
        )

    weight_specs = [own_spec] + [slot_spec(6, cut)] * 3 + [slot_spec(3, cut)] * 2
    weights = (own_w, *far_w)
    full = whole((block_len, features))
    ctx_spec = whole((CTX, features))
    head = lambda n, width: pl.BlockSpec((n, width), lambda j, place: (0, j))
    lse_spec = pl.BlockSpec((1, rows, 1), lambda j, place: (j, 0, 0))
    q, k, v = timed(8)(
        project, place, (slots,),
        [full] * 2 + weight_specs,
        [head(rows, DH)] * 3,
        [like((rows, slots * DH))] * 3,
        (x, x_other, *weights),
        [pltpu.VMEM((3, DH, features), BF16)],
    )
    attended = timed(20)(
        attend, place, (slots,),
        [ctx_spec] * 2 + weight_specs + [head(rows, DH)] * 3,
        [full] * 2 + [head(2 * CTX, 2 * DH), head(rows, DH), lse_spec],
        [like((block_len, features), F32), like((block_len, features))]
        + [like((2 * CTX, slots * 2 * DH)), like((rows, slots * DH)), like((slots, rows, 1), F32)],
        (after(context, line_m), context_other, *weights, q, k, v),
        [
            pltpu.VMEM((3, DH, features), BF16),
            pltpu.VMEM((2, CTX + block_len, DH), BF16),
            pltpu.VMEM((2, CTX + block_len, DH), BF16),
            pltpu.VMEM((rows, features), F32),
        ],
    )
    part, part_other, state, mix, lse = attended
    group = 128
    steps = block_len // group
    row_spec = pl.BlockSpec((group, features), lambda i, place: (i, 0))
    seq_spec = pl.BlockSpec((1, group, features), lambda i, place: (place[1], i, 0))
    gain_spec = whole((1, features))
    mid_gain = feedforward_norm_gain.reshape(1, -1)
    residual, m = timed(4)(
        middle, place, (steps,),
        [seq_spec, row_spec, row_spec, gain_spec], [row_spec] * 2,
        [like((block_len, features), F32), like((block_len, features))],
        (tokens, part, after(flip(part_other, 1), *near_m), mid_gain),
    )
    m_other = flip(m, 1)

    chunk = 4 * wide
    def fixed(shape):
        return pl.BlockSpec(shape, lambda *_: (0,) * len(shape), pipeline_mode=pl.Buffered(1))

    def own_spec_of(count, first):
        return pl.BlockSpec((1, count, wide, features), lambda p, place: (p + first, 0, 0, 0))

    def feeding(first, count, far, far_specs, earlier):
        return timed(4 * count)(
            partial(feed_in, first), place, (count,),
            [full] * 2 + [own_spec_of(1, first)] + far_specs,
            [head(rows, chunk)] * 2,
            [like((rows, count * chunk))] * 2,
            (after(m, *earlier), m_other, own_m, *far),
            [pltpu.VMEM((chunk, features), BF16)],
        )

    act_a, slope_a = feeding(0, 3, far_m[:3], [fixed((3, 1, wide, features))] * 3, ())
    act_b, slope_b = feeding(3, 1, far_m[3:4], [fixed((3, wide, features))], (act_a,))
    early = pl.BlockSpec((rows, chunk), lambda p, place: (0, jnp.minimum(p, 2)))
    last = fixed((rows, chunk))
    mlp, mlp_other, mid, mid_other, pre = timed(21)(
        feed_out, place, (4,),
        [full] * 2 + [own_spec_of(2, 0)] + [fixed((3, 2, wide, features))] * 3
        + [fixed((3, wide, features))] * 2 + [early] * 2 + [last] * 2,
        [full] * 4 + [head(rows, chunk)],
        [like((block_len, features), F32), like((block_len, features))] * 2
        + [like((rows, 4 * chunk))],
        (grad_out, grad_out_other, own_m, *far_m, act_a, slope_a, act_b, slope_b),
        [pltpu.VMEM((chunk, features), BF16)] * 2 + [pltpu.VMEM((rows, features), F32)] * 2,
    )
    mid_got, mlp_got = flip(mid_other, 1), flip(mlp_other, 1)
    def hidden_grads(keeps, keep_at, rows_of, parts, part_specs):
        def spec(at):
            return pl.BlockSpec(
                (1, slots, wide, features), lambda p, place: (at(p), 0, 0, 0)
            )

        return timed(8)(
            partial(feed_weights, keeps), place, (4,),
            [full] * 2 + part_specs,
            [spec(keep_at), spec(lambda p: jnp.maximum(p - 2, 0))],
            [like((2, slots, wide, features))] * 2,
            (*rows_of, *map(far_away, parts)),
        )

    keep_r, send_r = hidden_grads(
        (0, 1), lambda p: jnp.minimum(p, 1), (grad_out, grad_out_other),
        (after(act_a, pre), act_b), [early, last],
    )
    mlp_got = after(mlp_got, keep_r)
    mid_got = after(mid_got, keep_r)
    (output,) = timed(3)(
        finish, place, (steps,),
        [row_spec] * 3, [row_spec], [like((block_len, features))], (residual, mlp, mlp_got),
    )
    output_all = lax.all_gather(output, "tp")
    resid, resid_b, sums_mid = timed(5)(
        middle_back, place, (steps,),
        [row_spec] * 3 + [seq_spec, gain_spec], [row_spec] * 2 + [gain_spec],
        [
            like((block_len, features), F32), like((block_len, features)),
            like((1, features), F32),
        ],
        (after(residual, output), mid, mid_got, cotangent, mid_gain),
    )
    resid_other = flip(resid_b, 1)
    keep_h, send_h = hidden_grads(
        (0, 2), lambda p: p // 2, (m, m_other), (after(pre, resid_b),), [head(rows, chunk)]
    )

    grad_in, grad_in_other, grad_ctx, grad_ctx_other, d, ds = timed(27)(
        attend_back, place, (slots,),
        [full] * 2 + weight_specs + [head(rows, DH)] * 3 + [head(2 * CTX, 2 * DH), lse_spec],
        [full] * 2 + [ctx_spec] * 2 + [head(rows, 3 * DH), head(2 * CTX, 2 * DH)],
        [
            like((block_len, features), F32), like((block_len, features)),
            like((CTX, features), F32), like((CTX, features)),
            like((rows, slots * 3 * DH)), like((2 * CTX, slots * 2 * DH)),
        ],
        (after(resid_b, keep_h), resid_other, *map(far_away, weights), q, k, v, state, lse),
        [
            pltpu.VMEM((6, DH, features), BF16),
            pltpu.VMEM((2, CTX + block_len, DH), BF16),
            pltpu.VMEM((2, CTX + block_len, DH), BF16),
            pltpu.VMEM((2, block_len, DH), BF16),
            pltpu.VMEM((2, CTX + block_len, DH), F32),
            pltpu.VMEM((2, CTX + block_len, DH), F32),
            pltpu.VMEM((rows, features), F32),
            pltpu.VMEM((2 * CTX, features), F32),
        ],
    )
    grad_ctx_got = flip(grad_ctx_other, 1)
    grad_in_got = flip(grad_in_other, 1)
    part_spec = pl.BlockSpec((2, 1, 3, cut, features), lambda j, place: (0, j, 0, 0, 0))
    keep_a, send_a, keep_b, send_b = timed(10)(
        attend_weights, place, (slots,),
        [full] * 2 + [ctx_spec] * 2 + [full] * 2
        + [head(rows, 3 * DH), head(2 * CTX, 2 * DH), head(rows, DH)],
        [part_spec] * 4,
        [like((2, slots, 3, cut, features))] * 4,
        (x, x_other, context, context_other, resid_b, resid_other, d, ds, mix),
    )

    got_r = flip(after(send_r, resid_b), 4)
    got_h = flip(after(send_h, resid_b), 2)
    near_h, away_h = add(keep_h[0], got_h[0]), add(keep_h[1], got_h[1])
    near_r, away_r = add(keep_r[0], got_r[0]), add(keep_r[1], got_r[1])
    grad_context = (grad_ctx + grad_ctx_got.astype(F32)).astype(BF16)
    grad_conv = tiles(after(grad_context, got_r, got_h))
    grad_later = tiles(shifted(grad_context, -1))
    (local_back,) = call(scan_back_in, [(grid, F32)], decay, grad_conv)
    late = tail_power * states_around(local_back, block_power, -1, 2, keep_a, away_h, away_r)
    grad_signal, end = call(
        scan_rows, [((block_len,) + grid[1:], F32), (grid, F32)], decay, gain, late, grad_later
    )
    grad_signal = grad_signal.reshape(block_len, features).astype(BF16)
    grad_tokens, sums_in = timed(5)(
        first_back, place, (steps,),
        [seq_spec] + [row_spec] * 4 + [gain_spec], [row_spec, gain_spec],
        [like((block_len, features)), like((1, features), F32)],
        (tokens, grad_in, grad_in_got, grad_signal, after(resid, output_all), attention_norm_gain.reshape(1, -1)),
    )

    lefts, rights = line_steps(grad_tokens)
    line = [grad_tokens] + [
        jnp.where(tp_index >= j, lefts[j], rights[slots - j]) for j in range(1, slots)
    ]
    line = jnp.stack(line)
    tokens_all = jnp.stack(
        [
            lax.dynamic_index_in_dim(line, (tp_index - b) % slots, 0, keepdims=False)
            for b in range(sequences)
        ]
    ).astype(F32)
    grad_gain, grad_moment = call(
        scan_sums, [(grid, F32)] * 2, decay, after(start, lefts[2], rights[2]), signal[:CTX], grad_conv
    )
    end_moment = block_len * block_power[1] * start + local_moment
    grad_rate = -gain * (grad_moment + end * end_moment)

    def regather(total):
        held = [total, flip(total, 2), flip(total, 4), flip(total, 6)]
        return held + [flip(value, 1) for value in held]

    ready = (late, grad_later)
    more_h, more_r = flip(after(away_h, *ready), 4), flip(after(away_r, *ready), 2)
    more_h, more_r = after(more_h, grad_tokens), after(more_r, grad_tokens)
    got_a = flip(after(send_a, more_h, more_r), 2)
    got_b = flip(after(send_b, more_h, more_r), 4)
    pairs = (near_h, more_h), (near_r, more_r)
    total_m = line_reduce(
        [jnp.stack([add(a[j], b[j]) for a, b in pairs]) for j in range(slots)],
        [(lefts[1], rights[1])] + [()] * (slots - 2),
    )
    near_a, away_a = add(keep_a[0], got_a[0]), add(keep_a[1], got_a[1])
    near_b, away_b = add(keep_b[0], got_b[0]), add(keep_b[1], got_b[1])
    pairs = (near_a, flip(away_a, 4)), (near_b, flip(away_b, 2))
    total_a = line_reduce(
        [jnp.stack([add(a[j], b[j]) for a, b in pairs]) for j in range(slots)]
    )
    pieces_m = regather(total_m)
    pieces_a = regather(total_a.reshape(6, cut, features))
    grad_hidden, grad_return = timed(5)(
        unpack_hidden, place, (1,),
        [whole((2, wide, features))] * 8,
        [whole((features, hidden_cols)), whole((hidden_cols, features))],
        [like((features, hidden_cols), F32), like((hidden_cols, features), F32)],
        pieces_m,
    )
    grad_q, grad_k, grad_v, grad_o, grad_sk, grad_sv = timed(5)(
        unpack_heads, place, (1,),
        [whole((6, cut, features))] * 8,
        [whole((features, 2 * DH))] * 3 + [whole((2 * DH, features))] + [whole((features, 2 * DH))] * 2,
        [like((features, 2 * DH), F32)] * 3
        + [like((2 * DH, features), F32)]
        + [like((features, 2 * DH), F32)] * 2,
        pieces_a,
        [pltpu.VMEM((2 * DH, features), F32)],
    )

    small = jnp.stack([grad_gain, grad_rate]).reshape(2, states, devices, channels)
    small = jnp.transpose(small, (2, 3, 0, 1)).reshape(devices, -1, 128)
    sums = jnp.concatenate([sums_in, sums_mid]).reshape(1, -1, 128)
    sums = jnp.broadcast_to(sums, (devices,) + sums.shape[1:])
    count = small.shape[1]
    small = jnp.sum(
        lax.all_to_all(
            after(jnp.concatenate([small, sums], axis=1), total_a), ("seq", "tp"), 0, 0
        ),
        axis=0,
    )
    kernel_grads = small[:count].reshape(channels, 2, states)
    gains = small[count:].reshape(2, features)

    return (
        output_all, tokens_all, gains[0], grad_q, grad_k, grad_v, grad_o, grad_sk, grad_sv,
        kernel_grads[:, 0], kernel_grads[:, 1], gains[1], grad_hidden, grad_return,
    )


def choose(tokens, *others):
    query_weight = others[2]
    fits = (
        lax.axis_size("seq") == 8
        and lax.axis_size("tp") == tokens.shape[0]
        and query_weight.shape[1] == 2 * DH
        and others[11].shape[1] % 1024 == 0
        and tokens.shape[1] % 512 == 0
        and tokens.shape[2] == 1024
    )
    return (fast_body if fits else body)(tokens, *others)


def solution(mesh):
    rows = P(None, "seq", None)
    columns = P(None, "tp")
    heads = P("tp", None)
    channels = P(("seq", "tp"), None)
    return jax.shard_map(
        choose,
        mesh=mesh,
        in_specs=(
            rows, P(), P(), columns, columns, columns, heads, columns, columns,
            channels, channels, P(), columns, heads, rows,
        ),
        out_specs=(
            rows, rows, P(), columns, columns, columns, heads, columns, columns,
            channels, channels, P(), columns, heads,
        ),
        check_vma=False,
    )
```

```python
from functools import partial
import math

import jax
import jax.numpy as jnp
from jax import lax
from jax.experimental import pallas as pl
from jax.experimental.pallas import tpu as pltpu
from jax.sharding import PartitionSpec as P

DH = 128
CTX = 128
EPS = 1e-05
NEGATIVE = -1e30
F32 = jnp.float32
BF16 = jnp.bfloat16


def normalize(values):
    center = values - jnp.mean(values, axis=-1, keepdims=True)
    inverse = lax.rsqrt(jnp.mean(center * center, axis=-1, keepdims=True) + EPS)
    return (center * inverse, inverse)


def norm_back(normed, inverse, grad_normed):
    mean_grad = jnp.mean(grad_normed, axis=-1, keepdims=True)
    mean_cross = jnp.mean(grad_normed * normed, axis=-1, keepdims=True)
    return inverse * (grad_normed - mean_grad - normed * mean_cross)


def flip(value, mask):
    count = lax.axis_size("seq")
    return lax.ppermute(value, "seq", [(i, i ^ mask) for i in range(count)])


def shifted(value, steps):
    count = lax.axis_size("seq")
    first, last = (max(0, -steps), min(count, count - steps))
    return lax.ppermute(value, "seq", [(i, i + steps) for i in range(first, last)])


def line_steps(value):
    count = lax.axis_size("tp")
    lefts, rights = [value], [value]
    for k in range(1, count):
        lefts.append(lax.ppermute(lefts[-1], "tp", [(i, i + 1) for i in range(k - 1, count - 1)]))
        rights.append(
            lax.ppermute(rights[-1], "tp", [(i, i - 1) for i in range(1, count - k + 1)])
        )
    return lefts, rights


def line_gather(value):
    count = lax.axis_size("tp")
    place = lax.axis_index("tp")
    lefts, rights = line_steps(value)
    return [value] + [
        jnp.where(place >= j, lefts[j], rights[count - j]) for j in range(1, count)
    ]


def line_reduce(chunks, pace=None):
    count = lax.axis_size("tp")

    def add(a, b, k):
        if pace:
            a = lax.optimization_barrier((a, *pace[k - 1]))[0]
        return a if b is None else (a.astype(F32) + b.astype(F32)).astype(BF16)

    going, coming = None, None
    for k in range(1, count):
        going = lax.ppermute(add(chunks[k], going, k), "tp", [(i, i + 1) for i in range(k)])
        coming = lax.ppermute(
            add(chunks[count - k], coming, k), "tp", [(i, i - 1) for i in range(count - k, count)]
        )
    return (chunks[0].astype(F32) + going.astype(F32) + coming.astype(F32)).astype(BF16)


def plane_bits(reverse):
    count = lax.axis_size("seq") // 2
    bits = [1 << b for b in range(count.bit_length() - 1)]
    return bits[::-1] if reverse else bits


def plane_gather(value, reverse):
    held = {0: value}
    for bit in plane_bits(reverse):
        held.update({p | bit: flip(v, 2 * bit) for p, v in list(held.items())})
    return held


def plane_reduce(pieces, reverse):
    held = dict(pieces)
    for bit in plane_bits(reverse):
        for p in [p for p in held if p & bit]:
            got = flip(held.pop(p), 2 * bit)
            held[p ^ bit] = (held[p ^ bit].astype(F32) + got.astype(F32)).astype(BF16)
    return held[0]


def scan_in(decay_ref, u_ref, state_ref, moment_ref):
    decay = decay_ref[...]

    def step(t, carry):
        h, m = carry
        return decay * h + u_ref[t], decay * (m + h)

    zero = jnp.zeros(decay.shape, F32)
    h, m = lax.fori_loop(0, u_ref.shape[0], step, (zero, zero))
    state_ref[...] = h
    moment_ref[...] = m


def scan_out(decay_ref, gain_ref, start_ref, u_ref, y_ref):
    decay, gain = decay_ref[...], gain_ref[...]

    def step(t, h):
        h = decay * h + u_ref[t]
        y_ref[t] = jnp.sum(gain * h, axis=0)
        return h

    lax.fori_loop(0, u_ref.shape[0], step, start_ref[...])


def scan_back_in(decay_ref, g_ref, state_ref):
    decay = decay_ref[...]
    last = g_ref.shape[0] - 1

    def step(t, lam):
        return decay * (lam + g_ref[last - t])

    state_ref[...] = lax.fori_loop(0, last + 1, step, jnp.zeros(decay.shape, F32))


def scan_back_out(decay_ref, gain_ref, end_ref, start_ref, u_ref, g_ref, y_ref, gh_ref, gm_ref):
    decay, gain = decay_ref[...], gain_ref[...]
    rows, count = y_ref.shape[0], g_ref.shape[0]

    def empty(t, lam):
        y_ref[rows - 1 - t] = jnp.sum(gain * lam, axis=0)
        return decay * lam

    def full(t, lam):
        lam = lam + g_ref[count - 1 - t]
        y_ref[count - 1 - t] = jnp.sum(gain * lam, axis=0)
        return decay * lam

    lam = lax.fori_loop(0, rows - count, empty, end_ref[...])
    lax.fori_loop(0, count, full, lam)

    def again(t, carry):
        h, m, gh, gm = carry
        h, m = decay * h + u_ref[t], decay * (m + h)
        g = g_ref[t]
        return h, m, gh + g * h, gm + g * m

    zero = jnp.zeros(decay.shape, F32)
    _, _, gh, gm = lax.fori_loop(0, count, again, (start_ref[...], zero, zero, zero))
    gh_ref[...] = gh
    gm_ref[...] = gm


def call(kernel, outs, *operands, us=5):
    return pl.pallas_call(
        kernel,
        out_shape=[jax.ShapeDtypeStruct(shape, dtype) for shape, dtype in outs],
        compiler_params=pltpu.CompilerParams(vmem_limit_bytes=42 * 2**20),
        cost_estimate=pl.CostEstimate(flops=int(us * 1.1e9), bytes_accessed=0, transcendentals=0),
    )(*operands)


def tiles(values):
    return values.astype(F32).reshape(values.shape[0], values.shape[1] // 128, 128)


def dot(a, b, dims):
    return lax.dot_general(a, b, (dims, ((), ())), preferred_element_type=F32)


NN = ((1,), (0,))
NT = ((1,), (1,))
TN = ((0,), (0,))


def body(
    tokens,
    lengths,
    attention_norm_gain,
    query_weight,
    key_weight,
    value_weight,
    output_weight,
    state_key_weight,
    state_value_weight,
    state_coefficient,
    state_rate,
    feedforward_norm_gain,
    hidden_weight,
    return_weight,
    cotangent,
):
    sequences, block_len, features = tokens.shape
    seq_count = lax.axis_size("seq")
    tp_count = lax.axis_size("tp")
    seq_index = lax.axis_index("seq")
    tp_index = lax.axis_index("tp")
    planes = seq_count // 2
    copies = tp_count // sequences
    sequence = tp_index // copies
    head_cols = query_weight.shape[1]
    hidden_cols = hidden_weight.shape[1]
    heads = head_cols * tp_count // DH
    head_rows = head_cols // seq_count
    hidden_rows = hidden_cols // seq_count
    scale = DH ** (-0.5)

    shard_a = [query_weight.T, key_weight.T, value_weight.T]
    shard_b = [state_key_weight.T, state_value_weight.T, output_weight]
    shard_m = [hidden_weight.T, return_weight]

    def head_slice(shard, relative):
        other = seq_index ^ relative
        at = (other & 1) * planes + (other >> 1)
        return lax.dynamic_slice_in_dim(shard, at * head_rows, head_rows, 0)

    def hidden_slice(shard, relative):
        return lax.dynamic_slice_in_dim(
            shard, (seq_index ^ relative) * hidden_rows, hidden_rows, 0
        )

    def gather_heads(shards, reverse):
        mine = jnp.stack([head_slice(w, 0) for w in shards])
        line = jnp.stack(line_gather(mine)[1:])
        plane = plane_gather(line, reverse)
        other = {p: flip(v, 1) for p, v in plane.items()}
        far = jnp.stack(
            [jnp.stack([group[p] for p in range(planes)]) for group in (plane, other)]
        )
        far = jnp.transpose(far, (3, 2, 0, 1, 4, 5))
        own = jnp.stack(
            [
                jnp.concatenate([head_slice(w, 2 * p + c) for c in range(2) for p in range(planes)])
                for w in shards
            ]
        )
        far = far.reshape(len(shards), (tp_count - 1) * head_cols, features)
        return jnp.concatenate([own, far], axis=1)

    def gather_hidden(shard, reverse):
        line = line_gather(hidden_slice(shard, 0))
        plane = plane_gather(jnp.concatenate(line[1:]), reverse)
        return jnp.concatenate(
            [
                piece
                for p in range(planes)
                for piece in (hidden_slice(shard, 2 * p), plane[p])
            ]
        )

    wq, wk, wv = gather_heads(shard_a, False)
    wsk, wsv, wo = gather_heads(shard_b, True)
    wh = gather_hidden(shard_m[0], False)
    wr = gather_hidden(shard_m[1], True)

    own_tokens = lax.dynamic_index_in_dim(tokens, sequence, 0, keepdims=False)
    own_cot = lax.dynamic_index_in_dim(cotangent, sequence, 0, keepdims=False)
    length = lax.dynamic_index_in_dim(lengths, sequence, 0, keepdims=False)
    before = shifted(own_tokens[block_len - CTX :], 1)
    positions = seq_index * block_len - CTX + jnp.arange(block_len + CTX)
    live = ((positions < length) & (positions >= 0)).astype(F32)[:, None]
    valid = live[CTX:]
    inputs = own_tokens.astype(F32)
    normed_in, inverse_in = normalize(inputs)
    attn_input = (normed_in * attention_norm_gain).astype(BF16)
    early = (normalize(before.astype(F32))[0] * attention_norm_gain).astype(BF16)
    window = jnp.concatenate([early, attn_input[: block_len - CTX]]).astype(F32) * live[:block_len]
    signal = tiles(window)

    both = jnp.stack([state_rate, state_coefficient])
    both = lax.all_gather(both, ("seq", "tp"), axis=1, tiled=True)
    states = both.shape[2]
    both = jnp.transpose(both, (0, 2, 1)).reshape(2, states, features // 128, 128)
    rate, gain = both[0], both[1]
    decay = jnp.exp(-rate)
    grid = rate.shape
    local_state, local_moment = call(scan_in, [(grid, F32)] * 2, decay, signal)
    start = 0.0
    for m in range(1, seq_count):
        start = start + jnp.exp(-rate * (block_len * (m - 1))) * shifted(local_state, m)
    (context,) = call(
        scan_out, [((CTX,) + grid[1:], F32)], decay, gain, start, signal[:CTX]
    )
    context = context.reshape(CTX, features).astype(BF16)

    queries = dot(attn_input, wq, NT).astype(BF16)
    token_keys = dot(attn_input, wk, NT).astype(BF16)
    token_values = dot(attn_input, wv, NT).astype(BF16)
    state_keys = dot(context, wsk, NT).astype(BF16)
    state_values = dot(context, wsv, NT).astype(BF16)
    query_heads = queries.reshape(block_len, heads, DH)
    key_heads = jnp.concatenate([token_keys, state_keys]).reshape(-1, heads, DH)
    value_heads = jnp.concatenate([token_values, state_values]).reshape(-1, heads, DH)
    causal = jnp.arange(block_len)[:, None] >= jnp.arange(block_len)[None, :]
    allowed = jnp.concatenate([causal, jnp.broadcast_to(seq_index > 0, (block_len, CTX))], axis=1)
    raw = jnp.einsum("qhd,khd->hqk", query_heads, key_heads, preferred_element_type=F32) * scale
    scores = jnp.where(allowed, raw, NEGATIVE)
    row_max = jnp.max(scores, axis=-1, keepdims=True)
    exp_scores = jnp.exp(scores - row_max)
    row_total = jnp.sum(exp_scores, axis=-1, keepdims=True)
    probs_full = exp_scores / row_total
    attn_probs = probs_full.astype(BF16)
    head_mix = jnp.einsum("hqk,khd->qhd", attn_probs, value_heads, preferred_element_type=F32)
    head_mix = head_mix.reshape(block_len, heads * DH).astype(BF16)
    residual = inputs + dot(head_mix, wo, NN)
    normed_mid, inverse_mid = normalize(residual)
    mlp_input = (normed_mid * feedforward_norm_gain).astype(BF16)

    grad_out = own_cot.astype(F32) * valid
    grad_out_b = grad_out.astype(BF16)
    mlp_rows = jnp.concatenate([mlp_input, flip(mlp_input, 1)])
    out_rows = jnp.concatenate([grad_out_b, flip(grad_out_b, 1)])
    pre_act = dot(mlp_rows, wh, NT)
    activated, gelu_back = jax.vjp(partial(jax.nn.gelu, approximate=False), pre_act)
    activated = activated.astype(BF16)
    mlp_part = dot(activated, wr, NN)
    grad_act = dot(out_rows, wr, NT)
    grad_pre = gelu_back(grad_act)[0].astype(BF16)
    mid_part = dot(grad_pre, wh, NN)
    grad_mid = mid_part[:block_len] + flip(mid_part[block_len:].astype(BF16), 1).astype(F32)
    mlp_out = mlp_part[:block_len] + flip(mlp_part[block_len:].astype(BF16), 1).astype(F32)
    output = ((residual + mlp_out) * valid).astype(BF16)
    output_line = line_gather(output)
    grad_return = dot(activated, out_rows, TN).astype(BF16)
    grad_hidden = dot(grad_pre, mlp_rows, TN).astype(BF16)

    def reduce_hidden(grad, reverse):
        grad = grad.reshape(planes, tp_count * hidden_rows, features)
        mine = plane_reduce({p: grad[p] for p in range(planes)}, reverse)
        mine = mine.reshape(tp_count, hidden_rows, features)
        return line_reduce([mine[j] for j in range(tp_count)])

    sum_hidden = reduce_hidden(grad_hidden, False)
    sum_return = reduce_hidden(grad_return, True)

    grad_mlp_gain = jnp.sum(grad_mid * normed_mid, axis=0)
    grad_resid = grad_out + norm_back(normed_mid, inverse_mid, grad_mid * feedforward_norm_gain)
    grad_resid_b = grad_resid.astype(BF16)
    grad_heads = dot(grad_resid_b, wo, NT).astype(BF16).reshape(block_len, heads, DH)
    grad_probs = jnp.einsum("qhd,khd->hqk", grad_heads, value_heads, preferred_element_type=F32)
    delta = jnp.sum(probs_full * grad_probs, axis=-1, keepdims=True)
    grad_scores = (probs_full * (grad_probs - delta)).astype(BF16)
    grad_queries = (
        jnp.einsum("hqk,khd->qhd", grad_scores, key_heads, preferred_element_type=F32) * scale
    )
    grad_keys_all = (
        jnp.einsum("hqk,qhd->khd", grad_scores, query_heads, preferred_element_type=F32) * scale
    )
    grad_values_all = jnp.einsum(
        "hqk,qhd->khd", attn_probs, grad_heads, preferred_element_type=F32
    )
    wide = heads * DH
    grad_queries = grad_queries.reshape(block_len, wide).astype(BF16)
    grad_keys_all = grad_keys_all.reshape(block_len + CTX, wide).astype(BF16)
    grad_values_all = grad_values_all.reshape(block_len + CTX, wide).astype(BF16)
    grad_token_keys, grad_state_keys = grad_keys_all[:block_len], grad_keys_all[block_len:]
    grad_token_values, grad_state_values = grad_values_all[:block_len], grad_values_all[block_len:]
    grad_context = (
        dot(grad_state_keys, wsk, NN) + dot(grad_state_values, wsv, NN)
    ).astype(BF16)

    grad_conv = tiles(grad_context)
    (local_back,) = call(scan_back_in, [(grid, F32)], decay, grad_conv)
    end = 0.0
    for m in range(1, seq_count):
        end = end + jnp.exp(-rate * (block_len * (m - 1))) * shifted(local_back, -m)
    grad_signal, grad_gain, grad_moment = call(
        scan_back_out,
        [((block_len,) + grid[1:], F32), (grid, F32), (grid, F32)],
        decay,
        gain,
        end,
        start,
        signal[:CTX],
        grad_conv,
    )
    end_moment = block_len * jnp.exp(-rate * block_len) * start + local_moment
    grad_rate = -gain * (grad_moment + end * end_moment)
    grad_signal = grad_signal.reshape(block_len, features).astype(BF16)
    grad_signal = jnp.concatenate([grad_signal[CTX:], shifted(grad_signal[:CTX], -1)])

    grad_in = (
        dot(grad_queries, wq, NN)
        + dot(grad_token_keys, wk, NN)
        + dot(grad_token_values, wv, NN)
        + grad_signal.astype(F32) * valid
    )
    grad_attn_gain = jnp.sum(grad_in * normed_in, axis=0)
    grad_tokens = grad_resid + norm_back(normed_in, inverse_in, grad_in * attention_norm_gain)
    tokens_line = line_gather(grad_tokens.astype(BF16))

    def split(values):
        return values.reshape(values.shape[0], tp_count, 2, head_cols // 2)

    def both_rows(values):
        values = split(values)
        mine, other = values[:, :, 0], values[:, :, 1]
        joined = jnp.concatenate([mine, flip(other, 1)])
        return joined.reshape(joined.shape[0], -1)

    def both_full(values):
        return jnp.concatenate([values, flip(values, 1)])

    x_rows, c_rows, r_rows = both_full(attn_input), both_full(context), both_full(grad_resid_b)
    grads_a = [
        dot(both_rows(grad_queries), x_rows, TN),
        dot(both_rows(grad_token_keys), x_rows, TN),
        dot(both_rows(grad_token_values), x_rows, TN),
    ]
    grads_b = [
        dot(both_rows(grad_state_keys), c_rows, TN),
        dot(both_rows(grad_state_values), c_rows, TN),
        dot(both_rows(head_mix), r_rows, TN),
    ]

    def reduce_heads(grads, reverse):
        stack = jnp.stack([g.astype(BF16) for g in grads]).reshape(
            len(grads), tp_count, planes, head_rows, features
        )
        mine = plane_reduce(
            {p: jnp.transpose(stack[:, :, p], (1, 0, 2, 3)) for p in range(planes)}, reverse
        )
        return line_reduce([mine[j] for j in range(tp_count)])

    sum_a = reduce_heads(grads_a, False)
    sum_b = reduce_heads(grads_b, True)

    def spread(value, reverse):
        plane = plane_gather(value, reverse)
        other = {p: flip(v, 1) for p, v in plane.items()}
        return jnp.stack([(plane, other)[i & 1][i >> 1] for i in range(seq_count)])

    def ordered(stack):
        return [
            lax.dynamic_index_in_dim(stack, seq_index ^ i, 0, keepdims=False)
            for i in range(seq_count)
        ]

    fix = 1.0 / copies

    def head_grads(value, reverse):
        parts = ordered(spread(value, reverse))
        parts = [parts[2 * p + c] for c in range(2) for p in range(planes)]
        return jnp.concatenate(parts, axis=1).astype(F32) * fix

    def hidden_grads(value, reverse):
        return jnp.concatenate(ordered(spread(value, reverse))).astype(F32) * fix

    full_a = head_grads(sum_a, False)
    full_b = head_grads(sum_b, True)
    full_hidden = hidden_grads(sum_hidden, False)
    full_return = hidden_grads(sum_return, True)

    gains = lax.psum(jnp.stack([grad_attn_gain, grad_mlp_gain]), ("seq", "tp")) * fix
    kernel_grads = jnp.stack([grad_gain, grad_rate]).reshape(2, states, features)
    kernel_grads = lax.psum_scatter(
        jnp.transpose(kernel_grads, (2, 0, 1)).reshape(features, 2 * states),
        ("seq", "tp"),
        scatter_dimension=0,
        tiled=True,
    )
    kernel_grads = kernel_grads * fix

    def lined(line, dtype):
        stack = jnp.stack(line)
        return jnp.stack(
            [
                lax.dynamic_index_in_dim(
                    stack, (tp_index - b * copies) % tp_count, 0, keepdims=False
                )
                for b in range(sequences)
            ]
        ).astype(dtype)

    return (
        lined(output_line, BF16),
        lined(tokens_line, F32),
        gains[0],
        full_a[0].T,
        full_a[1].T,
        full_a[2].T,
        full_b[2],
        full_b[0].T,
        full_b[1].T,
        kernel_grads[:, :states],
        kernel_grads[:, states:],
        gains[1],
        full_hidden.T,
        full_return,
    )


LOG2E = math.log2(math.e)
SCALE = DH ** (-0.5)


def cost(us):
    return pl.CostEstimate(flops=int(us * 1.1e9), bytes_accessed=0, transcendentals=0)


def params(limit=50):
    return pltpu.CompilerParams(vmem_limit_bytes=limit * 2**20)


def like(shape, dtype=BF16):
    return jax.ShapeDtypeStruct(shape, dtype)


def whole(shape):
    return pl.BlockSpec(shape, lambda *_: (0,) * len(shape))


def launch(kernel, place, grid, in_specs, out_specs, outs, operands, scratch=(), us=5):
    return pl.pallas_call(
        kernel,
        grid_spec=pltpu.PrefetchScalarGridSpec(
            num_scalar_prefetch=1,
            grid=grid,
            in_specs=in_specs,
            out_specs=out_specs,
            scratch_shapes=list(scratch),
        ),
        out_shape=outs,
        compiler_params=params(),
        cost_estimate=cost(us),
    )(place, *operands)


def timed(us):
    return partial(launch, us=us)


def cycle(value, steps):
    count = lax.axis_size("tp")
    return lax.ppermute(value, "tp", [(i, (i + steps) % count) for i in range(count)])


def pack_heads(place, wq, wk, wv, wsk, wsv, wo, out, mine, turned):
    chip = place[0] >> 1
    rows = out.shape[2]
    for w, ref in enumerate((wq, wk, wv, wsk, wsv, wo)):
        turned[...] = ref[...].astype(F32) if ref is wo else ref[...].astype(F32).T
        for p in range(4):
            cut = pl.ds(pl.multiple_of((chip ^ p) * rows, rows), rows)
            out[p, w] = turned[cut, :].astype(BF16)
        mine[w] = out[0, w]


def pack_hidden(place, wh, wr, out, mine, turned):
    chip = place[0] >> 1
    rows = out.shape[2]
    for w, ref in enumerate((wh, wr)):
        turned[...] = ref[...].astype(F32).T if ref is wh else ref[...].astype(F32)
        for p in range(4):
            cut = pl.ds(pl.multiple_of((chip ^ p) * rows, rows), rows)
            out[p, w] = turned[cut, :].astype(BF16)
        mine[w] = out[0, w]


def load_heads(j, own, far, into, first, count):
    rows = own.shape[2]

    @pl.when(j == 0)
    def _():
        for p in range(4):
            for w in range(count):
                into[w, p * rows : (p + 1) * rows] = own[p, first + w]

    @pl.when(j > 0)
    def _():
        for p in range(4):
            for w in range(count):
                if p < 3:
                    into[w, p * rows : (p + 1) * rows] = far[p][0, first + w]
                else:
                    into[w, p * rows : (p + 1) * rows] = far[3 + (first + w) // 3][0, (first + w) % 3]


def masked(raw, r, block):
    n = raw.shape[1]
    column = lax.broadcasted_iota(jnp.int32, raw.shape, 1)
    row = lax.broadcasted_iota(jnp.int32, raw.shape, 0)
    keep = (column - (n - 128) <= row) & ((column >= CTX) | (block > 0))
    return jnp.where(keep, raw * (SCALE * LOG2E), NEGATIVE)


def project(place, x0, x1, own, f0, f1, f2, f3, f4, q_ref, k_ref, v_ref, weight):
    j = pl.program_id(0)
    load_heads(j, own, (f0, f1, f2, f3, f4), weight, 0, 3)
    rows = x0.shape[0]
    qkv_w = weight[0:3].reshape(3 * DH, -1)
    for half, x in enumerate((x0, x1)):
        saved = slice(half * rows, (half + 1) * rows)
        qkv = dot(x[...], qkv_w, NT).astype(BF16)
        q_ref[saved] = qkv[:, :DH]
        k_ref[saved] = qkv[:, DH : 2 * DH]
        v_ref[saved] = qkv[:, 2 * DH :]


def attend(place, c0, c1, own, f0, f1, f2, f3, f4, q_ref, k_ref, v_ref,
           part0, part1, s_ref, o_ref, lse_ref, weight, keys, values, total):
    j = pl.program_id(0)
    load_heads(j, own, (f0, f1, f2, f3, f4), weight, 3, 3)
    rows = part0.shape[0]

    @pl.when(j == 0)
    def _():
        total[...] = jnp.zeros_like(total)

    st_w = weight[0:2].reshape(2 * DH, -1)
    for half, c in enumerate((c0, c1)):
        base = half * rows
        state = dot(c[...], st_w, NT).astype(BF16)
        s_ref[half * CTX : (half + 1) * CTX] = state
        keys[half, 0:CTX] = state[:, :DH]
        values[half, 0:CTX] = state[:, DH:]
        keys[half, CTX:] = k_ref[base : base + rows]
        values[half, CTX:] = v_ref[base : base + rows]
    for half in range(2):
        block = place[0] ^ half
        base = half * rows
        for r in range(rows // 128):
            saved = slice(base + r * 128, base + (r + 1) * 128)
            n = CTX + (r + 1) * 128
            scores = masked(dot(q_ref[saved], keys[half, 0:n], NT), r, block)
            top = jnp.max(scores, axis=1, keepdims=True)
            power = jnp.exp2(scores - top)
            summed = jnp.sum(power, axis=1, keepdims=True)
            lse_ref[0, saved] = top + jnp.log2(summed)
            probs = (power * (1.0 / summed)).astype(BF16)
            o_ref[saved] = dot(probs, values[half, 0:n], NN).astype(BF16)
    for half in range(2):
        base = half * rows
        total[base : base + rows] += dot(o_ref[base : base + rows], weight[2], NN)

    @pl.when(j == pl.num_programs(0) - 1)
    def _():
        part0[...] = total[0:rows].astype(part0.dtype)
        part1[...] = total[rows:].astype(part1.dtype)


def attend_back(place, g0, g1, own, f0, f1, f2, f3, f4,
                q_ref, k_ref, v_ref, s_ref, lse_ref,
                in0, in1, ctx0, ctx1, d_ref, ds_ref,
                weight, keys, values, heads, grad_k, grad_v, total, ctx_total):
    j = pl.program_id(0)
    load_heads(j, own, (f0, f1, f2, f3, f4), weight, 0, 6)
    rows = g0.shape[0]

    @pl.when(j == 0)
    def _():
        total[...] = jnp.zeros_like(total)
        ctx_total[...] = jnp.zeros_like(ctx_total)

    qkv_w = weight[0:3].reshape(3 * DH, -1)
    st_w = weight[3:5].reshape(2 * DH, -1)
    for half, g in enumerate((g0, g1)):
        base = half * rows
        keys[half, 0:CTX] = s_ref[half * CTX : (half + 1) * CTX, :DH]
        values[half, 0:CTX] = s_ref[half * CTX : (half + 1) * CTX, DH:]
        keys[half, CTX:] = k_ref[base : base + rows]
        values[half, CTX:] = v_ref[base : base + rows]
        heads[half] = dot(g[...], weight[5], NT).astype(BF16)
    for half in range(2):
        block = place[0] ^ half
        base = half * rows
        for r in reversed(range(rows // 128)):
            saved = slice(base + r * 128, base + (r + 1) * 128)
            n = CTX + (r + 1) * 128
            q = q_ref[saved]
            own = heads[half, r * 128 : (r + 1) * 128]
            probs = jnp.exp2(masked(dot(q, keys[half, 0:n], NT), r, block) - lse_ref[0, saved])
            grad = dot(own, values[half, 0:n], NT)
            delta = jnp.sum(probs * grad, axis=1, keepdims=True)
            scores = (probs * (grad - delta)).astype(BF16)
            d_ref[saved, 0:DH] = (dot(scores, keys[half, 0:n], NN) * SCALE).astype(BF16)
            to_k = dot(scores, q, TN)
            to_v = dot(probs.astype(BF16), own, TN)
            if r == rows // 128 - 1:
                grad_k[half, 0:n] = to_k
                grad_v[half, 0:n] = to_v
            else:
                grad_k[half, 0:n] += to_k
                grad_v[half, 0:n] += to_v
    for half in range(2):
        base = half * rows
        d_ref[base : base + rows, DH : 2 * DH] = (grad_k[half, CTX:] * SCALE).astype(BF16)
        d_ref[base : base + rows, 2 * DH :] = grad_v[half, CTX:].astype(BF16)
        state = slice(half * CTX, (half + 1) * CTX)
        ds_ref[state, :DH] = (grad_k[half, 0:CTX] * SCALE).astype(BF16)
        ds_ref[state, DH:] = grad_v[half, 0:CTX].astype(BF16)
        ctx_total[state] += dot(ds_ref[state], st_w, NN)
        total[base : base + rows] += dot(d_ref[base : base + rows], qkv_w, NN)

    @pl.when(j == pl.num_programs(0) - 1)
    def _():
        in0[...] = total[0:rows].astype(in0.dtype)
        in1[...] = total[rows:].astype(in1.dtype)
        ctx0[...] = ctx_total[0:CTX].astype(ctx0.dtype)
        ctx1[...] = ctx_total[CTX:].astype(ctx1.dtype)


def attend_weights(place, x0, x1, c0, c1, g0, g1, d_ref, ds_ref, o_ref, keep_a, send_a, keep_b, send_b):
    rows = x0.shape[0]
    cut = keep_a.shape[3]
    to_qkv = (dot(d_ref[0:rows], x0[...], TN) + dot(d_ref[rows:], x1[...], TN)).astype(BF16)
    to_state = (dot(ds_ref[0:CTX], c0[...], TN) + dot(ds_ref[CTX:], c1[...], TN)).astype(BF16)
    to_out = (dot(o_ref[0:rows], g0[...], TN) + dot(o_ref[rows:], g1[...], TN)).astype(BF16)
    spots_a = {0: (keep_a, 0), 2: (keep_a, 1), 1: (send_a, 0), 3: (send_a, 1)}
    spots_b = {0: (keep_b, 0), 1: (keep_b, 1), 2: (send_b, 0), 3: (send_b, 1)}
    for p in range(4):
        out, at = spots_a[p]
        for w in range(3):
            out[at, 0, w] = to_qkv[w * DH + p * cut : w * DH + (p + 1) * cut]
        out, at = spots_b[p]
        for w in range(2):
            out[at, 0, w] = to_state[w * DH + p * cut : w * DH + (p + 1) * cut]
        out[at, 0, 2] = to_out[p * cut : (p + 1) * cut]


def gelu_parts(x):
    size = jnp.abs(x) * math.sqrt(0.5)
    bell = jnp.exp2(x * x * (-0.5 * LOG2E))
    t = 1.0 / (1.0 + 0.3275911 * size)
    poly = 1.061405429 * t - 1.453152027
    poly = poly * t + 1.421413741
    poly = poly * t - 0.284496736
    poly = poly * t + 0.254829592
    tail = 0.5 * poly * t * bell
    return jnp.where(x >= 0, 1.0 - tail, tail), bell * (1.0 / math.sqrt(2.0 * math.pi))


def load_hidden(p, w, own, far, first, into):
    rows = into.shape[0] // 4
    into[0:rows] = own[0, w]
    for i, piece in enumerate(far):
        @pl.when(p == first + i)
        def _():
            for slot in range(3):
                held = piece[slot, w] if len(piece.shape) == 4 else piece[slot]
                into[(1 + slot) * rows : (2 + slot) * rows] = held


def feed_in(first, place, m0, m1, own, *rest):
    *far, act_ref, slope_ref, wh = rest
    load_hidden(pl.program_id(0) + first, 0, own, far, first, wh)
    rows = m0.shape[0]
    for half, m in enumerate((m0, m1)):
        saved = slice(half * rows, (half + 1) * rows)
        pre = dot(m[...], wh[...], NT)
        part, bell = gelu_parts(pre)
        act_ref[saved] = (pre * part).astype(BF16)
        slope_ref[saved] = (part + pre * bell).astype(BF16)


def feed_out(place, g0, g1, own, f0, f1, f2, h3, r3, act_a, slope_a, act_b, slope_b,
             mlp0, mlp1, mid0, mid1, pre_ref, wh, wr, mlp, mid):
    p = pl.program_id(0)
    load_hidden(p, 0, own, (f0, f1, f2, h3), 0, wh)
    load_hidden(p, 1, own, (f0, f1, f2, r3), 0, wr)
    rows = g0.shape[0]

    @pl.when(p == 0)
    def _():
        mlp[...] = jnp.zeros_like(mlp)
        mid[...] = jnp.zeros_like(mid)

    def step(act, slope):
        for half, g in enumerate((g0, g1)):
            saved = slice(half * rows, (half + 1) * rows)
            back = dot(g[...], wr[...], NT)
            pre_ref[saved] = (back * slope[saved].astype(F32)).astype(BF16)
            mlp[saved] += dot(act[saved], wr[...], NN)
            mid[saved] += dot(pre_ref[saved], wh[...], NN)

    @pl.when(p < 3)
    def _():
        step(act_a, slope_a)

    @pl.when(p == 3)
    def _():
        step(act_b, slope_b)

    @pl.when(p == 3)
    def _():
        mlp0[...] = mlp[0:rows].astype(mlp0.dtype)
        mlp1[...] = mlp[rows:].astype(mlp1.dtype)
        mid0[...] = mid[0:rows].astype(mid0.dtype)
        mid1[...] = mid[rows:].astype(mid1.dtype)


def feed_weights(keeps, place, a0, a1, *rest):
    *parts, keep, send = rest
    p = pl.program_id(0)
    rows = a0.shape[0]
    cut = keep.shape[2]

    def step(b, out):
        grad = (dot(b[0:rows], a0[...], TN) + dot(b[rows:], a1[...], TN)).astype(BF16)
        for slot in range(4):
            out[0, slot] = grad[slot * cut : (slot + 1) * cut]

    for i in range(4):
        @pl.when(p == i)
        def _():
            step(parts[-1] if i == 3 else parts[0], keep if i in keeps else send)


def live_rows(place, count):
    at = place[0] * (count * pl.num_programs(0)) + pl.program_id(0) * count
    position = at + lax.broadcasted_iota(jnp.int32, (count, 1), 0)
    return (position < place[2]).astype(F32)


def middle(place, tokens, own, got, gain, residual, m_ref):
    value = tokens[0].astype(F32) + own[...] + got[...].astype(F32)
    residual[...] = value
    m_ref[...] = (normalize(value)[0] * gain[...]).astype(BF16)


def finish(place, residual, own, got, out):
    value = residual[...] + own[...] + got[...].astype(F32)
    out[...] = (value * live_rows(place, value.shape[0])).astype(BF16)


def middle_back(place, residual, own, got, cot, gain, grad, grad_b, sums):
    value = residual[...]
    normed, inverse = normalize(value)
    valid = live_rows(place, value.shape[0])
    back = own[...] + got[...].astype(F32)
    total = jnp.sum(back * normed, axis=0, keepdims=True)

    @pl.when(pl.program_id(0) == 0)
    def _():
        sums[...] = total

    @pl.when(pl.program_id(0) > 0)
    def _():
        sums[...] += total

    value = cot[0].astype(F32) * valid + norm_back(normed, inverse, back * gain[...])
    grad[...] = value
    grad_b[...] = value.astype(BF16)


def first_back(place, tokens, own, got, signal, grad, gain, out, sums):
    normed, inverse = normalize(tokens[0].astype(F32))
    valid = live_rows(place, out.shape[0])
    back = own[...] + got[...].astype(F32) + signal[...].astype(F32) * valid
    total = jnp.sum(back * normed, axis=0, keepdims=True)

    @pl.when(pl.program_id(0) == 0)
    def _():
        sums[...] = total

    @pl.when(pl.program_id(0) > 0)
    def _():
        sums[...] += total

    out[...] = (grad[...] + norm_back(normed, inverse, back * gain[...])).astype(BF16)


def unpack_heads(place, n0, n1, n2, n3, f0, f1, f2, f3, q, k, v, o, sk, sv, rows_ref):
    core, chip = place[0] & 1, place[0] >> 1
    cut = n0.shape[1]
    for w, out in ((0, q), (1, k), (2, v), (3, sk), (4, sv), (5, o)):
        for other, pieces in ((0, (n0, n1, n2, n3)), (1, (f0, f1, f2, f3))):
            for p, piece in enumerate(pieces):
                at = (core ^ other) * DH + (chip ^ p) * cut
                rows_ref[pl.ds(pl.multiple_of(at, cut), cut), :] = piece[w].astype(F32)
        out[...] = rows_ref[...] if out is o else rows_ref[...].T


def unpack_hidden(place, n0, n1, n2, n3, f0, f1, f2, f3, h, r):
    core, chip = place[0] & 1, place[0] >> 1
    cut = n0.shape[1]
    for other, pieces in ((0, (n0, n1, n2, n3)), (1, (f0, f1, f2, f3))):
        for p, piece in enumerate(pieces):
            at = pl.multiple_of((core ^ other) * 4 * cut + (chip ^ p) * cut, cut)
            r[pl.ds(at, cut), :] = piece[1].astype(F32)
            h[:, pl.ds(at, cut)] = piece[0].astype(F32).T


def far_away(value):
    return pltpu.with_memory_space_constraint(value, pltpu.HBM)


def add(a, b):
    return (a.astype(F32) + b.astype(F32)).astype(BF16)


def after(value, *earlier):
    return lax.optimization_barrier((value, *earlier))[0]


def powers(lengths, rate_ref, *outs):
    for length, out in zip(lengths, outs):
        out[...] = jnp.exp(-rate_ref[...] * float(length))


def states_around(local, power, sign, first, *earlier):
    group = local
    for m in (1, 2):
        group = group + power[m] * shifted(local, sign * m)
    group = after(group, *earlier)
    total = shifted(group, sign * first)
    for m in range(first + 3, 8, 3):
        total = total + power[m - first] * shifted(group, sign * m)
    return total


def scan_rows(decay_ref, gain_ref, late_ref, g_ref, y_ref, end_ref):
    decay, gain = decay_ref[...], gain_ref[...]
    rows, count = y_ref.shape[0], g_ref.shape[0]

    def full(t, lam):
        lam = lam + g_ref[count - 1 - t]
        y_ref[rows - 1 - t] = jnp.sum(gain * lam, axis=0)
        return decay * lam

    def empty(t, lam):
        y_ref[rows - count - 1 - t] = jnp.sum(gain * lam, axis=0)
        return decay * lam

    lam = lax.fori_loop(0, count, full, late_ref[...], unroll=8)
    end_ref[...] = lam
    lax.fori_loop(0, rows - count, empty, lam, unroll=8)


def scan_sums(decay_ref, start_ref, u_ref, g_ref, gh_ref, gm_ref):
    decay = decay_ref[...]

    def again(t, carry):
        h, m, gh, gm = carry
        h, m = decay * h + u_ref[t], decay * (m + h)
        g = g_ref[t]
        return h, m, gh + g * h, gm + g * m

    zero = jnp.zeros(decay.shape, F32)
    _, _, gh, gm = lax.fori_loop(0, u_ref.shape[0], again, (start_ref[...], zero, zero, zero))
    gh_ref[...] = gh
    gm_ref[...] = gm


def fast_body(
    tokens, lengths, attention_norm_gain, query_weight, key_weight, value_weight, output_weight,
    state_key_weight, state_value_weight, state_coefficient, state_rate, feedforward_norm_gain,
    hidden_weight, return_weight, cotangent,
):
    sequences, block_len, features = tokens.shape
    tp_count = lax.axis_size("tp")
    seq_index = lax.axis_index("seq")
    tp_index = lax.axis_index("tp")
    hidden_cols = hidden_weight.shape[1]
    cut = DH // 4
    wide = hidden_cols // 8
    length = lax.dynamic_index_in_dim(lengths, tp_index, 0, keepdims=False)
    place = jnp.stack([seq_index, tp_index, length]).astype(jnp.int32)

    column = pl.BlockSpec((features, DH), lambda i, place: (0, place[0] & 1))
    own_w, mine_w = timed(4)(
        pack_heads, place, (1,),
        [column] * 5 + [pl.BlockSpec((DH, features), lambda i, place: (place[0] & 1, 0))],
        [whole((4, 6, cut, features)), whole((6, cut, features))],
        [like((4, 6, cut, features)), like((6, cut, features))],
        tuple(map(far_away, (
            query_weight, key_weight, value_weight, state_key_weight, state_value_weight, output_weight
        ))),
        [pltpu.VMEM((DH, features), F32)],
    )
    own_m, mine_m = timed(5)(
        pack_hidden, place, (1,),
        [
            pl.BlockSpec((features, hidden_cols // 2), lambda i, place: (0, place[0] & 1)),
            pl.BlockSpec((hidden_cols // 2, features), lambda i, place: (place[0] & 1, 0)),
        ],
        [whole((4, 2, wide, features)), whole((2, wide, features))],
        [like((4, 2, wide, features)), like((2, wide, features))],
        (far_away(hidden_weight), far_away(return_weight)),
        [pltpu.VMEM((hidden_cols // 2, features), F32)],
    )

    def line_of(own):
        return jnp.stack([cycle(own, j) for j in range(1, tp_count)])

    line_w = line_of(mine_w)

    own_tokens = lax.dynamic_index_in_dim(tokens, tp_index, 0, keepdims=False)
    own_cot = lax.dynamic_index_in_dim(cotangent, tp_index, 0, keepdims=False)
    before = shifted(own_tokens[block_len - CTX :], 1)
    positions = seq_index * block_len - CTX + jnp.arange(block_len + CTX)
    live = ((positions < length) & (positions >= 0)).astype(F32)[:, None]
    x = (normalize(own_tokens.astype(F32))[0] * attention_norm_gain).astype(BF16)
    x_other = flip(x, 1)
    grad_out = (own_cot.astype(F32) * live[CTX:]).astype(BF16)
    grad_out_other = flip(grad_out, 1)
    early = (normalize(before.astype(F32))[0] * attention_norm_gain).astype(BF16)
    signal = tiles(
        jnp.concatenate([early, x[: block_len - CTX]]).astype(F32) * live[:block_len]
    )

    states = state_rate.shape[1]
    channels = state_rate.shape[0]
    both = jnp.stack([state_rate, state_coefficient]).reshape(1, -1, 128)
    devices = features // channels
    both = lax.all_to_all(
        jnp.broadcast_to(both, (devices,) + both.shape[1:]), ("seq", "tp"), 0, 0
    )
    both = after(both, line_w)
    both = jnp.transpose(both.reshape(devices, 2, channels, states), (1, 3, 0, 2))
    both = both.reshape(2, states, features // 128, 128)
    rate, gain = both[0], both[1]
    grid = rate.shape
    spans = [1, block_len - CTX] + [block_len * m for m in (1, 2, 3, 6)]
    decay, tail_power, *blocks = call(
        partial(powers, spans), [(grid, F32)] * len(spans), rate, us=1
    )
    block_power = dict(zip((1, 2, 3, 6), blocks))

    def plane_of(line, by_x, by_y, half):
        return [line, by_x, by_y, flip(by_y[:, :half], 2), flip(by_x[:, half:], 4)]

    near_w = flip(line_w, 2), flip(line_w, 4)
    far_w = plane_of(line_w, *near_w, 3)
    line_m = line_of(after(mine_m, line_w))
    near_m = flip(after(line_m, *near_w), 2), flip(after(line_m, *near_w), 4)
    far_m = plane_of(line_m, *near_m, 1)
    far_m[3:] = [value[:, 0] for value in far_m[3:]]

    local_state, local_moment = call(
        scan_in, [(grid, F32)] * 2, decay, after(signal, line_w, own_m, x_other, grad_out_other), us=8
    )
    start = states_around(after(local_state, *near_w), block_power, 1, 1)
    (context,) = call(scan_out, [((CTX,) + grid[1:], F32)], decay, gain, start, signal[:CTX], us=3)
    context = context.reshape(CTX, features).astype(BF16)
    context_other = flip(context, 1)
    rows = 2 * block_len
    slots = tp_count
    own_spec = whole((4, 6, cut, features))

    def slot_spec(*shape):
        return pl.BlockSpec(
            (1, *shape, features),
            lambda j, place: (jnp.maximum(j - 1, 0),) + (0,) * (len(shape) + 1),
        )

    weight_specs = [own_spec] + [slot_spec(6, cut)] * 3 + [slot_spec(3, cut)] * 2
    weights = (own_w, *far_w)
    full = whole((block_len, features))
    ctx_spec = whole((CTX, features))
    head = lambda n, width: pl.BlockSpec((n, width), lambda j, place: (0, j))
    lse_spec = pl.BlockSpec((1, rows, 1), lambda j, place: (j, 0, 0))
    q, k, v = timed(8)(
        project, place, (slots,),
        [full] * 2 + weight_specs,
        [head(rows, DH)] * 3,
        [like((rows, slots * DH))] * 3,
        (x, x_other, *weights),
        [pltpu.VMEM((3, DH, features), BF16)],
    )
    attended = timed(20)(
        attend, place, (slots,),
        [ctx_spec] * 2 + weight_specs + [head(rows, DH)] * 3,
        [full] * 2 + [head(2 * CTX, 2 * DH), head(rows, DH), lse_spec],
        [like((block_len, features), F32), like((block_len, features))]
        + [like((2 * CTX, slots * 2 * DH)), like((rows, slots * DH)), like((slots, rows, 1), F32)],
        (after(context, line_m), context_other, *weights, q, k, v),
        [
            pltpu.VMEM((3, DH, features), BF16),
            pltpu.VMEM((2, CTX + block_len, DH), BF16),
            pltpu.VMEM((2, CTX + block_len, DH), BF16),
            pltpu.VMEM((rows, features), F32),
        ],
    )
    part, part_other, state, mix, lse = attended
    group = 128
    steps = block_len // group
    row_spec = pl.BlockSpec((group, features), lambda i, place: (i, 0))
    seq_spec = pl.BlockSpec((1, group, features), lambda i, place: (place[1], i, 0))
    gain_spec = whole((1, features))
    mid_gain = feedforward_norm_gain.reshape(1, -1)
    residual, m = timed(4)(
        middle, place, (steps,),
        [seq_spec, row_spec, row_spec, gain_spec], [row_spec] * 2,
        [like((block_len, features), F32), like((block_len, features))],
        (tokens, part, after(flip(part_other, 1), *near_m), mid_gain),
    )
    m_other = flip(m, 1)

    chunk = 4 * wide
    def fixed(shape):
        return pl.BlockSpec(shape, lambda *_: (0,) * len(shape), pipeline_mode=pl.Buffered(1))

    def own_spec_of(count, first):
        return pl.BlockSpec((1, count, wide, features), lambda p, place: (p + first, 0, 0, 0))

    def feeding(first, count, far, far_specs, earlier):
        return timed(4 * count)(
            partial(feed_in, first), place, (count,),
            [full] * 2 + [own_spec_of(1, first)] + far_specs,
            [head(rows, chunk)] * 2,
            [like((rows, count * chunk))] * 2,
            (after(m, *earlier), m_other, own_m, *far),
            [pltpu.VMEM((chunk, features), BF16)],
        )

    act_a, slope_a = feeding(0, 3, far_m[:3], [fixed((3, 1, wide, features))] * 3, ())
    act_b, slope_b = feeding(3, 1, far_m[3:4], [fixed((3, wide, features))], (act_a,))
    early = pl.BlockSpec((rows, chunk), lambda p, place: (0, jnp.minimum(p, 2)))
    last = fixed((rows, chunk))
    mlp, mlp_other, mid, mid_other, pre = timed(21)(
        feed_out, place, (4,),
        [full] * 2 + [own_spec_of(2, 0)] + [fixed((3, 2, wide, features))] * 3
        + [fixed((3, wide, features))] * 2 + [early] * 2 + [last] * 2,
        [full] * 4 + [head(rows, chunk)],
        [like((block_len, features), F32), like((block_len, features))] * 2
        + [like((rows, 4 * chunk))],
        (grad_out, grad_out_other, own_m, *far_m, act_a, slope_a, act_b, slope_b),
        [pltpu.VMEM((chunk, features), BF16)] * 2 + [pltpu.VMEM((rows, features), F32)] * 2,
    )
    mid_got, mlp_got = flip(mid_other, 1), flip(mlp_other, 1)
    def hidden_grads(keeps, keep_at, rows_of, parts, part_specs):
        def spec(at):
            return pl.BlockSpec(
                (1, slots, wide, features), lambda p, place: (at(p), 0, 0, 0)
            )

        return timed(8)(
            partial(feed_weights, keeps), place, (4,),
            [full] * 2 + part_specs,
            [spec(keep_at), spec(lambda p: jnp.maximum(p - 2, 0))],
            [like((2, slots, wide, features))] * 2,
            (*rows_of, *map(far_away, parts)),
        )

    keep_r, send_r = hidden_grads(
        (0, 1), lambda p: jnp.minimum(p, 1), (grad_out, grad_out_other),
        (after(act_a, pre), act_b), [early, last],
    )
    mlp_got = after(mlp_got, keep_r)
    mid_got = after(mid_got, keep_r)
    (output,) = timed(3)(
        finish, place, (steps,),
        [row_spec] * 3, [row_spec], [like((block_len, features))], (residual, mlp, mlp_got),
    )
    output_all = lax.all_gather(output, "tp")
    resid, resid_b, sums_mid = timed(5)(
        middle_back, place, (steps,),
        [row_spec] * 3 + [seq_spec, gain_spec], [row_spec] * 2 + [gain_spec],
        [
            like((block_len, features), F32), like((block_len, features)),
            like((1, features), F32),
        ],
        (after(residual, output), mid, mid_got, cotangent, mid_gain),
    )
    resid_other = flip(resid_b, 1)
    keep_h, send_h = hidden_grads(
        (0, 2), lambda p: p // 2, (m, m_other), (after(pre, resid_b),), [head(rows, chunk)]
    )

    grad_in, grad_in_other, grad_ctx, grad_ctx_other, d, ds = timed(27)(
        attend_back, place, (slots,),
        [full] * 2 + weight_specs + [head(rows, DH)] * 3 + [head(2 * CTX, 2 * DH), lse_spec],
        [full] * 2 + [ctx_spec] * 2 + [head(rows, 3 * DH), head(2 * CTX, 2 * DH)],
        [
            like((block_len, features), F32), like((block_len, features)),
            like((CTX, features), F32), like((CTX, features)),
            like((rows, slots * 3 * DH)), like((2 * CTX, slots * 2 * DH)),
        ],
        (after(resid_b, keep_h), resid_other, *map(far_away, weights), q, k, v, state, lse),
        [
            pltpu.VMEM((6, DH, features), BF16),
            pltpu.VMEM((2, CTX + block_len, DH), BF16),
            pltpu.VMEM((2, CTX + block_len, DH), BF16),
            pltpu.VMEM((2, block_len, DH), BF16),
            pltpu.VMEM((2, CTX + block_len, DH), F32),
            pltpu.VMEM((2, CTX + block_len, DH), F32),
            pltpu.VMEM((rows, features), F32),
            pltpu.VMEM((2 * CTX, features), F32),
        ],
    )
    grad_ctx_got = flip(grad_ctx_other, 1)
    grad_in_got = flip(grad_in_other, 1)
    part_spec = pl.BlockSpec((2, 1, 3, cut, features), lambda j, place: (0, j, 0, 0, 0))
    keep_a, send_a, keep_b, send_b = timed(10)(
        attend_weights, place, (slots,),
        [full] * 2 + [ctx_spec] * 2 + [full] * 2
        + [head(rows, 3 * DH), head(2 * CTX, 2 * DH), head(rows, DH)],
        [part_spec] * 4,
        [like((2, slots, 3, cut, features))] * 4,
        (x, x_other, context, context_other, resid_b, resid_other, d, ds, mix),
    )

    got_r = flip(after(send_r, resid_b), 4)
    got_h = flip(after(send_h, resid_b), 2)
    near_h, away_h = add(keep_h[0], got_h[0]), add(keep_h[1], got_h[1])
    near_r, away_r = add(keep_r[0], got_r[0]), add(keep_r[1], got_r[1])
    grad_context = (grad_ctx + grad_ctx_got.astype(F32)).astype(BF16)
    grad_conv = tiles(after(grad_context, got_r, got_h))
    grad_later = tiles(shifted(grad_context, -1))
    (local_back,) = call(scan_back_in, [(grid, F32)], decay, grad_conv)
    late = tail_power * states_around(local_back, block_power, -1, 2, keep_a, away_h, away_r)
    grad_signal, end = call(
        scan_rows, [((block_len,) + grid[1:], F32), (grid, F32)], decay, gain, late, grad_later
    )
    grad_signal = grad_signal.reshape(block_len, features).astype(BF16)
    grad_tokens, sums_in = timed(5)(
        first_back, place, (steps,),
        [seq_spec] + [row_spec] * 4 + [gain_spec], [row_spec, gain_spec],
        [like((block_len, features)), like((1, features), F32)],
        (tokens, grad_in, grad_in_got, grad_signal, after(resid, output_all), attention_norm_gain.reshape(1, -1)),
    )

    lefts, rights = line_steps(grad_tokens)
    line = [grad_tokens] + [
        jnp.where(tp_index >= j, lefts[j], rights[slots - j]) for j in range(1, slots)
    ]
    line = jnp.stack(line)
    tokens_all = jnp.stack(
        [
            lax.dynamic_index_in_dim(line, (tp_index - b) % slots, 0, keepdims=False)
            for b in range(sequences)
        ]
    ).astype(F32)
    grad_gain, grad_moment = call(
        scan_sums, [(grid, F32)] * 2, decay, after(start, lefts[2], rights[2]), signal[:CTX], grad_conv
    )
    end_moment = block_len * block_power[1] * start + local_moment
    grad_rate = -gain * (grad_moment + end * end_moment)

    def regather(total):
        held = [total, flip(total, 2), flip(total, 4), flip(total, 6)]
        return held + [flip(value, 1) for value in held]

    ready = (late, grad_later)
    more_h, more_r = flip(after(away_h, *ready), 4), flip(after(away_r, *ready), 2)
    more_h, more_r = after(more_h, grad_tokens), after(more_r, grad_tokens)
    got_a = flip(after(send_a, more_h, more_r), 2)
    got_b = flip(after(send_b, more_h, more_r), 4)
    pairs = (near_h, more_h), (near_r, more_r)
    total_m = line_reduce(
        [jnp.stack([add(a[j], b[j]) for a, b in pairs]) for j in range(slots)],
        [(lefts[1], rights[1])] + [()] * (slots - 2),
    )
    near_a, away_a = add(keep_a[0], got_a[0]), add(keep_a[1], got_a[1])
    near_b, away_b = add(keep_b[0], got_b[0]), add(keep_b[1], got_b[1])
    pairs = (near_a, flip(away_a, 4)), (near_b, flip(away_b, 2))
    total_a = line_reduce(
        [jnp.stack([add(a[j], b[j]) for a, b in pairs]) for j in range(slots)],
        [()] * (slots - 2) + [(total_m,)],
    )
    pieces_m = regather(total_m)
    pieces_a = regather(total_a.reshape(6, cut, features))
    grad_hidden, grad_return = timed(5)(
        unpack_hidden, place, (1,),
        [whole((2, wide, features))] * 8,
        [whole((features, hidden_cols)), whole((hidden_cols, features))],
        [like((features, hidden_cols), F32), like((hidden_cols, features), F32)],
        pieces_m,
    )
    grad_q, grad_k, grad_v, grad_o, grad_sk, grad_sv = timed(5)(
        unpack_heads, place, (1,),
        [whole((6, cut, features))] * 8,
        [whole((features, 2 * DH))] * 3 + [whole((2 * DH, features))] + [whole((features, 2 * DH))] * 2,
        [like((features, 2 * DH), F32)] * 3
        + [like((2 * DH, features), F32)]
        + [like((features, 2 * DH), F32)] * 2,
        pieces_a,
        [pltpu.VMEM((2 * DH, features), F32)],
    )

    small = jnp.stack([grad_gain, grad_rate]).reshape(2, states, devices, channels)
    small = jnp.transpose(small, (2, 3, 0, 1)).reshape(devices, -1, 128)
    sums = jnp.concatenate([sums_in, sums_mid]).reshape(1, -1, 128)
    sums = jnp.broadcast_to(sums, (devices,) + sums.shape[1:])
    count = small.shape[1]
    small = jnp.sum(
        lax.all_to_all(
            after(jnp.concatenate([small, sums], axis=1), total_a), ("seq", "tp"), 0, 0
        ),
        axis=0,
    )
    kernel_grads = small[:count].reshape(channels, 2, states)
    gains = small[count:].reshape(2, features)

    return (
        output_all, tokens_all, gains[0], grad_q, grad_k, grad_v, grad_o, grad_sk, grad_sv,
        kernel_grads[:, 0], kernel_grads[:, 1], gains[1], grad_hidden, grad_return,
    )


def choose(tokens, *others):
    query_weight = others[2]
    fits = (
        lax.axis_size("seq") == 8
        and lax.axis_size("tp") == tokens.shape[0]
        and query_weight.shape[1] == 2 * DH
        and others[11].shape[1] % 1024 == 0
        and tokens.shape[1] % 512 == 0
        and tokens.shape[2] == 1024
    )
    return (fast_body if fits else body)(tokens, *others)


def solution(mesh):
    rows = P(None, "seq", None)
    columns = P(None, "tp")
    heads = P("tp", None)
    channels = P(("seq", "tp"), None)
    return jax.shard_map(
        choose,
        mesh=mesh,
        in_specs=(
            rows, P(), P(), columns, columns, columns, heads, columns, columns,
            channels, channels, P(), columns, heads, rows,
        ),
        out_specs=(
            rows, rows, P(), columns, columns, columns, heads, columns, columns,
            channels, channels, P(), columns, heads,
        ),
        check_vma=False,
    )
```

```python
from functools import partial
import math

import jax
import jax.numpy as jnp
from jax import lax
from jax.experimental import pallas as pl
from jax.experimental.pallas import tpu as pltpu
from jax.sharding import PartitionSpec as P

DH = 128
CTX = 128
EPS = 1e-05
NEGATIVE = -1e30
F32 = jnp.float32
BF16 = jnp.bfloat16


def normalize(values):
    center = values - jnp.mean(values, axis=-1, keepdims=True)
    inverse = lax.rsqrt(jnp.mean(center * center, axis=-1, keepdims=True) + EPS)
    return (center * inverse, inverse)


def norm_back(normed, inverse, grad_normed):
    mean_grad = jnp.mean(grad_normed, axis=-1, keepdims=True)
    mean_cross = jnp.mean(grad_normed * normed, axis=-1, keepdims=True)
    return inverse * (grad_normed - mean_grad - normed * mean_cross)


def flip(value, mask):
    count = lax.axis_size("seq")
    return lax.ppermute(value, "seq", [(i, i ^ mask) for i in range(count)])


def shifted(value, steps):
    count = lax.axis_size("seq")
    first, last = (max(0, -steps), min(count, count - steps))
    return lax.ppermute(value, "seq", [(i, i + steps) for i in range(first, last)])


def line_steps(value):
    count = lax.axis_size("tp")
    lefts, rights = [value], [value]
    for k in range(1, count):
        lefts.append(lax.ppermute(lefts[-1], "tp", [(i, i + 1) for i in range(k - 1, count - 1)]))
        rights.append(
            lax.ppermute(rights[-1], "tp", [(i, i - 1) for i in range(1, count - k + 1)])
        )
    return lefts, rights


def line_gather(value):
    count = lax.axis_size("tp")
    place = lax.axis_index("tp")
    lefts, rights = line_steps(value)
    return [value] + [
        jnp.where(place >= j, lefts[j], rights[count - j]) for j in range(1, count)
    ]


def line_reduce(chunks, pace=None):
    count = lax.axis_size("tp")

    def add(a, b, k):
        if pace:
            a = lax.optimization_barrier((a, *pace[k - 1]))[0]
        return a if b is None else (a.astype(F32) + b.astype(F32)).astype(BF16)

    going, coming = None, None
    for k in range(1, count):
        going = lax.ppermute(add(chunks[k], going, k), "tp", [(i, i + 1) for i in range(k)])
        coming = lax.ppermute(
            add(chunks[count - k], coming, k), "tp", [(i, i - 1) for i in range(count - k, count)]
        )
    return (chunks[0].astype(F32) + going.astype(F32) + coming.astype(F32)).astype(BF16)


def plane_bits(reverse):
    count = lax.axis_size("seq") // 2
    bits = [1 << b for b in range(count.bit_length() - 1)]
    return bits[::-1] if reverse else bits


def plane_gather(value, reverse):
    held = {0: value}
    for bit in plane_bits(reverse):
        held.update({p | bit: flip(v, 2 * bit) for p, v in list(held.items())})
    return held


def plane_reduce(pieces, reverse):
    held = dict(pieces)
    for bit in plane_bits(reverse):
        for p in [p for p in held if p & bit]:
            got = flip(held.pop(p), 2 * bit)
            held[p ^ bit] = (held[p ^ bit].astype(F32) + got.astype(F32)).astype(BF16)
    return held[0]


def scan_in(decay_ref, u_ref, state_ref, moment_ref):
    decay = decay_ref[...]

    def step(t, carry):
        h, m = carry
        return decay * h + u_ref[t], decay * (m + h)

    zero = jnp.zeros(decay.shape, F32)
    h, m = lax.fori_loop(0, u_ref.shape[0], step, (zero, zero))
    state_ref[...] = h
    moment_ref[...] = m


def scan_out(decay_ref, gain_ref, start_ref, u_ref, y_ref):
    decay, gain = decay_ref[...], gain_ref[...]

    def step(t, h):
        h = decay * h + u_ref[t]
        y_ref[t] = jnp.sum(gain * h, axis=0)
        return h

    lax.fori_loop(0, u_ref.shape[0], step, start_ref[...])


def scan_back_in(decay_ref, g_ref, state_ref):
    decay = decay_ref[...]
    last = g_ref.shape[0] - 1

    def step(t, lam):
        return decay * (lam + g_ref[last - t])

    state_ref[...] = lax.fori_loop(0, last + 1, step, jnp.zeros(decay.shape, F32))


def scan_back_out(decay_ref, gain_ref, end_ref, start_ref, u_ref, g_ref, y_ref, gh_ref, gm_ref):
    decay, gain = decay_ref[...], gain_ref[...]
    rows, count = y_ref.shape[0], g_ref.shape[0]

    def empty(t, lam):
        y_ref[rows - 1 - t] = jnp.sum(gain * lam, axis=0)
        return decay * lam

    def full(t, lam):
        lam = lam + g_ref[count - 1 - t]
        y_ref[count - 1 - t] = jnp.sum(gain * lam, axis=0)
        return decay * lam

    lam = lax.fori_loop(0, rows - count, empty, end_ref[...])
    lax.fori_loop(0, count, full, lam)

    def again(t, carry):
        h, m, gh, gm = carry
        h, m = decay * h + u_ref[t], decay * (m + h)
        g = g_ref[t]
        return h, m, gh + g * h, gm + g * m

    zero = jnp.zeros(decay.shape, F32)
    _, _, gh, gm = lax.fori_loop(0, count, again, (start_ref[...], zero, zero, zero))
    gh_ref[...] = gh
    gm_ref[...] = gm


def call(kernel, outs, *operands, us=5):
    return pl.pallas_call(
        kernel,
        out_shape=[jax.ShapeDtypeStruct(shape, dtype) for shape, dtype in outs],
        compiler_params=pltpu.CompilerParams(vmem_limit_bytes=42 * 2**20),
        cost_estimate=pl.CostEstimate(flops=int(us * 1.1e9), bytes_accessed=0, transcendentals=0),
    )(*operands)


def tiles(values):
    return values.astype(F32).reshape(values.shape[0], values.shape[1] // 128, 128)


def dot(a, b, dims):
    return lax.dot_general(a, b, (dims, ((), ())), preferred_element_type=F32)


NN = ((1,), (0,))
NT = ((1,), (1,))
TN = ((0,), (0,))


def body(
    tokens,
    lengths,
    attention_norm_gain,
    query_weight,
    key_weight,
    value_weight,
    output_weight,
    state_key_weight,
    state_value_weight,
    state_coefficient,
    state_rate,
    feedforward_norm_gain,
    hidden_weight,
    return_weight,
    cotangent,
):
    sequences, block_len, features = tokens.shape
    seq_count = lax.axis_size("seq")
    tp_count = lax.axis_size("tp")
    seq_index = lax.axis_index("seq")
    tp_index = lax.axis_index("tp")
    planes = seq_count // 2
    copies = tp_count // sequences
    sequence = tp_index // copies
    head_cols = query_weight.shape[1]
    hidden_cols = hidden_weight.shape[1]
    heads = head_cols * tp_count // DH
    head_rows = head_cols // seq_count
    hidden_rows = hidden_cols // seq_count
    scale = DH ** (-0.5)

    shard_a = [query_weight.T, key_weight.T, value_weight.T]
    shard_b = [state_key_weight.T, state_value_weight.T, output_weight]
    shard_m = [hidden_weight.T, return_weight]

    def head_slice(shard, relative):
        other = seq_index ^ relative
        at = (other & 1) * planes + (other >> 1)
        return lax.dynamic_slice_in_dim(shard, at * head_rows, head_rows, 0)

    def hidden_slice(shard, relative):
        return lax.dynamic_slice_in_dim(
            shard, (seq_index ^ relative) * hidden_rows, hidden_rows, 0
        )

    def gather_heads(shards, reverse):
        mine = jnp.stack([head_slice(w, 0) for w in shards])
        line = jnp.stack(line_gather(mine)[1:])
        plane = plane_gather(line, reverse)
        other = {p: flip(v, 1) for p, v in plane.items()}
        far = jnp.stack(
            [jnp.stack([group[p] for p in range(planes)]) for group in (plane, other)]
        )
        far = jnp.transpose(far, (3, 2, 0, 1, 4, 5))
        own = jnp.stack(
            [
                jnp.concatenate([head_slice(w, 2 * p + c) for c in range(2) for p in range(planes)])
                for w in shards
            ]
        )
        far = far.reshape(len(shards), (tp_count - 1) * head_cols, features)
        return jnp.concatenate([own, far], axis=1)

    def gather_hidden(shard, reverse):
        line = line_gather(hidden_slice(shard, 0))
        plane = plane_gather(jnp.concatenate(line[1:]), reverse)
        return jnp.concatenate(
            [
                piece
                for p in range(planes)
                for piece in (hidden_slice(shard, 2 * p), plane[p])
            ]
        )

    wq, wk, wv = gather_heads(shard_a, False)
    wsk, wsv, wo = gather_heads(shard_b, True)
    wh = gather_hidden(shard_m[0], False)
    wr = gather_hidden(shard_m[1], True)

    own_tokens = lax.dynamic_index_in_dim(tokens, sequence, 0, keepdims=False)
    own_cot = lax.dynamic_index_in_dim(cotangent, sequence, 0, keepdims=False)
    length = lax.dynamic_index_in_dim(lengths, sequence, 0, keepdims=False)
    before = shifted(own_tokens[block_len - CTX :], 1)
    positions = seq_index * block_len - CTX + jnp.arange(block_len + CTX)
    live = ((positions < length) & (positions >= 0)).astype(F32)[:, None]
    valid = live[CTX:]
    inputs = own_tokens.astype(F32)
    normed_in, inverse_in = normalize(inputs)
    attn_input = (normed_in * attention_norm_gain).astype(BF16)
    early = (normalize(before.astype(F32))[0] * attention_norm_gain).astype(BF16)
    window = jnp.concatenate([early, attn_input[: block_len - CTX]]).astype(F32) * live[:block_len]
    signal = tiles(window)

    both = jnp.stack([state_rate, state_coefficient])
    both = lax.all_gather(both, ("seq", "tp"), axis=1, tiled=True)
    states = both.shape[2]
    both = jnp.transpose(both, (0, 2, 1)).reshape(2, states, features // 128, 128)
    rate, gain = both[0], both[1]
    decay = jnp.exp(-rate)
    grid = rate.shape
    local_state, local_moment = call(scan_in, [(grid, F32)] * 2, decay, signal)
    start = 0.0
    for m in range(1, seq_count):
        start = start + jnp.exp(-rate * (block_len * (m - 1))) * shifted(local_state, m)
    (context,) = call(
        scan_out, [((CTX,) + grid[1:], F32)], decay, gain, start, signal[:CTX]
    )
    context = context.reshape(CTX, features).astype(BF16)

    queries = dot(attn_input, wq, NT).astype(BF16)
    token_keys = dot(attn_input, wk, NT).astype(BF16)
    token_values = dot(attn_input, wv, NT).astype(BF16)
    state_keys = dot(context, wsk, NT).astype(BF16)
    state_values = dot(context, wsv, NT).astype(BF16)
    query_heads = queries.reshape(block_len, heads, DH)
    key_heads = jnp.concatenate([token_keys, state_keys]).reshape(-1, heads, DH)
    value_heads = jnp.concatenate([token_values, state_values]).reshape(-1, heads, DH)
    causal = jnp.arange(block_len)[:, None] >= jnp.arange(block_len)[None, :]
    allowed = jnp.concatenate([causal, jnp.broadcast_to(seq_index > 0, (block_len, CTX))], axis=1)
    raw = jnp.einsum("qhd,khd->hqk", query_heads, key_heads, preferred_element_type=F32) * scale
    scores = jnp.where(allowed, raw, NEGATIVE)
    row_max = jnp.max(scores, axis=-1, keepdims=True)
    exp_scores = jnp.exp(scores - row_max)
    row_total = jnp.sum(exp_scores, axis=-1, keepdims=True)
    probs_full = exp_scores / row_total
    attn_probs = probs_full.astype(BF16)
    head_mix = jnp.einsum("hqk,khd->qhd", attn_probs, value_heads, preferred_element_type=F32)
    head_mix = head_mix.reshape(block_len, heads * DH).astype(BF16)
    residual = inputs + dot(head_mix, wo, NN)
    normed_mid, inverse_mid = normalize(residual)
    mlp_input = (normed_mid * feedforward_norm_gain).astype(BF16)

    grad_out = own_cot.astype(F32) * valid
    grad_out_b = grad_out.astype(BF16)
    mlp_rows = jnp.concatenate([mlp_input, flip(mlp_input, 1)])
    out_rows = jnp.concatenate([grad_out_b, flip(grad_out_b, 1)])
    pre_act = dot(mlp_rows, wh, NT)
    activated, gelu_back = jax.vjp(partial(jax.nn.gelu, approximate=False), pre_act)
    activated = activated.astype(BF16)
    mlp_part = dot(activated, wr, NN)
    grad_act = dot(out_rows, wr, NT)
    grad_pre = gelu_back(grad_act)[0].astype(BF16)
    mid_part = dot(grad_pre, wh, NN)
    grad_mid = mid_part[:block_len] + flip(mid_part[block_len:].astype(BF16), 1).astype(F32)
    mlp_out = mlp_part[:block_len] + flip(mlp_part[block_len:].astype(BF16), 1).astype(F32)
    output = ((residual + mlp_out) * valid).astype(BF16)
    output_line = line_gather(output)
    grad_return = dot(activated, out_rows, TN).astype(BF16)
    grad_hidden = dot(grad_pre, mlp_rows, TN).astype(BF16)

    def reduce_hidden(grad, reverse):
        grad = grad.reshape(planes, tp_count * hidden_rows, features)
        mine = plane_reduce({p: grad[p] for p in range(planes)}, reverse)
        mine = mine.reshape(tp_count, hidden_rows, features)
        return line_reduce([mine[j] for j in range(tp_count)])

    sum_hidden = reduce_hidden(grad_hidden, False)
    sum_return = reduce_hidden(grad_return, True)

    grad_mlp_gain = jnp.sum(grad_mid * normed_mid, axis=0)
    grad_resid = grad_out + norm_back(normed_mid, inverse_mid, grad_mid * feedforward_norm_gain)
    grad_resid_b = grad_resid.astype(BF16)
    grad_heads = dot(grad_resid_b, wo, NT).astype(BF16).reshape(block_len, heads, DH)
    grad_probs = jnp.einsum("qhd,khd->hqk", grad_heads, value_heads, preferred_element_type=F32)
    delta = jnp.sum(probs_full * grad_probs, axis=-1, keepdims=True)
    grad_scores = (probs_full * (grad_probs - delta)).astype(BF16)
    grad_queries = (
        jnp.einsum("hqk,khd->qhd", grad_scores, key_heads, preferred_element_type=F32) * scale
    )
    grad_keys_all = (
        jnp.einsum("hqk,qhd->khd", grad_scores, query_heads, preferred_element_type=F32) * scale
    )
    grad_values_all = jnp.einsum(
        "hqk,qhd->khd", attn_probs, grad_heads, preferred_element_type=F32
    )
    wide = heads * DH
    grad_queries = grad_queries.reshape(block_len, wide).astype(BF16)
    grad_keys_all = grad_keys_all.reshape(block_len + CTX, wide).astype(BF16)
    grad_values_all = grad_values_all.reshape(block_len + CTX, wide).astype(BF16)
    grad_token_keys, grad_state_keys = grad_keys_all[:block_len], grad_keys_all[block_len:]
    grad_token_values, grad_state_values = grad_values_all[:block_len], grad_values_all[block_len:]
    grad_context = (
        dot(grad_state_keys, wsk, NN) + dot(grad_state_values, wsv, NN)
    ).astype(BF16)

    grad_conv = tiles(grad_context)
    (local_back,) = call(scan_back_in, [(grid, F32)], decay, grad_conv)
    end = 0.0
    for m in range(1, seq_count):
        end = end + jnp.exp(-rate * (block_len * (m - 1))) * shifted(local_back, -m)
    grad_signal, grad_gain, grad_moment = call(
        scan_back_out,
        [((block_len,) + grid[1:], F32), (grid, F32), (grid, F32)],
        decay,
        gain,
        end,
        start,
        signal[:CTX],
        grad_conv,
    )
    end_moment = block_len * jnp.exp(-rate * block_len) * start + local_moment
    grad_rate = -gain * (grad_moment + end * end_moment)
    grad_signal = grad_signal.reshape(block_len, features).astype(BF16)
    grad_signal = jnp.concatenate([grad_signal[CTX:], shifted(grad_signal[:CTX], -1)])

    grad_in = (
        dot(grad_queries, wq, NN)
        + dot(grad_token_keys, wk, NN)
        + dot(grad_token_values, wv, NN)
        + grad_signal.astype(F32) * valid
    )
    grad_attn_gain = jnp.sum(grad_in * normed_in, axis=0)
    grad_tokens = grad_resid + norm_back(normed_in, inverse_in, grad_in * attention_norm_gain)
    tokens_line = line_gather(grad_tokens.astype(BF16))

    def split(values):
        return values.reshape(values.shape[0], tp_count, 2, head_cols // 2)

    def both_rows(values):
        values = split(values)
        mine, other = values[:, :, 0], values[:, :, 1]
        joined = jnp.concatenate([mine, flip(other, 1)])
        return joined.reshape(joined.shape[0], -1)

    def both_full(values):
        return jnp.concatenate([values, flip(values, 1)])

    x_rows, c_rows, r_rows = both_full(attn_input), both_full(context), both_full(grad_resid_b)
    grads_a = [
        dot(both_rows(grad_queries), x_rows, TN),
        dot(both_rows(grad_token_keys), x_rows, TN),
        dot(both_rows(grad_token_values), x_rows, TN),
    ]
    grads_b = [
        dot(both_rows(grad_state_keys), c_rows, TN),
        dot(both_rows(grad_state_values), c_rows, TN),
        dot(both_rows(head_mix), r_rows, TN),
    ]

    def reduce_heads(grads, reverse):
        stack = jnp.stack([g.astype(BF16) for g in grads]).reshape(
            len(grads), tp_count, planes, head_rows, features
        )
        mine = plane_reduce(
            {p: jnp.transpose(stack[:, :, p], (1, 0, 2, 3)) for p in range(planes)}, reverse
        )
        return line_reduce([mine[j] for j in range(tp_count)])

    sum_a = reduce_heads(grads_a, False)
    sum_b = reduce_heads(grads_b, True)

    def spread(value, reverse):
        plane = plane_gather(value, reverse)
        other = {p: flip(v, 1) for p, v in plane.items()}
        return jnp.stack([(plane, other)[i & 1][i >> 1] for i in range(seq_count)])

    def ordered(stack):
        return [
            lax.dynamic_index_in_dim(stack, seq_index ^ i, 0, keepdims=False)
            for i in range(seq_count)
        ]

    fix = 1.0 / copies

    def head_grads(value, reverse):
        parts = ordered(spread(value, reverse))
        parts = [parts[2 * p + c] for c in range(2) for p in range(planes)]
        return jnp.concatenate(parts, axis=1).astype(F32) * fix

    def hidden_grads(value, reverse):
        return jnp.concatenate(ordered(spread(value, reverse))).astype(F32) * fix

    full_a = head_grads(sum_a, False)
    full_b = head_grads(sum_b, True)
    full_hidden = hidden_grads(sum_hidden, False)
    full_return = hidden_grads(sum_return, True)

    gains = lax.psum(jnp.stack([grad_attn_gain, grad_mlp_gain]), ("seq", "tp")) * fix
    kernel_grads = jnp.stack([grad_gain, grad_rate]).reshape(2, states, features)
    kernel_grads = lax.psum_scatter(
        jnp.transpose(kernel_grads, (2, 0, 1)).reshape(features, 2 * states),
        ("seq", "tp"),
        scatter_dimension=0,
        tiled=True,
    )
    kernel_grads = kernel_grads * fix

    def lined(line, dtype):
        stack = jnp.stack(line)
        return jnp.stack(
            [
                lax.dynamic_index_in_dim(
                    stack, (tp_index - b * copies) % tp_count, 0, keepdims=False
                )
                for b in range(sequences)
            ]
        ).astype(dtype)

    return (
        lined(output_line, BF16),
        lined(tokens_line, F32),
        gains[0],
        full_a[0].T,
        full_a[1].T,
        full_a[2].T,
        full_b[2],
        full_b[0].T,
        full_b[1].T,
        kernel_grads[:, :states],
        kernel_grads[:, states:],
        gains[1],
        full_hidden.T,
        full_return,
    )


LOG2E = math.log2(math.e)
SCALE = DH ** (-0.5)


def cost(us):
    return pl.CostEstimate(flops=int(us * 1.1e9), bytes_accessed=0, transcendentals=0)


def params(limit=50):
    return pltpu.CompilerParams(vmem_limit_bytes=limit * 2**20)


def like(shape, dtype=BF16):
    return jax.ShapeDtypeStruct(shape, dtype)


def whole(shape):
    return pl.BlockSpec(shape, lambda *_: (0,) * len(shape))


def launch(kernel, place, grid, in_specs, out_specs, outs, operands, scratch=(), us=5):
    return pl.pallas_call(
        kernel,
        grid_spec=pltpu.PrefetchScalarGridSpec(
            num_scalar_prefetch=1,
            grid=grid,
            in_specs=in_specs,
            out_specs=out_specs,
            scratch_shapes=list(scratch),
        ),
        out_shape=outs,
        compiler_params=params(),
        cost_estimate=cost(us),
    )(place, *operands)


def timed(us):
    return partial(launch, us=us)


def cycle(value, steps):
    count = lax.axis_size("tp")
    return lax.ppermute(value, "tp", [(i, (i + steps) % count) for i in range(count)])


def pack_heads(place, wq, wk, wv, wsk, wsv, wo, out, mine, turned):
    chip = place[0] >> 1
    rows = out.shape[2]
    for w, ref in enumerate((wq, wk, wv, wsk, wsv, wo)):
        turned[...] = ref[...].astype(F32) if ref is wo else ref[...].astype(F32).T
        for p in range(4):
            cut = pl.ds(pl.multiple_of((chip ^ p) * rows, rows), rows)
            out[p, w] = turned[cut, :].astype(BF16)
        mine[w] = out[0, w]


def pack_hidden(place, wh, wr, out, mine, turned):
    chip = place[0] >> 1
    rows = out.shape[2]
    for w, ref in enumerate((wh, wr)):
        turned[...] = ref[...].astype(F32).T if ref is wh else ref[...].astype(F32)
        for p in range(4):
            cut = pl.ds(pl.multiple_of((chip ^ p) * rows, rows), rows)
            out[p, w] = turned[cut, :].astype(BF16)
        mine[w] = out[0, w]


def load_heads(j, own, far, into, first, count):
    rows = own.shape[2]

    @pl.when(j == 0)
    def _():
        for p in range(4):
            for w in range(count):
                into[w, p * rows : (p + 1) * rows] = own[p, first + w]

    @pl.when(j > 0)
    def _():
        for p in range(4):
            for w in range(count):
                if p < 3:
                    into[w, p * rows : (p + 1) * rows] = far[p][0, first + w]
                else:
                    into[w, p * rows : (p + 1) * rows] = far[3 + (first + w) // 3][0, (first + w) % 3]


def masked(raw, r, block):
    n = raw.shape[1]
    column = lax.broadcasted_iota(jnp.int32, raw.shape, 1)
    row = lax.broadcasted_iota(jnp.int32, raw.shape, 0)
    keep = (column - (n - 128) <= row) & ((column >= CTX) | (block > 0))
    return jnp.where(keep, raw * (SCALE * LOG2E), NEGATIVE)


def project(place, x0, x1, own, f0, f1, f2, f3, f4, q_ref, k_ref, v_ref, weight):
    j = pl.program_id(0)
    load_heads(j, own, (f0, f1, f2, f3, f4), weight, 0, 3)
    rows = x0.shape[0]
    qkv_w = weight[0:3].reshape(3 * DH, -1)
    for half, x in enumerate((x0, x1)):
        saved = slice(half * rows, (half + 1) * rows)
        qkv = dot(x[...], qkv_w, NT).astype(BF16)
        q_ref[saved] = qkv[:, :DH]
        k_ref[saved] = qkv[:, DH : 2 * DH]
        v_ref[saved] = qkv[:, 2 * DH :]


def attend(place, c0, c1, own, f0, f1, f2, f3, f4, q_ref, k_ref, v_ref,
           part0, part1, s_ref, o_ref, lse_ref, weight, keys, values, total):
    j = pl.program_id(0)
    load_heads(j, own, (f0, f1, f2, f3, f4), weight, 3, 3)
    rows = part0.shape[0]

    @pl.when(j == 0)
    def _():
        total[...] = jnp.zeros_like(total)

    st_w = weight[0:2].reshape(2 * DH, -1)
    for half, c in enumerate((c0, c1)):
        base = half * rows
        state = dot(c[...], st_w, NT).astype(BF16)
        s_ref[half * CTX : (half + 1) * CTX] = state
        keys[half, 0:CTX] = state[:, :DH]
        values[half, 0:CTX] = state[:, DH:]
        keys[half, CTX:] = k_ref[base : base + rows]
        values[half, CTX:] = v_ref[base : base + rows]
    for half in range(2):
        block = place[0] ^ half
        base = half * rows
        for r in range(rows // 128):
            saved = slice(base + r * 128, base + (r + 1) * 128)
            n = CTX + (r + 1) * 128
            scores = masked(dot(q_ref[saved], keys[half, 0:n], NT), r, block)
            top = jnp.max(scores, axis=1, keepdims=True)
            power = jnp.exp2(scores - top)
            summed = jnp.sum(power, axis=1, keepdims=True)
            lse_ref[0, saved] = top + jnp.log2(summed)
            probs = (power * (1.0 / summed)).astype(BF16)
            o_ref[saved] = dot(probs, values[half, 0:n], NN).astype(BF16)
    for half in range(2):
        base = half * rows
        total[base : base + rows] += dot(o_ref[base : base + rows], weight[2], NN)

    @pl.when(j == pl.num_programs(0) - 1)
    def _():
        part0[...] = total[0:rows].astype(part0.dtype)
        part1[...] = total[rows:].astype(part1.dtype)


def attend_back(place, g0, g1, own, f0, f1, f2, f3, f4,
                q_ref, k_ref, v_ref, s_ref, lse_ref,
                in0, in1, ctx0, ctx1, d_ref, ds_ref,
                weight, keys, values, heads, grad_k, grad_v, total, ctx_total):
    j = pl.program_id(0)
    load_heads(j, own, (f0, f1, f2, f3, f4), weight, 0, 6)
    rows = g0.shape[0]

    @pl.when(j == 0)
    def _():
        total[...] = jnp.zeros_like(total)
        ctx_total[...] = jnp.zeros_like(ctx_total)

    qkv_w = weight[0:3].reshape(3 * DH, -1)
    st_w = weight[3:5].reshape(2 * DH, -1)
    for half, g in enumerate((g0, g1)):
        base = half * rows
        keys[half, 0:CTX] = s_ref[half * CTX : (half + 1) * CTX, :DH]
        values[half, 0:CTX] = s_ref[half * CTX : (half + 1) * CTX, DH:]
        keys[half, CTX:] = k_ref[base : base + rows]
        values[half, CTX:] = v_ref[base : base + rows]
        heads[half] = dot(g[...], weight[5], NT).astype(BF16)
    for half in range(2):
        block = place[0] ^ half
        base = half * rows
        for r in reversed(range(rows // 128)):
            saved = slice(base + r * 128, base + (r + 1) * 128)
            n = CTX + (r + 1) * 128
            q = q_ref[saved]
            own = heads[half, r * 128 : (r + 1) * 128]
            probs = jnp.exp2(masked(dot(q, keys[half, 0:n], NT), r, block) - lse_ref[0, saved])
            grad = dot(own, values[half, 0:n], NT)
            delta = jnp.sum(probs * grad, axis=1, keepdims=True)
            scores = (probs * (grad - delta)).astype(BF16)
            d_ref[saved, 0:DH] = (dot(scores, keys[half, 0:n], NN) * SCALE).astype(BF16)
            to_k = dot(scores, q, TN)
            to_v = dot(probs.astype(BF16), own, TN)
            if r == rows // 128 - 1:
                grad_k[half, 0:n] = to_k
                grad_v[half, 0:n] = to_v
            else:
                grad_k[half, 0:n] += to_k
                grad_v[half, 0:n] += to_v
    for half in range(2):
        base = half * rows
        d_ref[base : base + rows, DH : 2 * DH] = (grad_k[half, CTX:] * SCALE).astype(BF16)
        d_ref[base : base + rows, 2 * DH :] = grad_v[half, CTX:].astype(BF16)
        state = slice(half * CTX, (half + 1) * CTX)
        ds_ref[state, :DH] = (grad_k[half, 0:CTX] * SCALE).astype(BF16)
        ds_ref[state, DH:] = grad_v[half, 0:CTX].astype(BF16)
        ctx_total[state] += dot(ds_ref[state], st_w, NN)
        total[base : base + rows] += dot(d_ref[base : base + rows], qkv_w, NN)

    @pl.when(j == pl.num_programs(0) - 1)
    def _():
        in0[...] = total[0:rows].astype(in0.dtype)
        in1[...] = total[rows:].astype(in1.dtype)
        ctx0[...] = ctx_total[0:CTX].astype(ctx0.dtype)
        ctx1[...] = ctx_total[CTX:].astype(ctx1.dtype)


def attend_weights(place, x0, x1, c0, c1, g0, g1, d_ref, ds_ref, o_ref, keep_a, send_a, keep_b, send_b):
    rows = x0.shape[0]
    cut = keep_a.shape[3]
    to_qkv = (dot(d_ref[0:rows], x0[...], TN) + dot(d_ref[rows:], x1[...], TN)).astype(BF16)
    to_state = (dot(ds_ref[0:CTX], c0[...], TN) + dot(ds_ref[CTX:], c1[...], TN)).astype(BF16)
    to_out = (dot(o_ref[0:rows], g0[...], TN) + dot(o_ref[rows:], g1[...], TN)).astype(BF16)
    spots_a = {0: (keep_a, 0), 2: (keep_a, 1), 1: (send_a, 0), 3: (send_a, 1)}
    spots_b = {0: (keep_b, 0), 1: (keep_b, 1), 2: (send_b, 0), 3: (send_b, 1)}
    for p in range(4):
        out, at = spots_a[p]
        for w in range(3):
            out[at, 0, w] = to_qkv[w * DH + p * cut : w * DH + (p + 1) * cut]
        out, at = spots_b[p]
        for w in range(2):
            out[at, 0, w] = to_state[w * DH + p * cut : w * DH + (p + 1) * cut]
        out[at, 0, 2] = to_out[p * cut : (p + 1) * cut]


def gelu_parts(x):
    size = jnp.abs(x) * math.sqrt(0.5)
    bell = jnp.exp2(x * x * (-0.5 * LOG2E))
    t = 1.0 / (1.0 + 0.3275911 * size)
    poly = 1.061405429 * t - 1.453152027
    poly = poly * t + 1.421413741
    poly = poly * t - 0.284496736
    poly = poly * t + 0.254829592
    tail = 0.5 * poly * t * bell
    return jnp.where(x >= 0, 1.0 - tail, tail), bell * (1.0 / math.sqrt(2.0 * math.pi))


def load_hidden(p, w, own, far, first, into):
    rows = into.shape[0] // 4
    into[0:rows] = own[0, w]
    for i, piece in enumerate(far):
        @pl.when(p == first + i)
        def _():
            for slot in range(3):
                held = piece[slot, w] if len(piece.shape) == 4 else piece[slot]
                into[(1 + slot) * rows : (2 + slot) * rows] = held


def feed_in(first, place, m0, m1, own, *rest):
    *far, act_ref, slope_ref, wh = rest
    load_hidden(pl.program_id(0) + first, 0, own, far, first, wh)
    rows = m0.shape[0]
    for half, m in enumerate((m0, m1)):
        saved = slice(half * rows, (half + 1) * rows)
        pre = dot(m[...], wh[...], NT)
        part, bell = gelu_parts(pre)
        act_ref[saved] = (pre * part).astype(BF16)
        slope_ref[saved] = (part + pre * bell).astype(BF16)


def feed_out(place, g0, g1, own, f0, f1, f2, h3, r3, act_a, slope_a, act_b, slope_b,
             mlp0, mlp1, mid0, mid1, pre_ref, wh, wr, mlp, mid):
    p = pl.program_id(0)
    load_hidden(p, 0, own, (f0, f1, f2, h3), 0, wh)
    load_hidden(p, 1, own, (f0, f1, f2, r3), 0, wr)
    rows = g0.shape[0]

    @pl.when(p == 0)
    def _():
        mlp[...] = jnp.zeros_like(mlp)
        mid[...] = jnp.zeros_like(mid)

    def step(act, slope):
        for half, g in enumerate((g0, g1)):
            saved = slice(half * rows, (half + 1) * rows)
            back = dot(g[...], wr[...], NT)
            pre_ref[saved] = (back * slope[saved].astype(F32)).astype(BF16)
            mlp[saved] += dot(act[saved], wr[...], NN)
            mid[saved] += dot(pre_ref[saved], wh[...], NN)

    @pl.when(p < 3)
    def _():
        step(act_a, slope_a)

    @pl.when(p == 3)
    def _():
        step(act_b, slope_b)

    @pl.when(p == 3)
    def _():
        mlp0[...] = mlp[0:rows].astype(mlp0.dtype)
        mlp1[...] = mlp[rows:].astype(mlp1.dtype)
        mid0[...] = mid[0:rows].astype(mid0.dtype)
        mid1[...] = mid[rows:].astype(mid1.dtype)


def feed_weights(keeps, place, a0, a1, *rest):
    *parts, keep, send = rest
    p = pl.program_id(0)
    rows = a0.shape[0]
    cut = keep.shape[2]

    def step(b, out):
        grad = (dot(b[0:rows], a0[...], TN) + dot(b[rows:], a1[...], TN)).astype(BF16)
        for slot in range(4):
            out[0, slot] = grad[slot * cut : (slot + 1) * cut]

    for i in range(4):
        @pl.when(p == i)
        def _():
            step(parts[-1] if i == 3 else parts[0], keep if i in keeps else send)


def live_rows(place, count):
    at = place[0] * (count * pl.num_programs(0)) + pl.program_id(0) * count
    position = at + lax.broadcasted_iota(jnp.int32, (count, 1), 0)
    return (position < place[2]).astype(F32)


def middle(place, tokens, own, got, gain, residual, m_ref):
    value = tokens[0].astype(F32) + own[...] + got[...].astype(F32)
    residual[...] = value
    m_ref[...] = (normalize(value)[0] * gain[...]).astype(BF16)


def finish(place, residual, own, got, out):
    value = residual[...] + own[...] + got[...].astype(F32)
    out[...] = (value * live_rows(place, value.shape[0])).astype(BF16)


def middle_back(place, residual, own, got, cot, gain, grad, grad_b, sums):
    value = residual[...]
    normed, inverse = normalize(value)
    valid = live_rows(place, value.shape[0])
    back = own[...] + got[...].astype(F32)
    total = jnp.sum(back * normed, axis=0, keepdims=True)

    @pl.when(pl.program_id(0) == 0)
    def _():
        sums[...] = total

    @pl.when(pl.program_id(0) > 0)
    def _():
        sums[...] += total

    value = cot[0].astype(F32) * valid + norm_back(normed, inverse, back * gain[...])
    grad[...] = value
    grad_b[...] = value.astype(BF16)


def first_back(place, tokens, own, got, signal, grad, gain, out, sums):
    normed, inverse = normalize(tokens[0].astype(F32))
    valid = live_rows(place, out.shape[0])
    back = own[...] + got[...].astype(F32) + signal[...].astype(F32) * valid
    total = jnp.sum(back * normed, axis=0, keepdims=True)

    @pl.when(pl.program_id(0) == 0)
    def _():
        sums[...] = total

    @pl.when(pl.program_id(0) > 0)
    def _():
        sums[...] += total

    out[...] = (grad[...] + norm_back(normed, inverse, back * gain[...])).astype(BF16)


def unpack_heads(place, n0, n1, n2, n3, f0, f1, f2, f3, q, k, v, o, sk, sv, rows_ref):
    core, chip = place[0] & 1, place[0] >> 1
    cut = n0.shape[1]
    for w, out in ((0, q), (1, k), (2, v), (3, sk), (4, sv), (5, o)):
        for other, pieces in ((0, (n0, n1, n2, n3)), (1, (f0, f1, f2, f3))):
            for p, piece in enumerate(pieces):
                at = (core ^ other) * DH + (chip ^ p) * cut
                rows_ref[pl.ds(pl.multiple_of(at, cut), cut), :] = piece[w].astype(F32)
        out[...] = rows_ref[...] if out is o else rows_ref[...].T


def unpack_hidden(place, n0, n1, n2, n3, f0, f1, f2, f3, h, r):
    core, chip = place[0] & 1, place[0] >> 1
    cut = n0.shape[1]
    for other, pieces in ((0, (n0, n1, n2, n3)), (1, (f0, f1, f2, f3))):
        for p, piece in enumerate(pieces):
            at = pl.multiple_of((core ^ other) * 4 * cut + (chip ^ p) * cut, cut)
            r[pl.ds(at, cut), :] = piece[1].astype(F32)
            h[:, pl.ds(at, cut)] = piece[0].astype(F32).T


def far_away(value):
    return pltpu.with_memory_space_constraint(value, pltpu.HBM)


def add(a, b):
    return (a.astype(F32) + b.astype(F32)).astype(BF16)


def after(value, *earlier):
    return lax.optimization_barrier((value, *earlier))[0]


def powers(lengths, rate_ref, *outs):
    for length, out in zip(lengths, outs):
        out[...] = jnp.exp(-rate_ref[...] * float(length))


def states_around(local, power, sign, first, *earlier):
    group = local
    for m in (1, 2):
        group = group + power[m] * shifted(local, sign * m)
    group = after(group, *earlier)
    total = shifted(group, sign * first)
    for m in range(first + 3, 8, 3):
        total = total + power[m - first] * shifted(group, sign * m)
    return total


def scan_rows(decay_ref, gain_ref, late_ref, g_ref, y_ref, end_ref):
    decay, gain = decay_ref[...], gain_ref[...]
    rows, count = y_ref.shape[0], g_ref.shape[0]

    def full(t, lam):
        lam = lam + g_ref[count - 1 - t]
        y_ref[rows - 1 - t] = jnp.sum(gain * lam, axis=0)
        return decay * lam

    def empty(t, lam):
        y_ref[rows - count - 1 - t] = jnp.sum(gain * lam, axis=0)
        return decay * lam

    lam = lax.fori_loop(0, count, full, late_ref[...], unroll=8)
    end_ref[...] = lam
    lax.fori_loop(0, rows - count, empty, lam, unroll=8)


def scan_sums(decay_ref, start_ref, u_ref, g_ref, gh_ref, gm_ref):
    decay = decay_ref[...]

    def again(t, carry):
        h, m, gh, gm = carry
        h, m = decay * h + u_ref[t], decay * (m + h)
        g = g_ref[t]
        return h, m, gh + g * h, gm + g * m

    zero = jnp.zeros(decay.shape, F32)
    _, _, gh, gm = lax.fori_loop(0, u_ref.shape[0], again, (start_ref[...], zero, zero, zero))
    gh_ref[...] = gh
    gm_ref[...] = gm


def fast_body(
    tokens, lengths, attention_norm_gain, query_weight, key_weight, value_weight, output_weight,
    state_key_weight, state_value_weight, state_coefficient, state_rate, feedforward_norm_gain,
    hidden_weight, return_weight, cotangent,
):
    sequences, block_len, features = tokens.shape
    tp_count = lax.axis_size("tp")
    seq_index = lax.axis_index("seq")
    tp_index = lax.axis_index("tp")
    hidden_cols = hidden_weight.shape[1]
    cut = DH // 4
    wide = hidden_cols // 8
    length = lax.dynamic_index_in_dim(lengths, tp_index, 0, keepdims=False)
    place = jnp.stack([seq_index, tp_index, length]).astype(jnp.int32)

    column = pl.BlockSpec((features, DH), lambda i, place: (0, place[0] & 1))
    own_w, mine_w = timed(4)(
        pack_heads, place, (1,),
        [column] * 5 + [pl.BlockSpec((DH, features), lambda i, place: (place[0] & 1, 0))],
        [whole((4, 6, cut, features)), whole((6, cut, features))],
        [like((4, 6, cut, features)), like((6, cut, features))],
        tuple(map(far_away, (
            query_weight, key_weight, value_weight, state_key_weight, state_value_weight, output_weight
        ))),
        [pltpu.VMEM((DH, features), F32)],
    )
    own_m, mine_m = timed(5)(
        pack_hidden, place, (1,),
        [
            pl.BlockSpec((features, hidden_cols // 2), lambda i, place: (0, place[0] & 1)),
            pl.BlockSpec((hidden_cols // 2, features), lambda i, place: (place[0] & 1, 0)),
        ],
        [whole((4, 2, wide, features)), whole((2, wide, features))],
        [like((4, 2, wide, features)), like((2, wide, features))],
        (far_away(hidden_weight), far_away(return_weight)),
        [pltpu.VMEM((hidden_cols // 2, features), F32)],
    )

    def line_of(own):
        return jnp.stack([cycle(own, j) for j in range(1, tp_count)])

    line_w = line_of(mine_w)

    own_tokens = lax.dynamic_index_in_dim(tokens, tp_index, 0, keepdims=False)
    own_cot = lax.dynamic_index_in_dim(cotangent, tp_index, 0, keepdims=False)
    before = shifted(own_tokens[block_len - CTX :], 1)
    positions = seq_index * block_len - CTX + jnp.arange(block_len + CTX)
    live = ((positions < length) & (positions >= 0)).astype(F32)[:, None]
    x = (normalize(own_tokens.astype(F32))[0] * attention_norm_gain).astype(BF16)
    x_other = flip(x, 1)
    grad_out = (own_cot.astype(F32) * live[CTX:]).astype(BF16)
    grad_out_other = flip(grad_out, 1)
    early = (normalize(before.astype(F32))[0] * attention_norm_gain).astype(BF16)
    signal = tiles(
        jnp.concatenate([early, x[: block_len - CTX]]).astype(F32) * live[:block_len]
    )

    states = state_rate.shape[1]
    channels = state_rate.shape[0]
    both = jnp.stack([state_rate, state_coefficient]).reshape(1, -1, 128)
    devices = features // channels
    both = lax.all_to_all(
        jnp.broadcast_to(both, (devices,) + both.shape[1:]), ("seq", "tp"), 0, 0
    )
    both = after(both, line_w)
    both = jnp.transpose(both.reshape(devices, 2, channels, states), (1, 3, 0, 2))
    both = both.reshape(2, states, features // 128, 128)
    rate, gain = both[0], both[1]
    grid = rate.shape
    spans = [1, block_len - CTX] + [block_len * m for m in (1, 2, 3, 6)]
    decay, tail_power, *blocks = call(
        partial(powers, spans), [(grid, F32)] * len(spans), rate, us=1
    )
    block_power = dict(zip((1, 2, 3, 6), blocks))

    def plane_of(line, by_x, by_y, half):
        return [line, by_x, by_y, flip(by_y[:, :half], 2), flip(by_x[:, half:], 4)]

    near_w = flip(line_w, 2), flip(line_w, 4)
    far_w = plane_of(line_w, *near_w, 3)
    line_m = line_of(after(mine_m, line_w))
    near_m = flip(after(line_m, *near_w), 2), flip(after(line_m, *near_w), 4)
    far_m = plane_of(line_m, *near_m, 1)
    far_m[3:] = [value[:, 0] for value in far_m[3:]]

    local_state, local_moment = call(
        scan_in, [(grid, F32)] * 2, decay, after(signal, line_w, own_m, x_other, grad_out_other), us=8
    )
    start = states_around(after(local_state, *near_w), block_power, 1, 1)
    (context,) = call(scan_out, [((CTX,) + grid[1:], F32)], decay, gain, start, signal[:CTX], us=3)
    context = context.reshape(CTX, features).astype(BF16)
    context_other = flip(context, 1)
    rows = 2 * block_len
    slots = tp_count
    own_spec = whole((4, 6, cut, features))

    def slot_spec(*shape):
        return pl.BlockSpec(
            (1, *shape, features),
            lambda j, place: (jnp.maximum(j - 1, 0),) + (0,) * (len(shape) + 1),
        )

    weight_specs = [own_spec] + [slot_spec(6, cut)] * 3 + [slot_spec(3, cut)] * 2
    weights = (own_w, *far_w)
    full = whole((block_len, features))
    ctx_spec = whole((CTX, features))
    head = lambda n, width: pl.BlockSpec((n, width), lambda j, place: (0, j))
    lse_spec = pl.BlockSpec((1, rows, 1), lambda j, place: (j, 0, 0))
    q, k, v = timed(8)(
        project, place, (slots,),
        [full] * 2 + weight_specs,
        [head(rows, DH)] * 3,
        [like((rows, slots * DH))] * 3,
        (x, x_other, *weights),
        [pltpu.VMEM((3, DH, features), BF16)],
    )
    attended = timed(20)(
        attend, place, (slots,),
        [ctx_spec] * 2 + weight_specs + [head(rows, DH)] * 3,
        [full] * 2 + [head(2 * CTX, 2 * DH), head(rows, DH), lse_spec],
        [like((block_len, features), F32), like((block_len, features))]
        + [like((2 * CTX, slots * 2 * DH)), like((rows, slots * DH)), like((slots, rows, 1), F32)],
        (after(context, line_m), context_other, *weights, q, k, v),
        [
            pltpu.VMEM((3, DH, features), BF16),
            pltpu.VMEM((2, CTX + block_len, DH), BF16),
            pltpu.VMEM((2, CTX + block_len, DH), BF16),
            pltpu.VMEM((rows, features), F32),
        ],
    )
    part, part_other, state, mix, lse = attended
    group = 256
    steps = block_len // group
    row_spec = pl.BlockSpec((group, features), lambda i, place: (i, 0))
    seq_spec = pl.BlockSpec((1, group, features), lambda i, place: (place[1], i, 0))
    gain_spec = whole((1, features))
    mid_gain = feedforward_norm_gain.reshape(1, -1)
    residual, m = timed(4)(
        middle, place, (steps,),
        [seq_spec, row_spec, row_spec, gain_spec], [row_spec] * 2,
        [like((block_len, features), F32), like((block_len, features))],
        (tokens, part, after(flip(part_other, 1), *near_m), mid_gain),
    )
    m_other = flip(m, 1)

    chunk = 4 * wide
    def fixed(shape):
        return pl.BlockSpec(shape, lambda *_: (0,) * len(shape), pipeline_mode=pl.Buffered(1))

    def own_spec_of(count, first):
        return pl.BlockSpec((1, count, wide, features), lambda p, place: (p + first, 0, 0, 0))

    def feeding(first, count, far, far_specs, earlier):
        return timed(4 * count)(
            partial(feed_in, first), place, (count,),
            [full] * 2 + [own_spec_of(1, first)] + far_specs,
            [head(rows, chunk)] * 2,
            [like((rows, count * chunk))] * 2,
            (after(m, *earlier), m_other, own_m, *far),
            [pltpu.VMEM((chunk, features), BF16)],
        )

    act_a, slope_a = feeding(0, 3, far_m[:3], [fixed((3, 1, wide, features))] * 3, ())
    act_b, slope_b = feeding(3, 1, far_m[3:4], [fixed((3, wide, features))], (act_a,))
    early = pl.BlockSpec((rows, chunk), lambda p, place: (0, jnp.minimum(p, 2)))
    last = fixed((rows, chunk))
    mlp, mlp_other, mid, mid_other, pre = timed(21)(
        feed_out, place, (4,),
        [full] * 2 + [own_spec_of(2, 0)] + [fixed((3, 2, wide, features))] * 3
        + [fixed((3, wide, features))] * 2 + [early] * 2 + [last] * 2,
        [full] * 4 + [head(rows, chunk)],
        [like((block_len, features), F32), like((block_len, features))] * 2
        + [like((rows, 4 * chunk))],
        (grad_out, grad_out_other, own_m, *far_m, act_a, slope_a, act_b, slope_b),
        [pltpu.VMEM((chunk, features), BF16)] * 2 + [pltpu.VMEM((rows, features), F32)] * 2,
    )
    mid_got, mlp_got = flip(mid_other, 1), flip(mlp_other, 1)
    def hidden_grads(keeps, keep_at, rows_of, parts, part_specs):
        def spec(at):
            return pl.BlockSpec(
                (1, slots, wide, features), lambda p, place: (at(p), 0, 0, 0)
            )

        return timed(8)(
            partial(feed_weights, keeps), place, (4,),
            [full] * 2 + part_specs,
            [spec(keep_at), spec(lambda p: jnp.maximum(p - 2, 0))],
            [like((2, slots, wide, features))] * 2,
            (*rows_of, *map(far_away, parts)),
        )

    keep_r, send_r = hidden_grads(
        (0, 1), lambda p: jnp.minimum(p, 1), (grad_out, grad_out_other),
        (after(act_a, pre), act_b), [early, last],
    )
    mlp_got = after(mlp_got, keep_r)
    mid_got = after(mid_got, keep_r)
    (output,) = timed(3)(
        finish, place, (steps,),
        [row_spec] * 3, [row_spec], [like((block_len, features))], (residual, mlp, mlp_got),
    )
    output_all = lax.all_gather(output, "tp")
    resid, resid_b, sums_mid = timed(5)(
        middle_back, place, (steps,),
        [row_spec] * 3 + [seq_spec, gain_spec], [row_spec] * 2 + [gain_spec],
        [
            like((block_len, features), F32), like((block_len, features)),
            like((1, features), F32),
        ],
        (after(residual, output), mid, mid_got, cotangent, mid_gain),
    )
    resid_other = flip(resid_b, 1)
    keep_h, send_h = hidden_grads(
        (0, 2), lambda p: p // 2, (m, m_other), (after(pre, resid_b),), [head(rows, chunk)]
    )

    grad_in, grad_in_other, grad_ctx, grad_ctx_other, d, ds = timed(27)(
        attend_back, place, (slots,),
        [full] * 2 + weight_specs + [head(rows, DH)] * 3 + [head(2 * CTX, 2 * DH), lse_spec],
        [full] * 2 + [ctx_spec] * 2 + [head(rows, 3 * DH), head(2 * CTX, 2 * DH)],
        [
            like((block_len, features), F32), like((block_len, features)),
            like((CTX, features), F32), like((CTX, features)),
            like((rows, slots * 3 * DH)), like((2 * CTX, slots * 2 * DH)),
        ],
        (after(resid_b, keep_h), resid_other, *map(far_away, weights), q, k, v, state, lse),
        [
            pltpu.VMEM((6, DH, features), BF16),
            pltpu.VMEM((2, CTX + block_len, DH), BF16),
            pltpu.VMEM((2, CTX + block_len, DH), BF16),
            pltpu.VMEM((2, block_len, DH), BF16),
            pltpu.VMEM((2, CTX + block_len, DH), F32),
            pltpu.VMEM((2, CTX + block_len, DH), F32),
            pltpu.VMEM((rows, features), F32),
            pltpu.VMEM((2 * CTX, features), F32),
        ],
    )
    grad_ctx_got = flip(grad_ctx_other, 1)
    grad_in_got = flip(grad_in_other, 1)
    part_spec = pl.BlockSpec((2, 1, 3, cut, features), lambda j, place: (0, j, 0, 0, 0))
    keep_a, send_a, keep_b, send_b = timed(10)(
        attend_weights, place, (slots,),
        [full] * 2 + [ctx_spec] * 2 + [full] * 2
        + [head(rows, 3 * DH), head(2 * CTX, 2 * DH), head(rows, DH)],
        [part_spec] * 4,
        [like((2, slots, 3, cut, features))] * 4,
        (x, x_other, context, context_other, resid_b, resid_other, d, ds, mix),
    )

    got_r = flip(after(send_r, resid_b), 4)
    got_h = flip(after(send_h, resid_b), 2)
    near_h, away_h = add(keep_h[0], got_h[0]), add(keep_h[1], got_h[1])
    near_r, away_r = add(keep_r[0], got_r[0]), add(keep_r[1], got_r[1])
    grad_context = (grad_ctx + grad_ctx_got.astype(F32)).astype(BF16)
    grad_conv = tiles(after(grad_context, got_r, got_h))
    grad_later = tiles(shifted(grad_context, -1))
    (local_back,) = call(scan_back_in, [(grid, F32)], decay, grad_conv)
    late = tail_power * states_around(local_back, block_power, -1, 2, keep_a, away_h, away_r)
    grad_signal, end = call(
        scan_rows, [((block_len,) + grid[1:], F32), (grid, F32)], decay, gain, late, grad_later
    )
    grad_signal = grad_signal.reshape(block_len, features).astype(BF16)
    grad_tokens, sums_in = timed(5)(
        first_back, place, (steps,),
        [seq_spec] + [row_spec] * 4 + [gain_spec], [row_spec, gain_spec],
        [like((block_len, features)), like((1, features), F32)],
        (tokens, grad_in, grad_in_got, grad_signal, after(resid, output_all), attention_norm_gain.reshape(1, -1)),
    )

    lefts, rights = line_steps(grad_tokens)
    line = [grad_tokens] + [
        jnp.where(tp_index >= j, lefts[j], rights[slots - j]) for j in range(1, slots)
    ]
    line = jnp.stack(line)
    tokens_all = jnp.stack(
        [
            lax.dynamic_index_in_dim(line, (tp_index - b) % slots, 0, keepdims=False)
            for b in range(sequences)
        ]
    ).astype(F32)
    grad_gain, grad_moment = call(
        scan_sums, [(grid, F32)] * 2, decay, after(start, lefts[2], rights[2]), signal[:CTX], grad_conv
    )
    end_moment = block_len * block_power[1] * start + local_moment
    grad_rate = -gain * (grad_moment + end * end_moment)

    def regather(total):
        held = [total, flip(total, 2), flip(total, 4), flip(total, 6)]
        return held + [flip(value, 1) for value in held]

    ready = (late, grad_later)
    more_h, more_r = flip(after(away_h, *ready), 4), flip(after(away_r, *ready), 2)
    more_h, more_r = after(more_h, grad_tokens), after(more_r, grad_tokens)
    got_a = flip(after(send_a, more_h, more_r), 2)
    got_b = flip(after(send_b, more_h, more_r), 4)
    pairs = (near_h, more_h), (near_r, more_r)
    total_m = line_reduce(
        [jnp.stack([add(a[j], b[j]) for a, b in pairs]) for j in range(slots)],
        [(lefts[1], rights[1])] + [()] * (slots - 2),
    )
    near_a, away_a = add(keep_a[0], got_a[0]), add(keep_a[1], got_a[1])
    near_b, away_b = add(keep_b[0], got_b[0]), add(keep_b[1], got_b[1])
    pairs = (near_a, flip(away_a, 4)), (near_b, flip(away_b, 2))
    total_a = line_reduce(
        [jnp.stack([add(a[j], b[j]) for a, b in pairs]) for j in range(slots)],
        [()] * (slots - 2) + [(total_m,)],
    )
    pieces_m = regather(total_m)
    pieces_a = regather(total_a.reshape(6, cut, features))
    grad_hidden, grad_return = timed(5)(
        unpack_hidden, place, (1,),
        [whole((2, wide, features))] * 8,
        [whole((features, hidden_cols)), whole((hidden_cols, features))],
        [like((features, hidden_cols), F32), like((hidden_cols, features), F32)],
        pieces_m,
    )
    grad_q, grad_k, grad_v, grad_o, grad_sk, grad_sv = timed(5)(
        unpack_heads, place, (1,),
        [whole((6, cut, features))] * 8,
        [whole((features, 2 * DH))] * 3 + [whole((2 * DH, features))] + [whole((features, 2 * DH))] * 2,
        [like((features, 2 * DH), F32)] * 3
        + [like((2 * DH, features), F32)]
        + [like((features, 2 * DH), F32)] * 2,
        pieces_a,
        [pltpu.VMEM((2 * DH, features), F32)],
    )

    small = jnp.stack([grad_gain, grad_rate]).reshape(2, states, devices, channels)
    small = jnp.transpose(small, (2, 3, 0, 1)).reshape(devices, -1, 128)
    sums = jnp.concatenate([sums_in, sums_mid]).reshape(1, -1, 128)
    sums = jnp.broadcast_to(sums, (devices,) + sums.shape[1:])
    count = small.shape[1]
    small = jnp.sum(
        lax.all_to_all(
            after(jnp.concatenate([small, sums], axis=1), total_a), ("seq", "tp"), 0, 0
        ),
        axis=0,
    )
    kernel_grads = small[:count].reshape(channels, 2, states)
    gains = small[count:].reshape(2, features)

    return (
        output_all, tokens_all, gains[0], grad_q, grad_k, grad_v, grad_o, grad_sk, grad_sv,
        kernel_grads[:, 0], kernel_grads[:, 1], gains[1], grad_hidden, grad_return,
    )


def choose(tokens, *others):
    query_weight = others[2]
    fits = (
        lax.axis_size("seq") == 8
        and lax.axis_size("tp") == tokens.shape[0]
        and query_weight.shape[1] == 2 * DH
        and others[11].shape[1] % 1024 == 0
        and tokens.shape[1] % 512 == 0
        and tokens.shape[2] == 1024
    )
    return (fast_body if fits else body)(tokens, *others)


def solution(mesh):
    rows = P(None, "seq", None)
    columns = P(None, "tp")
    heads = P("tp", None)
    channels = P(("seq", "tp"), None)
    return jax.shard_map(
        choose,
        mesh=mesh,
        in_specs=(
            rows, P(), P(), columns, columns, columns, heads, columns, columns,
            channels, channels, P(), columns, heads, rows,
        ),
        out_specs=(
            rows, rows, P(), columns, columns, columns, heads, columns, columns,
            channels, channels, P(), columns, heads,
        ),
        check_vma=False,
    )
```
